32 devices in a mesh: group: 2 (over x), row: 4 (over y, core), tilt: 4 (over z).
Axes of the slice: x: 2, y: 2, z: 4, core: 2. Of those that a mesh axis runs over, the one named last changes fastest.
Arguments:
- projections: bfloat16 [8, 256, 2048], P(('group', 'tilt'), 'row'), parts along dimension 0, may hold values from -6 to 6
- tilt_angle: float32 [8], P('group'), parts along dimension 0, may hold values from -1.05 to 1.05
- band_start: int32 [8, 4, 4], P('group'), parts along dimension 0, may hold values from 0 to 1792
- defocus: int32 [8, 4], P('group'), parts along dimension 0, may hold values from 60 to 239
Outputs:
- volume: bfloat16 [128, 256, 512], P(('group', 'tilt'), 'row'), parts along dimension 0
The draws below stay inside these ranges and needn't reach their ends.
There are 2 independent parts, one for each index of `group`. The reference program is written for one: setup_inputs(seed, part) draws one part's arguments, and reference() takes and returns one part's arrays. A program takes and returns all parts, laid end to end along the dimension named above; each array names one. Nothing has to cross between parts.
All inputs are finite; a program needn't handle non-finite values.
Results may differ from the reference program's by a relative error of at most 0.0061.
Values may be sent and summed in bfloat16 or wider, within the bound.
No kernel may reach another device: no remote copies, remote signals or barrier semaphores. Data moves between devices by JAX's collectives and lax.ppermute only.
A program may use at most 128 MiB of HBM per device.

```python
import math
import jax
import jax.numpy as jnp
from jax import lax

U = 2048
SLAB = 16
SLABS = 4
XBW = 128
BAND = 256
XBLK = 4
SLICES = 64
TILTS = 4
R = 256


def with_ends(array, own_key, low, high):
    spot = [jax.random.randint(jax.random.fold_in(own_key, axis), (), 0, length) for axis, length in enumerate(array.shape)]
    longest = array.shape.index(max(array.shape))
    neighbour = spot[:longest] + [(spot[longest] + 1) % array.shape[longest]] + spot[longest + 1:]
    return array.at[tuple(spot)].set(low).at[tuple(neighbour)].set(high)


def level_of(key, dims, shards, least, high):
    level, own = 1.0, jax.random.fold_in(key, 6)
    for position, blocks in shards:
        heights = jnp.exp(jax.random.uniform(jax.random.fold_in(own, position), (blocks,), jnp.float32, least / len(shards), high / len(shards)))
        level = level * jnp.repeat(heights, dims[position] // blocks).reshape([-1 if axis == position else 1 for axis in range(len(dims))])
    return level


def centred(key, shape, deviation, most, pieces=(), held_as=jnp.bfloat16):
    level = level_of(key, shape, pieces, -0.22, 0.18) if pieces else 1.0
    drawn = jax.random.normal(key, shape, jnp.float32) * deviation * level
    return jnp.minimum(jnp.maximum(drawn, -most), most).astype(held_as)


def setup_inputs(seed: int = 0, part: int = 0) -> dict:
    key_list = jax.random.split(jax.random.key(seed), 5)
    own_keys = jax.random.split(jax.random.fold_in(key_list[4], part), 5)
    return {
        "projections": centred(own_keys[0], (TILTS, R, U), 1.0, 6.0, ((0, 4), (1, 4))),
        "tilt_angle": jnp.clip(jax.random.uniform(own_keys[1], (TILTS,), jnp.float32, -1.05, 1.05), -1.05, 1.05),
        "band_start": with_ends(jax.random.randint(own_keys[2], (TILTS, SLABS, XBLK), 0, U - BAND + 1), jax.random.fold_in(own_keys[2], 1), 0, U - BAND).astype(jnp.int32),
        "defocus": with_ends(jax.random.randint(own_keys[3], (TILTS, SLABS), 60, 240), jax.random.fold_in(own_keys[3], 1), 60, 239).astype(jnp.int32),
    }


def ramp_filter(first_frequency, length, full_length):
    frequency = first_frequency + jnp.arange(length, dtype=jnp.int32)
    folded = jnp.minimum(frequency, full_length - frequency).astype(jnp.float32)
    return (folded + 0.5) / (0.5 * full_length)

def triangle_kernel_weights(angles, offset):
    column = jnp.arange(XBW, dtype=jnp.float32)
    tap_index = jnp.arange(BAND, dtype=jnp.float32)
    centre = 0.5 * XBW + column[None, :] * jnp.cos(angles)[:, None] + offset * jnp.sin(angles)[:, None]
    return jnp.maximum(0.0, 1.0 - jnp.abs(tap_index[None, :, None] - centre[:, None, :])).astype(jnp.bfloat16)

def cut_patches(images, starts):

    def one_tilt(one_image, tilt_starts):
        return jax.vmap(lambda start_col: lax.dynamic_slice_in_dim(one_image, start_col.astype(jnp.int32), BAND, 1))(tilt_starts)
    return jax.vmap(one_tilt)(images, starts)

def reference(projections, tilt_angle, band_start, defocus):
    ramp_gain = ramp_filter(0, U, U)
    column_position_index = jnp.arange(U, dtype=jnp.int32)
    col_fold = jnp.minimum(column_position_index, U - column_position_index)
    row_index = jnp.arange(R, dtype=jnp.int32)
    row_fold = jnp.minimum(row_index, R - row_index)

    def apply_phase_correction(inputs):
        one_image, one_defocus = inputs
        spec = jnp.fft.fft2(one_image.astype(jnp.float32))
        col_cycles = col_fold[None, None, :] * col_fold[None, None, :] * one_defocus[:, None, None] // (U * U)
        row_cycles = row_fold[None, :, None] * row_fold[None, :, None] * one_defocus[:, None, None] // (R * R)
        flip = (col_cycles + row_cycles) % 2
        filters = (1.0 - 2.0 * flip.astype(jnp.float32)) * ramp_gain[None, None, :]
        image_out = jnp.real(jnp.fft.ifft2(filters * spec[None]))
        return image_out.astype(jnp.bfloat16)
    corrected = lax.map(apply_phase_correction, (projections, defocus))
    factor = 1.0 / math.sqrt(TILTS)

    def single_section(slice_index):
        slab_index = slice_index // SLAB
        local_slice = (slice_index % SLAB).astype(jnp.float32)
        images = lax.dynamic_index_in_dim(corrected, slab_index, 1, keepdims=False)
        starts = lax.dynamic_index_in_dim(band_start, slab_index, 1, keepdims=False)
        patches = cut_patches(images, starts).astype(jnp.float32)
        weights = triangle_kernel_weights(tilt_angle, local_slice - 0.5 * (SLAB - 1)).astype(jnp.float32)
        summed = jnp.einsum('tbyj,tjx->ybx', patches, weights)
        return (factor * summed.reshape(summed.shape[0], -1)).astype(jnp.bfloat16)
    return lax.map(single_section, jnp.arange(SLICES, dtype=jnp.int32))
```

```python
import functools
import math

import jax
import jax.numpy as jnp
import numpy as np
from jax import lax
from jax.experimental import pallas as pl
from jax.experimental.pallas import tpu as pltpu
from jax.sharding import PartitionSpec as P

SLAB = 16
XBW = 128
BAND = 256
XBLK = 4
SLICES = 64
RADIX = 8
WINDOW = BAND + 128


def column_blocks(columns):
    size = columns // RADIX
    return [(0, size), (size, size)] + [(2 * size * j, 2 * size) for j in (1, 2, 3)]


def packed_frequencies(columns):
    size = columns // RADIX
    half = size // 2
    parts = [RADIX * np.arange(half + 1), RADIX * np.arange(1, half)]
    parts += [RADIX * np.arange(half) + 4] * 2
    for j in (1, 2, 3):
        parts += [RADIX * np.arange(size) + j] * 2
    freq = np.concatenate(parts)
    count = np.where((freq == 0) | (freq == columns // 2), 1.0, 2.0)
    return np.minimum(freq, columns - freq), count


def column_tables(columns):
    size = columns // RADIX
    half = size // 2
    u = np.arange(size)[:, None]

    def angles(freq):
        return 2.0 * np.pi * ((u * freq[None, :]) % columns) / columns

    k0, s0 = RADIX * np.arange(half + 1), RADIX * np.arange(1, half)
    k4 = RADIX * np.arange(half) + 4
    m0 = np.concatenate([np.cos(angles(k0)), -np.sin(angles(s0))], 1)
    m4 = np.concatenate([np.cos(angles(k4)), -np.sin(angles(k4))], 1)
    forward, backward = [np.concatenate([m0, m4])], [np.concatenate([m0.T, m4.T])]
    for j in (1, 2, 3):
        t = angles(RADIX * np.arange(size) + j)
        m = np.block([[np.cos(t), -np.sin(t)], [np.sin(t), np.cos(t)]])
        forward.append(m)
        backward.append(m.T)
    forward, backward = np.concatenate(forward, 1), np.concatenate(backward, 1)
    high = forward.astype(jnp.bfloat16)
    low = (forward - high.astype(np.float64)).astype(jnp.bfloat16)
    return high, low, backward.astype(jnp.bfloat16)


def row_table(full_rows):
    half = full_rows // 2
    y = np.arange(full_rows)[:, None]
    freq = np.concatenate([np.arange(half + 1), np.arange(1, half)])
    angle = 2.0 * np.pi * (y * freq[None, :] % full_rows) / full_rows
    waves = np.where(np.arange(full_rows)[None, :] <= half, np.cos(angle), np.sin(angle))
    return waves, freq, np.where((freq == 0) | (freq == half), 1.0, 2.0)


def table_slices(columns):
    size = columns // RADIX
    places = column_blocks(columns)
    out = [(places[0], slice(0, size), slice(0, size)), (places[1], slice(size, 2 * size), slice(0, size))]
    for i, place in enumerate(places[2:]):
        first = size + 2 * size * i
        out.append((place, slice(0, 2 * size), slice(first, first + 2 * size)))
    return out


def filter_kernel(slots, row_blocks, meta, a_ref, gain_ref, high_ref, low_ref, back_ref, *refs):
    block_refs = refs[:row_blocks]
    out_refs = refs[row_blocks : row_blocks + slots]
    zhi, zlo, spec, turned = refs[row_blocks + slots :]
    rows, columns = block_refs[0].shape
    size = columns // RADIX
    full_rows = rows * row_blocks
    row_index = meta[0]
    root = math.sqrt(0.5)

    for distance in range(row_blocks):
        source = block_refs[distance]
        first_row = (row_index ^ distance) * rows

        def butterfly(step, carry):
            here = pl.ds(pl.multiple_of(step * 16, 16), 16)
            there = pl.ds(pl.multiple_of(first_row + step * 16, 16), 16)
            x = [source[here, m * size : (m + 1) * size].astype(jnp.float32) for m in range(8)]
            p0, p1, p2, p3 = (x[m] + x[m + 4] for m in range(4))
            q0, q1, q2, q3 = (x[m] - x[m + 4] for m in range(4))
            e, f = p0 + p2, p1 + p3
            g, h = root * (q1 - q3), root * (q1 + q3)
            z = [e + f, e - f, q0 + g, -q2 - h, p0 - p2, p3 - p1, q0 - g, q2 - h]
            for i in range(8):
                top = z[i].astype(jnp.bfloat16)
                zhi[there, i * size : (i + 1) * size] = top
                zlo[there, i * size : (i + 1) * size] = (z[i] - top.astype(jnp.float32)).astype(jnp.bfloat16)
            return carry

        lax.fori_loop(0, rows // 16, butterfly, 0)

    chunk = min(full_rows, 256)
    tables = table_slices(columns)
    for (first, width), table_rows, table_columns in tables:
        high, low = high_ref[table_rows, table_columns], low_ref[table_rows, table_columns]
        for c in range(full_rows // chunk):
            here = slice(c * chunk, (c + 1) * chunk)
            top, rest = zhi[here, first : first + width], zlo[here, first : first + width]
            total = jnp.dot(top, high, preferred_element_type=jnp.float32)
            total += jnp.dot(top, low, preferred_element_type=jnp.float32)
            total += jnp.dot(rest, high, preferred_element_type=jnp.float32)
            spec[here, first : first + width] = total.astype(jnp.bfloat16)

    row_filter = a_ref[...]
    for (first, width), table_rows, table_columns in tables:
        there = slice(first, first + width)
        y = jnp.dot(row_filter, spec[:, there], preferred_element_type=jnp.float32)
        filtered = [
            (y[slot * rows : (slot + 1) * rows] * gain_ref[slot : slot + 1, there]).astype(jnp.bfloat16)
            for slot in range(slots)
        ]
        turned[:, there] = jnp.dot(
            jnp.concatenate(filtered, 0), back_ref[table_rows, table_columns], preferred_element_type=jnp.float32
        )

    def inverse_butterfly(step, carry):
        here = pl.ds(pl.multiple_of(step * 16, 16), 16)
        z0, z4, r1, i1, r2, i2, r3, i3 = (turned[here, i * size : (i + 1) * size] for i in range(8))
        e, f = z0 + z4, z0 - z4
        a, b = r1 + r3, r1 - r3
        c, d = i1 + i3, i1 - i3
        even0, even2 = e + r2, e - r2
        odd1, odd3 = f - i2, f + i2
        g, h = root * (b - c), root * (b + c)
        out = [even0 + a, odd1 + g, even2 - d, odd3 - h, even0 - a, odd1 - g, even2 + d, odd3 + h]
        for m in range(8):
            turned[here, m * size : (m + 1) * size] = out[m]
        return carry

    lax.fori_loop(0, slots * rows // 16, inverse_butterfly, 0)

    for slot in range(slots):
        for block in range(XBLK):
            start = meta[1 + slot * XBLK + block]
            base = pl.multiple_of(jnp.minimum((start // 128) * 128, columns - WINDOW), 128)
            window = turned[slot * rows : (slot + 1) * rows, pl.ds(base, WINDOW)]
            shift = base - start
            shift = jnp.where(shift < 0, shift + WINDOW, shift)
            out_refs[slot][block] = pltpu.roll(window, shift, 1)[:, :BAND].astype(jnp.bfloat16)


def filtered_patches(meta, row_filters, gains, tables, blocks):
    slots, row_blocks = gains.shape[0], len(blocks)
    rows, columns = blocks[0].shape
    full_rows = rows * row_blocks
    vmem = pl.BlockSpec(memory_space=pltpu.VMEM)
    flops = 2 * columns * (3 * full_rows * columns // 4 + slots * rows * (full_rows + columns // 4))
    return pl.pallas_call(
        functools.partial(filter_kernel, slots, row_blocks),
        out_shape=[jax.ShapeDtypeStruct((XBLK, rows, BAND), jnp.bfloat16)] * slots,
        in_specs=[pl.BlockSpec(memory_space=pltpu.SMEM)] + [vmem] * (5 + row_blocks),
        out_specs=[vmem] * slots,
        scratch_shapes=[
            pltpu.VMEM((full_rows, columns), jnp.bfloat16),
            pltpu.VMEM((full_rows, columns), jnp.bfloat16),
            pltpu.VMEM((full_rows, columns), jnp.bfloat16),
            pltpu.VMEM((slots * rows, columns), jnp.float32),
        ],
        compiler_params=pltpu.CompilerParams(vmem_limit_bytes=40 * 2**20),
        cost_estimate=pl.CostEstimate(flops=flops, bytes_accessed=10 * 2**20, transcendentals=0),
        name="filter",
    )(meta, row_filters, gains, *tables, *blocks)


def interpolate_kernel(slots, factor, weights_ref, *refs):
    patch_refs, out_ref = refs[:slots], refs[slots]
    blocks, rows, taps = patch_refs[0].shape
    total = jnp.zeros((blocks * rows, weights_ref.shape[2]), jnp.float32)
    for slot in range(slots):
        total += jnp.dot(
            patch_refs[slot][...].reshape(blocks * rows, taps), weights_ref[slot], preferred_element_type=jnp.float32
        )
    for c in range(out_ref.shape[0]):
        for block in range(blocks):
            out_ref[c, :, block * XBW : (block + 1) * XBW] = (
                factor * total[block * rows : (block + 1) * rows, c * XBW : (c + 1) * XBW]
            ).astype(jnp.bfloat16)


def interpolated(weights, patches, factor):
    slots, taps, width = weights.shape
    blocks, rows, _ = patches[0].shape
    slices = width // XBW
    step = math.gcd(slices, 4)
    return pl.pallas_call(
        functools.partial(interpolate_kernel, slots, factor),
        grid=(slices // step,),
        out_shape=jax.ShapeDtypeStruct((slices, rows, blocks * XBW), jnp.bfloat16),
        in_specs=[pl.BlockSpec((slots, taps, step * XBW), lambda i: (0, 0, i))]
        + [pl.BlockSpec((blocks, rows, taps), lambda i: (0, 0, 0))] * slots,
        out_specs=pl.BlockSpec((step, rows, blocks * XBW), lambda i: (i, 0, 0)),
        compiler_params=pltpu.CompilerParams(vmem_limit_bytes=24 * 2**20),
        cost_estimate=pl.CostEstimate(
            flops=2 * blocks * rows * slots * taps * width, bytes_accessed=6 * 2**20, transcendentals=0
        ),
        name="interpolate",
    )(weights, *patches)


def exchange(array, axis, distance):
    count = lax.axis_size(axis)
    return lax.ppermute(array, axis, [(i, i ^ distance) for i in range(count)])


def per_device(projections, tilt_angle, band_start, defocus):
    _, rows, columns = projections.shape
    row_devices, tilt_devices = lax.axis_size("row"), lax.axis_size("tilt")
    full_rows = rows * row_devices
    row_index, tilt_index = lax.axis_index("row"), lax.axis_index("tilt")
    image = projections[0]

    blocks = {0: image}
    bit = row_devices // 2
    while bit:
        blocks.update({d ^ bit: exchange(block, "row", bit) for d, block in blocks.items()})
        bit //= 2

    slices_owned = SLICES // tilt_devices
    distances = jnp.arange(tilt_devices, dtype=jnp.int32)
    owners = tilt_index ^ distances
    slabs = owners * slices_owned // SLAB
    own_defocus = jnp.take(lax.dynamic_index_in_dim(defocus, tilt_index, 0, keepdims=False), slabs)
    own_starts = jnp.take(lax.dynamic_index_in_dim(band_start, tilt_index, 0, keepdims=False), slabs, axis=0)
    meta = jnp.concatenate([row_index[None].astype(jnp.int32), own_starts.reshape(-1)])

    row_waves, row_fold, row_count = row_table(full_rows)
    row_fold = jnp.asarray(row_fold, jnp.int32)
    row_cycles = row_fold * row_fold * own_defocus[:, None] // (full_rows * full_rows)
    row_sign = (1 - 2 * (row_cycles % 2)).astype(jnp.float32) * jnp.asarray(row_count / full_rows, jnp.float32)
    row_waves = jnp.asarray(row_waves, jnp.float32)
    own_waves = lax.dynamic_slice_in_dim(row_waves, row_index * rows, rows, 0)
    row_filters = lax.dot_general(
        (row_sign[:, None, :] * own_waves[None]).reshape(tilt_devices * rows, full_rows),
        row_waves,
        (((1,), (1,)), ((), ())),
        precision=lax.Precision.HIGHEST,
    ).astype(jnp.bfloat16)
    column_fold, count = packed_frequencies(columns)
    ramp = jnp.asarray(count * (column_fold + 0.5) / (0.5 * columns) / columns, jnp.float32)
    column_fold = jnp.asarray(column_fold, jnp.int32)
    column_cycles = column_fold * column_fold * own_defocus[:, None] // (columns * columns)
    gains = (1 - 2 * (column_cycles % 2)).astype(jnp.float32) * ramp

    tables = [jnp.asarray(t) for t in column_tables(columns)]
    sent = filtered_patches(meta, row_filters, gains, tables, [blocks[d] for d in range(row_devices)])
    patches = [sent[0]] + [exchange(sent[d], "tilt", d) for d in range(1, tilt_devices)]

    angles = jnp.take(tilt_angle, owners)
    local_first = tilt_index * slices_owned % SLAB
    offsets = (local_first + jnp.arange(slices_owned, dtype=jnp.int32)).astype(jnp.float32) - 0.5 * (SLAB - 1)
    column = jnp.arange(XBW, dtype=jnp.float32)
    centre = (
        0.5 * XBW
        + column[None, None, :] * jnp.cos(angles)[:, None, None]
        + offsets[None, :, None] * jnp.sin(angles)[:, None, None]
    ).reshape(tilt_devices, 1, slices_owned * XBW)
    tap = jnp.arange(BAND, dtype=jnp.float32)[None, :, None]
    weights = jnp.maximum(0.0, 1.0 - jnp.abs(tap - centre)).astype(jnp.bfloat16)
    return interpolated(weights, patches, 1.0 / math.sqrt(tilt_devices))


def solution(mesh):
    in_specs = (
        P(("group", "tilt"), "row", None),
        P("group"),
        P("group", None, None),
        P("group", None),
    )
    out_specs = P(("group", "tilt"), "row", None)
    return jax.shard_map(
        per_device, mesh=mesh, in_specs=in_specs, out_specs=out_specs, check_vma=False
    )
```

```python
import functools
import math

import jax
import jax.numpy as jnp
import numpy as np
from jax import lax
from jax.experimental import pallas as pl
from jax.experimental.pallas import tpu as pltpu
from jax.sharding import PartitionSpec as P

SLAB = 16
XBW = 128
BAND = 256
XBLK = 4
SLICES = 64
RADIX = 8
WINDOW = BAND + 128


def column_blocks(columns):
    size = columns // RADIX
    return [(0, size), (size, size)] + [(2 * size * j, 2 * size) for j in (1, 2, 3)]


def packed_frequencies(columns):
    size = columns // RADIX
    half = size // 2
    parts = [RADIX * np.arange(half + 1), RADIX * np.arange(1, half)]
    parts += [RADIX * np.arange(half) + 4] * 2
    for j in (1, 2, 3):
        parts += [RADIX * np.arange(size) + j] * 2
    freq = np.concatenate(parts)
    count = np.where((freq == 0) | (freq == columns // 2), 1.0, 2.0)
    return np.minimum(freq, columns - freq), count


def column_tables(columns):
    size = columns // RADIX
    half = size // 2
    u = np.arange(size)[:, None]

    def angles(freq):
        return 2.0 * np.pi * ((u * freq[None, :]) % columns) / columns

    k0, s0 = RADIX * np.arange(half + 1), RADIX * np.arange(1, half)
    k4 = RADIX * np.arange(half) + 4
    m0 = np.concatenate([np.cos(angles(k0)), -np.sin(angles(s0))], 1)
    m4 = np.concatenate([np.cos(angles(k4)), -np.sin(angles(k4))], 1)
    forward, backward = [np.concatenate([m0, m4])], [np.concatenate([m0.T, m4.T])]
    for j in (1, 2, 3):
        t = angles(RADIX * np.arange(size) + j)
        m = np.block([[np.cos(t), -np.sin(t)], [np.sin(t), np.cos(t)]])
        forward.append(m)
        backward.append(m.T)
    forward, backward = np.concatenate(forward, 1), np.concatenate(backward, 1)
    high = forward.astype(jnp.bfloat16)
    low = (forward - high.astype(np.float64)).astype(jnp.bfloat16)
    return high, low, backward.astype(jnp.bfloat16)


def row_table(full_rows):
    half = full_rows // 2
    y = np.arange(full_rows)[:, None]
    freq = np.concatenate([np.arange(half + 1), np.arange(1, half)])
    angle = 2.0 * np.pi * (y * freq[None, :] % full_rows) / full_rows
    waves = np.where(np.arange(full_rows)[None, :] <= half, np.cos(angle), np.sin(angle))
    return waves, freq, np.where((freq == 0) | (freq == half), 1.0, 2.0)


def table_slices(columns):
    size = columns // RADIX
    places = column_blocks(columns)
    out = [(places[0], slice(0, size), slice(0, size)), (places[1], slice(size, 2 * size), slice(0, size))]
    for i, place in enumerate(places[2:]):
        first = size + 2 * size * i
        out.append((place, slice(0, 2 * size), slice(first, first + 2 * size)))
    return out


def filter_kernel(slots, row_blocks, meta, a_ref, gain_ref, high_ref, low_ref, back_ref, *refs):
    block_refs = refs[0]
    out_refs = refs[1 : 1 + slots]
    zhi, zlo, spec, turned = refs[1 + slots :]
    _, rows, columns = block_refs.shape
    size = columns // RADIX
    full_rows = rows * row_blocks
    root = math.sqrt(0.5)

    for distance in range(row_blocks):
        source = block_refs.at[distance]
        first_row = distance * rows

        def butterfly(step, carry):
            here = pl.ds(pl.multiple_of(step * 16, 16), 16)
            there = pl.ds(pl.multiple_of(first_row + step * 16, 16), 16)
            x = [source[here, m * size : (m + 1) * size].astype(jnp.float32) for m in range(8)]
            p0, p1, p2, p3 = (x[m] + x[m + 4] for m in range(4))
            q0, q1, q2, q3 = (x[m] - x[m + 4] for m in range(4))
            e, f = p0 + p2, p1 + p3
            g, h = root * (q1 - q3), root * (q1 + q3)
            z = [e + f, e - f, q0 + g, -q2 - h, p0 - p2, p3 - p1, q0 - g, q2 - h]
            for i in range(8):
                top = z[i].astype(jnp.bfloat16)
                zhi[there, i * size : (i + 1) * size] = top
                zlo[there, i * size : (i + 1) * size] = (z[i] - top.astype(jnp.float32)).astype(jnp.bfloat16)
            return carry

        lax.fori_loop(0, rows // 16, butterfly, 0)

    chunk = min(full_rows, 256)
    tables = table_slices(columns)
    for (first, width), table_rows, table_columns in tables:
        high, low = high_ref[table_rows, table_columns], low_ref[table_rows, table_columns]
        for c in range(full_rows // chunk):
            here = slice(c * chunk, (c + 1) * chunk)
            top, rest = zhi[here, first : first + width], zlo[here, first : first + width]
            total = jnp.dot(top, high, preferred_element_type=jnp.float32)
            total += jnp.dot(top, low, preferred_element_type=jnp.float32)
            total += jnp.dot(rest, high, preferred_element_type=jnp.float32)
            spec[here, first : first + width] = total.astype(jnp.bfloat16)

    row_filter = a_ref[...]
    for (first, width), table_rows, table_columns in tables:
        there = slice(first, first + width)
        y = jnp.dot(row_filter, spec[:, there], preferred_element_type=jnp.float32)
        filtered = [
            (y[slot * rows : (slot + 1) * rows] * gain_ref[slot : slot + 1, there]).astype(jnp.bfloat16)
            for slot in range(slots)
        ]
        turned[:, there] = jnp.dot(
            jnp.concatenate(filtered, 0), back_ref[table_rows, table_columns], preferred_element_type=jnp.float32
        )

    def inverse_butterfly(step, carry):
        here = pl.ds(pl.multiple_of(step * 16, 16), 16)
        z0, z4, r1, i1, r2, i2, r3, i3 = (turned[here, i * size : (i + 1) * size] for i in range(8))
        e, f = z0 + z4, z0 - z4
        a, b = r1 + r3, r1 - r3
        c, d = i1 + i3, i1 - i3
        even0, even2 = e + r2, e - r2
        odd1, odd3 = f - i2, f + i2
        g, h = root * (b - c), root * (b + c)
        out = [even0 + a, odd1 + g, even2 - d, odd3 - h, even0 - a, odd1 - g, even2 + d, odd3 + h]
        for m in range(8):
            turned[here, m * size : (m + 1) * size] = out[m]
        return carry

    lax.fori_loop(0, slots * rows // 16, inverse_butterfly, 0)

    for slot in range(slots):
        for block in range(XBLK):
            start = meta[1 + slot * XBLK + block]
            base = pl.multiple_of(jnp.minimum((start // 128) * 128, columns - WINDOW), 128)
            window = turned[slot * rows : (slot + 1) * rows, pl.ds(base, WINDOW)]
            shift = base - start
            shift = jnp.where(shift < 0, shift + WINDOW, shift)
            out_refs[slot][block] = pltpu.roll(window, shift, 1)[:, :BAND].astype(jnp.bfloat16)


def filtered_patches(meta, row_filters, gains, tables, blocks):
    slots = gains.shape[0]
    row_blocks, rows, columns = blocks.shape
    full_rows = rows * row_blocks
    vmem = pl.BlockSpec(memory_space=pltpu.VMEM)
    flops = 2 * columns * (3 * full_rows * columns // 4 + slots * rows * (full_rows + columns // 4))
    return pl.pallas_call(
        functools.partial(filter_kernel, slots, row_blocks),
        out_shape=[jax.ShapeDtypeStruct((XBLK, rows, BAND), jnp.bfloat16)] * slots,
        in_specs=[pl.BlockSpec(memory_space=pltpu.SMEM)] + [vmem] * 6,
        out_specs=[vmem] * slots,
        scratch_shapes=[
            pltpu.VMEM((full_rows, columns), jnp.bfloat16),
            pltpu.VMEM((full_rows, columns), jnp.bfloat16),
            pltpu.VMEM((full_rows, columns), jnp.bfloat16),
            pltpu.VMEM((slots * rows, columns), jnp.float32),
        ],
        compiler_params=pltpu.CompilerParams(vmem_limit_bytes=40 * 2**20),
        cost_estimate=pl.CostEstimate(flops=flops, bytes_accessed=10 * 2**20, transcendentals=0),
        name="filter",
    )(meta, row_filters, gains, *tables, blocks)


def interpolate_kernel(slots, factor, weights_ref, *refs):
    patch_refs, out_ref = refs[:slots], refs[slots]
    blocks, rows, taps = patch_refs[0].shape
    total = jnp.zeros((blocks * rows, weights_ref.shape[2]), jnp.float32)
    for slot in range(slots):
        total += jnp.dot(
            patch_refs[slot][...].reshape(blocks * rows, taps), weights_ref[slot], preferred_element_type=jnp.float32
        )
    for c in range(out_ref.shape[0]):
        for block in range(blocks):
            out_ref[c, :, block * XBW : (block + 1) * XBW] = (
                factor * total[block * rows : (block + 1) * rows, c * XBW : (c + 1) * XBW]
            ).astype(jnp.bfloat16)


def interpolated(weights, patches, factor):
    slots, taps, width = weights.shape
    blocks, rows, _ = patches[0].shape
    slices = width // XBW
    step = math.gcd(slices, 4)
    return pl.pallas_call(
        functools.partial(interpolate_kernel, slots, factor),
        grid=(slices // step,),
        out_shape=jax.ShapeDtypeStruct((slices, rows, blocks * XBW), jnp.bfloat16),
        in_specs=[pl.BlockSpec((slots, taps, step * XBW), lambda i: (0, 0, i))]
        + [pl.BlockSpec((blocks, rows, taps), lambda i: (0, 0, 0))] * slots,
        out_specs=pl.BlockSpec((step, rows, blocks * XBW), lambda i: (i, 0, 0)),
        compiler_params=pltpu.CompilerParams(vmem_limit_bytes=24 * 2**20),
        cost_estimate=pl.CostEstimate(
            flops=2 * blocks * rows * slots * taps * width, bytes_accessed=6 * 2**20, transcendentals=0
        ),
        name="interpolate",
    )(weights, *patches)


def exchange(array, axis, distance):
    count = lax.axis_size(axis)
    return lax.ppermute(array, axis, [(i, i ^ distance) for i in range(count)])


def per_device(projections, tilt_angle, band_start, defocus):
    _, rows, columns = projections.shape
    row_devices, tilt_devices = lax.axis_size("row"), lax.axis_size("tilt")
    full_rows = rows * row_devices
    row_index, tilt_index = lax.axis_index("row"), lax.axis_index("tilt")
    image = projections[0]

    blocks = lax.all_gather(image, "row")

    slices_owned = SLICES // tilt_devices
    distances = jnp.arange(tilt_devices, dtype=jnp.int32)
    owners = tilt_index ^ distances
    slabs = owners * slices_owned // SLAB
    own_defocus = jnp.take(lax.dynamic_index_in_dim(defocus, tilt_index, 0, keepdims=False), slabs)
    own_starts = jnp.take(lax.dynamic_index_in_dim(band_start, tilt_index, 0, keepdims=False), slabs, axis=0)
    meta = jnp.concatenate([row_index[None].astype(jnp.int32), own_starts.reshape(-1)])

    row_waves, row_fold, row_count = row_table(full_rows)
    row_fold = jnp.asarray(row_fold, jnp.int32)
    row_cycles = row_fold * row_fold * own_defocus[:, None] // (full_rows * full_rows)
    row_sign = (1 - 2 * (row_cycles % 2)).astype(jnp.float32) * jnp.asarray(row_count / full_rows, jnp.float32)
    row_waves = jnp.asarray(row_waves, jnp.float32)
    own_waves = lax.dynamic_slice_in_dim(row_waves, row_index * rows, rows, 0)
    row_filters = lax.dot_general(
        (row_sign[:, None, :] * own_waves[None]).reshape(tilt_devices * rows, full_rows),
        row_waves,
        (((1,), (1,)), ((), ())),
        precision=lax.Precision.HIGHEST,
    ).astype(jnp.bfloat16)
    column_fold, count = packed_frequencies(columns)
    ramp = jnp.asarray(count * (column_fold + 0.5) / (0.5 * columns) / columns, jnp.float32)
    column_fold = jnp.asarray(column_fold, jnp.int32)
    column_cycles = column_fold * column_fold * own_defocus[:, None] // (columns * columns)
    gains = (1 - 2 * (column_cycles % 2)).astype(jnp.float32) * ramp

    tables = [jnp.asarray(t) for t in column_tables(columns)]
    sent = filtered_patches(meta, row_filters, gains, tables, blocks)
    patches = [sent[0]] + [None] * (tilt_devices - 1)
    for d in sorted(range(1, tilt_devices), key=lambda d: -(d & -d)):
        patches[d] = exchange(sent[d], "tilt", d)

    angles = jnp.take(tilt_angle, owners)
    local_first = tilt_index * slices_owned % SLAB
    offsets = (local_first + jnp.arange(slices_owned, dtype=jnp.int32)).astype(jnp.float32) - 0.5 * (SLAB - 1)
    column = jnp.arange(XBW, dtype=jnp.float32)
    centre = (
        0.5 * XBW
        + column[None, None, :] * jnp.cos(angles)[:, None, None]
        + offsets[None, :, None] * jnp.sin(angles)[:, None, None]
    ).reshape(tilt_devices, 1, slices_owned * XBW)
    tap = jnp.arange(BAND, dtype=jnp.float32)[None, :, None]
    weights = jnp.maximum(0.0, 1.0 - jnp.abs(tap - centre)).astype(jnp.bfloat16)
    return interpolated(weights, patches, 1.0 / math.sqrt(tilt_devices))


def solution(mesh):
    in_specs = (
        P(("group", "tilt"), "row", None),
        P("group"),
        P("group", None, None),
        P("group", None),
    )
    out_specs = P(("group", "tilt"), "row", None)
    return jax.shard_map(
        per_device, mesh=mesh, in_specs=in_specs, out_specs=out_specs, check_vma=False
    )
```

```python
import functools
import math

import jax
import jax.numpy as jnp
import numpy as np
from jax import lax
from jax.experimental import pallas as pl
from jax.experimental.pallas import tpu as pltpu
from jax.sharding import PartitionSpec as P

SLAB = 16
XBW = 128
BAND = 256
XBLK = 4
SLICES = 64
RADIX = 8
WINDOW = BAND + 128
ROOT = math.sqrt(0.5)


def column_tables(columns):
    size = columns // RADIX
    half = size // 2
    u = np.arange(size)[:, None]

    def angles(freq):
        return 2.0 * np.pi * ((u * freq[None, :]) % columns) / columns

    k0, s0 = RADIX * np.arange(half + 1), RADIX * np.arange(1, half)
    k4 = RADIX * np.arange(half) + 4
    m0 = np.concatenate([np.cos(angles(k0)), -np.sin(angles(s0))], 1)
    m4 = np.concatenate([np.cos(angles(k4)), -np.sin(angles(k4))], 1)
    full = angles(RADIX * np.arange(size))
    waves = np.concatenate([np.cos(full), np.sin(full)], 1)
    ends = np.concatenate([m0, m4], 1)

    def split(table):
        high = table.astype(jnp.bfloat16)
        return high, (table - high.astype(np.float64)).astype(jnp.bfloat16)

    matrices = np.stack([*split(ends), *split(waves), np.concatenate([m0.T, m4.T], 1).astype(jnp.bfloat16)])
    freq = [np.concatenate([k0, s0]), np.concatenate([k4, k4])]
    turns = []
    for j in (1, 2, 3):
        freq += [RADIX * np.arange(size) + j] * 2
        angle = 2.0 * np.pi * np.arange(size) * j / columns
        turns += [np.cos(angle), np.sin(angle)]
    freq = np.stack(freq)
    count = np.where((freq == 0) | (freq == columns // 2), 1.0, 2.0)
    fold = np.minimum(freq, columns - freq)
    ramp = count * (fold + 0.5) / (0.5 * columns) / columns
    lines = np.concatenate([ramp, np.stack(turns + [np.zeros(size)] * 2)]).astype(np.float32)
    return matrices, lines, (fold * fold).astype(np.int32)


def row_tables(full_rows):
    half = full_rows // 2
    y = np.arange(full_rows)[:, None]
    freq = np.concatenate([np.arange(half + 1), np.arange(1, half)])
    angle = 2.0 * np.pi * (y * freq[None, :] % full_rows) / full_rows
    waves = np.where(np.arange(full_rows)[None, :] <= half, np.cos(angle), np.sin(angle))
    count = np.where((freq == 0) | (freq == half), 1.0, 2.0) / full_rows
    return waves.astype(np.float32), (freq * freq).astype(np.int32)[None], count.astype(np.float32)[None]


def flip_sign(squares, defocus, length):
    cycles = lax.div(squares * defocus, jnp.int32(length * length))
    return (1 - 2 * (cycles & 1)).astype(jnp.float32)


def column_kernel(slots, slices_owned, defocus, starts, image_ref, matrix_ref, lines_ref, squares_ref, *refs):
    out_refs = refs[:slots]
    image, matrix, zhi, zlo, ends, waves, turned, image_sem, matrix_sem = refs[slots:]
    rows, columns = image.shape
    size = columns // RADIX
    copies = [pltpu.make_async_copy(image_ref, image, image_sem)]
    copies += [pltpu.make_async_copy(matrix_ref.at[i], matrix.at[i], matrix_sem.at[i]) for i in range(5)]
    for copy in copies:
        copy.start()
    tilt = lax.axis_index("tilt")
    turns = [lines_ref[8 + i : 9 + i, :] for i in range(6)]
    copies[0].wait()

    def butterfly(step, carry):
        here = pl.ds(pl.multiple_of(step * 16, 16), 16)
        x = [image[here, m * size : (m + 1) * size].astype(jnp.float32) for m in range(8)]
        p0, p1, p2, p3 = (x[m] + x[m + 4] for m in range(4))
        q0, q1, q2, q3 = (x[m] - x[m + 4] for m in range(4))
        e, f = p0 + p2, p1 + p3
        g, h = ROOT * (q1 - q3), ROOT * (q1 + q3)
        z = [e + f, e - f]
        for j, (real, imag) in enumerate([(q0 + g, -q2 - h), (p0 - p2, p3 - p1), (q0 - g, q2 - h)]):
            c, s = turns[2 * j], turns[2 * j + 1]
            z += [real * c + imag * s, imag * c - real * s]
        for i in range(8):
            top = z[i].astype(jnp.bfloat16)
            zhi[i, here, :] = top
            zlo[i, here, :] = (z[i] - top.astype(jnp.float32)).astype(jnp.bfloat16)
        return carry

    lax.fori_loop(0, rows // 16, butterfly, 0)
    for copy in copies[1:5]:
        copy.wait()

    def product(first, count, table, here):
        top = zhi[first : first + count].reshape(count * rows, size)
        rest = zlo[first : first + count].reshape(count * rows, size)
        total = jnp.dot(top, matrix[table, :, here], preferred_element_type=jnp.float32)
        total += jnp.dot(top, matrix[table + 1, :, here], preferred_element_type=jnp.float32)
        return total + jnp.dot(rest, matrix[table, :, here], preferred_element_type=jnp.float32)

    spectrum = [product(0, 1, 0, slice(0, size)), product(1, 1, 0, slice(size, 2 * size))]
    mixed = product(2, 6, 2, slice(None))
    for j in range(3):
        real, imag = mixed[2 * j * rows : (2 * j + 1) * rows], mixed[(2 * j + 1) * rows : (2 * j + 2) * rows]
        spectrum += [real[:, :size] + imag[:, size:], imag[:, :size] - real[:, size:]]

    slabs = [(tilt ^ slot) * slices_owned // SLAB for slot in range(slots)]
    gains = [
        flip_sign(squares_ref[...], defocus[tilt, slabs[slot]], columns) * lines_ref[:8, :] for slot in range(slots)
    ]
    filtered = [
        jnp.concatenate(
            [(spectrum[i] * gains[slot][i : i + 1, :]).astype(jnp.bfloat16) for slot in range(slots)], 0
        )
        for i in range(8)
    ]
    copies[5].wait()
    for i in range(2):
        ends[i] = jnp.dot(filtered[i], matrix[4, :, i * size : (i + 1) * size], preferred_element_type=jnp.float32)
    for i in range(6):
        waves[i] = jnp.dot(filtered[2 + i], matrix[2], preferred_element_type=jnp.float32)

    def inverse_butterfly(step, carry):
        here = pl.ds(pl.multiple_of(step * 8, 8), 8)
        r, s = [], []
        for j in range(3):
            c, d = turns[2 * j], turns[2 * j + 1]
            real = waves[2 * j, here, :size] - waves[2 * j + 1, here, size:]
            imag = waves[2 * j, here, size:] + waves[2 * j + 1, here, :size]
            r.append(real * c - imag * d)
            s.append(real * d + imag * c)
        e, f = ends[0, here, :] + ends[1, here, :], ends[0, here, :] - ends[1, here, :]
        a, b, c, d = r[0] + r[2], r[0] - r[2], s[0] + s[2], s[0] - s[2]
        even0, even2, odd1, odd3 = e + r[1], e - r[1], f - s[1], f + s[1]
        g, h = ROOT * (b - c), ROOT * (b + c)
        out = [even0 + a, odd1 + g, even2 - d, odd3 - h, even0 - a, odd1 - g, even2 + d, odd3 + h]
        for m in range(8):
            turned[here, m * size : (m + 1) * size] = out[m]
        return carry

    lax.fori_loop(0, slots * rows // 8, inverse_butterfly, 0)

    for slot in range(slots):
        for block in range(XBLK):
            start = starts[tilt, slabs[slot], block]
            base = pl.multiple_of(jnp.minimum((start // 128) * 128, columns - WINDOW), 128)
            window = turned[slot * rows : (slot + 1) * rows, pl.ds(base, WINDOW)]
            shift = base - start
            shift = jnp.where(shift < 0, shift + WINDOW, shift)
            out_refs[slot][:, block * BAND : (block + 1) * BAND] = pltpu.roll(window, shift, 1)[:, :BAND].astype(
                jnp.bfloat16
            )


def column_filtered(slots, slices_owned, defocus, starts, image):
    rows, columns = image.shape
    size = columns // RADIX
    matrices, lines, squares = column_tables(columns)
    smem, vmem = pl.BlockSpec(memory_space=pltpu.SMEM), pl.BlockSpec(memory_space=pltpu.VMEM)
    away = pl.BlockSpec(memory_space=pl.ANY)
    return pl.pallas_call(
        functools.partial(column_kernel, slots, slices_owned),
        out_shape=[jax.ShapeDtypeStruct((rows, XBLK * BAND), jnp.bfloat16)] * slots,
        in_specs=[smem, smem, away, away, vmem, vmem],
        out_specs=[vmem] * slots,
        scratch_shapes=[
            pltpu.VMEM((rows, columns), jnp.bfloat16),
            pltpu.VMEM(matrices.shape, jnp.bfloat16),
            pltpu.VMEM((8, rows, size), jnp.bfloat16),
            pltpu.VMEM((8, rows, size), jnp.bfloat16),
            pltpu.VMEM((2, slots * rows, size), jnp.float32),
            pltpu.VMEM((6, slots * rows, 2 * size), jnp.float32),
            pltpu.VMEM((slots * rows, columns), jnp.float32),
            pltpu.SemaphoreType.DMA,
            pltpu.SemaphoreType.DMA((5,)),
        ],
        compiler_params=pltpu.CompilerParams(vmem_limit_bytes=40 * 2**20),
        cost_estimate=pl.CostEstimate(flops=2 * rows * columns * 2048 * 2, bytes_accessed=4 * 2**20, transcendentals=0),
        name="column_filter",
    )(defocus, starts, image, jnp.asarray(matrices), jnp.asarray(lines), jnp.asarray(squares))


def prepare_kernel(slots, slices_owned, defocus, cosines, sines, waves, squares, count, rows_ref, weights_ref, mine, order):
    tilt, row = lax.axis_index("tilt"), lax.axis_index("row")
    slab, local_first = tilt * slices_owned // SLAB, tilt * slices_owned % SLAB
    full_rows = waves.shape[0]
    rows = rows_ref.shape[0] // slots
    own = waves[pl.ds(pl.multiple_of(row * rows, rows), rows), :]
    for slot in range(slots):
        sign = flip_sign(squares[...], defocus[tilt ^ slot, slab], full_rows)
        mine[slot * rows : (slot + 1) * rows, :] = own * (sign * count[...])
    for block in range(full_rows // rows):
        order[block * rows : (block + 1) * rows, :] = waves[pl.ds(pl.multiple_of((row ^ block) * rows, rows), rows), :]
    rows_ref[...] = lax.dot_general(
        mine[...],
        order[...],
        (((1,), (1,)), ((), ())),
        precision=lax.Precision.HIGHEST,
        preferred_element_type=jnp.float32,
    ).astype(jnp.bfloat16)

    column = lax.broadcasted_iota(jnp.int32, (1, XBW), 1).astype(jnp.float32)
    tap = lax.broadcasted_iota(jnp.int32, (BAND, XBW), 0).astype(jnp.float32)
    for slot in range(slots):
        cosine, sine = cosines[tilt ^ slot], sines[tilt ^ slot]

        def one_slice(c, carry):
            offset = (local_first + c).astype(jnp.float32) - 0.5 * (SLAB - 1)
            centre = 0.5 * XBW + column * cosine + offset * sine
            there = pl.ds(pl.multiple_of(c * XBW, XBW), XBW)
            weights_ref[slot, :, there] = jnp.maximum(0.0, 1.0 - jnp.abs(tap - centre)).astype(jnp.bfloat16)
            return carry

        lax.fori_loop(0, slices_owned, one_slice, 0)


def prepared(slots, slices_owned, rows, full_rows, defocus, tilt_angle):
    smem, vmem = pl.BlockSpec(memory_space=pltpu.SMEM), pl.BlockSpec(memory_space=pltpu.VMEM)
    tables = [jnp.asarray(t) for t in row_tables(full_rows)]
    return pl.pallas_call(
        functools.partial(prepare_kernel, slots, slices_owned),
        out_shape=[
            jax.ShapeDtypeStruct((slots * rows, full_rows), jnp.bfloat16),
            jax.ShapeDtypeStruct((slots, BAND, slices_owned * XBW), jnp.bfloat16),
        ],
        in_specs=[smem] * 3 + [vmem] * 3,
        out_specs=[vmem] * 2,
        scratch_shapes=[
            pltpu.VMEM((slots * rows, full_rows), jnp.float32),
            pltpu.VMEM((full_rows, full_rows), jnp.float32),
        ],
        compiler_params=pltpu.CompilerParams(vmem_limit_bytes=32 * 2**20),
        cost_estimate=pl.CostEstimate(flops=2**30, bytes_accessed=6 * 2**20, transcendentals=0),
        name="prepare",
    )(defocus, jnp.cos(tilt_angle), jnp.sin(tilt_angle), *tables)


def interpolate_kernel(slots, row_devices, factor, rows_ref, weights_ref, *refs):
    patch_refs = refs[: slots * row_devices]
    out_ref, out, sems = refs[slots * row_devices :]
    rows = patch_refs[0].shape[0]
    slices = out.shape[0]
    corrected = []
    for slot in range(slots):
        patches = jnp.concatenate([patch_refs[slot * row_devices + r][...] for r in range(row_devices)], 0)
        image = jnp.dot(rows_ref[slot * rows : (slot + 1) * rows, :], patches, preferred_element_type=jnp.float32)
        image = image.astype(jnp.bfloat16)
        corrected.append(
            jnp.concatenate([image[:, block * BAND : (block + 1) * BAND] for block in range(XBLK)], 0)
        )
    step = math.gcd(slices, 4)
    copies = []
    for group in range(slices // step):
        here = slice(group * step * XBW, (group + 1) * step * XBW)
        total = jnp.dot(corrected[0], weights_ref[0, :, here], preferred_element_type=jnp.float32)
        for slot in range(1, slots):
            total += jnp.dot(corrected[slot], weights_ref[slot, :, here], preferred_element_type=jnp.float32)
        for c in range(step):
            for block in range(XBLK):
                out[group * step + c, :, block * XBW : (block + 1) * XBW] = (
                    factor * total[block * rows : (block + 1) * rows, c * XBW : (c + 1) * XBW]
                ).astype(jnp.bfloat16)
        part = pl.ds(group * step, step)
        copies.append(pltpu.make_async_copy(out.at[part], out_ref.at[part], sems.at[group]))
        copies[-1].start()
    for copy in copies:
        copy.wait()


def interpolated(row_filters, weights, patches, factor):
    slots, _, width = weights.shape
    row_devices = len(patches[0])
    rows = patches[0][0].shape[0]
    shape = (width // XBW, rows, XBLK * XBW)
    vmem = pl.BlockSpec(memory_space=pltpu.VMEM)
    return pl.pallas_call(
        functools.partial(interpolate_kernel, slots, row_devices, factor),
        out_shape=jax.ShapeDtypeStruct(shape, jnp.bfloat16),
        in_specs=[vmem] * (2 + slots * row_devices),
        out_specs=pl.BlockSpec(memory_space=pl.ANY),
        scratch_shapes=[
            pltpu.VMEM(shape, jnp.bfloat16),
            pltpu.SemaphoreType.DMA((shape[0] // math.gcd(shape[0], 4),)),
        ],
        compiler_params=pltpu.CompilerParams(vmem_limit_bytes=32 * 2**20),
        cost_estimate=pl.CostEstimate(
            flops=2 * slots * BAND * width * XBLK * rows, bytes_accessed=6 * 2**20, transcendentals=0
        ),
        name="interpolate",
    )(row_filters, weights, *[block for slot in patches for block in slot])


def exchange(array, axis, distance):
    count = lax.axis_size(axis)
    return lax.ppermute(array, axis, [(i, i ^ distance) for i in range(count)])


def gather_rows(array):
    blocks = {0: array}
    bit = lax.axis_size("row") // 2
    while bit:
        blocks.update({d ^ bit: exchange(block, "row", bit) for d, block in blocks.items()})
        bit //= 2
    return [blocks[d] for d in sorted(blocks)]


def per_device(projections, tilt_angle, band_start, defocus):
    _, rows, _ = projections.shape
    row_devices, tilt_devices = lax.axis_size("row"), lax.axis_size("tilt")
    slices_owned = SLICES // tilt_devices
    sent = column_filtered(tilt_devices, slices_owned, defocus, band_start, projections[0])
    arrived = {0: sent[0]}
    for d in sorted(range(1, tilt_devices), reverse=True):
        arrived[d] = exchange(sent[d], "tilt", d)
    patches = [gather_rows(arrived[d]) for d in range(tilt_devices)]
    row_filters, weights = prepared(tilt_devices, slices_owned, rows, rows * row_devices, defocus, tilt_angle)
    return interpolated(row_filters, weights, patches, 1.0 / math.sqrt(tilt_devices))


def solution(mesh):
    in_specs = (
        P(("group", "tilt"), "row", None),
        P("group"),
        P("group", None, None),
        P("group", None),
    )
    out_specs = P(("group", "tilt"), "row", None)
    return jax.shard_map(
        per_device, mesh=mesh, in_specs=in_specs, out_specs=out_specs, check_vma=False
    )
```

```python
import functools
import math

import jax
import jax.numpy as jnp
import numpy as np
from jax import lax
from jax.experimental import pallas as pl
from jax.experimental.pallas import tpu as pltpu
from jax.sharding import PartitionSpec as P

SLAB = 16
XBW = 128
BAND = 256
XBLK = 4
SLICES = 64
RADIX = 8
MAIN = 128
REST = 32
REACH = MAIN + REST
PACKED = XBLK * REACH
WINDOW = 384
ROOT = math.sqrt(0.5)


def column_tables(columns):
    size = columns // RADIX
    half = size // 2
    u = np.arange(size)[:, None]

    def angles(freq):
        return 2.0 * np.pi * ((u * freq[None, :]) % columns) / columns

    k0, s0 = RADIX * np.arange(half + 1), RADIX * np.arange(1, half)
    k4 = RADIX * np.arange(half) + 4
    m0 = np.concatenate([np.cos(angles(k0)), -np.sin(angles(s0))], 1)
    m4 = np.concatenate([np.cos(angles(k4)), -np.sin(angles(k4))], 1)
    full = angles(RADIX * np.arange(size))
    waves = np.concatenate([np.cos(full), np.sin(full)], 1)
    ends = np.concatenate([m0, m4], 1)

    def split(table):
        high = table.astype(jnp.bfloat16)
        return high, (table - high.astype(np.float64)).astype(jnp.bfloat16)

    matrices = np.stack([*split(ends), *split(waves), np.concatenate([m0.T, m4.T], 1).astype(jnp.bfloat16)])
    freq = [np.concatenate([k0, s0]), np.concatenate([k4, k4])]
    turns = []
    for j in (1, 2, 3):
        freq += [RADIX * np.arange(size) + j] * 2
        angle = 2.0 * np.pi * np.arange(size) * j / columns
        turns += [np.cos(angle), np.sin(angle)]
    freq = np.stack(freq)
    count = np.where((freq == 0) | (freq == columns // 2), 1.0, 2.0)
    fold = np.minimum(freq, columns - freq)
    ramp = count * (fold + 0.5) / (0.5 * columns) / columns
    lines = np.concatenate([ramp, fold * fold, np.stack(turns + [np.zeros(size)] * 2)])
    return matrices, lines.astype(np.float32)


def row_tables(full_rows):
    half = full_rows // 2
    y = np.arange(full_rows)[:, None]
    freq = np.concatenate([np.arange(half + 1), np.arange(1, half)])
    angle = 2.0 * np.pi * (y * freq[None, :] % full_rows) / full_rows
    waves = np.where(np.arange(full_rows)[None, :] <= half, np.cos(angle), np.sin(angle))
    count = np.where((freq == 0) | (freq == half), 1.0, 2.0) / full_rows
    return np.concatenate([waves, count[None], (freq * freq)[None], np.zeros((6, full_rows))]).astype(np.float32)


def flip_sign(squares, defocus, length):
    cycles = lax.div(squares.astype(jnp.int32) * defocus, jnp.int32(length * length))
    return (1 - 2 * (cycles & 1)).astype(jnp.float32)


def fetched(sources, targets, sems):
    copies = [pltpu.make_async_copy(s, t, sems.at[i]) for i, (s, t) in enumerate(zip(sources, targets))]
    for copy in copies:
        copy.start()
    return copies


def column_kernel(slots, slices_owned, image_ref, lines_ref, matrix_ref, defocus_ref, starts_ref, first_ref, *refs):
    out_refs = refs[:slots]
    image, lines, matrix, defocus, starts, first_tap, zhi, zlo, ends, waves, turned, sems = refs[slots:]
    rows, columns = image.shape
    size = columns // RADIX
    copies = fetched(
        [image_ref, lines_ref] + [matrix_ref.at[i] for i in range(5)] + [defocus_ref, starts_ref, first_ref],
        [image, lines] + [matrix.at[i] for i in range(5)] + [defocus, starts, first_tap],
        sems,
    )
    tilt = lax.axis_index("tilt")
    copies[0].wait()
    copies[1].wait()
    turns = [lines[16 + i : 17 + i, :] for i in range(6)]

    def butterfly(step, carry):
        here = pl.ds(pl.multiple_of(step * 16, 16), 16)
        x = [image[here, m * size : (m + 1) * size].astype(jnp.float32) for m in range(8)]
        p0, p1, p2, p3 = (x[m] + x[m + 4] for m in range(4))
        q0, q1, q2, q3 = (x[m] - x[m + 4] for m in range(4))
        e, f = p0 + p2, p1 + p3
        g, h = ROOT * (q1 - q3), ROOT * (q1 + q3)
        z = [e + f, e - f]
        for j, (real, imag) in enumerate([(q0 + g, -q2 - h), (p0 - p2, p3 - p1), (q0 - g, q2 - h)]):
            c, s = turns[2 * j], turns[2 * j + 1]
            z += [real * c + imag * s, imag * c - real * s]
        for i in range(8):
            top = z[i].astype(jnp.bfloat16)
            zhi[i, here, :] = top
            zlo[i, here, :] = (z[i] - top.astype(jnp.float32)).astype(jnp.bfloat16)
        return carry

    lax.fori_loop(0, rows // 16, butterfly, 0)
    for copy in copies[2:6]:
        copy.wait()

    def product(first, count, table, here):
        top = zhi[first : first + count].reshape(count * rows, size)
        rest = zlo[first : first + count].reshape(count * rows, size)
        total = jnp.dot(top, matrix[table, :, here], preferred_element_type=jnp.float32)
        total += jnp.dot(top, matrix[table + 1, :, here], preferred_element_type=jnp.float32)
        return total + jnp.dot(rest, matrix[table, :, here], preferred_element_type=jnp.float32)

    spectrum = [product(0, 1, 0, slice(0, size)), product(1, 1, 0, slice(size, 2 * size))]
    mixed = product(2, 6, 2, slice(None))
    for j in range(3):
        real, imag = mixed[2 * j * rows : (2 * j + 1) * rows], mixed[(2 * j + 1) * rows : (2 * j + 2) * rows]
        spectrum += [real[:, :size] + imag[:, size:], imag[:, :size] - real[:, size:]]

    for copy in copies[6:]:
        copy.wait()
    slabs = [(tilt ^ slot) * slices_owned // SLAB for slot in range(slots)]
    gains = [
        flip_sign(lines[8:16, :], defocus[tilt, slabs[slot]], columns) * lines[:8, :] for slot in range(slots)
    ]
    filtered = [
        jnp.concatenate(
            [(spectrum[i] * gains[slot][i : i + 1, :]).astype(jnp.bfloat16) for slot in range(slots)], 0
        )
        for i in range(8)
    ]
    for i in range(2):
        ends[i] = jnp.dot(filtered[i], matrix[4, :, i * size : (i + 1) * size], preferred_element_type=jnp.float32)
    for i in range(6):
        waves[i] = jnp.dot(filtered[2 + i], matrix[2], preferred_element_type=jnp.float32)

    def inverse_butterfly(step, carry):
        here = pl.ds(pl.multiple_of(step * 8, 8), 8)
        r, s = [], []
        for j in range(3):
            c, d = turns[2 * j], turns[2 * j + 1]
            real = waves[2 * j, here, :size] - waves[2 * j + 1, here, size:]
            imag = waves[2 * j, here, size:] + waves[2 * j + 1, here, :size]
            r.append(real * c - imag * d)
            s.append(real * d + imag * c)
        e, f = ends[0, here, :] + ends[1, here, :], ends[0, here, :] - ends[1, here, :]
        a, b, c, d = r[0] + r[2], r[0] - r[2], s[0] + s[2], s[0] - s[2]
        even0, even2, odd1, odd3 = e + r[1], e - r[1], f - s[1], f + s[1]
        g, h = ROOT * (b - c), ROOT * (b + c)
        out = [even0 + a, odd1 + g, even2 - d, odd3 - h, even0 - a, odd1 - g, even2 + d, odd3 + h]
        for m in range(8):
            turned[here, m * size : (m + 1) * size] = out[m]
        return carry

    lax.fori_loop(0, slots * rows // 8, inverse_butterfly, 0)

    lane = lax.broadcasted_iota(jnp.int32, (rows, MAIN), 1) // REST
    for slot in range(slots):
        rest = jnp.zeros((rows, MAIN), jnp.float32)
        for block in range(XBLK):
            start = starts[tilt, slabs[slot], block] + first_tap[tilt]
            base = pl.multiple_of(jnp.minimum((start // 128) * 128, columns - WINDOW), 128)
            window = turned[slot * rows : (slot + 1) * rows, pl.ds(base, WINDOW)]
            shift = base - start
            reach = pltpu.roll(window, jnp.where(shift < 0, shift + WINDOW, shift), 1)[:, : 2 * MAIN]
            out_refs[slot][:, block * MAIN : (block + 1) * MAIN] = reach[:, :MAIN].astype(jnp.bfloat16)
            last = reach[:, MAIN:]
            rest = jnp.where(lane == block, pltpu.roll(last, block * REST, 1) if block else last, rest)
        out_refs[slot][:, XBLK * MAIN :] = rest.astype(jnp.bfloat16)


def column_filtered(slots, slices_owned, defocus, starts, first_tap, image):
    rows, columns = image.shape
    size = columns // RADIX
    matrices, lines = column_tables(columns)
    vmem, away = pl.BlockSpec(memory_space=pltpu.VMEM), pl.BlockSpec(memory_space=pl.ANY)
    return pl.pallas_call(
        functools.partial(column_kernel, slots, slices_owned),
        out_shape=[jax.ShapeDtypeStruct((rows, PACKED), jnp.bfloat16)] * slots,
        in_specs=[away] * 6,
        out_specs=[vmem] * slots,
        scratch_shapes=[
            pltpu.VMEM((rows, columns), jnp.bfloat16),
            pltpu.VMEM(lines.shape, jnp.float32),
            pltpu.VMEM(matrices.shape, jnp.bfloat16),
            pltpu.SMEM(defocus.shape, jnp.int32),
            pltpu.SMEM(starts.shape, jnp.int32),
            pltpu.SMEM(first_tap.shape, jnp.int32),
            pltpu.VMEM((8, rows, size), jnp.bfloat16),
            pltpu.VMEM((8, rows, size), jnp.bfloat16),
            pltpu.VMEM((2, slots * rows, size), jnp.float32),
            pltpu.VMEM((6, slots * rows, 2 * size), jnp.float32),
            pltpu.VMEM((slots * rows, columns), jnp.float32),
            pltpu.SemaphoreType.DMA((10,)),
        ],
        compiler_params=pltpu.CompilerParams(vmem_limit_bytes=40 * 2**20),
        cost_estimate=pl.CostEstimate(flops=2 * rows * columns * 2048 * 2, bytes_accessed=4 * 2**20, transcendentals=0),
        name="column_filter",
    )(image, jnp.asarray(lines), jnp.asarray(matrices), defocus, starts, first_tap)


def prepare_kernel(slots, slices_owned, passed, table_ref, defocus_ref, first_ref, cosine_ref, sine_ref, *refs):
    rows_ref, weights_ref = refs[passed : passed + 2]
    table, defocus, first_tap, cosines, sines, mine, order, sems = refs[2 * passed + 2 :]
    copies = fetched(
        [table_ref, defocus_ref, first_ref, cosine_ref, sine_ref], [table, defocus, first_tap, cosines, sines], sems
    )
    tilt, row = lax.axis_index("tilt"), lax.axis_index("row")
    slab, local_first = tilt * slices_owned // SLAB, tilt * slices_owned % SLAB
    full_rows = table.shape[1]
    rows = rows_ref.shape[0] // slots
    for copy in copies:
        copy.wait()
    own = table[pl.ds(pl.multiple_of(row * rows, rows), rows), :]
    for slot in range(slots):
        sign = flip_sign(table[full_rows + 1 : full_rows + 2, :], defocus[tilt ^ slot, slab], full_rows)
        mine[slot * rows : (slot + 1) * rows, :] = own * (sign * table[full_rows : full_rows + 1, :])
    for block in range(full_rows // rows):
        order[block * rows : (block + 1) * rows, :] = table[pl.ds(pl.multiple_of((row ^ block) * rows, rows), rows), :]
    rows_ref[...] = lax.dot_general(
        mine[...],
        order[...],
        (((1,), (1,)), ((), ())),
        precision=lax.Precision.HIGHEST,
        preferred_element_type=jnp.float32,
    ).astype(jnp.bfloat16)

    column = lax.broadcasted_iota(jnp.int32, (1, XBW), 1).astype(jnp.float32)
    place = lax.broadcasted_iota(jnp.int32, (2 * MAIN, XBW), 0)
    place = jnp.where(place < MAIN, place, MAIN + place % REST)
    for slot in range(slots):
        cosine, sine = cosines[tilt ^ slot], sines[tilt ^ slot]
        tap = (place + first_tap[tilt ^ slot]).astype(jnp.float32)

        def one_slice(c, carry):
            offset = (local_first + c).astype(jnp.float32) - 0.5 * (SLAB - 1)
            centre = 0.5 * XBW + column * cosine + offset * sine
            there = pl.ds(pl.multiple_of(c * XBW, XBW), XBW)
            weights_ref[slot, :, there] = jnp.maximum(0.0, 1.0 - jnp.abs(tap - centre)).astype(jnp.bfloat16)
            return carry

        lax.fori_loop(0, slices_owned, one_slice, 0)


def prepared(slots, slices_owned, rows, full_rows, defocus, first_tap, cosines, sines, passed):
    vmem, away = pl.BlockSpec(memory_space=pltpu.VMEM), pl.BlockSpec(memory_space=pl.ANY)
    table = row_tables(full_rows)
    count = len(passed)
    out = pl.pallas_call(
        functools.partial(prepare_kernel, slots, slices_owned, count),
        out_shape=[
            jax.ShapeDtypeStruct((slots * rows, full_rows), jnp.bfloat16),
            jax.ShapeDtypeStruct((slots, 2 * MAIN, slices_owned * XBW), jnp.bfloat16),
        ]
        + [jax.ShapeDtypeStruct(p.shape, p.dtype) for p in passed],
        in_specs=[away] * (5 + count),
        out_specs=[vmem] * 2 + [away] * count,
        scratch_shapes=[
            pltpu.VMEM(table.shape, jnp.float32),
            pltpu.SMEM(defocus.shape, jnp.int32),
            pltpu.SMEM(first_tap.shape, jnp.int32),
            pltpu.SMEM(cosines.shape, jnp.float32),
            pltpu.SMEM(sines.shape, jnp.float32),
            pltpu.VMEM((slots * rows, full_rows), jnp.float32),
            pltpu.VMEM((full_rows, full_rows), jnp.float32),
            pltpu.SemaphoreType.DMA((5,)),
        ],
        input_output_aliases={5 + i: 2 + i for i in range(count)},
        compiler_params=pltpu.CompilerParams(vmem_limit_bytes=32 * 2**20),
        cost_estimate=pl.CostEstimate(flops=2**30, bytes_accessed=6 * 2**20, transcendentals=0),
        name="prepare",
    )(jnp.asarray(table), defocus, first_tap, cosines, sines, *passed)
    return out[0], out[1], out[2:]


def interpolate_kernel(slots, row_devices, factor, rows_ref, weights_ref, *refs):
    patch_refs = refs[: slots * row_devices]
    out_ref, out, sems = refs[slots * row_devices :]
    rows = patch_refs[0].shape[0]
    slices = out.shape[0]
    lane = lax.broadcasted_iota(jnp.int32, (rows, MAIN), 1) // REST
    corrected = []
    for slot in range(slots):
        patches = jnp.concatenate([patch_refs[slot * row_devices + r][...] for r in range(row_devices)], 0)
        image = jnp.dot(rows_ref[slot * rows : (slot + 1) * rows, :], patches, preferred_element_type=jnp.float32)
        main = jnp.concatenate([image[:, block * MAIN : (block + 1) * MAIN] for block in range(XBLK)], 0)
        rest = jnp.concatenate(
            [jnp.where(lane == block, image[:, XBLK * MAIN :], 0.0) for block in range(XBLK)], 0
        )
        corrected.append(jnp.concatenate([main, rest], 1).astype(jnp.bfloat16))
    step = math.gcd(slices, 4)
    copies = []
    for group in range(slices // step):
        here = slice(group * step * XBW, (group + 1) * step * XBW)
        total = jnp.dot(corrected[0], weights_ref[0, :, here], preferred_element_type=jnp.float32)
        for slot in range(1, slots):
            total += jnp.dot(corrected[slot], weights_ref[slot, :, here], preferred_element_type=jnp.float32)
        for c in range(step):
            for block in range(XBLK):
                out[group * step + c, :, block * XBW : (block + 1) * XBW] = (
                    factor * total[block * rows : (block + 1) * rows, c * XBW : (c + 1) * XBW]
                ).astype(jnp.bfloat16)
        part = pl.ds(group * step, step)
        copies.append(pltpu.make_async_copy(out.at[part], out_ref.at[part], sems.at[group]))
        copies[-1].start()
    for copy in copies:
        copy.wait()


def interpolated(row_filters, weights, patches, factor):
    slots, _, width = weights.shape
    row_devices = len(patches[0])
    rows = patches[0][0].shape[0]
    shape = (width // XBW, rows, XBLK * XBW)
    vmem = pl.BlockSpec(memory_space=pltpu.VMEM)
    return pl.pallas_call(
        functools.partial(interpolate_kernel, slots, row_devices, factor),
        out_shape=jax.ShapeDtypeStruct(shape, jnp.bfloat16),
        in_specs=[vmem] * (2 + slots * row_devices),
        out_specs=pl.BlockSpec(memory_space=pl.ANY),
        scratch_shapes=[
            pltpu.VMEM(shape, jnp.bfloat16),
            pltpu.SemaphoreType.DMA((shape[0] // math.gcd(shape[0], 4),)),
        ],
        compiler_params=pltpu.CompilerParams(vmem_limit_bytes=32 * 2**20),
        cost_estimate=pl.CostEstimate(
            flops=2 * slots * 2 * MAIN * width * XBLK * rows, bytes_accessed=6 * 2**20, transcendentals=0
        ),
        name="interpolate",
    )(row_filters, weights, *[block for slot in patches for block in slot])


def exchange(array, axis, distance):
    count = lax.axis_size(axis)
    return lax.ppermute(array, axis, [(i, i ^ distance) for i in range(count)])


def gather_rows(array):
    blocks = {0: array}
    bit = lax.axis_size("row") // 2
    while bit:
        blocks.update({d ^ bit: exchange(block, "row", bit) for d, block in blocks.items()})
        bit //= 2
    return [blocks[d] for d in sorted(blocks)]


def per_device(projections, tilt_angle, band_start, defocus):
    _, rows, _ = projections.shape
    row_devices, tilt_devices = lax.axis_size("row"), lax.axis_size("tilt")
    slices_owned = SLICES // tilt_devices
    cosines, sines = jnp.cos(tilt_angle), jnp.sin(tilt_angle)
    lowest = 0.5 * XBW + jnp.minimum((XBW - 1) * cosines, 0.0) - 0.5 * (SLAB - 1) * jnp.abs(sines)
    first_tap = jnp.clip(jnp.floor(lowest).astype(jnp.int32) - 8, 0, BAND - REACH)
    sent = column_filtered(tilt_devices, slices_owned, defocus, band_start, first_tap, projections[0])
    last = tilt_devices - 1
    arrived = {last: exchange(sent[last], "tilt", last)}
    row_filters, weights, sent = prepared(
        tilt_devices, slices_owned, rows, rows * row_devices, defocus, first_tap, cosines, sines, sent[:last]
    )
    for d in range(last - 1, 0, -1):
        arrived[d] = exchange(sent[d], "tilt", d)
    arrived[0] = sent[0]
    patches = [gather_rows(arrived[d]) for d in range(tilt_devices)]
    return interpolated(row_filters, weights, patches, 1.0 / math.sqrt(tilt_devices))


def solution(mesh):
    in_specs = (
        P(("group", "tilt"), "row", None),
        P("group"),
        P("group", None, None),
        P("group", None),
    )
    out_specs = P(("group", "tilt"), "row", None)
    return jax.shard_map(
        per_device, mesh=mesh, in_specs=in_specs, out_specs=out_specs, check_vma=False
    )
```

```python
import functools
import math

import jax
import jax.numpy as jnp
import numpy as np
from jax import lax
from jax.experimental import pallas as pl
from jax.experimental.pallas import tpu as pltpu
from jax.sharding import PartitionSpec as P

SLAB = 16
XBW = 128
BAND = 256
XBLK = 4
SLICES = 64
RADIX = 8
MAIN = 128
REST = 32
REACH = MAIN + REST
PACKED = XBLK * REACH
WINDOW = 384
ROOT = math.sqrt(0.5)


def column_tables(columns):
    size = columns // RADIX
    half = size // 2
    u = np.arange(size)[:, None]

    def angles(freq):
        return 2.0 * np.pi * ((u * freq[None, :]) % columns) / columns

    k0, s0 = RADIX * np.arange(half + 1), RADIX * np.arange(1, half)
    k4 = RADIX * np.arange(half) + 4
    m0 = np.concatenate([np.cos(angles(k0)), -np.sin(angles(s0))], 1)
    m4 = np.concatenate([np.cos(angles(k4)), -np.sin(angles(k4))], 1)
    full = angles(RADIX * np.arange(size))
    waves = np.concatenate([np.cos(full), np.sin(full)], 1)
    ends = np.concatenate([m0, m4], 1)

    def split(table):
        high = table.astype(jnp.bfloat16)
        return high, (table - high.astype(np.float64)).astype(jnp.bfloat16)

    matrices = np.stack([*split(ends), *split(waves), np.concatenate([m0.T, m4.T], 1).astype(jnp.bfloat16)])
    return matrices


def column_lines(columns):
    size = columns // RADIX
    half = size // 2
    line = lax.broadcasted_iota(jnp.int32, (8, size), 0)
    u = lax.broadcasted_iota(jnp.int32, (8, size), 1)
    freq = jnp.where(line == 0, RADIX * jnp.where(u <= half, u, u - half), RADIX * (u & (half - 1)) + 4)
    freq = jnp.where(line < 2, freq, RADIX * u + line // 2)
    fold = jnp.minimum(freq, columns - freq)
    count = jnp.where((fold == 0) | (fold == columns // 2), 1.0, 2.0)
    gain = count * (fold.astype(jnp.float32) + 0.5) * (2.0 / (columns * columns))
    angle = (u * (line + 1)).astype(jnp.float32) * (2.0 * math.pi / columns)
    return fold * fold, gain, jnp.cos(angle), jnp.sin(angle)


def flip_sign(squares, defocus, length):
    cycles = lax.div(squares * defocus, jnp.int32(length * length))
    return (1 - 2 * (cycles & 1)).astype(jnp.float32)


def fetched(sources, targets, sems):
    copies = [pltpu.make_async_copy(s, t, sems.at[i]) for i, (s, t) in enumerate(zip(sources, targets))]
    for copy in copies:
        copy.start()
    return copies


def reach_of(angle):
    line = jnp.full((8, XBW), angle, jnp.float32)
    cosine, sine = jnp.cos(line), jnp.sin(line)
    lowest = 0.5 * XBW + jnp.minimum((XBW - 1) * cosine, 0.0) - 0.5 * (SLAB - 1) * jnp.abs(sine)
    first = jnp.clip(jnp.floor(lowest) - 8.0, 0.0, float(BAND - REACH))
    return cosine[:1], sine[:1], jnp.max(first).astype(jnp.int32)


def column_kernel(slots, slices_owned, image_ref, matrix_ref, angle_ref, defocus_ref, starts_ref, *refs):
    out_refs = refs[:slots]
    image, matrix, angles, defocus, starts, zhi, zlo, ends, waves, turned, out, sems, out_sems = refs[slots:]
    rows, columns = image.shape
    size = columns // RADIX
    copies = fetched(
        [image_ref, angle_ref, defocus_ref, starts_ref] + [matrix_ref.at[i] for i in range(5)],
        [image, angles, defocus, starts] + [matrix.at[i] for i in range(5)],
        sems,
    )
    tilt = lax.axis_index("tilt")
    squares, ramp, cosine_turns, sine_turns = column_lines(columns)
    turns = [t[j : j + 1, :] for j in range(3) for t in (cosine_turns, sine_turns)]
    copies[0].wait()

    def butterfly(step, carry):
        here = pl.ds(pl.multiple_of(step * 16, 16), 16)
        x = [image[here, m * size : (m + 1) * size].astype(jnp.float32) for m in range(8)]
        p0, p1, p2, p3 = (x[m] + x[m + 4] for m in range(4))
        q0, q1, q2, q3 = (x[m] - x[m + 4] for m in range(4))
        e, f = p0 + p2, p1 + p3
        g, h = ROOT * (q1 - q3), ROOT * (q1 + q3)
        z = [e + f, e - f]
        for j, (real, imag) in enumerate([(q0 + g, -q2 - h), (p0 - p2, p3 - p1), (q0 - g, q2 - h)]):
            c, s = turns[2 * j], turns[2 * j + 1]
            z += [real * c + imag * s, imag * c - real * s]
        for i in range(8):
            top = z[i].astype(jnp.bfloat16)
            zhi[i, here, :] = top
            zlo[i, here, :] = (z[i] - top.astype(jnp.float32)).astype(jnp.bfloat16)
        return carry

    lax.fori_loop(0, rows // 16, butterfly, 0)
    for copy in copies[4:]:
        copy.wait()

    def product(first, count, table, here):
        top = zhi[first : first + count].reshape(count * rows, size)
        rest = zlo[first : first + count].reshape(count * rows, size)
        total = jnp.dot(top, matrix[table, :, here], preferred_element_type=jnp.float32)
        total += jnp.dot(top, matrix[table + 1, :, here], preferred_element_type=jnp.float32)
        return total + jnp.dot(rest, matrix[table, :, here], preferred_element_type=jnp.float32)

    spectrum = [product(0, 1, 0, slice(0, size)), product(1, 1, 0, slice(size, 2 * size))]
    mixed = product(2, 6, 2, slice(None))
    for j in range(3):
        real, imag = mixed[2 * j * rows : (2 * j + 1) * rows], mixed[(2 * j + 1) * rows : (2 * j + 2) * rows]
        spectrum += [real[:, :size] + imag[:, size:], imag[:, :size] - real[:, size:]]

    for copy in copies[1:4]:
        copy.wait()
    slabs = [(tilt ^ slot) * slices_owned // SLAB for slot in range(slots)]
    gains = [
        flip_sign(squares, defocus[tilt, slab], columns) * ramp for slab in slabs
    ]
    filtered = [
        jnp.concatenate(
            [(spectrum[i] * gains[slot][i : i + 1, :]).astype(jnp.bfloat16) for slot in range(slots)], 0
        )
        for i in range(8)
    ]
    for i in range(2):
        ends[i] = jnp.dot(filtered[i], matrix[4, :, i * size : (i + 1) * size], preferred_element_type=jnp.float32)
    for i in range(6):
        waves[i] = jnp.dot(filtered[2 + i], matrix[2], preferred_element_type=jnp.float32)

    def inverse_butterfly(step, carry):
        here = pl.ds(pl.multiple_of(step * 8, 8), 8)
        r, s = [], []
        for j in range(3):
            c, d = turns[2 * j], turns[2 * j + 1]
            real = waves[2 * j, here, :size] - waves[2 * j + 1, here, size:]
            imag = waves[2 * j, here, size:] + waves[2 * j + 1, here, :size]
            r.append(real * c - imag * d)
            s.append(real * d + imag * c)
        e, f = ends[0, here, :] + ends[1, here, :], ends[0, here, :] - ends[1, here, :]
        a, b, c, d = r[0] + r[2], r[0] - r[2], s[0] + s[2], s[0] - s[2]
        even0, even2, odd1, odd3 = e + r[1], e - r[1], f - s[1], f + s[1]
        g, h = ROOT * (b - c), ROOT * (b + c)
        out = [even0 + a, odd1 + g, even2 - d, odd3 - h, even0 - a, odd1 - g, even2 + d, odd3 + h]
        for m in range(8):
            turned[here, m * size : (m + 1) * size] = out[m]
        return carry

    lax.fori_loop(0, slots * rows // 8, inverse_butterfly, 0)

    lane = lax.broadcasted_iota(jnp.int32, (rows, MAIN), 1) // REST
    _, _, first_tap = reach_of(angles[tilt])
    sends = []
    for slot in reversed(range(slots)):
        rest = jnp.zeros((rows, MAIN), jnp.float32)
        for block in range(XBLK):
            start = starts[tilt, slabs[slot], block] + first_tap
            base = pl.multiple_of(jnp.minimum((start // 128) * 128, columns - WINDOW), 128)
            window = turned[slot * rows : (slot + 1) * rows, pl.ds(base, WINDOW)]
            shift = base - start
            reach = pltpu.roll(window, jnp.where(shift < 0, shift + WINDOW, shift), 1)[:, : 2 * MAIN]
            out[slot, :, block * MAIN : (block + 1) * MAIN] = reach[:, :MAIN].astype(jnp.bfloat16)
            last = reach[:, MAIN:]
            rest = jnp.where(lane == block, pltpu.roll(last, block * REST, 1) if block else last, rest)
        out[slot, :, XBLK * MAIN :] = rest.astype(jnp.bfloat16)
        sends.append(pltpu.make_async_copy(out.at[slot], out_refs[slot], out_sems.at[slot]))
        sends[-1].start()
    for copy in sends:
        copy.wait()


def column_filtered(slots, slices_owned, image, angles, defocus, starts):
    rows, columns = image.shape
    size = columns // RADIX
    matrices = column_tables(columns)
    away = pl.BlockSpec(memory_space=pl.ANY)
    return pl.pallas_call(
        functools.partial(column_kernel, slots, slices_owned),
        out_shape=[jax.ShapeDtypeStruct((rows, PACKED), jnp.bfloat16)] * slots,
        in_specs=[away] * 5,
        out_specs=[away] * slots,
        scratch_shapes=[
            pltpu.VMEM((rows, columns), jnp.bfloat16),
            pltpu.VMEM(matrices.shape, jnp.bfloat16),
            pltpu.SMEM(angles.shape, jnp.float32),
            pltpu.SMEM(defocus.shape, jnp.int32),
            pltpu.SMEM(starts.shape, jnp.int32),
            pltpu.VMEM((8, rows, size), jnp.bfloat16),
            pltpu.VMEM((8, rows, size), jnp.bfloat16),
            pltpu.VMEM((2, slots * rows, size), jnp.float32),
            pltpu.VMEM((6, slots * rows, 2 * size), jnp.float32),
            pltpu.VMEM((slots * rows, columns), jnp.float32),
            pltpu.VMEM((slots, rows, PACKED), jnp.bfloat16),
            pltpu.SemaphoreType.DMA((9,)),
            pltpu.SemaphoreType.DMA((slots,)),
        ],
        compiler_params=pltpu.CompilerParams(vmem_limit_bytes=60 * 2**20),
        cost_estimate=pl.CostEstimate(flops=2 * rows * columns * 2048 * 2, bytes_accessed=4 * 2**20, transcendentals=0),
        name="column_filter",
    )(image, jnp.asarray(matrices), angles, defocus, starts)


def prepare_kernel(slots, slices_owned, passed, angles, defocus, *refs):
    rows_ref, weights_ref = refs[passed : passed + 2]
    waves, mine, order = refs[2 * passed + 2 :]
    tilt, row = lax.axis_index("tilt"), lax.axis_index("row")
    slab, local_first = tilt * slices_owned // SLAB, tilt * slices_owned % SLAB
    full_rows = waves.shape[0]
    rows = rows_ref.shape[0] // slots
    half = full_rows // 2

    def row_waves(block, carry):
        here = pl.ds(pl.multiple_of(block * rows, rows), rows)
        y = block * rows + lax.broadcasted_iota(jnp.int32, (rows, full_rows), 0)
        column = lax.broadcasted_iota(jnp.int32, (rows, full_rows), 1)
        freq = jnp.where(column <= half, column, column - half)
        angle = ((y * freq) & (full_rows - 1)).astype(jnp.float32) * (2.0 * math.pi / full_rows)
        waves[here, :] = jnp.where(column <= half, jnp.cos(angle), jnp.sin(angle))
        return carry

    lax.fori_loop(0, full_rows // rows, row_waves, 0)
    own = waves[pl.ds(pl.multiple_of(row * rows, rows), rows), :]
    column = lax.broadcasted_iota(jnp.int32, (8, full_rows), 1)
    freq = jnp.where(column <= half, column, column - half)
    count = jnp.where((freq == 0) | (freq == half), 1.0, 2.0) / full_rows
    for slot in range(slots):
        sign = flip_sign(freq * freq, defocus[tilt ^ slot, slab], full_rows)
        mine[slot * rows : (slot + 1) * rows, :] = own * (sign * count)[:1]
    for block in range(full_rows // rows):
        order[block * rows : (block + 1) * rows, :] = waves[pl.ds(pl.multiple_of((row ^ block) * rows, rows), rows), :]
    rows_ref[...] = lax.dot_general(
        mine[...],
        order[...],
        (((1,), (1,)), ((), ())),
        precision=lax.Precision.HIGHEST,
        preferred_element_type=jnp.float32,
    ).astype(jnp.bfloat16)

    column = lax.broadcasted_iota(jnp.int32, (1, XBW), 1).astype(jnp.float32)
    place = lax.broadcasted_iota(jnp.int32, (2 * MAIN, XBW), 0)
    place = jnp.where(place < MAIN, place, MAIN + place % REST).astype(jnp.float32)
    for slot in range(slots):
        cosine, sine, first_tap = reach_of(angles[tilt ^ slot])
        tap = place + first_tap.astype(jnp.float32)

        def one_slice(c, carry):
            offset = (local_first + c).astype(jnp.float32) - 0.5 * (SLAB - 1)
            centre = 0.5 * XBW + column * cosine + offset * sine
            there = pl.ds(pl.multiple_of(c * XBW, XBW), XBW)
            weights_ref[slot, :, there] = jnp.maximum(0.0, 1.0 - jnp.abs(tap - centre)).astype(jnp.bfloat16)
            return carry

        lax.fori_loop(0, slices_owned, one_slice, 0)


def prepared(slots, slices_owned, rows, full_rows, angles, defocus, passed):
    smem, vmem = pl.BlockSpec(memory_space=pltpu.SMEM), pl.BlockSpec(memory_space=pltpu.VMEM)
    handed = pl.BlockSpec(memory_space=pl.ANY)
    count = len(passed)
    out = pl.pallas_call(
        functools.partial(prepare_kernel, slots, slices_owned, count),
        out_shape=[
            jax.ShapeDtypeStruct((slots * rows, full_rows), jnp.bfloat16),
            jax.ShapeDtypeStruct((slots, 2 * MAIN, slices_owned * XBW), jnp.bfloat16),
        ]
        + [jax.ShapeDtypeStruct(p.shape, p.dtype) for p in passed],
        in_specs=[smem] * 2 + [handed] * count,
        out_specs=[vmem] * 2 + [handed] * count,
        scratch_shapes=[
            pltpu.VMEM((full_rows, full_rows), jnp.float32),
            pltpu.VMEM((slots * rows, full_rows), jnp.float32),
            pltpu.VMEM((full_rows, full_rows), jnp.float32),
        ],
        input_output_aliases={2 + i: 2 + i for i in range(count)},
        compiler_params=pltpu.CompilerParams(vmem_limit_bytes=32 * 2**20),
        cost_estimate=pl.CostEstimate(flops=2**30, bytes_accessed=6 * 2**20, transcendentals=0),
        name="prepare",
    )(angles, defocus, *passed)
    return out[0], out[1], out[2:]


def interpolate_kernel(slots, row_devices, factor, rows_ref, weights_ref, *refs):
    patch_refs = refs[: slots * row_devices]
    out_ref, out, sems = refs[slots * row_devices :]
    rows = patch_refs[0].shape[0]
    slices = out.shape[0]
    lane = lax.broadcasted_iota(jnp.int32, (rows, MAIN), 1) // REST
    corrected = []
    for slot in range(slots):
        patches = jnp.concatenate([patch_refs[slot * row_devices + r][...] for r in range(row_devices)], 0)
        image = jnp.dot(rows_ref[slot * rows : (slot + 1) * rows, :], patches, preferred_element_type=jnp.float32)
        main = jnp.concatenate([image[:, block * MAIN : (block + 1) * MAIN] for block in range(XBLK)], 0)
        rest = jnp.concatenate(
            [jnp.where(lane == block, image[:, XBLK * MAIN :], 0.0) for block in range(XBLK)], 0
        )
        corrected.append(jnp.concatenate([main, rest], 1).astype(jnp.bfloat16))
    step = math.gcd(slices, 4)
    copies = []
    for group in range(slices // step):
        here = slice(group * step * XBW, (group + 1) * step * XBW)
        total = jnp.dot(corrected[0], weights_ref[0, :, here], preferred_element_type=jnp.float32)
        for slot in range(1, slots):
            total += jnp.dot(corrected[slot], weights_ref[slot, :, here], preferred_element_type=jnp.float32)
        for c in range(step):
            for block in range(XBLK):
                out[group * step + c, :, block * XBW : (block + 1) * XBW] = (
                    factor * total[block * rows : (block + 1) * rows, c * XBW : (c + 1) * XBW]
                ).astype(jnp.bfloat16)
        part = pl.ds(group * step, step)
        copies.append(pltpu.make_async_copy(out.at[part], out_ref.at[part], sems.at[group]))
        copies[-1].start()
    for copy in copies:
        copy.wait()


def interpolated(row_filters, weights, patches, factor):
    slots, _, width = weights.shape
    row_devices = len(patches[0])
    rows = patches[0][0].shape[0]
    shape = (width // XBW, rows, XBLK * XBW)
    vmem = pl.BlockSpec(memory_space=pltpu.VMEM)
    return pl.pallas_call(
        functools.partial(interpolate_kernel, slots, row_devices, factor),
        out_shape=jax.ShapeDtypeStruct(shape, jnp.bfloat16),
        in_specs=[vmem] * (2 + slots * row_devices),
        out_specs=pl.BlockSpec(memory_space=pl.ANY),
        scratch_shapes=[
            pltpu.VMEM(shape, jnp.bfloat16),
            pltpu.SemaphoreType.DMA((shape[0] // math.gcd(shape[0], 4),)),
        ],
        compiler_params=pltpu.CompilerParams(vmem_limit_bytes=32 * 2**20),
        cost_estimate=pl.CostEstimate(
            flops=2 * slots * 2 * MAIN * width * XBLK * rows, bytes_accessed=6 * 2**20, transcendentals=0
        ),
        name="interpolate",
    )(row_filters, weights, *[block for slot in patches for block in slot])


def exchange(array, axis, distance):
    count = lax.axis_size(axis)
    return lax.ppermute(array, axis, [(i, i ^ distance) for i in range(count)])


def gather_rows(array):
    blocks = {0: array}
    bit = lax.axis_size("row") // 2
    while bit:
        blocks.update({d ^ bit: exchange(block, "row", bit) for d, block in blocks.items()})
        bit //= 2
    return [blocks[d] for d in sorted(blocks)]


def per_device(projections, tilt_angle, band_start, defocus):
    _, rows, _ = projections.shape
    row_devices, tilt_devices = lax.axis_size("row"), lax.axis_size("tilt")
    slices_owned = SLICES // tilt_devices
    sent = column_filtered(tilt_devices, slices_owned, projections[0], tilt_angle, defocus, band_start)
    arrived = {0: sent[0]}
    for d in range(tilt_devices - 1, 1, -1):
        arrived[d] = exchange(sent[d], "tilt", d)
    row_filters, weights, (near,) = prepared(
        tilt_devices, slices_owned, rows, rows * row_devices, tilt_angle, defocus, sent[1:2]
    )
    arrived[1] = exchange(near, "tilt", 1)
    patches = [gather_rows(arrived[d]) for d in range(tilt_devices)]
    return interpolated(row_filters, weights, patches, 1.0 / math.sqrt(tilt_devices))


def solution(mesh):
    in_specs = (
        P(("group", "tilt"), "row", None),
        P("group"),
        P("group", None, None),
        P("group", None),
    )
    out_specs = P(("group", "tilt"), "row", None)
    return jax.shard_map(
        per_device, mesh=mesh, in_specs=in_specs, out_specs=out_specs, check_vma=False
    )
```

```python
import functools
import math

import jax
import jax.numpy as jnp
import numpy as np
from jax import lax
from jax.experimental import pallas as pl
from jax.experimental.pallas import tpu as pltpu
from jax.sharding import PartitionSpec as P

SLAB = 16
XBW = 128
BAND = 256
XBLK = 4
SLICES = 64
RADIX = 8
MAIN = 128
REST = 32
REACH = MAIN + REST
PACKED = XBLK * REACH
WINDOW = 384
ROOT = math.sqrt(0.5)


def column_tables(columns):
    size = columns // RADIX
    half = size // 2
    u = np.arange(size)[:, None]

    def angles(freq):
        return 2.0 * np.pi * ((u * freq[None, :]) % columns) / columns

    k0, s0 = RADIX * np.arange(half + 1), RADIX * np.arange(1, half)
    k4 = RADIX * np.arange(half) + 4
    m0 = np.concatenate([np.cos(angles(k0)), -np.sin(angles(s0))], 1)
    m4 = np.concatenate([np.cos(angles(k4)), -np.sin(angles(k4))], 1)
    full = angles(RADIX * np.arange(size))
    waves = np.concatenate([np.cos(full), np.sin(full)], 1)
    ends = np.concatenate([m0, m4], 1)

    def split(table):
        high = table.astype(jnp.bfloat16)
        return high, (table - high.astype(np.float64)).astype(jnp.bfloat16)

    matrices = np.stack([*split(ends), *split(waves), np.concatenate([m0.T, m4.T], 1).astype(jnp.bfloat16)])
    return matrices


def column_lines(columns):
    size = columns // RADIX
    half = size // 2
    line = lax.broadcasted_iota(jnp.int32, (8, size), 0)
    u = lax.broadcasted_iota(jnp.int32, (8, size), 1)
    freq = jnp.where(line == 0, RADIX * jnp.where(u <= half, u, u - half), RADIX * (u & (half - 1)) + 4)
    freq = jnp.where(line < 2, freq, RADIX * u + line // 2)
    fold = jnp.minimum(freq, columns - freq)
    count = jnp.where((fold == 0) | (fold == columns // 2), 1.0, 2.0)
    gain = count * (fold.astype(jnp.float32) + 0.5) * (2.0 / (columns * columns))
    angle = (u * (line + 1)).astype(jnp.float32) * (2.0 * math.pi / columns)
    return fold * fold, gain, jnp.cos(angle), jnp.sin(angle)


def flip_sign(squares, defocus, length):
    cycles = lax.div(squares * defocus, jnp.int32(length * length))
    return (1 - 2 * (cycles & 1)).astype(jnp.float32)


def fetched(sources, targets, sems):
    copies = [pltpu.make_async_copy(s, t, sems.at[i]) for i, (s, t) in enumerate(zip(sources, targets))]
    for copy in copies:
        copy.start()
    return copies


def reach_of(angle):
    line = jnp.full((8, XBW), angle, jnp.float32)
    cosine, sine = jnp.cos(line), jnp.sin(line)
    lowest = 0.5 * XBW + jnp.minimum((XBW - 1) * cosine, 0.0) - 0.5 * (SLAB - 1) * jnp.abs(sine)
    first = jnp.clip(jnp.floor(lowest) - 8.0, 0.0, float(BAND - REACH))
    return cosine[:1], sine[:1], jnp.max(first).astype(jnp.int32)


def butterflies(image, turns, zhi, zlo):
    rows, columns = image.shape
    size = columns // RADIX

    def step(i, carry):
        here = pl.ds(pl.multiple_of(i * 16, 16), 16)
        x = [image[here, m * size : (m + 1) * size].astype(jnp.float32) for m in range(8)]
        p0, p1, p2, p3 = (x[m] + x[m + 4] for m in range(4))
        q0, q1, q2, q3 = (x[m] - x[m + 4] for m in range(4))
        e, f = p0 + p2, p1 + p3
        g, h = ROOT * (q1 - q3), ROOT * (q1 + q3)
        z = [e + f, e - f]
        for j, (real, imag) in enumerate([(q0 + g, -q2 - h), (p0 - p2, p3 - p1), (q0 - g, q2 - h)]):
            c, s = turns[2 * j], turns[2 * j + 1]
            z += [real * c + imag * s, imag * c - real * s]
        for line in range(8):
            top = z[line].astype(jnp.bfloat16)
            zhi[line, here, :] = top
            zlo[line, here, :] = (z[line] - top.astype(jnp.float32)).astype(jnp.bfloat16)
        return carry

    lax.fori_loop(0, rows // 16, step, 0)


def inverse_butterflies(ends, waves, turns, turned):
    rows, columns = turned.shape
    size = columns // RADIX

    def step(i, carry):
        here = pl.ds(pl.multiple_of(i * 8, 8), 8)
        r, s = [], []
        for j in range(3):
            c, d = turns[2 * j], turns[2 * j + 1]
            real = waves[2 * j, here, :size] - waves[2 * j + 1, here, size:]
            imag = waves[2 * j, here, size:] + waves[2 * j + 1, here, :size]
            r.append(real * c - imag * d)
            s.append(real * d + imag * c)
        e, f = ends[0, here, :] + ends[1, here, :], ends[0, here, :] - ends[1, here, :]
        a, b, c, d = r[0] + r[2], r[0] - r[2], s[0] + s[2], s[0] - s[2]
        even0, even2, odd1, odd3 = e + r[1], e - r[1], f - s[1], f + s[1]
        g, h = ROOT * (b - c), ROOT * (b + c)
        out = [even0 + a, odd1 + g, even2 - d, odd3 - h, even0 - a, odd1 - g, even2 + d, odd3 + h]
        for m in range(8):
            turned[here, m * size : (m + 1) * size] = out[m]
        return carry

    lax.fori_loop(0, rows // 8, step, 0)


def send_patches(slots, slices_owned, spectrum, wave_table, end_table, columns, facts, scratch, out_refs):
    squares, ramp, turns, angles, defocus, starts = facts
    ends, waves, turned, out, out_sems = scratch
    rows, size = spectrum[0].shape
    tilt = lax.axis_index("tilt")
    slabs = [(tilt ^ slot) * slices_owned // SLAB for slot in slots]
    gains = [flip_sign(squares, defocus[tilt, slab], columns) * ramp for slab in slabs]
    filtered = [
        jnp.concatenate([(spectrum[i] * gain[i : i + 1, :]).astype(jnp.bfloat16) for gain in gains], 0) for i in range(8)
    ]
    for i in range(2):
        ends[i] = jnp.dot(filtered[i], end_table[:, i * size : (i + 1) * size], preferred_element_type=jnp.float32)
    for i in range(6):
        waves[i] = jnp.dot(filtered[2 + i], wave_table[...], preferred_element_type=jnp.float32)
    inverse_butterflies(ends, waves, turns, turned)
    lane = lax.broadcasted_iota(jnp.int32, (rows, MAIN), 1) // REST
    _, _, first_tap = reach_of(angles[tilt])
    sends = []
    for i, slab in enumerate(slabs):
        rest = jnp.zeros((rows, MAIN), jnp.float32)
        for block in range(XBLK):
            start = starts[tilt, slab, block] + first_tap
            base = pl.multiple_of(jnp.minimum((start // 128) * 128, columns - WINDOW), 128)
            window = turned[i * rows : (i + 1) * rows, pl.ds(base, WINDOW)]
            shift = base - start
            reach = pltpu.roll(window, jnp.where(shift < 0, shift + WINDOW, shift), 1)[:, : 2 * MAIN]
            out[i, :, block * MAIN : (block + 1) * MAIN] = reach[:, :MAIN].astype(jnp.bfloat16)
            last = reach[:, MAIN:]
            rest = jnp.where(lane == block, pltpu.roll(last, block * REST, 1) if block else last, rest)
        out[i, :, XBLK * MAIN :] = rest.astype(jnp.bfloat16)
        sends.append(pltpu.make_async_copy(out.at[i], out_refs[i], out_sems.at[i]))
        sends[-1].start()
    return sends


def first_kernel(slots, slices_owned, image_ref, matrix_ref, angle_ref, defocus_ref, starts_ref, *refs):
    count = len(slots)
    out_refs, spectrum_ref = refs[:count], refs[count]
    image, matrix, angles, defocus, starts, zhi, zlo, held, *scratch, sems, held_sem = refs[count + 1 :]
    rows, columns = image.shape
    size = columns // RADIX
    copies = fetched(
        [image_ref, angle_ref, defocus_ref, starts_ref] + [matrix_ref.at[i] for i in range(5)],
        [image, angles, defocus, starts] + [matrix.at[i] for i in range(5)],
        sems,
    )
    squares, ramp, cosine_turns, sine_turns = column_lines(columns)
    turns = [t[j : j + 1, :] for j in range(3) for t in (cosine_turns, sine_turns)]
    copies[0].wait()
    butterflies(image, turns, zhi, zlo)
    for copy in copies[1:]:
        copy.wait()

    def product(first, lines, table, here):
        top = zhi[first : first + lines].reshape(lines * rows, size)
        rest = zlo[first : first + lines].reshape(lines * rows, size)
        total = jnp.dot(top, matrix[table, :, here], preferred_element_type=jnp.float32)
        total += jnp.dot(top, matrix[table + 1, :, here], preferred_element_type=jnp.float32)
        return total + jnp.dot(rest, matrix[table, :, here], preferred_element_type=jnp.float32)

    spectrum = [product(0, 1, 0, slice(0, size)), product(1, 1, 0, slice(size, 2 * size))]
    mixed = product(2, 6, 2, slice(None))
    for j in range(3):
        real, imag = mixed[2 * j * rows : (2 * j + 1) * rows], mixed[(2 * j + 1) * rows : (2 * j + 2) * rows]
        spectrum += [real[:, :size] + imag[:, size:], imag[:, :size] - real[:, size:]]
    for i in range(8):
        held[i] = spectrum[i]
    keep = pltpu.make_async_copy(held, spectrum_ref, held_sem)
    keep.start()
    facts = (squares, ramp, turns, angles, defocus, starts)
    sends = send_patches(
        slots, slices_owned, spectrum, matrix.at[2], matrix.at[4], columns, facts, scratch, out_refs
    )
    for copy in sends + [keep]:
        copy.wait()


def second_kernel(slots, slices_owned, spectrum_ref, matrix_ref, angle_ref, defocus_ref, starts_ref, *refs):
    count = len(slots)
    out_refs = refs[:count]
    held, matrix, angles, defocus, starts, *scratch, sems = refs[count:]
    columns = RADIX * held.shape[2]
    copies = fetched(
        [spectrum_ref, angle_ref, defocus_ref, starts_ref, matrix_ref.at[2], matrix_ref.at[4]],
        [held, angles, defocus, starts, matrix.at[0], matrix.at[1]],
        sems,
    )
    squares, ramp, cosine_turns, sine_turns = column_lines(columns)
    turns = [t[j : j + 1, :] for j in range(3) for t in (cosine_turns, sine_turns)]
    for copy in copies:
        copy.wait()
    facts = (squares, ramp, turns, angles, defocus, starts)
    sends = send_patches(
        slots, slices_owned, [held[i] for i in range(8)], matrix.at[0], matrix.at[1], columns, facts, scratch, out_refs
    )
    for copy in sends:
        copy.wait()


def column_filtered(slots, later, slices_owned, image, angles, defocus, starts):
    rows, columns = image.shape
    size = columns // RADIX
    matrices = jnp.asarray(column_tables(columns))
    away = pl.BlockSpec(memory_space=pl.ANY)
    spectrum = jax.ShapeDtypeStruct((8, rows, size), jnp.float32)
    patch = jax.ShapeDtypeStruct((rows, PACKED), jnp.bfloat16)
    small = [
        pltpu.SMEM(angles.shape, jnp.float32),
        pltpu.SMEM(defocus.shape, jnp.int32),
        pltpu.SMEM(starts.shape, jnp.int32),
    ]

    def buffers(count):
        return [
            pltpu.VMEM((2, count * rows, size), jnp.float32),
            pltpu.VMEM((6, count * rows, 2 * size), jnp.float32),
            pltpu.VMEM((count * rows, columns), jnp.float32),
            pltpu.VMEM((count, rows, PACKED), jnp.bfloat16),
            pltpu.SemaphoreType.DMA((count,)),
        ]

    def cost(products):
        return pl.CostEstimate(flops=2 * rows * size * size * products, bytes_accessed=3 * 2**20, transcendentals=0)

    params = pltpu.CompilerParams(vmem_limit_bytes=60 * 2**20)
    *first, held = pl.pallas_call(
        functools.partial(first_kernel, slots, slices_owned),
        out_shape=[patch] * len(slots) + [spectrum],
        in_specs=[away] * 5,
        out_specs=[away] * (len(slots) + 1),
        scratch_shapes=[
            pltpu.VMEM((rows, columns), jnp.bfloat16),
            pltpu.VMEM(matrices.shape, jnp.bfloat16),
            *small,
            pltpu.VMEM((8, rows, size), jnp.bfloat16),
            pltpu.VMEM((8, rows, size), jnp.bfloat16),
            pltpu.VMEM(spectrum.shape, jnp.float32),
            *buffers(len(slots)),
            pltpu.SemaphoreType.DMA((9,)),
            pltpu.SemaphoreType.DMA,
        ],
        compiler_params=params,
        cost_estimate=cost(42 + 14 * len(slots)),
        name="forward_and_first_slots",
    )(image, matrices, angles, defocus, starts)
    second = pl.pallas_call(
        functools.partial(second_kernel, later, slices_owned),
        out_shape=[patch] * len(later),
        in_specs=[away] * 5,
        out_specs=[away] * len(later),
        scratch_shapes=[
            pltpu.VMEM(spectrum.shape, jnp.float32),
            pltpu.VMEM((2,) + matrices.shape[1:], jnp.bfloat16),
            *small,
            *buffers(len(later)),
            pltpu.SemaphoreType.DMA((6,)),
        ],
        compiler_params=params,
        cost_estimate=cost(14 * len(later)),
        name="later_slots",
    )(held, matrices, angles, defocus, starts)
    return dict(zip(slots, first)) | dict(zip(later, second))


def after(array, *others):
    away = pl.BlockSpec(memory_space=pl.ANY)
    return pl.pallas_call(
        lambda *refs: None,
        out_shape=jax.ShapeDtypeStruct(array.shape, array.dtype),
        in_specs=[away] * (1 + len(others)),
        out_specs=away,
        input_output_aliases={0: 0},
        cost_estimate=pl.CostEstimate(flops=0, bytes_accessed=0, transcendentals=0),
        name="after",
    )(array, *others)


def prepare_kernel(slots, slices_owned, angles, defocus, rows_ref, weights_ref, waves, mine, order):
    tilt, row = lax.axis_index("tilt"), lax.axis_index("row")
    slab, local_first = tilt * slices_owned // SLAB, tilt * slices_owned % SLAB
    full_rows = waves.shape[0]
    rows = rows_ref.shape[0] // slots
    half = full_rows // 2

    def row_waves(block, carry):
        here = pl.ds(pl.multiple_of(block * rows, rows), rows)
        y = block * rows + lax.broadcasted_iota(jnp.int32, (rows, full_rows), 0)
        column = lax.broadcasted_iota(jnp.int32, (rows, full_rows), 1)
        freq = jnp.where(column <= half, column, column - half)
        angle = ((y * freq) & (full_rows - 1)).astype(jnp.float32) * (2.0 * math.pi / full_rows)
        waves[here, :] = jnp.cos(jnp.where(column <= half, angle, angle - 0.5 * math.pi))
        return carry

    lax.fori_loop(0, full_rows // rows, row_waves, 0)
    own = waves[pl.ds(pl.multiple_of(row * rows, rows), rows), :]
    column = lax.broadcasted_iota(jnp.int32, (8, full_rows), 1)
    freq = jnp.where(column <= half, column, column - half)
    count = jnp.where((freq == 0) | (freq == half), 1.0, 2.0) / full_rows
    for slot in range(slots):
        sign = flip_sign(freq * freq, defocus[tilt ^ slot, slab], full_rows)
        mine[slot * rows : (slot + 1) * rows, :] = own * (sign * count)[:1]
    for block in range(full_rows // rows):
        order[block * rows : (block + 1) * rows, :] = waves[pl.ds(pl.multiple_of((row ^ block) * rows, rows), rows), :]
    rows_ref[...] = lax.dot_general(
        mine[...],
        order[...],
        (((1,), (1,)), ((), ())),
        precision=lax.Precision.HIGHEST,
        preferred_element_type=jnp.float32,
    ).astype(jnp.bfloat16)

    column = lax.broadcasted_iota(jnp.int32, (1, XBW), 1).astype(jnp.float32)
    place = lax.broadcasted_iota(jnp.int32, (2 * MAIN, XBW), 0)
    place = jnp.where(place < MAIN, place, MAIN + place % REST).astype(jnp.float32)
    for slot in range(slots):
        cosine, sine, first_tap = reach_of(angles[tilt ^ slot])
        tap = place + first_tap.astype(jnp.float32)

        def one_slice(c, carry):
            offset = (local_first + c).astype(jnp.float32) - 0.5 * (SLAB - 1)
            centre = 0.5 * XBW + column * cosine + offset * sine
            there = pl.ds(pl.multiple_of(c * XBW, XBW), XBW)
            weights_ref[slot, :, there] = jnp.maximum(0.0, 1.0 - jnp.abs(tap - centre)).astype(jnp.bfloat16)
            return carry

        lax.fori_loop(0, slices_owned, one_slice, 0)


def prepared(slots, slices_owned, rows, full_rows, angles, defocus):
    smem, vmem = pl.BlockSpec(memory_space=pltpu.SMEM), pl.BlockSpec(memory_space=pltpu.VMEM)
    return pl.pallas_call(
        functools.partial(prepare_kernel, slots, slices_owned),
        out_shape=[
            jax.ShapeDtypeStruct((slots * rows, full_rows), jnp.bfloat16),
            jax.ShapeDtypeStruct((slots, 2 * MAIN, slices_owned * XBW), jnp.bfloat16),
        ],
        in_specs=[smem] * 2,
        out_specs=[vmem] * 2,
        scratch_shapes=[
            pltpu.VMEM((full_rows, full_rows), jnp.float32),
            pltpu.VMEM((slots * rows, full_rows), jnp.float32),
            pltpu.VMEM((full_rows, full_rows), jnp.float32),
        ],
        compiler_params=pltpu.CompilerParams(vmem_limit_bytes=32 * 2**20),
        cost_estimate=pl.CostEstimate(flops=2**31, bytes_accessed=6 * 2**20, transcendentals=0),
        name="prepare",
    )(angles, defocus)


def corrected_patches(slot, rows_ref, patch_refs):
    rows = patch_refs[0].shape[0]
    patches = jnp.concatenate([ref[...] for ref in patch_refs], 0)
    image = jnp.dot(rows_ref[slot * rows : (slot + 1) * rows, :], patches, preferred_element_type=jnp.float32)
    lane = lax.broadcasted_iota(jnp.int32, (rows, MAIN), 1) // REST
    main = jnp.concatenate([image[:, block * MAIN : (block + 1) * MAIN] for block in range(XBLK)], 0)
    rest = jnp.concatenate([jnp.where(lane == block, image[:, XBLK * MAIN :], 0.0) for block in range(XBLK)], 0)
    return jnp.concatenate([main, rest], 1).astype(jnp.bfloat16)


def sum_kernel(slots, row_devices, rows_ref, weights_ref, *refs):
    patch_refs, total_ref = refs[:-1], refs[-1]
    parts = [
        corrected_patches(slot, rows_ref, patch_refs[i * row_devices : (i + 1) * row_devices])
        for i, slot in enumerate(slots)
    ]
    step = 4 * XBW
    for first in range(0, total_ref.shape[1], step):
        here = slice(first, first + step)
        total = jnp.dot(parts[0], weights_ref[slots[0], :, here], preferred_element_type=jnp.float32)
        for part, slot in zip(parts[1:], slots[1:]):
            total += jnp.dot(part, weights_ref[slot, :, here], preferred_element_type=jnp.float32)
        total_ref[:, here] = total


def finish_kernel(factor, slots, row_devices, rows_ref, weights_ref, total_ref, *refs):
    patch_refs = refs[: len(slots) * row_devices]
    out_ref, out, sems = refs[len(slots) * row_devices :]
    rows = patch_refs[0].shape[0]
    parts = [
        corrected_patches(slot, rows_ref, patch_refs[i * row_devices : (i + 1) * row_devices])
        for i, slot in enumerate(slots)
    ]
    step = 4
    copies = []
    for group in range(out.shape[0] // step):
        here = slice(group * step * XBW, (group + 1) * step * XBW)
        total = total_ref[:, here]
        for part, slot in zip(parts, slots):
            total += jnp.dot(part, weights_ref[slot, :, here], preferred_element_type=jnp.float32)
        for c in range(step):
            for block in range(XBLK):
                out[group * step + c, :, block * XBW : (block + 1) * XBW] = (
                    factor * total[block * rows : (block + 1) * rows, c * XBW : (c + 1) * XBW]
                ).astype(jnp.bfloat16)
        part = pl.ds(group * step, step)
        copies.append(pltpu.make_async_copy(out.at[part], out_ref.at[part], sems.at[group]))
        copies[-1].start()
    for copy in copies:
        copy.wait()


def interpolation(kernel, slots, weights, row_filters, patches, totals, **call):
    _, _, width = weights.shape
    rows = patches[0][0].shape[0]
    vmem = pl.BlockSpec(memory_space=pltpu.VMEM)
    operands = [row_filters, weights, *totals, *(block for slot in slots for block in patches[slot])]
    flops = 4 * len(slots) * MAIN * width * XBLK * rows
    return pl.pallas_call(
        functools.partial(kernel, slots, len(patches[0])),
        in_specs=[vmem] * len(operands),
        compiler_params=pltpu.CompilerParams(vmem_limit_bytes=32 * 2**20),
        cost_estimate=pl.CostEstimate(flops=flops, bytes_accessed=3 * 2**20, transcendentals=0),
        **call,
    )(*operands)


def summed(row_filters, weights, patches, slots):
    return interpolation(
        sum_kernel,
        slots,
        weights,
        row_filters,
        patches,
        [],
        out_shape=jax.ShapeDtypeStruct((XBLK * patches[0][0].shape[0], weights.shape[2]), jnp.float32),
        out_specs=pl.BlockSpec(memory_space=pltpu.VMEM),
        name="sum_early_tilts",
    )


def finished(row_filters, weights, total, patches, slots, factor):
    shape = (weights.shape[2] // XBW, patches[0][0].shape[0], XBLK * XBW)
    return interpolation(
        functools.partial(finish_kernel, factor),
        slots,
        weights,
        row_filters,
        patches,
        [total],
        out_shape=jax.ShapeDtypeStruct(shape, jnp.bfloat16),
        out_specs=pl.BlockSpec(memory_space=pl.ANY),
        scratch_shapes=[pltpu.VMEM(shape, jnp.bfloat16), pltpu.SemaphoreType.DMA((shape[0] // 4,))],
        name="finish_volume",
    )


def exchange(array, axis, distance):
    count = lax.axis_size(axis)
    return lax.ppermute(array, axis, [(i, i ^ distance) for i in range(count)])


def gather_rows(array, awaited=()):
    blocks = {0: array}
    bit = lax.axis_size("row") // 2
    while bit:
        if bit == 1 and awaited:
            blocks = {d: after(block, *awaited) if d else block for d, block in blocks.items()}
        blocks.update({d ^ bit: exchange(block, "row", bit) for d, block in blocks.items()})
        bit //= 2
    return [blocks[d] for d in sorted(blocks)]


def per_device(projections, tilt_angle, band_start, defocus):
    _, rows, _ = projections.shape
    row_devices, tilt_devices = lax.axis_size("row"), lax.axis_size("tilt")
    slices_owned = SLICES // tilt_devices
    odd, even = list(range(tilt_devices - 1, 0, -2)), list(range(tilt_devices - 2, 0, -2))
    sent = column_filtered(odd, even + [0], slices_owned, projections[0], tilt_angle, defocus, band_start)
    arrived = {0: sent[0]} | {d: exchange(sent[d], "tilt", d) for d in odd}
    row_filters, weights = prepared(tilt_devices, slices_owned, rows, rows * row_devices, tilt_angle, defocus)
    patches = {0: gather_rows(arrived[0], (row_filters,))} | {d: gather_rows(arrived[d]) for d in odd}
    total = summed(row_filters, weights, patches, [0] + odd)
    for d in even:
        arrived[d] = exchange(after(sent[d], *(arrived[o] for o in odd)), "tilt", d)
        patches[d] = gather_rows(arrived[d], (total,))
    return finished(row_filters, weights, total, patches, even, 1.0 / math.sqrt(tilt_devices))


def solution(mesh):
    in_specs = (
        P(("group", "tilt"), "row", None),
        P("group"),
        P("group", None, None),
        P("group", None),
    )
    out_specs = P(("group", "tilt"), "row", None)
    return jax.shard_map(
        per_device, mesh=mesh, in_specs=in_specs, out_specs=out_specs, check_vma=False
    )
```

```python
import functools
import math

import jax
import jax.numpy as jnp
import numpy as np
from jax import lax
from jax.experimental import pallas as pl
from jax.experimental.pallas import tpu as pltpu
from jax.sharding import PartitionSpec as P

SLAB = 16
XBW = 128
BAND = 256
XBLK = 4
SLICES = 64
RADIX = 8
MAIN = 128
REST = 32
REACH = MAIN + REST
PACKED = XBLK * REACH
WINDOW = 384
ROOT = math.sqrt(0.5)


def column_tables(columns):
    size = columns // RADIX
    half = size // 2
    u = np.arange(size)[:, None]

    def angles(freq):
        return 2.0 * np.pi * ((u * freq[None, :]) % columns) / columns

    k0, s0 = RADIX * np.arange(half + 1), RADIX * np.arange(1, half)
    k4 = RADIX * np.arange(half) + 4
    m0 = np.concatenate([np.cos(angles(k0)), -np.sin(angles(s0))], 1)
    m4 = np.concatenate([np.cos(angles(k4)), -np.sin(angles(k4))], 1)
    full = angles(RADIX * np.arange(size))
    waves = np.concatenate([np.cos(full), np.sin(full)], 1)
    ends = np.concatenate([m0, m4], 1)

    def split(table):
        high = table.astype(jnp.bfloat16)
        return high, (table - high.astype(np.float64)).astype(jnp.bfloat16)

    matrices = np.stack([*split(ends), *split(waves), np.concatenate([m0.T, m4.T], 1).astype(jnp.bfloat16)])
    return matrices


def column_lines(columns):
    size = columns // RADIX
    half = size // 2
    line = lax.broadcasted_iota(jnp.int32, (8, size), 0)
    u = lax.broadcasted_iota(jnp.int32, (8, size), 1)
    freq = jnp.where(line == 0, RADIX * jnp.where(u <= half, u, u - half), RADIX * (u & (half - 1)) + 4)
    freq = jnp.where(line < 2, freq, RADIX * u + line // 2)
    fold = jnp.minimum(freq, columns - freq)
    count = jnp.where((fold == 0) | (fold == columns // 2), 1.0, 2.0)
    gain = count * (fold.astype(jnp.float32) + 0.5) * (2.0 / (columns * columns))
    angle = (u * (line + 1)).astype(jnp.float32) * (2.0 * math.pi / columns)
    return fold * fold, gain, jnp.cos(angle), jnp.sin(angle)


def flip_sign(squares, defocus, length):
    cycles = lax.div(squares * defocus, jnp.int32(length * length))
    return (1 - 2 * (cycles & 1)).astype(jnp.float32)


def fetched(sources, targets, sems):
    copies = [pltpu.make_async_copy(s, t, sems.at[i]) for i, (s, t) in enumerate(zip(sources, targets))]
    for copy in copies:
        copy.start()
    return copies


def reach_of(angle):
    line = jnp.full((8, XBW), angle, jnp.float32)
    cosine, sine = jnp.cos(line), jnp.sin(line)
    lowest = 0.5 * XBW + jnp.minimum((XBW - 1) * cosine, 0.0) - 0.5 * (SLAB - 1) * jnp.abs(sine)
    first = jnp.clip(jnp.floor(lowest) - 8.0, 0.0, float(BAND - REACH))
    return cosine[:1], sine[:1], jnp.max(first).astype(jnp.int32)


def butterflies(image, turns, zhi, zlo):
    rows, columns = image.shape
    size = columns // RADIX

    def step(i, carry):
        here = pl.ds(pl.multiple_of(i * 16, 16), 16)
        x = [image[here, m * size : (m + 1) * size].astype(jnp.float32) for m in range(8)]
        p0, p1, p2, p3 = (x[m] + x[m + 4] for m in range(4))
        q0, q1, q2, q3 = (x[m] - x[m + 4] for m in range(4))
        e, f = p0 + p2, p1 + p3
        g, h = ROOT * (q1 - q3), ROOT * (q1 + q3)
        z = [e + f, e - f]
        for j, (real, imag) in enumerate([(q0 + g, -q2 - h), (p0 - p2, p3 - p1), (q0 - g, q2 - h)]):
            c, s = turns[2 * j], turns[2 * j + 1]
            z += [real * c + imag * s, imag * c - real * s]
        for line in range(8):
            top = z[line].astype(jnp.bfloat16)
            zhi[line, here, :] = top
            zlo[line, here, :] = (z[line] - top.astype(jnp.float32)).astype(jnp.bfloat16)
        return carry

    lax.fori_loop(0, rows // 16, step, 0)


def inverse_butterflies(ends, waves, turns, turned):
    rows, columns = turned.shape
    size = columns // RADIX

    def step(i, carry):
        here = pl.ds(pl.multiple_of(i * 8, 8), 8)
        r, s = [], []
        for j in range(3):
            c, d = turns[2 * j], turns[2 * j + 1]
            real = waves[2 * j, here, :size] - waves[2 * j + 1, here, size:]
            imag = waves[2 * j, here, size:] + waves[2 * j + 1, here, :size]
            r.append(real * c - imag * d)
            s.append(real * d + imag * c)
        e, f = ends[0, here, :] + ends[1, here, :], ends[0, here, :] - ends[1, here, :]
        a, b, c, d = r[0] + r[2], r[0] - r[2], s[0] + s[2], s[0] - s[2]
        even0, even2, odd1, odd3 = e + r[1], e - r[1], f - s[1], f + s[1]
        g, h = ROOT * (b - c), ROOT * (b + c)
        out = [even0 + a, odd1 + g, even2 - d, odd3 - h, even0 - a, odd1 - g, even2 + d, odd3 + h]
        for m in range(8):
            turned[here, m * size : (m + 1) * size] = out[m]
        return carry

    lax.fori_loop(0, rows // 8, step, 0)


def send_patches(slots, slices_owned, spectrum, wave_table, end_table, columns, facts, scratch, out_refs):
    squares, ramp, turns, angles, defocus, starts = facts
    ends, waves, turned, out, out_sems = scratch
    rows, size = spectrum[0].shape
    tilt = lax.axis_index("tilt")
    slabs = [(tilt ^ slot) * slices_owned // SLAB for slot in slots]
    gains = [flip_sign(squares, defocus[tilt, slab], columns) * ramp for slab in slabs]
    filtered = [
        jnp.concatenate([(spectrum[i] * gain[i : i + 1, :]).astype(jnp.bfloat16) for gain in gains], 0) for i in range(8)
    ]
    for i in range(2):
        ends[i] = jnp.dot(filtered[i], end_table[:, i * size : (i + 1) * size], preferred_element_type=jnp.float32)
    for i in range(6):
        waves[i] = jnp.dot(filtered[2 + i], wave_table[...], preferred_element_type=jnp.float32)
    inverse_butterflies(ends, waves, turns, turned)
    lane = lax.broadcasted_iota(jnp.int32, (rows, MAIN), 1) // REST
    _, _, first_tap = reach_of(angles[tilt])
    sends = []
    for i, slab in enumerate(slabs):
        rest = jnp.zeros((rows, MAIN), jnp.float32)
        for block in range(XBLK):
            start = starts[tilt, slab, block] + first_tap
            base = pl.multiple_of(jnp.minimum((start // 128) * 128, columns - WINDOW), 128)
            window = turned[i * rows : (i + 1) * rows, pl.ds(base, WINDOW)]
            shift = base - start
            reach = pltpu.roll(window, jnp.where(shift < 0, shift + WINDOW, shift), 1)[:, : 2 * MAIN]
            out[i, :, block * MAIN : (block + 1) * MAIN] = reach[:, :MAIN].astype(jnp.bfloat16)
            last = reach[:, MAIN:]
            rest = jnp.where(lane == block, pltpu.roll(last, block * REST, 1) if block else last, rest)
        out[i, :, XBLK * MAIN :] = rest.astype(jnp.bfloat16)
        sends.append(pltpu.make_async_copy(out.at[i], out_refs[i], out_sems.at[i]))
        sends[-1].start()
    return sends


def first_kernel(slots, slices_owned, image_ref, matrix_ref, angle_ref, defocus_ref, starts_ref, *refs):
    count = len(slots)
    out_refs, spectrum_ref = refs[:count], refs[count]
    image, matrix, angles, defocus, starts, zhi, zlo, held, *scratch, sems, held_sem = refs[count + 1 :]
    rows, columns = image.shape
    size = columns // RADIX
    copies = fetched(
        [image_ref, angle_ref, defocus_ref, starts_ref] + [matrix_ref.at[i] for i in range(5)],
        [image, angles, defocus, starts] + [matrix.at[i] for i in range(5)],
        sems,
    )
    squares, ramp, cosine_turns, sine_turns = column_lines(columns)
    turns = [t[j : j + 1, :] for j in range(3) for t in (cosine_turns, sine_turns)]
    copies[0].wait()
    butterflies(image, turns, zhi, zlo)
    for copy in copies[1:]:
        copy.wait()

    def product(first, lines, table, here):
        top = zhi[first : first + lines].reshape(lines * rows, size)
        rest = zlo[first : first + lines].reshape(lines * rows, size)
        total = jnp.dot(top, matrix[table, :, here], preferred_element_type=jnp.float32)
        total += jnp.dot(top, matrix[table + 1, :, here], preferred_element_type=jnp.float32)
        return total + jnp.dot(rest, matrix[table, :, here], preferred_element_type=jnp.float32)

    spectrum = [product(0, 1, 0, slice(0, size)), product(1, 1, 0, slice(size, 2 * size))]
    mixed = product(2, 6, 2, slice(None))
    for j in range(3):
        real, imag = mixed[2 * j * rows : (2 * j + 1) * rows], mixed[(2 * j + 1) * rows : (2 * j + 2) * rows]
        spectrum += [real[:, :size] + imag[:, size:], imag[:, :size] - real[:, size:]]
    for i in range(8):
        held[i] = spectrum[i]
    keep = pltpu.make_async_copy(held, spectrum_ref, held_sem)
    keep.start()
    facts = (squares, ramp, turns, angles, defocus, starts)
    sends = send_patches(
        slots, slices_owned, spectrum, matrix.at[2], matrix.at[4], columns, facts, scratch, out_refs
    )
    for copy in sends + [keep]:
        copy.wait()


def second_kernel(slots, slices_owned, spectrum_ref, matrix_ref, angle_ref, defocus_ref, starts_ref, *refs):
    count = len(slots)
    out_refs = refs[:count]
    held, matrix, angles, defocus, starts, *scratch, sems = refs[count:]
    columns = RADIX * held.shape[2]
    copies = fetched(
        [spectrum_ref, angle_ref, defocus_ref, starts_ref, matrix_ref.at[2], matrix_ref.at[4]],
        [held, angles, defocus, starts, matrix.at[0], matrix.at[1]],
        sems,
    )
    squares, ramp, cosine_turns, sine_turns = column_lines(columns)
    turns = [t[j : j + 1, :] for j in range(3) for t in (cosine_turns, sine_turns)]
    for copy in copies:
        copy.wait()
    facts = (squares, ramp, turns, angles, defocus, starts)
    sends = send_patches(
        slots, slices_owned, [held[i] for i in range(8)], matrix.at[0], matrix.at[1], columns, facts, scratch, out_refs
    )
    for copy in sends:
        copy.wait()


def column_filtered(slots, later, slices_owned, image, angles, defocus, starts):
    rows, columns = image.shape
    size = columns // RADIX
    matrices = jnp.asarray(column_tables(columns))
    away = pl.BlockSpec(memory_space=pl.ANY)
    spectrum = jax.ShapeDtypeStruct((8, rows, size), jnp.float32)
    patch = jax.ShapeDtypeStruct((rows, PACKED), jnp.bfloat16)
    small = [
        pltpu.SMEM(angles.shape, jnp.float32),
        pltpu.SMEM(defocus.shape, jnp.int32),
        pltpu.SMEM(starts.shape, jnp.int32),
    ]

    def buffers(count):
        return [
            pltpu.VMEM((2, count * rows, size), jnp.float32),
            pltpu.VMEM((6, count * rows, 2 * size), jnp.float32),
            pltpu.VMEM((count * rows, columns), jnp.float32),
            pltpu.VMEM((count, rows, PACKED), jnp.bfloat16),
            pltpu.SemaphoreType.DMA((count,)),
        ]

    def cost(products):
        return pl.CostEstimate(flops=2 * rows * size * size * products, bytes_accessed=3 * 2**20, transcendentals=0)

    params = pltpu.CompilerParams(vmem_limit_bytes=60 * 2**20)
    *first, held = pl.pallas_call(
        functools.partial(first_kernel, slots, slices_owned),
        out_shape=[patch] * len(slots) + [spectrum],
        in_specs=[away] * 5,
        out_specs=[away] * (len(slots) + 1),
        scratch_shapes=[
            pltpu.VMEM((rows, columns), jnp.bfloat16),
            pltpu.VMEM(matrices.shape, jnp.bfloat16),
            *small,
            pltpu.VMEM((8, rows, size), jnp.bfloat16),
            pltpu.VMEM((8, rows, size), jnp.bfloat16),
            pltpu.VMEM(spectrum.shape, jnp.float32),
            *buffers(len(slots)),
            pltpu.SemaphoreType.DMA((9,)),
            pltpu.SemaphoreType.DMA,
        ],
        compiler_params=params,
        cost_estimate=cost(42 + 14 * len(slots)),
        name="forward_and_first_slots",
    )(image, matrices, angles, defocus, starts)
    second = pl.pallas_call(
        functools.partial(second_kernel, later, slices_owned),
        out_shape=[patch] * len(later),
        in_specs=[away] * 5,
        out_specs=[away] * len(later),
        scratch_shapes=[
            pltpu.VMEM(spectrum.shape, jnp.float32),
            pltpu.VMEM((2,) + matrices.shape[1:], jnp.bfloat16),
            *small,
            *buffers(len(later)),
            pltpu.SemaphoreType.DMA((6,)),
        ],
        compiler_params=params,
        cost_estimate=cost(14 * len(later)),
        name="later_slots",
    )(held, matrices, angles, defocus, starts)
    return dict(zip(slots, first)) | dict(zip(later, second))


def after(array, *others):
    away = pl.BlockSpec(memory_space=pl.ANY)
    return pl.pallas_call(
        lambda *refs: None,
        out_shape=jax.ShapeDtypeStruct(array.shape, array.dtype),
        in_specs=[away] * (1 + len(others)),
        out_specs=away,
        input_output_aliases={0: 0},
        compiler_params=pltpu.CompilerParams(vmem_limit_bytes=2**20),
        cost_estimate=pl.CostEstimate(flops=0, bytes_accessed=0, transcendentals=0),
        name="after",
    )(array, *others)


def prepare_kernel(slots, slices_owned, angles, defocus, rows_ref, weights_ref, waves, mine, order):
    tilt, row = lax.axis_index("tilt"), lax.axis_index("row")
    slab, local_first = tilt * slices_owned // SLAB, tilt * slices_owned % SLAB
    full_rows = waves.shape[0]
    rows = rows_ref.shape[0] // slots
    half = full_rows // 2

    def row_waves(block, carry):
        here = pl.ds(pl.multiple_of(block * rows, rows), rows)
        y = block * rows + lax.broadcasted_iota(jnp.int32, (rows, full_rows), 0)
        column = lax.broadcasted_iota(jnp.int32, (rows, full_rows), 1)
        freq = jnp.where(column <= half, column, column - half)
        angle = ((y * freq) & (full_rows - 1)).astype(jnp.float32) * (2.0 * math.pi / full_rows)
        waves[here, :] = jnp.cos(jnp.where(column <= half, angle, angle - 0.5 * math.pi))
        return carry

    lax.fori_loop(0, full_rows // rows, row_waves, 0)
    own = waves[pl.ds(pl.multiple_of(row * rows, rows), rows), :]
    column = lax.broadcasted_iota(jnp.int32, (8, full_rows), 1)
    freq = jnp.where(column <= half, column, column - half)
    count = jnp.where((freq == 0) | (freq == half), 1.0, 2.0) / full_rows
    for slot in range(slots):
        sign = flip_sign(freq * freq, defocus[tilt ^ slot, slab], full_rows)
        mine[slot * rows : (slot + 1) * rows, :] = own * (sign * count)[:1]
    for block in range(full_rows // rows):
        order[block * rows : (block + 1) * rows, :] = waves[pl.ds(pl.multiple_of((row ^ block) * rows, rows), rows), :]
    rows_ref[...] = lax.dot_general(
        mine[...],
        order[...],
        (((1,), (1,)), ((), ())),
        precision=lax.Precision.HIGHEST,
        preferred_element_type=jnp.float32,
    ).astype(jnp.bfloat16)

    column = lax.broadcasted_iota(jnp.int32, (1, XBW), 1).astype(jnp.float32)
    place = lax.broadcasted_iota(jnp.int32, (2 * MAIN, XBW), 0)
    place = jnp.where(place < MAIN, place, MAIN + place % REST).astype(jnp.float32)
    for slot in range(slots):
        cosine, sine, first_tap = reach_of(angles[tilt ^ slot])
        tap = place + first_tap.astype(jnp.float32)

        def one_slice(c, carry):
            offset = (local_first + c).astype(jnp.float32) - 0.5 * (SLAB - 1)
            centre = 0.5 * XBW + column * cosine + offset * sine
            there = pl.ds(pl.multiple_of(c * XBW, XBW), XBW)
            weights_ref[slot, :, there] = jnp.maximum(0.0, 1.0 - jnp.abs(tap - centre)).astype(jnp.bfloat16)
            return carry

        lax.fori_loop(0, slices_owned, one_slice, 0)


def prepared(slots, slices_owned, rows, full_rows, angles, defocus):
    smem, vmem = pl.BlockSpec(memory_space=pltpu.SMEM), pl.BlockSpec(memory_space=pltpu.VMEM)
    return pl.pallas_call(
        functools.partial(prepare_kernel, slots, slices_owned),
        out_shape=[
            jax.ShapeDtypeStruct((slots * rows, full_rows), jnp.bfloat16),
            jax.ShapeDtypeStruct((slots, 2 * MAIN, slices_owned * XBW), jnp.bfloat16),
        ],
        in_specs=[smem] * 2,
        out_specs=[vmem] * 2,
        scratch_shapes=[
            pltpu.VMEM((full_rows, full_rows), jnp.float32),
            pltpu.VMEM((slots * rows, full_rows), jnp.float32),
            pltpu.VMEM((full_rows, full_rows), jnp.float32),
        ],
        compiler_params=pltpu.CompilerParams(vmem_limit_bytes=32 * 2**20),
        cost_estimate=pl.CostEstimate(flops=2**31, bytes_accessed=6 * 2**20, transcendentals=0),
        name="prepare",
    )(angles, defocus)


def corrected_patches(slot, rows_ref, patch_refs):
    rows = patch_refs[0].shape[0]
    patches = jnp.concatenate([ref[...] for ref in patch_refs], 0)
    image = jnp.dot(rows_ref[slot * rows : (slot + 1) * rows, :], patches, preferred_element_type=jnp.float32)
    lane = lax.broadcasted_iota(jnp.int32, (rows, MAIN), 1) // REST
    main = jnp.concatenate([image[:, block * MAIN : (block + 1) * MAIN] for block in range(XBLK)], 0)
    rest = jnp.concatenate([jnp.where(lane == block, image[:, XBLK * MAIN :], 0.0) for block in range(XBLK)], 0)
    return jnp.concatenate([main, rest], 1).astype(jnp.bfloat16)


def sum_kernel(slots, row_devices, rows_ref, weights_ref, *refs):
    patch_refs, total_ref = refs[:-1], refs[-1]
    parts = [
        corrected_patches(slot, rows_ref, patch_refs[i * row_devices : (i + 1) * row_devices])
        for i, slot in enumerate(slots)
    ]
    step = 4 * XBW
    for first in range(0, total_ref.shape[1], step):
        here = slice(first, first + step)
        total = jnp.dot(parts[0], weights_ref[slots[0], :, here], preferred_element_type=jnp.float32)
        for part, slot in zip(parts[1:], slots[1:]):
            total += jnp.dot(part, weights_ref[slot, :, here], preferred_element_type=jnp.float32)
        total_ref[:, here] = total


def finish_kernel(factor, slots, row_devices, rows_ref, weights_ref, total_ref, *refs):
    patch_refs = refs[: len(slots) * row_devices]
    out_ref, out, sems = refs[len(slots) * row_devices :]
    rows = patch_refs[0].shape[0]
    parts = [
        corrected_patches(slot, rows_ref, patch_refs[i * row_devices : (i + 1) * row_devices])
        for i, slot in enumerate(slots)
    ]
    step = 4
    copies = []
    for group in range(out.shape[0] // step):
        here = slice(group * step * XBW, (group + 1) * step * XBW)
        total = total_ref[:, here]
        for part, slot in zip(parts, slots):
            total += jnp.dot(part, weights_ref[slot, :, here], preferred_element_type=jnp.float32)
        for c in range(step):
            for block in range(XBLK):
                out[group * step + c, :, block * XBW : (block + 1) * XBW] = (
                    factor * total[block * rows : (block + 1) * rows, c * XBW : (c + 1) * XBW]
                ).astype(jnp.bfloat16)
        part = pl.ds(group * step, step)
        copies.append(pltpu.make_async_copy(out.at[part], out_ref.at[part], sems.at[group]))
        copies[-1].start()
    for copy in copies:
        copy.wait()


def interpolation(kernel, slots, weights, row_filters, patches, totals, **call):
    _, _, width = weights.shape
    rows = patches[0][0].shape[0]
    vmem = pl.BlockSpec(memory_space=pltpu.VMEM)
    operands = [row_filters, weights, *totals, *(block for slot in slots for block in patches[slot])]
    flops = 4 * len(slots) * MAIN * width * XBLK * rows
    return pl.pallas_call(
        functools.partial(kernel, slots, len(patches[0])),
        in_specs=[vmem] * len(operands),
        compiler_params=pltpu.CompilerParams(vmem_limit_bytes=32 * 2**20),
        cost_estimate=pl.CostEstimate(flops=flops, bytes_accessed=3 * 2**20, transcendentals=0),
        **call,
    )(*operands)


def summed(row_filters, weights, patches, slots):
    return interpolation(
        sum_kernel,
        slots,
        weights,
        row_filters,
        patches,
        [],
        out_shape=jax.ShapeDtypeStruct((XBLK * patches[0][0].shape[0], weights.shape[2]), jnp.float32),
        out_specs=pl.BlockSpec(memory_space=pltpu.VMEM),
        name="sum_early_tilts",
    )


def finished(row_filters, weights, total, patches, slots, factor):
    shape = (weights.shape[2] // XBW, patches[0][0].shape[0], XBLK * XBW)
    return interpolation(
        functools.partial(finish_kernel, factor),
        slots,
        weights,
        row_filters,
        patches,
        [total],
        out_shape=jax.ShapeDtypeStruct(shape, jnp.bfloat16),
        out_specs=pl.BlockSpec(memory_space=pl.ANY),
        scratch_shapes=[pltpu.VMEM(shape, jnp.bfloat16), pltpu.SemaphoreType.DMA((shape[0] // 4,))],
        name="finish_volume",
    )


def exchange(array, axis, distance):
    count = lax.axis_size(axis)
    return lax.ppermute(array, axis, [(i, i ^ distance) for i in range(count)])


def gather_rows(array, awaited=()):
    blocks = {0: array}
    bit = lax.axis_size("row") // 2
    while bit:
        if bit == 1 and awaited:
            blocks = {d: after(block, *awaited) if d else block for d, block in blocks.items()}
        blocks.update({d ^ bit: exchange(block, "row", bit) for d, block in blocks.items()})
        bit //= 2
    return [blocks[d] for d in sorted(blocks)]


def per_device(projections, tilt_angle, band_start, defocus):
    _, rows, _ = projections.shape
    row_devices, tilt_devices = lax.axis_size("row"), lax.axis_size("tilt")
    slices_owned = SLICES // tilt_devices
    odd, even = list(range(tilt_devices - 1, 0, -2)), list(range(tilt_devices - 2, 0, -2))
    sent = column_filtered(odd, even + [0], slices_owned, projections[0], tilt_angle, defocus, band_start)
    arrived = {0: sent[0]} | {d: exchange(sent[d], "tilt", d) for d in odd}
    row_filters, weights = prepared(tilt_devices, slices_owned, rows, rows * row_devices, tilt_angle, defocus)
    patches = {0: gather_rows(arrived[0], (row_filters,))} | {d: gather_rows(arrived[d]) for d in odd}
    total = summed(row_filters, weights, patches, [0] + odd)
    for d in even:
        arrived[d] = exchange(after(sent[d], *(arrived[o] for o in odd)), "tilt", d)
        patches[d] = gather_rows(arrived[d], (total,))
    return finished(row_filters, weights, total, patches, even, 1.0 / math.sqrt(tilt_devices))


def solution(mesh):
    in_specs = (
        P(("group", "tilt"), "row", None),
        P("group"),
        P("group", None, None),
        P("group", None),
    )
    out_specs = P(("group", "tilt"), "row", None)
    return jax.shard_map(
        per_device, mesh=mesh, in_specs=in_specs, out_specs=out_specs, check_vma=False
    )
```

```python
import functools
import math

import jax
import jax.numpy as jnp
import numpy as np
from jax import lax
from jax.experimental import pallas as pl
from jax.experimental.pallas import tpu as pltpu
from jax.sharding import PartitionSpec as P

SLAB = 16
XBW = 128
BAND = 256
XBLK = 4
SLICES = 64
RADIX = 8
MAIN = 128
REST = 16
REACH = MAIN + REST
WINDOW = 384
ROOT = math.sqrt(0.5)


def split(table):
    high = table.astype(jnp.bfloat16)
    return high, (table - high.astype(np.float64)).astype(jnp.bfloat16)


def column_tables(columns):
    size = columns // RADIX
    half = size // 2
    u = np.arange(size)[:, None]

    def angles(freq):
        return 2.0 * np.pi * ((u * freq[None, :]) % columns) / columns

    k0, s0 = RADIX * np.arange(half + 1), RADIX * np.arange(1, half)
    k4 = RADIX * np.arange(half) + 4
    m0 = np.concatenate([np.cos(angles(k0)), -np.sin(angles(s0))], 1)
    m4 = np.concatenate([np.cos(angles(k4)), -np.sin(angles(k4))], 1)
    full = angles(RADIX * np.arange(size))
    waves = np.concatenate([np.cos(full), np.sin(full)], 1)
    ends = np.concatenate([m0, m4], 1)

    matrices = np.stack([*split(ends), *split(waves), np.concatenate([m0.T, m4.T], 1).astype(jnp.bfloat16)])
    return matrices


def column_lines(columns):
    size = columns // RADIX
    half = size // 2
    line = lax.broadcasted_iota(jnp.int32, (8, size), 0)
    u = lax.broadcasted_iota(jnp.int32, (8, size), 1)
    freq = jnp.where(line == 0, RADIX * jnp.where(u <= half, u, u - half), RADIX * (u & (half - 1)) + 4)
    freq = jnp.where(line < 2, freq, RADIX * u + line // 2)
    fold = jnp.minimum(freq, columns - freq)
    count = jnp.where((fold == 0) | (fold == columns // 2), 1.0, 2.0)
    gain = count * (fold.astype(jnp.float32) + 0.5) * (2.0 / (columns * columns))
    angle = (u * (line + 1)).astype(jnp.float32) * (2.0 * math.pi / columns)
    return fold * fold, gain, jnp.cos(angle), jnp.sin(angle)


def row_tables(full_rows):
    half = full_rows // 2
    column = np.arange(full_rows)
    freq = np.where(column <= half, column, column - half)
    angle = 2.0 * np.pi * (np.arange(full_rows)[:, None] * freq[None, :] % full_rows) / full_rows
    return np.stack(split(np.where(column[None, :] <= half, np.cos(angle), np.sin(angle))))


def packed_shape(rows):
    return (2 * rows + rows // 4, 2 * MAIN)


def flip_sign(squares, defocus, length):
    cycles = lax.div(squares * defocus, jnp.int32(length * length))
    return (1 - 2 * (cycles & 1)).astype(jnp.float32)


def fetched(sources, targets, sems):
    copies = [pltpu.make_async_copy(s, t, sems.at[i]) for i, (s, t) in enumerate(zip(sources, targets))]
    for copy in copies:
        copy.start()
    return copies


def reach_of(angle):
    line = jnp.full((8, XBW), angle, jnp.float32)
    cosine, sine = jnp.cos(line), jnp.sin(line)
    lowest = 0.5 * XBW + jnp.minimum((XBW - 1) * cosine, 0.0) - 0.5 * (SLAB - 1) * jnp.abs(sine)
    first = jnp.clip(jnp.floor(lowest) - 4.0, 0.0, float(BAND - REACH))
    return cosine[:1], sine[:1], jnp.max(first).astype(jnp.int32)


def butterflies(image, turns, zhi, zlo):
    rows, columns = image.shape
    size = columns // RADIX

    def step(i, carry):
        here = pl.ds(pl.multiple_of(i * 16, 16), 16)
        x = [image[here, m * size : (m + 1) * size].astype(jnp.float32) for m in range(8)]
        p0, p1, p2, p3 = (x[m] + x[m + 4] for m in range(4))
        q0, q1, q2, q3 = (x[m] - x[m + 4] for m in range(4))
        e, f = p0 + p2, p1 + p3
        g, h = ROOT * (q1 - q3), ROOT * (q1 + q3)
        z = [e + f, e - f]
        for j, (real, imag) in enumerate([(q0 + g, -q2 - h), (p0 - p2, p3 - p1), (q0 - g, q2 - h)]):
            c, s = turns[2 * j], turns[2 * j + 1]
            z += [real * c + imag * s, imag * c - real * s]
        for line in range(8):
            top = z[line].astype(jnp.bfloat16)
            zhi[line, here, :] = top
            zlo[line, here, :] = (z[line] - top.astype(jnp.float32)).astype(jnp.bfloat16)
        return carry

    lax.fori_loop(0, rows // 16, step, 0)


def inverse_butterflies(ends, waves, turns, turned):
    rows, columns = turned.shape
    size = columns // RADIX

    def step(i, carry):
        here = pl.ds(pl.multiple_of(i * 8, 8), 8)
        r, s = [], []
        for j in range(3):
            c, d = turns[2 * j], turns[2 * j + 1]
            real = waves[2 * j, here, :size] - waves[2 * j + 1, here, size:]
            imag = waves[2 * j, here, size:] + waves[2 * j + 1, here, :size]
            r.append(real * c - imag * d)
            s.append(real * d + imag * c)
        e, f = ends[0, here, :] + ends[1, here, :], ends[0, here, :] - ends[1, here, :]
        a, b, c, d = r[0] + r[2], r[0] - r[2], s[0] + s[2], s[0] - s[2]
        even0, even2, odd1, odd3 = e + r[1], e - r[1], f - s[1], f + s[1]
        g, h = ROOT * (b - c), ROOT * (b + c)
        out = [even0 + a, odd1 + g, even2 - d, odd3 - h, even0 - a, odd1 - g, even2 + d, odd3 + h]
        for m in range(8):
            turned[here, m * size : (m + 1) * size] = out[m]
        return carry

    lax.fori_loop(0, rows // 8, step, 0)


def send_patches(slots, slices_owned, spectrum, wave_table, end_table, columns, facts, scratch, out_refs):
    squares, ramp, turns, angles, defocus, starts = facts
    ends, waves, turned, out, out_sems = scratch
    rows, size = spectrum[0].shape
    tilt = lax.axis_index("tilt")
    slabs = [(tilt ^ slot) * slices_owned // SLAB for slot in slots]
    gains = [flip_sign(squares, defocus[tilt, slab], columns) * ramp for slab in slabs]
    filtered = [
        jnp.concatenate([(spectrum[i] * gain[i : i + 1, :]).astype(jnp.bfloat16) for gain in gains], 0) for i in range(8)
    ]
    for i in range(2):
        ends[i] = jnp.dot(filtered[i], end_table[:, i * size : (i + 1) * size], preferred_element_type=jnp.float32)
    for i in range(6):
        waves[i] = jnp.dot(filtered[2 + i], wave_table[...], preferred_element_type=jnp.float32)
    inverse_butterflies(ends, waves, turns, turned)
    lane = lax.broadcasted_iota(jnp.int32, (rows, MAIN), 1) // REST
    _, _, first_tap = reach_of(angles[tilt])
    sends = []
    for i, slab in enumerate(slabs):
        rest = jnp.zeros((rows, MAIN), jnp.float32)
        for block in range(XBLK):
            start = starts[tilt, slab, block] + first_tap
            base = pl.multiple_of(jnp.minimum((start // 128) * 128, columns - WINDOW), 128)
            window = turned[i * rows : (i + 1) * rows, pl.ds(base, WINDOW)]
            shift = base - start
            reach = pltpu.roll(window, jnp.where(shift < 0, shift + WINDOW, shift), 1)[:, : 2 * MAIN]
            there = slice(block // 2 * rows, (block // 2 + 1) * rows), slice(block % 2 * MAIN, (block % 2 + 1) * MAIN)
            out[i, *there] = reach[:, :MAIN].astype(jnp.bfloat16)
            last = reach[:, MAIN:]
            rest = jnp.where(lane == block, pltpu.roll(last, block * REST, 1) if block else last, rest)
        quarters = [rest[q * rows // 4 : (q + 1) * rows // 4] for q in range(4)]
        for tile in range(2):
            right = pltpu.roll(quarters[2 * tile + 1], XBLK * REST, 1)
            both = jnp.where(lane[: rows // 4] < XBLK, quarters[2 * tile], right)
            out[i, 2 * rows :, tile * MAIN : (tile + 1) * MAIN] = both.astype(jnp.bfloat16)
        sends.append(pltpu.make_async_copy(out.at[i], out_refs[i], out_sems.at[i]))
        sends[-1].start()
    return sends


def first_kernel(slots, slices_owned, image_ref, matrix_ref, angle_ref, defocus_ref, starts_ref, *refs):
    count = len(slots)
    out_refs, spectrum_ref = refs[:count], refs[count]
    image, matrix, angles, defocus, starts, zhi, zlo, held, *scratch, sems, held_sem = refs[count + 1 :]
    rows, columns = image.shape
    size = columns // RADIX
    copies = fetched(
        [image_ref, angle_ref, defocus_ref, starts_ref] + [matrix_ref.at[i] for i in range(5)],
        [image, angles, defocus, starts] + [matrix.at[i] for i in range(5)],
        sems,
    )
    squares, ramp, cosine_turns, sine_turns = column_lines(columns)
    turns = [t[j : j + 1, :] for j in range(3) for t in (cosine_turns, sine_turns)]
    copies[0].wait()
    butterflies(image, turns, zhi, zlo)
    for copy in copies[1:]:
        copy.wait()

    def product(first, lines, table, here):
        top = zhi[first : first + lines].reshape(lines * rows, size)
        rest = zlo[first : first + lines].reshape(lines * rows, size)
        total = jnp.dot(top, matrix[table, :, here], preferred_element_type=jnp.float32)
        total += jnp.dot(top, matrix[table + 1, :, here], preferred_element_type=jnp.float32)
        return total + jnp.dot(rest, matrix[table, :, here], preferred_element_type=jnp.float32)

    spectrum = [product(0, 1, 0, slice(0, size)), product(1, 1, 0, slice(size, 2 * size))]
    mixed = product(2, 6, 2, slice(None))
    for j in range(3):
        real, imag = mixed[2 * j * rows : (2 * j + 1) * rows], mixed[(2 * j + 1) * rows : (2 * j + 2) * rows]
        spectrum += [real[:, :size] + imag[:, size:], imag[:, :size] - real[:, size:]]
    for i in range(8):
        held[i] = spectrum[i]
    keep = pltpu.make_async_copy(held, spectrum_ref, held_sem)
    keep.start()
    facts = (squares, ramp, turns, angles, defocus, starts)
    sends = send_patches(
        slots, slices_owned, spectrum, matrix.at[2], matrix.at[4], columns, facts, scratch, out_refs
    )
    for copy in sends + [keep]:
        copy.wait()


def second_kernel(slots, slices_owned, spectrum_ref, matrix_ref, angle_ref, defocus_ref, starts_ref, *refs):
    count = len(slots)
    out_refs = refs[:count]
    held, matrix, angles, defocus, starts, *scratch, sems = refs[count:]
    columns = RADIX * held.shape[2]
    copies = fetched(
        [spectrum_ref, angle_ref, defocus_ref, starts_ref, matrix_ref.at[2], matrix_ref.at[4]],
        [held, angles, defocus, starts, matrix.at[0], matrix.at[1]],
        sems,
    )
    squares, ramp, cosine_turns, sine_turns = column_lines(columns)
    turns = [t[j : j + 1, :] for j in range(3) for t in (cosine_turns, sine_turns)]
    for copy in copies:
        copy.wait()
    facts = (squares, ramp, turns, angles, defocus, starts)
    sends = send_patches(
        slots, slices_owned, [held[i] for i in range(8)], matrix.at[0], matrix.at[1], columns, facts, scratch, out_refs
    )
    for copy in sends:
        copy.wait()


def column_filtered(slots, later, slices_owned, image, angles, defocus, starts):
    rows, columns = image.shape
    size = columns // RADIX
    matrices = jnp.asarray(column_tables(columns))
    away = pl.BlockSpec(memory_space=pl.ANY)
    spectrum = jax.ShapeDtypeStruct((8, rows, size), jnp.float32)
    patch = jax.ShapeDtypeStruct(packed_shape(rows), jnp.bfloat16)
    small = [
        pltpu.SMEM(angles.shape, jnp.float32),
        pltpu.SMEM(defocus.shape, jnp.int32),
        pltpu.SMEM(starts.shape, jnp.int32),
    ]

    def buffers(count):
        return [
            pltpu.VMEM((2, count * rows, size), jnp.float32),
            pltpu.VMEM((6, count * rows, 2 * size), jnp.float32),
            pltpu.VMEM((count * rows, columns), jnp.float32),
            pltpu.VMEM((count, *packed_shape(rows)), jnp.bfloat16),
            pltpu.SemaphoreType.DMA((count,)),
        ]

    def cost(products):
        return pl.CostEstimate(flops=2 * rows * size * size * products, bytes_accessed=3 * 2**20, transcendentals=0)

    params = pltpu.CompilerParams(vmem_limit_bytes=60 * 2**20)
    *first, held = pl.pallas_call(
        functools.partial(first_kernel, slots, slices_owned),
        out_shape=[patch] * len(slots) + [spectrum],
        in_specs=[away] * 5,
        out_specs=[away] * (len(slots) + 1),
        scratch_shapes=[
            pltpu.VMEM((rows, columns), jnp.bfloat16),
            pltpu.VMEM(matrices.shape, jnp.bfloat16),
            *small,
            pltpu.VMEM((8, rows, size), jnp.bfloat16),
            pltpu.VMEM((8, rows, size), jnp.bfloat16),
            pltpu.VMEM(spectrum.shape, jnp.float32),
            *buffers(len(slots)),
            pltpu.SemaphoreType.DMA((9,)),
            pltpu.SemaphoreType.DMA,
        ],
        compiler_params=params,
        cost_estimate=cost(42 + 14 * len(slots)),
        name="forward_and_first_slots",
    )(image, matrices, angles, defocus, starts)
    second = pl.pallas_call(
        functools.partial(second_kernel, later, slices_owned),
        out_shape=[patch] * len(later),
        in_specs=[away] * 5,
        out_specs=[away] * len(later),
        scratch_shapes=[
            pltpu.VMEM(spectrum.shape, jnp.float32),
            pltpu.VMEM((2,) + matrices.shape[1:], jnp.bfloat16),
            *small,
            *buffers(len(later)),
            pltpu.SemaphoreType.DMA((6,)),
        ],
        compiler_params=params,
        cost_estimate=cost(14 * len(later)),
        name="later_slots",
    )(held, matrices, angles, defocus, starts)
    return dict(zip(slots, first)) | dict(zip(later, second))


def after(array, *others):
    away = pl.BlockSpec(memory_space=pl.ANY)
    return pl.pallas_call(
        lambda *refs: None,
        out_shape=jax.ShapeDtypeStruct(array.shape, array.dtype),
        in_specs=[away] * (1 + len(others)),
        out_specs=away,
        input_output_aliases={0: 0},
        compiler_params=pltpu.CompilerParams(vmem_limit_bytes=2**20),
        cost_estimate=pl.CostEstimate(flops=0, bytes_accessed=0, transcendentals=0),
        name="after",
    )(array, *others)


def prepare_kernel(slots, slices_owned, angles, defocus, waves, rows_ref, weights_ref, mine, order):
    tilt, row = lax.axis_index("tilt"), lax.axis_index("row")
    slab, local_first = tilt * slices_owned // SLAB, tilt * slices_owned % SLAB
    full_rows = waves.shape[1]
    rows = rows_ref.shape[0] // slots
    half = full_rows // 2
    column = lax.broadcasted_iota(jnp.int32, (8, full_rows), 1)
    freq = jnp.where(column <= half, column, column - half)
    count = jnp.where((freq == 0) | (freq == half), 1.0, 2.0) / full_rows
    scales = [(flip_sign(freq * freq, defocus[tilt ^ slot, slab], full_rows) * count)[:1] for slot in range(slots)]
    for part in range(2):
        for block in range(full_rows // rows):
            there = pl.ds(pl.multiple_of((row ^ block) * rows, rows), rows)
            order[part, block * rows : (block + 1) * rows, :] = waves[part, there, :]
        own = order[part, :rows, :].astype(jnp.float32)
        for slot in range(slots):
            mine[part, slot * rows : (slot + 1) * rows, :] = (own * scales[slot]).astype(jnp.bfloat16)

    def product(left, right):
        over = (((1,), (1,)), ((), ()))
        return lax.dot_general(mine[left], order[right], over, preferred_element_type=jnp.float32)

    rows_ref[...] = (product(0, 0) + product(0, 1) + product(1, 0)).astype(jnp.bfloat16)

    place = lax.broadcasted_iota(jnp.int32, (REACH, XBW), 0).astype(jnp.float32)
    across = lax.broadcasted_iota(jnp.int32, (1, XBW), 1).astype(jnp.float32)
    for slot in range(slots):
        cosine, sine, first_tap = reach_of(angles[tilt ^ slot])
        tap = place + first_tap.astype(jnp.float32)

        def one_slice(c, carry):
            offset = (local_first + c).astype(jnp.float32) - 0.5 * (SLAB - 1)
            centre = 0.5 * XBW + across * cosine + offset * sine
            there = pl.ds(pl.multiple_of(c * XBW, XBW), XBW)
            weights = jnp.maximum(0.0, 1.0 - jnp.abs(tap - centre)).astype(jnp.bfloat16)
            weights_ref[slot, :REACH, there] = weights
            for block in range(1, XBLK):
                weights_ref[slot, MAIN + block * REST : MAIN + (block + 1) * REST, there] = weights[MAIN:]
            return carry

        lax.fori_loop(0, slices_owned, one_slice, 0, unroll=2)


def prepared(slots, slices_owned, rows, full_rows, angles, defocus):
    smem, vmem = pl.BlockSpec(memory_space=pltpu.SMEM), pl.BlockSpec(memory_space=pltpu.VMEM)
    return pl.pallas_call(
        functools.partial(prepare_kernel, slots, slices_owned),
        out_shape=[
            jax.ShapeDtypeStruct((slots * rows, full_rows), jnp.bfloat16),
            jax.ShapeDtypeStruct((slots, MAIN + XBLK * REST, slices_owned * XBW), jnp.bfloat16),
        ],
        in_specs=[smem] * 2 + [vmem],
        out_specs=[vmem] * 2,
        scratch_shapes=[
            pltpu.VMEM((2, slots * rows, full_rows), jnp.bfloat16),
            pltpu.VMEM((2, full_rows, full_rows), jnp.bfloat16),
        ],
        compiler_params=pltpu.CompilerParams(vmem_limit_bytes=32 * 2**20),
        cost_estimate=pl.CostEstimate(flops=2**31, bytes_accessed=6 * 2**20, transcendentals=0),
        name="prepare",
    )(angles, defocus, jnp.asarray(row_tables(full_rows)))


def unpacked(packed):
    rows = 4 * packed.shape[0] // 9
    rest = packed[2 * rows :].astype(jnp.float32)
    quarters = []
    for tile in range(2):
        both = rest[:, tile * MAIN : (tile + 1) * MAIN]
        quarters += [both, pltpu.roll(both, MAIN - XBLK * REST, 1)]
    rest = jnp.concatenate(quarters, 0).astype(jnp.bfloat16)
    return jnp.concatenate([packed[:rows], packed[rows : 2 * rows], rest], 1)


def corrected_patches(slot, rows_ref, patch_refs):
    patches = jnp.concatenate([unpacked(ref[...]) for ref in patch_refs], 0)
    rows = patches.shape[0] // len(patch_refs)
    image = jnp.dot(rows_ref[slot * rows : (slot + 1) * rows, :], patches, preferred_element_type=jnp.float32)
    lane = lax.broadcasted_iota(jnp.int32, (rows, MAIN), 1) // REST
    main = jnp.concatenate([image[:, block * MAIN : (block + 1) * MAIN] for block in range(XBLK)], 0)
    rest = jnp.concatenate([jnp.where(lane == block, image[:, XBLK * MAIN :], 0.0) for block in range(XBLK)], 0)
    return jnp.concatenate([main, rest[:, : XBLK * REST]], 1).astype(jnp.bfloat16)


def sum_kernel(slots, row_devices, rows_ref, weights_ref, *refs):
    patch_refs, total_ref = refs[:-1], refs[-1]
    parts = [
        corrected_patches(slot, rows_ref, patch_refs[i * row_devices : (i + 1) * row_devices])
        for i, slot in enumerate(slots)
    ]
    step = 4 * XBW
    for first in range(0, total_ref.shape[1], step):
        here = slice(first, first + step)
        total = jnp.dot(parts[0], weights_ref[slots[0], :, here], preferred_element_type=jnp.float32)
        for part, slot in zip(parts[1:], slots[1:]):
            total += jnp.dot(part, weights_ref[slot, :, here], preferred_element_type=jnp.float32)
        total_ref[:, here] = total


def finish_kernel(factor, slots, row_devices, rows_ref, weights_ref, total_ref, *refs):
    patch_refs = refs[: len(slots) * row_devices]
    out_ref, out, sems = refs[len(slots) * row_devices :]
    rows = total_ref.shape[0] // XBLK
    parts = [
        corrected_patches(slot, rows_ref, patch_refs[i * row_devices : (i + 1) * row_devices])
        for i, slot in enumerate(slots)
    ]
    step = 4
    copies = []
    for group in range(out.shape[0] // step):
        here = slice(group * step * XBW, (group + 1) * step * XBW)
        total = total_ref[:, here]
        for part, slot in zip(parts, slots):
            total += jnp.dot(part, weights_ref[slot, :, here], preferred_element_type=jnp.float32)
        for c in range(step):
            for block in range(XBLK):
                out[group * step + c, :, block * XBW : (block + 1) * XBW] = (
                    factor * total[block * rows : (block + 1) * rows, c * XBW : (c + 1) * XBW]
                ).astype(jnp.bfloat16)
        part = pl.ds(group * step, step)
        copies.append(pltpu.make_async_copy(out.at[part], out_ref.at[part], sems.at[group]))
        copies[-1].start()
    for copy in copies:
        copy.wait()


def interpolation(kernel, slots, weights, row_filters, patches, totals, **call):
    _, taps, width = weights.shape
    rows = row_filters.shape[0] // weights.shape[0]
    vmem = pl.BlockSpec(memory_space=pltpu.VMEM)
    operands = [row_filters, weights, *totals, *(block for slot in slots for block in patches[slot])]
    flops = 2 * len(slots) * taps * width * XBLK * rows
    return pl.pallas_call(
        functools.partial(kernel, slots, len(patches[0])),
        in_specs=[vmem] * len(operands),
        compiler_params=pltpu.CompilerParams(vmem_limit_bytes=32 * 2**20),
        cost_estimate=pl.CostEstimate(flops=flops, bytes_accessed=3 * 2**20, transcendentals=0),
        **call,
    )(*operands)


def summed(row_filters, weights, patches, slots):
    return interpolation(
        sum_kernel,
        slots,
        weights,
        row_filters,
        patches,
        [],
        out_shape=jax.ShapeDtypeStruct((XBLK * row_filters.shape[0] // weights.shape[0], weights.shape[2]), jnp.float32),
        out_specs=pl.BlockSpec(memory_space=pltpu.VMEM),
        name="sum_early_tilts",
    )


def finished(row_filters, weights, total, patches, slots, factor):
    shape = (weights.shape[2] // XBW, row_filters.shape[0] // weights.shape[0], XBLK * XBW)
    return interpolation(
        functools.partial(finish_kernel, factor),
        slots,
        weights,
        row_filters,
        patches,
        [total],
        out_shape=jax.ShapeDtypeStruct(shape, jnp.bfloat16),
        out_specs=pl.BlockSpec(memory_space=pl.ANY),
        scratch_shapes=[pltpu.VMEM(shape, jnp.bfloat16), pltpu.SemaphoreType.DMA((shape[0] // 4,))],
        name="finish_volume",
    )


def exchange(array, axis, distance):
    count = lax.axis_size(axis)
    return lax.ppermute(array, axis, [(i, i ^ distance) for i in range(count)])


def gather_rows(array, awaited=()):
    blocks = {0: array}
    bit = lax.axis_size("row") // 2
    while bit:
        if bit == 1 and awaited:
            blocks = {d: after(block, *awaited) if d else block for d, block in blocks.items()}
        blocks.update({d ^ bit: exchange(block, "row", bit) for d, block in blocks.items()})
        bit //= 2
    return [blocks[d] for d in sorted(blocks)]


def per_device(projections, tilt_angle, band_start, defocus):
    _, rows, _ = projections.shape
    row_devices, tilt_devices = lax.axis_size("row"), lax.axis_size("tilt")
    slices_owned = SLICES // tilt_devices
    odd, even = list(range(tilt_devices - 1, 0, -2)), list(range(tilt_devices - 2, 0, -2))
    sent = column_filtered(odd, even + [0], slices_owned, projections[0], tilt_angle, defocus, band_start)
    arrived = {0: sent[0]} | {d: exchange(sent[d], "tilt", d) for d in odd}
    row_filters, weights = prepared(tilt_devices, slices_owned, rows, rows * row_devices, tilt_angle, defocus)
    patches = {0: gather_rows(arrived[0], (row_filters,))} | {d: gather_rows(arrived[d]) for d in odd}
    total = summed(row_filters, weights, patches, [0] + odd)
    for d in even:
        arrived[d] = exchange(after(sent[d], arrived[1]), "tilt", d)
        patches[d] = gather_rows(arrived[d], (total,))
    return finished(row_filters, weights, total, patches, even, 1.0 / math.sqrt(tilt_devices))


def solution(mesh):
    in_specs = (
        P(("group", "tilt"), "row", None),
        P("group"),
        P("group", None, None),
        P("group", None),
    )
    out_specs = P(("group", "tilt"), "row", None)
    return jax.shard_map(
        per_device, mesh=mesh, in_specs=in_specs, out_specs=out_specs, check_vma=False
    )
```

```python
import functools
import math

import jax
import jax.numpy as jnp
import numpy as np
from jax import lax
from jax.experimental import pallas as pl
from jax.experimental.pallas import tpu as pltpu
from jax.sharding import PartitionSpec as P

SLAB = 16
XBW = 128
BAND = 256
XBLK = 4
SLICES = 64
RADIX = 8
MAIN = 128
REST = 16
REACH = MAIN + REST
WINDOW = 384
ROOT = math.sqrt(0.5)


def split(table):
    high = table.astype(jnp.bfloat16)
    return high, (table - high.astype(np.float64)).astype(jnp.bfloat16)


def column_tables(columns):
    size = columns // RADIX
    half = size // 2
    u = np.arange(size)[:, None]

    def angles(freq):
        return 2.0 * np.pi * ((u * freq[None, :]) % columns) / columns

    k0, s0 = RADIX * np.arange(half + 1), RADIX * np.arange(1, half)
    k4 = RADIX * np.arange(half) + 4
    m0 = np.concatenate([np.cos(angles(k0)), -np.sin(angles(s0))], 1)
    m4 = np.concatenate([np.cos(angles(k4)), -np.sin(angles(k4))], 1)
    full = angles(RADIX * np.arange(size))
    waves = np.concatenate([np.cos(full), np.sin(full)], 1)
    ends = np.concatenate([m0, m4], 1)

    matrices = np.stack([*split(ends), *split(waves), np.concatenate([m0.T, m4.T], 1).astype(jnp.bfloat16)])
    return matrices


def column_lines(columns):
    size = columns // RADIX
    half = size // 2
    line = lax.broadcasted_iota(jnp.int32, (8, size), 0)
    u = lax.broadcasted_iota(jnp.int32, (8, size), 1)
    freq = jnp.where(line == 0, RADIX * jnp.where(u <= half, u, u - half), RADIX * (u & (half - 1)) + 4)
    freq = jnp.where(line < 2, freq, RADIX * u + line // 2)
    fold = jnp.minimum(freq, columns - freq)
    count = jnp.where((fold == 0) | (fold == columns // 2), 1.0, 2.0)
    gain = count * (fold.astype(jnp.float32) + 0.5) * (2.0 / (columns * columns))
    angle = (u * (line + 1)).astype(jnp.float32) * (2.0 * math.pi / columns)
    return fold * fold, gain, jnp.cos(angle), jnp.sin(angle)


def row_tables(full_rows):
    half = full_rows // 2
    column = np.arange(full_rows)
    freq = np.where(column <= half, column, column - half)
    angle = 2.0 * np.pi * (np.arange(full_rows)[:, None] * freq[None, :] % full_rows) / full_rows
    return np.stack(split(np.where(column[None, :] <= half, np.cos(angle), np.sin(angle))))


def packed_shape(rows):
    return (2 * rows + rows // 4, 2 * MAIN)


def flip_sign(squares, defocus, length):
    cycles = lax.div(squares * defocus, jnp.int32(length * length))
    return (1 - 2 * (cycles & 1)).astype(jnp.float32)


def fetched(sources, targets, sems):
    copies = [pltpu.make_async_copy(s, t, sems.at[i]) for i, (s, t) in enumerate(zip(sources, targets))]
    for copy in copies:
        copy.start()
    return copies


def reach_of(angle):
    line = jnp.full((8, XBW), angle, jnp.float32)
    cosine, sine = jnp.cos(line), jnp.sin(line)
    lowest = 0.5 * XBW + jnp.minimum((XBW - 1) * cosine, 0.0) - 0.5 * (SLAB - 1) * jnp.abs(sine)
    first = jnp.clip(jnp.floor(lowest) - 4.0, 0.0, float(BAND - REACH))
    return cosine[:1], sine[:1], jnp.max(first).astype(jnp.int32)


def butterflies(image, turns, zhi, zlo):
    rows, columns = image.shape
    size = columns // RADIX

    def step(i, carry):
        here = pl.ds(pl.multiple_of(i * 16, 16), 16)
        x = [image[here, m * size : (m + 1) * size].astype(jnp.float32) for m in range(8)]
        p0, p1, p2, p3 = (x[m] + x[m + 4] for m in range(4))
        q0, q1, q2, q3 = (x[m] - x[m + 4] for m in range(4))
        e, f = p0 + p2, p1 + p3
        g, h = ROOT * (q1 - q3), ROOT * (q1 + q3)
        z = [e + f, e - f]
        for j, (real, imag) in enumerate([(q0 + g, -q2 - h), (p0 - p2, p3 - p1), (q0 - g, q2 - h)]):
            c, s = turns[2 * j], turns[2 * j + 1]
            z += [real * c + imag * s, imag * c - real * s]
        for line in range(8):
            top = z[line].astype(jnp.bfloat16)
            zhi[line, here, :] = top
            zlo[line, here, :] = (z[line] - top.astype(jnp.float32)).astype(jnp.bfloat16)
        return carry

    lax.fori_loop(0, rows // 16, step, 0)


def inverse_butterflies(ends, waves, turns, turned):
    rows, columns = turned.shape
    size = columns // RADIX

    def step(i, carry):
        here = pl.ds(pl.multiple_of(i * 8, 8), 8)
        r, s = [], []
        for j in range(3):
            c, d = turns[2 * j], turns[2 * j + 1]
            real = waves[2 * j, here, :size] - waves[2 * j + 1, here, size:]
            imag = waves[2 * j, here, size:] + waves[2 * j + 1, here, :size]
            r.append(real * c - imag * d)
            s.append(real * d + imag * c)
        e, f = ends[0, here, :] + ends[1, here, :], ends[0, here, :] - ends[1, here, :]
        a, b, c, d = r[0] + r[2], r[0] - r[2], s[0] + s[2], s[0] - s[2]
        even0, even2, odd1, odd3 = e + r[1], e - r[1], f - s[1], f + s[1]
        g, h = ROOT * (b - c), ROOT * (b + c)
        out = [even0 + a, odd1 + g, even2 - d, odd3 - h, even0 - a, odd1 - g, even2 + d, odd3 + h]
        for m in range(8):
            turned[here, m * size : (m + 1) * size] = out[m]
        return carry

    lax.fori_loop(0, rows // 8, step, 0)


def send_patches(slots, slices_owned, spectrum, wave_table, end_table, columns, facts, scratch, out_refs):
    squares, ramp, turns, angles, defocus, starts = facts
    ends, waves, turned, out, out_sems = scratch
    rows, size = spectrum[0].shape
    tilt = lax.axis_index("tilt")
    slabs = [(tilt ^ slot) * slices_owned // SLAB for slot in slots]
    gains = [flip_sign(squares, defocus[tilt, slab], columns) * ramp for slab in slabs]
    filtered = [
        jnp.concatenate([(spectrum[i] * gain[i : i + 1, :]).astype(jnp.bfloat16) for gain in gains], 0) for i in range(8)
    ]
    for i in range(2):
        ends[i] = jnp.dot(filtered[i], end_table[:, i * size : (i + 1) * size], preferred_element_type=jnp.float32)
    for i in range(6):
        waves[i] = jnp.dot(filtered[2 + i], wave_table[...], preferred_element_type=jnp.float32)
    inverse_butterflies(ends, waves, turns, turned)
    lane = lax.broadcasted_iota(jnp.int32, (rows, MAIN), 1) // REST
    _, _, first_tap = reach_of(angles[tilt])
    sends = []
    for i, slab in enumerate(slabs):
        rest = jnp.zeros((rows, MAIN), jnp.float32)
        for block in range(XBLK):
            start = starts[tilt, slab, block] + first_tap
            base = pl.multiple_of(jnp.minimum((start // 128) * 128, columns - WINDOW), 128)
            window = turned[i * rows : (i + 1) * rows, pl.ds(base, WINDOW)]
            shift = base - start
            reach = pltpu.roll(window, jnp.where(shift < 0, shift + WINDOW, shift), 1)[:, : 2 * MAIN]
            there = slice(block // 2 * rows, (block // 2 + 1) * rows), slice(block % 2 * MAIN, (block % 2 + 1) * MAIN)
            out[i, *there] = reach[:, :MAIN].astype(jnp.bfloat16)
            last = reach[:, MAIN:]
            rest = jnp.where(lane == block, pltpu.roll(last, block * REST, 1) if block else last, rest)
        quarters = [rest[q * rows // 4 : (q + 1) * rows // 4] for q in range(4)]
        for tile in range(2):
            right = pltpu.roll(quarters[2 * tile + 1], XBLK * REST, 1)
            both = jnp.where(lane[: rows // 4] < XBLK, quarters[2 * tile], right)
            out[i, 2 * rows :, tile * MAIN : (tile + 1) * MAIN] = both.astype(jnp.bfloat16)
        sends.append(pltpu.make_async_copy(out.at[i], out_refs[i], out_sems.at[i]))
        sends[-1].start()
    return sends


def column_kernel(slots, slices_owned, image_ref, matrix_ref, angle_ref, defocus_ref, starts_ref, *refs):
    count = len(slots)
    out_refs = refs[:count]
    image, matrix, angles, defocus, starts, zhi, zlo, *scratch, sems = refs[count:]
    rows, columns = image.shape
    size = columns // RADIX
    copies = fetched(
        [image_ref, angle_ref, defocus_ref, starts_ref] + [matrix_ref.at[i] for i in range(5)],
        [image, angles, defocus, starts] + [matrix.at[i] for i in range(5)],
        sems,
    )
    squares, ramp, cosine_turns, sine_turns = column_lines(columns)
    turns = [t[j : j + 1, :] for j in range(3) for t in (cosine_turns, sine_turns)]
    copies[0].wait()
    butterflies(image, turns, zhi, zlo)
    for copy in copies[1:]:
        copy.wait()

    def product(first, lines, table, here):
        top = zhi[first : first + lines].reshape(lines * rows, size)
        rest = zlo[first : first + lines].reshape(lines * rows, size)
        total = jnp.dot(top, matrix[table, :, here], preferred_element_type=jnp.float32)
        total += jnp.dot(top, matrix[table + 1, :, here], preferred_element_type=jnp.float32)
        return total + jnp.dot(rest, matrix[table, :, here], preferred_element_type=jnp.float32)

    spectrum = [product(0, 1, 0, slice(0, size)), product(1, 1, 0, slice(size, 2 * size))]
    mixed = product(2, 6, 2, slice(None))
    for j in range(3):
        real, imag = mixed[2 * j * rows : (2 * j + 1) * rows], mixed[(2 * j + 1) * rows : (2 * j + 2) * rows]
        spectrum += [real[:, :size] + imag[:, size:], imag[:, :size] - real[:, size:]]
    facts = (squares, ramp, turns, angles, defocus, starts)
    sends = send_patches(
        slots, slices_owned, spectrum, matrix.at[2], matrix.at[4], columns, facts, scratch, out_refs
    )
    for copy in sends:
        copy.wait()


def column_filtered(slots, slices_owned, image, angles, defocus, starts):
    rows, columns = image.shape
    size = columns // RADIX
    count = len(slots)
    matrices = jnp.asarray(column_tables(columns))
    away = pl.BlockSpec(memory_space=pl.ANY)
    flops = 2 * rows * size * size * (42 + 14 * count)
    sent = pl.pallas_call(
        functools.partial(column_kernel, slots, slices_owned),
        out_shape=[jax.ShapeDtypeStruct(packed_shape(rows), jnp.bfloat16)] * count,
        in_specs=[away] * 5,
        out_specs=[away] * count,
        scratch_shapes=[
            pltpu.VMEM((rows, columns), jnp.bfloat16),
            pltpu.VMEM(matrices.shape, jnp.bfloat16),
            pltpu.SMEM(angles.shape, jnp.float32),
            pltpu.SMEM(defocus.shape, jnp.int32),
            pltpu.SMEM(starts.shape, jnp.int32),
            pltpu.VMEM((8, rows, size), jnp.bfloat16),
            pltpu.VMEM((8, rows, size), jnp.bfloat16),
            pltpu.VMEM((2, count * rows, size), jnp.float32),
            pltpu.VMEM((6, count * rows, 2 * size), jnp.float32),
            pltpu.VMEM((count * rows, columns), jnp.float32),
            pltpu.VMEM((count, *packed_shape(rows)), jnp.bfloat16),
            pltpu.SemaphoreType.DMA((count,)),
            pltpu.SemaphoreType.DMA((9,)),
        ],
        compiler_params=pltpu.CompilerParams(vmem_limit_bytes=60 * 2**20),
        cost_estimate=pl.CostEstimate(flops=flops, bytes_accessed=3 * 2**20, transcendentals=0),
        name="column_filter",
    )(image, matrices, angles, defocus, starts)
    return dict(zip(slots, sent))


def after(array, *others):
    away = pl.BlockSpec(memory_space=pl.ANY)
    return pl.pallas_call(
        lambda *refs: None,
        out_shape=jax.ShapeDtypeStruct(array.shape, array.dtype),
        in_specs=[away] * (1 + len(others)),
        out_specs=away,
        input_output_aliases={0: 0},
        compiler_params=pltpu.CompilerParams(vmem_limit_bytes=2**20),
        cost_estimate=pl.CostEstimate(flops=0, bytes_accessed=0, transcendentals=0),
        name="after",
    )(array, *others)


def prepare_kernel(slots, slices_owned, angles, defocus, waves, rows_ref, weights_ref, mine, order):
    tilt, row = lax.axis_index("tilt"), lax.axis_index("row")
    slab, local_first = tilt * slices_owned // SLAB, tilt * slices_owned % SLAB
    full_rows = waves.shape[1]
    rows = rows_ref.shape[0] // slots
    half = full_rows // 2
    column = lax.broadcasted_iota(jnp.int32, (8, full_rows), 1)
    freq = jnp.where(column <= half, column, column - half)
    count = jnp.where((freq == 0) | (freq == half), 1.0, 2.0) / full_rows
    scales = [(flip_sign(freq * freq, defocus[tilt ^ slot, slab], full_rows) * count)[:1] for slot in range(slots)]
    for part in range(2):
        for block in range(full_rows // rows):
            there = pl.ds(pl.multiple_of((row ^ block) * rows, rows), rows)
            order[part, block * rows : (block + 1) * rows, :] = waves[part, there, :]
        own = order[part, :rows, :].astype(jnp.float32)
        for slot in range(slots):
            mine[part, slot * rows : (slot + 1) * rows, :] = (own * scales[slot]).astype(jnp.bfloat16)

    def product(left, right):
        over = (((1,), (1,)), ((), ()))
        return lax.dot_general(mine[left], order[right], over, preferred_element_type=jnp.float32)

    rows_ref[...] = (product(0, 0) + product(0, 1) + product(1, 0)).astype(jnp.bfloat16)

    place = lax.broadcasted_iota(jnp.int32, (REACH, XBW), 0).astype(jnp.float32)
    across = lax.broadcasted_iota(jnp.int32, (1, XBW), 1).astype(jnp.float32)
    for slot in range(slots):
        cosine, sine, first_tap = reach_of(angles[tilt ^ slot])
        tap = place + first_tap.astype(jnp.float32)

        def one_slice(c, carry):
            offset = (local_first + c).astype(jnp.float32) - 0.5 * (SLAB - 1)
            centre = 0.5 * XBW + across * cosine + offset * sine
            there = pl.ds(pl.multiple_of(c * XBW, XBW), XBW)
            weights = jnp.maximum(0.0, 1.0 - jnp.abs(tap - centre)).astype(jnp.bfloat16)
            weights_ref[slot, :REACH, there] = weights
            for block in range(1, XBLK):
                weights_ref[slot, MAIN + block * REST : MAIN + (block + 1) * REST, there] = weights[MAIN:]
            return carry

        lax.fori_loop(0, slices_owned, one_slice, 0, unroll=2)


def prepared(slots, slices_owned, rows, full_rows, angles, defocus):
    smem, vmem = pl.BlockSpec(memory_space=pltpu.SMEM), pl.BlockSpec(memory_space=pltpu.VMEM)
    return pl.pallas_call(
        functools.partial(prepare_kernel, slots, slices_owned),
        out_shape=[
            jax.ShapeDtypeStruct((slots * rows, full_rows), jnp.bfloat16),
            jax.ShapeDtypeStruct((slots, MAIN + XBLK * REST, slices_owned * XBW), jnp.bfloat16),
        ],
        in_specs=[smem] * 2 + [vmem],
        out_specs=[vmem] * 2,
        scratch_shapes=[
            pltpu.VMEM((2, slots * rows, full_rows), jnp.bfloat16),
            pltpu.VMEM((2, full_rows, full_rows), jnp.bfloat16),
        ],
        compiler_params=pltpu.CompilerParams(vmem_limit_bytes=32 * 2**20),
        cost_estimate=pl.CostEstimate(flops=2**31, bytes_accessed=6 * 2**20, transcendentals=0),
        name="prepare",
    )(angles, defocus, jnp.asarray(row_tables(full_rows)))


def unpacked(packed):
    rows = 4 * packed.shape[0] // 9
    rest = packed[2 * rows :].astype(jnp.float32)
    quarters = []
    for tile in range(2):
        both = rest[:, tile * MAIN : (tile + 1) * MAIN]
        quarters += [both, pltpu.roll(both, MAIN - XBLK * REST, 1)]
    rest = jnp.concatenate(quarters, 0).astype(jnp.bfloat16)
    return jnp.concatenate([packed[:rows], packed[rows : 2 * rows], rest], 1)


def corrected_patches(slot, rows_ref, patch_refs):
    patches = jnp.concatenate([unpacked(ref[...]) for ref in patch_refs], 0)
    rows = patches.shape[0] // len(patch_refs)
    image = jnp.dot(rows_ref[slot * rows : (slot + 1) * rows, :], patches, preferred_element_type=jnp.float32)
    lane = lax.broadcasted_iota(jnp.int32, (rows, MAIN), 1) // REST
    main = jnp.concatenate([image[:, block * MAIN : (block + 1) * MAIN] for block in range(XBLK)], 0)
    rest = jnp.concatenate([jnp.where(lane == block, image[:, XBLK * MAIN :], 0.0) for block in range(XBLK)], 0)
    return jnp.concatenate([main, rest[:, : XBLK * REST]], 1).astype(jnp.bfloat16)


def sum_kernel(slots, row_devices, rows_ref, weights_ref, *refs):
    patch_refs, total_ref = refs[:-1], refs[-1]
    parts = [
        corrected_patches(slot, rows_ref, patch_refs[i * row_devices : (i + 1) * row_devices])
        for i, slot in enumerate(slots)
    ]
    step = 4 * XBW
    for first in range(0, total_ref.shape[1], step):
        here = slice(first, first + step)
        total = jnp.dot(parts[0], weights_ref[slots[0], :, here], preferred_element_type=jnp.float32)
        for part, slot in zip(parts[1:], slots[1:]):
            total += jnp.dot(part, weights_ref[slot, :, here], preferred_element_type=jnp.float32)
        total_ref[:, here] = total


def finish_kernel(factor, slots, row_devices, rows_ref, weights_ref, total_ref, *refs):
    patch_refs = refs[: len(slots) * row_devices]
    out_ref, out, sems = refs[len(slots) * row_devices :]
    rows = total_ref.shape[0] // XBLK
    parts = [
        corrected_patches(slot, rows_ref, patch_refs[i * row_devices : (i + 1) * row_devices])
        for i, slot in enumerate(slots)
    ]
    step = 4
    copies = []
    for group in range(out.shape[0] // step):
        here = slice(group * step * XBW, (group + 1) * step * XBW)
        total = total_ref[:, here]
        for part, slot in zip(parts, slots):
            total += jnp.dot(part, weights_ref[slot, :, here], preferred_element_type=jnp.float32)
        for c in range(step):
            for block in range(XBLK):
                out[group * step + c, :, block * XBW : (block + 1) * XBW] = (
                    factor * total[block * rows : (block + 1) * rows, c * XBW : (c + 1) * XBW]
                ).astype(jnp.bfloat16)
        part = pl.ds(group * step, step)
        copies.append(pltpu.make_async_copy(out.at[part], out_ref.at[part], sems.at[group]))
        copies[-1].start()
    for copy in copies:
        copy.wait()


def interpolation(kernel, slots, weights, row_filters, patches, totals, **call):
    _, taps, width = weights.shape
    rows = row_filters.shape[0] // weights.shape[0]
    vmem = pl.BlockSpec(memory_space=pltpu.VMEM)
    operands = [row_filters, weights, *totals, *(block for slot in slots for block in patches[slot])]
    flops = 2 * len(slots) * taps * width * XBLK * rows
    return pl.pallas_call(
        functools.partial(kernel, slots, len(patches[0])),
        in_specs=[vmem] * len(operands),
        compiler_params=pltpu.CompilerParams(vmem_limit_bytes=32 * 2**20),
        cost_estimate=pl.CostEstimate(flops=flops, bytes_accessed=3 * 2**20, transcendentals=0),
        **call,
    )(*operands)


def summed(row_filters, weights, patches, slots):
    return interpolation(
        sum_kernel,
        slots,
        weights,
        row_filters,
        patches,
        [],
        out_shape=jax.ShapeDtypeStruct((XBLK * row_filters.shape[0] // weights.shape[0], weights.shape[2]), jnp.float32),
        out_specs=pl.BlockSpec(memory_space=pltpu.VMEM),
        name="sum_early_tilts",
    )


def finished(row_filters, weights, total, patches, slots, factor):
    shape = (weights.shape[2] // XBW, row_filters.shape[0] // weights.shape[0], XBLK * XBW)
    return interpolation(
        functools.partial(finish_kernel, factor),
        slots,
        weights,
        row_filters,
        patches,
        [total],
        out_shape=jax.ShapeDtypeStruct(shape, jnp.bfloat16),
        out_specs=pl.BlockSpec(memory_space=pl.ANY),
        scratch_shapes=[pltpu.VMEM(shape, jnp.bfloat16), pltpu.SemaphoreType.DMA((shape[0] // 4,))],
        name="finish_volume",
    )


def exchange(array, axis, distance):
    count = lax.axis_size(axis)
    return lax.ppermute(array, axis, [(i, i ^ distance) for i in range(count)])


def gather_rows(array, awaited=()):
    blocks = {0: array}
    bit = lax.axis_size("row") // 2
    while bit:
        if bit == 1 and awaited:
            blocks = {d: after(block, *awaited) if d else block for d, block in blocks.items()}
        blocks.update({d ^ bit: exchange(block, "row", bit) for d, block in blocks.items()})
        bit //= 2
    return [blocks[d] for d in sorted(blocks)]


def per_device(projections, tilt_angle, band_start, defocus):
    _, rows, _ = projections.shape
    row_devices, tilt_devices = lax.axis_size("row"), lax.axis_size("tilt")
    slices_owned = SLICES // tilt_devices
    far, near = list(range(tilt_devices - 1, 1, -1)), list(range(min(2, tilt_devices) - 1, -1, -1))
    sent = column_filtered(far + near, slices_owned, projections[0], tilt_angle, defocus, band_start)
    arrived = {d: exchange(sent[d], "tilt", d) if d else sent[d] for d in far + near}
    row_filters, weights = prepared(tilt_devices, slices_owned, rows, rows * row_devices, tilt_angle, defocus)
    patches = {d: gather_rows(after(arrived[d], row_filters) if d else arrived[d]) for d in near}
    total = summed(row_filters, weights, patches, near)
    for d in far:
        patches[d] = gather_rows(arrived[d], (total,) if d == far[-1] else ())
    return finished(row_filters, weights, total, patches, far, 1.0 / math.sqrt(tilt_devices))


def solution(mesh):
    in_specs = (
        P(("group", "tilt"), "row", None),
        P("group"),
        P("group", None, None),
        P("group", None),
    )
    out_specs = P(("group", "tilt"), "row", None)
    return jax.shard_map(
        per_device, mesh=mesh, in_specs=in_specs, out_specs=out_specs, check_vma=False
    )
```

```python
import functools
import math

import jax
import jax.numpy as jnp
import numpy as np
from jax import lax
from jax.experimental import pallas as pl
from jax.experimental.pallas import tpu as pltpu
from jax.sharding import PartitionSpec as P

SLAB = 16
XBW = 128
BAND = 256
XBLK = 4
SLICES = 64
RADIX = 8
MAIN = 128
REST = 16
REACH = MAIN + REST
WINDOW = 384
ROOT = math.sqrt(0.5)


def split(table):
    high = table.astype(jnp.bfloat16)
    return high, (table - high.astype(np.float64)).astype(jnp.bfloat16)


def column_tables(columns):
    size = columns // RADIX
    half = size // 2
    u = np.arange(size)[:, None]

    def angles(freq):
        return 2.0 * np.pi * ((u * freq[None, :]) % columns) / columns

    k0, s0 = RADIX * np.arange(half + 1), RADIX * np.arange(1, half)
    k4 = RADIX * np.arange(half) + 4
    m0 = np.concatenate([np.cos(angles(k0)), -np.sin(angles(s0))], 1)
    m4 = np.concatenate([np.cos(angles(k4)), -np.sin(angles(k4))], 1)
    full = angles(RADIX * np.arange(size))
    waves = np.concatenate([np.cos(full), np.sin(full)], 1)
    ends = np.concatenate([m0, m4], 1)

    matrices = np.stack([*split(ends), *split(waves), np.concatenate([m0.T, m4.T], 1).astype(jnp.bfloat16)])
    return matrices


def column_lines(columns):
    size = columns // RADIX
    half = size // 2
    line = lax.broadcasted_iota(jnp.int32, (8, size), 0)
    u = lax.broadcasted_iota(jnp.int32, (8, size), 1)
    freq = jnp.where(line == 0, RADIX * jnp.where(u <= half, u, u - half), RADIX * (u & (half - 1)) + 4)
    freq = jnp.where(line < 2, freq, RADIX * u + line // 2)
    fold = jnp.minimum(freq, columns - freq)
    count = jnp.where((fold == 0) | (fold == columns // 2), 1.0, 2.0)
    gain = count * (fold.astype(jnp.float32) + 0.5) * (2.0 / (columns * columns))
    angle = (u * (line + 1)).astype(jnp.float32) * (2.0 * math.pi / columns)
    return fold * fold, gain, jnp.cos(angle), jnp.sin(angle)


def row_tables(full_rows):
    half = full_rows // 2
    column = np.arange(full_rows)
    freq = np.where(column <= half, column, column - half)
    angle = 2.0 * np.pi * (np.arange(full_rows)[:, None] * freq[None, :] % full_rows) / full_rows
    return np.stack(split(np.where(column[None, :] <= half, np.cos(angle), np.sin(angle))))


def packed_shape(rows):
    return (2 * rows + rows // 4, 2 * MAIN)


def flip_sign(squares, defocus, length):
    cycles = lax.div(squares * defocus, jnp.int32(length * length))
    return (1 - 2 * (cycles & 1)).astype(jnp.float32)


def fetched(sources, targets, sems):
    copies = [pltpu.make_async_copy(s, t, sems.at[i]) for i, (s, t) in enumerate(zip(sources, targets))]
    for copy in copies:
        copy.start()
    return copies


def reach_of(angle):
    line = jnp.full((8, XBW), angle, jnp.float32)
    cosine, sine = jnp.cos(line), jnp.sin(line)
    lowest = 0.5 * XBW + jnp.minimum((XBW - 1) * cosine, 0.0) - 0.5 * (SLAB - 1) * jnp.abs(sine)
    first = jnp.clip(jnp.floor(lowest) - 4.0, 0.0, float(BAND - REACH))
    return cosine[:1], sine[:1], jnp.max(first).astype(jnp.int32)


def butterflies(image, turns, zhi, zlo):
    rows, columns = image.shape
    size = columns // RADIX

    def step(i, carry):
        here = pl.ds(pl.multiple_of(i * 16, 16), 16)
        x = [image[here, m * size : (m + 1) * size].astype(jnp.float32) for m in range(8)]
        p0, p1, p2, p3 = (x[m] + x[m + 4] for m in range(4))
        q0, q1, q2, q3 = (x[m] - x[m + 4] for m in range(4))
        e, f = p0 + p2, p1 + p3
        g, h = ROOT * (q1 - q3), ROOT * (q1 + q3)
        z = [e + f, e - f]
        for j, (real, imag) in enumerate([(q0 + g, -q2 - h), (p0 - p2, p3 - p1), (q0 - g, q2 - h)]):
            c, s = turns[2 * j], turns[2 * j + 1]
            z += [real * c + imag * s, imag * c - real * s]
        for line in range(8):
            top = z[line].astype(jnp.bfloat16)
            zhi[line, here, :] = top
            zlo[line, here, :] = (z[line] - top.astype(jnp.float32)).astype(jnp.bfloat16)
        return carry

    lax.fori_loop(0, rows // 16, step, 0)


def inverse_butterflies(ends, waves, turns, turned):
    rows, columns = turned.shape
    size = columns // RADIX

    def step(i, carry):
        here = pl.ds(pl.multiple_of(i * 8, 8), 8)
        r, s = [], []
        for j in range(3):
            c, d = turns[2 * j], turns[2 * j + 1]
            real = waves[2 * j, here, :size] - waves[2 * j + 1, here, size:]
            imag = waves[2 * j, here, size:] + waves[2 * j + 1, here, :size]
            r.append(real * c - imag * d)
            s.append(real * d + imag * c)
        e, f = ends[0, here, :] + ends[1, here, :], ends[0, here, :] - ends[1, here, :]
        a, b, c, d = r[0] + r[2], r[0] - r[2], s[0] + s[2], s[0] - s[2]
        even0, even2, odd1, odd3 = e + r[1], e - r[1], f - s[1], f + s[1]
        g, h = ROOT * (b - c), ROOT * (b + c)
        out = [even0 + a, odd1 + g, even2 - d, odd3 - h, even0 - a, odd1 - g, even2 + d, odd3 + h]
        for m in range(8):
            turned[here, m * size : (m + 1) * size] = out[m]
        return carry

    lax.fori_loop(0, rows // 8, step, 0)


def send_patches(slots, slices_owned, spectrum, wave_table, end_table, columns, facts, scratch, out_refs):
    squares, ramp, turns, angles, defocus, starts = facts
    ends, waves, turned, out, out_sems = scratch
    rows, size = spectrum[0].shape
    tilt = lax.axis_index("tilt")
    slabs = [(tilt ^ slot) * slices_owned // SLAB for slot in slots]
    gains = [flip_sign(squares, defocus[tilt, slab], columns) * ramp for slab in slabs]
    filtered = [
        jnp.concatenate([(spectrum[i] * gain[i : i + 1, :]).astype(jnp.bfloat16) for gain in gains], 0) for i in range(8)
    ]
    for i in range(2):
        ends[i] = jnp.dot(filtered[i], end_table[:, i * size : (i + 1) * size], preferred_element_type=jnp.float32)
    for i in range(6):
        waves[i] = jnp.dot(filtered[2 + i], wave_table[...], preferred_element_type=jnp.float32)
    inverse_butterflies(ends, waves, turns, turned)
    lane = lax.broadcasted_iota(jnp.int32, (rows, MAIN), 1) // REST
    _, _, first_tap = reach_of(angles[tilt])
    sends = []
    for i, slab in enumerate(slabs):
        rest = jnp.zeros((rows, MAIN), jnp.float32)
        for block in range(XBLK):
            start = starts[tilt, slab, block] + first_tap
            base = pl.multiple_of(jnp.minimum((start // 128) * 128, columns - WINDOW), 128)
            window = turned[i * rows : (i + 1) * rows, pl.ds(base, WINDOW)]
            shift = base - start
            reach = pltpu.roll(window, jnp.where(shift < 0, shift + WINDOW, shift), 1)[:, : 2 * MAIN]
            there = slice(block // 2 * rows, (block // 2 + 1) * rows), slice(block % 2 * MAIN, (block % 2 + 1) * MAIN)
            out[i, *there] = reach[:, :MAIN].astype(jnp.bfloat16)
            last = reach[:, MAIN:]
            rest = jnp.where(lane == block, pltpu.roll(last, block * REST, 1) if block else last, rest)
        quarters = [rest[q * rows // 4 : (q + 1) * rows // 4] for q in range(4)]
        for tile in range(2):
            right = pltpu.roll(quarters[2 * tile + 1], XBLK * REST, 1)
            both = jnp.where(lane[: rows // 4] < XBLK, quarters[2 * tile], right)
            out[i, 2 * rows :, tile * MAIN : (tile + 1) * MAIN] = both.astype(jnp.bfloat16)
        sends.append(pltpu.make_async_copy(out.at[i], out_refs[i], out_sems.at[i]))
        sends[-1].start()
    return sends


def column_kernel(slots, slices_owned, image_ref, matrix_ref, angle_ref, defocus_ref, starts_ref, *refs):
    count = len(slots)
    out_refs = refs[:count]
    image, matrix, angles, defocus, starts, zhi, zlo, *scratch, sems = refs[count:]
    rows, columns = image.shape
    size = columns // RADIX
    copies = fetched(
        [image_ref, angle_ref, defocus_ref, starts_ref] + [matrix_ref.at[i] for i in range(5)],
        [image, angles, defocus, starts] + [matrix.at[i] for i in range(5)],
        sems,
    )
    squares, ramp, cosine_turns, sine_turns = column_lines(columns)
    turns = [t[j : j + 1, :] for j in range(3) for t in (cosine_turns, sine_turns)]
    copies[0].wait()
    butterflies(image, turns, zhi, zlo)
    for copy in copies[1:]:
        copy.wait()

    def product(first, lines, table, here):
        top = zhi[first : first + lines].reshape(lines * rows, size)
        rest = zlo[first : first + lines].reshape(lines * rows, size)
        total = jnp.dot(top, matrix[table, :, here], preferred_element_type=jnp.float32)
        total += jnp.dot(top, matrix[table + 1, :, here], preferred_element_type=jnp.float32)
        return total + jnp.dot(rest, matrix[table, :, here], preferred_element_type=jnp.float32)

    spectrum = [product(0, 1, 0, slice(0, size)), product(1, 1, 0, slice(size, 2 * size))]
    mixed = product(2, 6, 2, slice(None))
    for j in range(3):
        real, imag = mixed[2 * j * rows : (2 * j + 1) * rows], mixed[(2 * j + 1) * rows : (2 * j + 2) * rows]
        spectrum += [real[:, :size] + imag[:, size:], imag[:, :size] - real[:, size:]]
    facts = (squares, ramp, turns, angles, defocus, starts)
    sends = send_patches(
        slots, slices_owned, spectrum, matrix.at[2], matrix.at[4], columns, facts, scratch, out_refs
    )
    for copy in sends:
        copy.wait()


def column_filtered(slots, slices_owned, image, angles, defocus, starts):
    rows, columns = image.shape
    size = columns // RADIX
    count = len(slots)
    matrices = jnp.asarray(column_tables(columns))
    away = pl.BlockSpec(memory_space=pl.ANY)
    flops = 2 * rows * size * size * (42 + 14 * count)
    sent = pl.pallas_call(
        functools.partial(column_kernel, slots, slices_owned),
        out_shape=[jax.ShapeDtypeStruct(packed_shape(rows), jnp.bfloat16)] * count,
        in_specs=[away] * 5,
        out_specs=[away] * count,
        scratch_shapes=[
            pltpu.VMEM((rows, columns), jnp.bfloat16),
            pltpu.VMEM(matrices.shape, jnp.bfloat16),
            pltpu.SMEM(angles.shape, jnp.float32),
            pltpu.SMEM(defocus.shape, jnp.int32),
            pltpu.SMEM(starts.shape, jnp.int32),
            pltpu.VMEM((8, rows, size), jnp.bfloat16),
            pltpu.VMEM((8, rows, size), jnp.bfloat16),
            pltpu.VMEM((2, count * rows, size), jnp.float32),
            pltpu.VMEM((6, count * rows, 2 * size), jnp.float32),
            pltpu.VMEM((count * rows, columns), jnp.float32),
            pltpu.VMEM((count, *packed_shape(rows)), jnp.bfloat16),
            pltpu.SemaphoreType.DMA((count,)),
            pltpu.SemaphoreType.DMA((9,)),
        ],
        compiler_params=pltpu.CompilerParams(vmem_limit_bytes=60 * 2**20),
        cost_estimate=pl.CostEstimate(flops=flops, bytes_accessed=3 * 2**20, transcendentals=0),
        name="column_filter",
    )(image, matrices, angles, defocus, starts)
    return dict(zip(slots, sent))


def after(array, *others):
    away = pl.BlockSpec(memory_space=pl.ANY)
    return pl.pallas_call(
        lambda *refs: None,
        out_shape=jax.ShapeDtypeStruct(array.shape, array.dtype),
        in_specs=[away] * (1 + len(others)),
        out_specs=away,
        input_output_aliases={0: 0},
        compiler_params=pltpu.CompilerParams(vmem_limit_bytes=2**20),
        cost_estimate=pl.CostEstimate(flops=0, bytes_accessed=0, transcendentals=0),
        name="after",
    )(array, *others)


def prepare_kernel(slots, slices_owned, angles, defocus, waves, rows_ref, weights_ref, mine, order):
    tilt, row = lax.axis_index("tilt"), lax.axis_index("row")
    slab, local_first = tilt * slices_owned // SLAB, tilt * slices_owned % SLAB
    full_rows = waves.shape[1]
    rows = rows_ref.shape[0] // slots
    half = full_rows // 2
    column = lax.broadcasted_iota(jnp.int32, (8, full_rows), 1)
    freq = jnp.where(column <= half, column, column - half)
    count = jnp.where((freq == 0) | (freq == half), 1.0, 2.0) / full_rows
    scales = [(flip_sign(freq * freq, defocus[tilt ^ slot, slab], full_rows) * count)[:1] for slot in range(slots)]
    for part in range(2):
        for block in range(full_rows // rows):
            there = pl.ds(pl.multiple_of((row ^ block) * rows, rows), rows)
            order[part, block * rows : (block + 1) * rows, :] = waves[part, there, :]
        own = order[part, :rows, :].astype(jnp.float32)
        for slot in range(slots):
            mine[part, slot * rows : (slot + 1) * rows, :] = (own * scales[slot]).astype(jnp.bfloat16)

    def product(left, right):
        over = (((1,), (1,)), ((), ()))
        return lax.dot_general(mine[left], order[right], over, preferred_element_type=jnp.float32)

    rows_ref[...] = (product(0, 0) + product(0, 1) + product(1, 0)).astype(jnp.bfloat16)

    place = lax.broadcasted_iota(jnp.int32, (REACH, XBW), 0).astype(jnp.float32)
    across = lax.broadcasted_iota(jnp.int32, (1, XBW), 1).astype(jnp.float32)
    for slot in range(slots):
        cosine, sine, first_tap = reach_of(angles[tilt ^ slot])
        tap = place + first_tap.astype(jnp.float32)

        def one_slice(c, carry):
            offset = (local_first + c).astype(jnp.float32) - 0.5 * (SLAB - 1)
            centre = 0.5 * XBW + across * cosine + offset * sine
            there = pl.ds(pl.multiple_of(c * XBW, XBW), XBW)
            weights = jnp.maximum(0.0, 1.0 - jnp.abs(tap - centre)).astype(jnp.bfloat16)
            weights_ref[slot, :REACH, there] = weights
            for block in range(1, XBLK):
                weights_ref[slot, MAIN + block * REST : MAIN + (block + 1) * REST, there] = weights[MAIN:]
            return carry

        lax.fori_loop(0, slices_owned, one_slice, 0, unroll=2)


def prepared(slots, slices_owned, rows, full_rows, angles, defocus):
    smem, vmem = pl.BlockSpec(memory_space=pltpu.SMEM), pl.BlockSpec(memory_space=pltpu.VMEM)
    return pl.pallas_call(
        functools.partial(prepare_kernel, slots, slices_owned),
        out_shape=[
            jax.ShapeDtypeStruct((slots * rows, full_rows), jnp.bfloat16),
            jax.ShapeDtypeStruct((slots, MAIN + XBLK * REST, slices_owned * XBW), jnp.bfloat16),
        ],
        in_specs=[smem] * 2 + [vmem],
        out_specs=[vmem] * 2,
        scratch_shapes=[
            pltpu.VMEM((2, slots * rows, full_rows), jnp.bfloat16),
            pltpu.VMEM((2, full_rows, full_rows), jnp.bfloat16),
        ],
        compiler_params=pltpu.CompilerParams(vmem_limit_bytes=32 * 2**20),
        cost_estimate=pl.CostEstimate(flops=2**31, bytes_accessed=6 * 2**20, transcendentals=0),
        name="prepare",
    )(angles, defocus, jnp.asarray(row_tables(full_rows)))


def unpacked(packed):
    rows = 4 * packed.shape[0] // 9
    rest = packed[2 * rows :].astype(jnp.float32)
    quarters = []
    for tile in range(2):
        both = rest[:, tile * MAIN : (tile + 1) * MAIN]
        quarters += [both, pltpu.roll(both, MAIN - XBLK * REST, 1)]
    rest = jnp.concatenate(quarters, 0).astype(jnp.bfloat16)
    return jnp.concatenate([packed[:rows], packed[rows : 2 * rows], rest], 1)


def corrected_patches(slot, rows_ref, patch_refs):
    patches = jnp.concatenate([unpacked(ref[...]) for ref in patch_refs], 0)
    rows = patches.shape[0] // len(patch_refs)
    image = jnp.dot(rows_ref[slot * rows : (slot + 1) * rows, :], patches, preferred_element_type=jnp.float32)
    lane = lax.broadcasted_iota(jnp.int32, (rows, MAIN), 1) // REST
    main = jnp.concatenate([image[:, block * MAIN : (block + 1) * MAIN] for block in range(XBLK)], 0)
    rest = jnp.concatenate([jnp.where(lane == block, image[:, XBLK * MAIN :], 0.0) for block in range(XBLK)], 0)
    return jnp.concatenate([main, rest[:, : XBLK * REST]], 1).astype(jnp.bfloat16)


def sum_kernel(slots, row_devices, rows_ref, weights_ref, *refs):
    patch_refs, total_ref = refs[:-1], refs[-1]
    parts = [
        corrected_patches(slot, rows_ref, patch_refs[i * row_devices : (i + 1) * row_devices])
        for i, slot in enumerate(slots)
    ]
    step = 4 * XBW
    for first in range(0, total_ref.shape[1], step):
        here = slice(first, first + step)
        total = jnp.dot(parts[0], weights_ref[slots[0], :, here], preferred_element_type=jnp.float32)
        for part, slot in zip(parts[1:], slots[1:]):
            total += jnp.dot(part, weights_ref[slot, :, here], preferred_element_type=jnp.float32)
        total_ref[:, here] = total


def finish_kernel(factor, slots, row_devices, rows_ref, weights_ref, total_ref, *refs):
    patch_refs = refs[: len(slots) * row_devices]
    out_ref, out, sems = refs[len(slots) * row_devices :]
    rows = total_ref.shape[0] // XBLK
    parts = [
        corrected_patches(slot, rows_ref, patch_refs[i * row_devices : (i + 1) * row_devices])
        for i, slot in enumerate(slots)
    ]
    step = 4
    copies = []
    for group in range(out.shape[0] // step):
        here = slice(group * step * XBW, (group + 1) * step * XBW)
        total = total_ref[:, here]
        for part, slot in zip(parts, slots):
            total += jnp.dot(part, weights_ref[slot, :, here], preferred_element_type=jnp.float32)
        for c in range(step):
            for block in range(XBLK):
                out[group * step + c, :, block * XBW : (block + 1) * XBW] = (
                    factor * total[block * rows : (block + 1) * rows, c * XBW : (c + 1) * XBW]
                ).astype(jnp.bfloat16)
        part = pl.ds(group * step, step)
        copies.append(pltpu.make_async_copy(out.at[part], out_ref.at[part], sems.at[group]))
        copies[-1].start()
    for copy in copies:
        copy.wait()


def interpolation(kernel, slots, weights, row_filters, patches, totals, **call):
    _, taps, width = weights.shape
    rows = row_filters.shape[0] // weights.shape[0]
    vmem = pl.BlockSpec(memory_space=pltpu.VMEM)
    operands = [row_filters, weights, *totals, *(block for slot in slots for block in patches[slot])]
    flops = 2 * len(slots) * taps * width * XBLK * rows
    return pl.pallas_call(
        functools.partial(kernel, slots, len(patches[0])),
        in_specs=[vmem] * len(operands),
        compiler_params=pltpu.CompilerParams(vmem_limit_bytes=32 * 2**20),
        cost_estimate=pl.CostEstimate(flops=0, bytes_accessed=0, transcendentals=0),
        **call,
    )(*operands)


def summed(row_filters, weights, patches, slots):
    return interpolation(
        sum_kernel,
        slots,
        weights,
        row_filters,
        patches,
        [],
        out_shape=jax.ShapeDtypeStruct((XBLK * row_filters.shape[0] // weights.shape[0], weights.shape[2]), jnp.float32),
        out_specs=pl.BlockSpec(memory_space=pltpu.VMEM),
        name="sum_early_tilts",
    )


def finished(row_filters, weights, total, patches, slots, factor):
    shape = (weights.shape[2] // XBW, row_filters.shape[0] // weights.shape[0], XBLK * XBW)
    return interpolation(
        functools.partial(finish_kernel, factor),
        slots,
        weights,
        row_filters,
        patches,
        [total],
        out_shape=jax.ShapeDtypeStruct(shape, jnp.bfloat16),
        out_specs=pl.BlockSpec(memory_space=pl.ANY),
        scratch_shapes=[pltpu.VMEM(shape, jnp.bfloat16), pltpu.SemaphoreType.DMA((shape[0] // 4,))],
        name="finish_volume",
    )


def exchange(array, axis, distance):
    count = lax.axis_size(axis)
    return lax.ppermute(array, axis, [(i, i ^ distance) for i in range(count)])


def gather_rows(array, awaited=()):
    blocks = {0: array}
    bit = lax.axis_size("row") // 2
    while bit:
        if bit == 1 and awaited:
            blocks = {d: after(block, *awaited) if d else block for d, block in blocks.items()}
        blocks.update({d ^ bit: exchange(block, "row", bit) for d, block in blocks.items()})
        bit //= 2
    return [blocks[d] for d in sorted(blocks)]


def per_device(projections, tilt_angle, band_start, defocus):
    _, rows, _ = projections.shape
    row_devices, tilt_devices = lax.axis_size("row"), lax.axis_size("tilt")
    slices_owned = SLICES // tilt_devices
    far, near = list(range(tilt_devices - 1, 1, -1)), list(range(min(2, tilt_devices) - 1, -1, -1))
    sent = column_filtered(far + near, slices_owned, projections[0], tilt_angle, defocus, band_start)
    arrived = {d: exchange(sent[d], "tilt", d) if d else sent[d] for d in far + near}
    row_filters, weights = prepared(tilt_devices, slices_owned, rows, rows * row_devices, tilt_angle, defocus)
    patches = {d: gather_rows(after(arrived[d], row_filters) if d else arrived[d]) for d in near}
    total = summed(row_filters, weights, patches, near)
    for d in far:
        patches[d] = gather_rows(arrived[d])
    return finished(row_filters, weights, total, patches, far, 1.0 / math.sqrt(tilt_devices))


def solution(mesh):
    in_specs = (
        P(("group", "tilt"), "row", None),
        P("group"),
        P("group", None, None),
        P("group", None),
    )
    out_specs = P(("group", "tilt"), "row", None)
    return jax.shard_map(
        per_device, mesh=mesh, in_specs=in_specs, out_specs=out_specs, check_vma=False
    )
```

```python
import functools
import math

import jax
import jax.numpy as jnp
import numpy as np
from jax import lax
from jax.experimental import pallas as pl
from jax.experimental.pallas import tpu as pltpu
from jax.sharding import PartitionSpec as P

SLAB = 16
XBW = 128
BAND = 256
XBLK = 4
SLICES = 64
RADIX = 8
MAIN = 128
REST = 16
REACH = MAIN + REST
WINDOW = 384
ROOT = math.sqrt(0.5)


def split(table):
    high = table.astype(jnp.bfloat16)
    return high, (table - high.astype(np.float64)).astype(jnp.bfloat16)


def column_tables(columns):
    size = columns // RADIX
    half = size // 2
    u = np.arange(size)[:, None]

    def angles(freq):
        return 2.0 * np.pi * ((u * freq[None, :]) % columns) / columns

    k0, s0 = RADIX * np.arange(half + 1), RADIX * np.arange(1, half)
    k4 = RADIX * np.arange(half) + 4
    m0 = np.concatenate([np.cos(angles(k0)), -np.sin(angles(s0))], 1)
    m4 = np.concatenate([np.cos(angles(k4)), -np.sin(angles(k4))], 1)
    full = angles(RADIX * np.arange(size))
    waves = np.concatenate([np.cos(full), np.sin(full)], 1)
    ends = np.concatenate([m0, m4], 1)

    matrices = np.stack([*split(ends), *split(waves), np.concatenate([m0.T, m4.T], 1).astype(jnp.bfloat16)])
    return matrices


def column_lines(columns):
    size = columns // RADIX
    half = size // 2
    line = lax.broadcasted_iota(jnp.int32, (8, size), 0)
    u = lax.broadcasted_iota(jnp.int32, (8, size), 1)
    freq = jnp.where(line == 0, RADIX * jnp.where(u <= half, u, u - half), RADIX * (u & (half - 1)) + 4)
    freq = jnp.where(line < 2, freq, RADIX * u + line // 2)
    fold = jnp.minimum(freq, columns - freq)
    count = jnp.where((fold == 0) | (fold == columns // 2), 1.0, 2.0)
    gain = count * (fold.astype(jnp.float32) + 0.5) * (2.0 / (columns * columns))
    angle = (u * (line + 1)).astype(jnp.float32) * (2.0 * math.pi / columns)
    return fold * fold, gain, jnp.cos(angle), jnp.sin(angle)


def row_tables(full_rows):
    half = full_rows // 2
    column = np.arange(full_rows)
    freq = np.where(column <= half, column, column - half)
    angle = 2.0 * np.pi * (np.arange(full_rows)[:, None] * freq[None, :] % full_rows) / full_rows
    return np.stack(split(np.where(column[None, :] <= half, np.cos(angle), np.sin(angle))))


def packed_shape(rows):
    return (2 * rows + rows // 4, 2 * MAIN)


def flip_sign(squares, defocus, length):
    cycles = lax.div(squares * defocus, jnp.int32(length * length))
    return (1 - 2 * (cycles & 1)).astype(jnp.float32)


def fetched(sources, targets, sems):
    copies = [pltpu.make_async_copy(s, t, sems.at[i]) for i, (s, t) in enumerate(zip(sources, targets))]
    for copy in copies:
        copy.start()
    return copies


def reach_of(angle):
    line = jnp.full((8, XBW), angle, jnp.float32)
    cosine, sine = jnp.cos(line), jnp.sin(line)
    lowest = 0.5 * XBW + jnp.minimum((XBW - 1) * cosine, 0.0) - 0.5 * (SLAB - 1) * jnp.abs(sine)
    first = jnp.clip(jnp.floor(lowest) - 4.0, 0.0, float(BAND - REACH))
    return cosine[:1], sine[:1], jnp.max(first).astype(jnp.int32)


def butterflies(image, turns, zhi, zlo):
    rows, columns = image.shape
    size = columns // RADIX

    def step(i, carry):
        here = pl.ds(pl.multiple_of(i * 16, 16), 16)
        x = [image[here, m * size : (m + 1) * size].astype(jnp.float32) for m in range(8)]
        p0, p1, p2, p3 = (x[m] + x[m + 4] for m in range(4))
        q0, q1, q2, q3 = (x[m] - x[m + 4] for m in range(4))
        e, f = p0 + p2, p1 + p3
        g, h = ROOT * (q1 - q3), ROOT * (q1 + q3)
        z = [e + f, e - f]
        for j, (real, imag) in enumerate([(q0 + g, -q2 - h), (p0 - p2, p3 - p1), (q0 - g, q2 - h)]):
            c, s = turns[2 * j], turns[2 * j + 1]
            z += [real * c + imag * s, imag * c - real * s]
        for line in range(8):
            top = z[line].astype(jnp.bfloat16)
            zhi[line, here, :] = top
            zlo[line, here, :] = (z[line] - top.astype(jnp.float32)).astype(jnp.bfloat16)
        return carry

    lax.fori_loop(0, rows // 16, step, 0)


def inverse_butterflies(ends, waves, turns, turned):
    rows, columns = turned.shape
    size = columns // RADIX

    def step(i, carry):
        here = pl.ds(pl.multiple_of(i * 8, 8), 8)
        r, s = [], []
        for j in range(3):
            c, d = turns[2 * j], turns[2 * j + 1]
            real = waves[2 * j, here, :size] - waves[2 * j + 1, here, size:]
            imag = waves[2 * j, here, size:] + waves[2 * j + 1, here, :size]
            r.append(real * c - imag * d)
            s.append(real * d + imag * c)
        e, f = ends[0, here, :] + ends[1, here, :], ends[0, here, :] - ends[1, here, :]
        a, b, c, d = r[0] + r[2], r[0] - r[2], s[0] + s[2], s[0] - s[2]
        even0, even2, odd1, odd3 = e + r[1], e - r[1], f - s[1], f + s[1]
        g, h = ROOT * (b - c), ROOT * (b + c)
        out = [even0 + a, odd1 + g, even2 - d, odd3 - h, even0 - a, odd1 - g, even2 + d, odd3 + h]
        for m in range(8):
            turned[here, m * size : (m + 1) * size] = out[m]
        return carry

    lax.fori_loop(0, rows // 8, step, 0)


def send_patches(slots, slices_owned, spectrum, wave_table, end_table, columns, facts, scratch, out_refs):
    squares, ramp, turns, angles, defocus, starts = facts
    ends, waves, turned, out, out_sems = scratch
    rows, size = spectrum[0].shape
    tilt = lax.axis_index("tilt")
    slabs = [(tilt ^ slot) * slices_owned // SLAB for slot in slots]
    gains = [flip_sign(squares, defocus[tilt, slab], columns) * ramp for slab in slabs]
    filtered = [
        jnp.concatenate([(spectrum[i] * gain[i : i + 1, :]).astype(jnp.bfloat16) for gain in gains], 0) for i in range(8)
    ]
    for i in range(2):
        ends[i] = jnp.dot(filtered[i], end_table[:, i * size : (i + 1) * size], preferred_element_type=jnp.float32)
    for i in range(6):
        waves[i] = jnp.dot(filtered[2 + i], wave_table[...], preferred_element_type=jnp.float32)
    inverse_butterflies(ends, waves, turns, turned)
    lane = lax.broadcasted_iota(jnp.int32, (rows, MAIN), 1) // REST
    _, _, first_tap = reach_of(angles[tilt])
    sends = []
    for i, slab in enumerate(slabs):
        rest = jnp.zeros((rows, MAIN), jnp.float32)
        for block in range(XBLK):
            start = starts[tilt, slab, block] + first_tap
            base = pl.multiple_of(jnp.minimum((start // 128) * 128, columns - WINDOW), 128)
            window = turned[i * rows : (i + 1) * rows, pl.ds(base, WINDOW)]
            shift = base - start
            reach = pltpu.roll(window, jnp.where(shift < 0, shift + WINDOW, shift), 1)[:, : 2 * MAIN]
            there = slice(block // 2 * rows, (block // 2 + 1) * rows), slice(block % 2 * MAIN, (block % 2 + 1) * MAIN)
            out[i, *there] = reach[:, :MAIN].astype(jnp.bfloat16)
            last = reach[:, MAIN:]
            rest = jnp.where(lane == block, pltpu.roll(last, block * REST, 1) if block else last, rest)
        quarters = [rest[q * rows // 4 : (q + 1) * rows // 4] for q in range(4)]
        for tile in range(2):
            right = pltpu.roll(quarters[2 * tile + 1], XBLK * REST, 1)
            both = jnp.where(lane[: rows // 4] < XBLK, quarters[2 * tile], right)
            out[i, 2 * rows :, tile * MAIN : (tile + 1) * MAIN] = both.astype(jnp.bfloat16)
        sends.append(pltpu.make_async_copy(out.at[i], out_refs[i], out_sems.at[i]))
        sends[-1].start()
    return sends


def column_kernel(slots, slices_owned, image_ref, matrix_ref, angle_ref, defocus_ref, starts_ref, *refs):
    count = len(slots)
    out_refs = refs[:count]
    image, matrix, angles, defocus, starts, zhi, zlo, *scratch, sems = refs[count:]
    rows, columns = image.shape
    size = columns // RADIX
    copies = fetched(
        [image_ref, angle_ref, defocus_ref, starts_ref] + [matrix_ref.at[i] for i in range(5)],
        [image, angles, defocus, starts] + [matrix.at[i] for i in range(5)],
        sems,
    )
    squares, ramp, cosine_turns, sine_turns = column_lines(columns)
    turns = [t[j : j + 1, :] for j in range(3) for t in (cosine_turns, sine_turns)]
    copies[0].wait()
    butterflies(image, turns, zhi, zlo)
    for copy in copies[1:]:
        copy.wait()

    def product(first, lines, table, here):
        top = zhi[first : first + lines].reshape(lines * rows, size)
        rest = zlo[first : first + lines].reshape(lines * rows, size)
        total = jnp.dot(top, matrix[table, :, here], preferred_element_type=jnp.float32)
        total += jnp.dot(top, matrix[table + 1, :, here], preferred_element_type=jnp.float32)
        return total + jnp.dot(rest, matrix[table, :, here], preferred_element_type=jnp.float32)

    spectrum = [product(0, 1, 0, slice(0, size)), product(1, 1, 0, slice(size, 2 * size))]
    mixed = product(2, 6, 2, slice(None))
    for j in range(3):
        real, imag = mixed[2 * j * rows : (2 * j + 1) * rows], mixed[(2 * j + 1) * rows : (2 * j + 2) * rows]
        spectrum += [real[:, :size] + imag[:, size:], imag[:, :size] - real[:, size:]]
    facts = (squares, ramp, turns, angles, defocus, starts)
    sends = send_patches(
        slots, slices_owned, spectrum, matrix.at[2], matrix.at[4], columns, facts, scratch, out_refs
    )
    for copy in sends:
        copy.wait()


def column_filtered(slots, slices_owned, image, angles, defocus, starts):
    rows, columns = image.shape
    size = columns // RADIX
    count = len(slots)
    matrices = jnp.asarray(column_tables(columns))
    away = pl.BlockSpec(memory_space=pl.ANY)
    flops = 2 * rows * size * size * (42 + 14 * count)
    sent = pl.pallas_call(
        functools.partial(column_kernel, slots, slices_owned),
        out_shape=[jax.ShapeDtypeStruct(packed_shape(rows), jnp.bfloat16)] * count,
        in_specs=[away] * 5,
        out_specs=[away] * count,
        scratch_shapes=[
            pltpu.VMEM((rows, columns), jnp.bfloat16),
            pltpu.VMEM(matrices.shape, jnp.bfloat16),
            pltpu.SMEM(angles.shape, jnp.float32),
            pltpu.SMEM(defocus.shape, jnp.int32),
            pltpu.SMEM(starts.shape, jnp.int32),
            pltpu.VMEM((8, rows, size), jnp.bfloat16),
            pltpu.VMEM((8, rows, size), jnp.bfloat16),
            pltpu.VMEM((2, count * rows, size), jnp.float32),
            pltpu.VMEM((6, count * rows, 2 * size), jnp.float32),
            pltpu.VMEM((count * rows, columns), jnp.float32),
            pltpu.VMEM((count, *packed_shape(rows)), jnp.bfloat16),
            pltpu.SemaphoreType.DMA((count,)),
            pltpu.SemaphoreType.DMA((9,)),
        ],
        compiler_params=pltpu.CompilerParams(vmem_limit_bytes=60 * 2**20),
        cost_estimate=pl.CostEstimate(flops=flops, bytes_accessed=3 * 2**20, transcendentals=0),
        name="column_filter",
    )(image, matrices, angles, defocus, starts)
    return dict(zip(slots, sent))


def after(array, *others):
    away = pl.BlockSpec(memory_space=pl.ANY)
    return pl.pallas_call(
        lambda *refs: None,
        out_shape=jax.ShapeDtypeStruct(array.shape, array.dtype),
        in_specs=[away] * (1 + len(others)),
        out_specs=away,
        input_output_aliases={0: 0},
        compiler_params=pltpu.CompilerParams(vmem_limit_bytes=2**20),
        cost_estimate=pl.CostEstimate(flops=0, bytes_accessed=0, transcendentals=0),
        name="after",
    )(array, *others)


def prepare_kernel(slots, slices_owned, angles, defocus, waves, rows_ref, weights_ref, mine, order):
    tilt, row = lax.axis_index("tilt"), lax.axis_index("row")
    slab, local_first = tilt * slices_owned // SLAB, tilt * slices_owned % SLAB
    full_rows = waves.shape[1]
    rows = rows_ref.shape[0] // slots
    half = full_rows // 2
    column = lax.broadcasted_iota(jnp.int32, (8, full_rows), 1)
    freq = jnp.where(column <= half, column, column - half)
    count = jnp.where((freq == 0) | (freq == half), 1.0, 2.0) / full_rows
    scales = [(flip_sign(freq * freq, defocus[tilt ^ slot, slab], full_rows) * count)[:1] for slot in range(slots)]
    for part in range(2):
        for block in range(full_rows // rows):
            there = pl.ds(pl.multiple_of((row ^ block) * rows, rows), rows)
            order[part, block * rows : (block + 1) * rows, :] = waves[part, there, :]
        own = order[part, :rows, :].astype(jnp.float32)
        for slot in range(slots):
            mine[part, slot * rows : (slot + 1) * rows, :] = (own * scales[slot]).astype(jnp.bfloat16)

    def product(left, right):
        over = (((1,), (1,)), ((), ()))
        return lax.dot_general(mine[left], order[right], over, preferred_element_type=jnp.float32)

    rows_ref[...] = (product(0, 0) + product(0, 1) + product(1, 0)).astype(jnp.bfloat16)

    place = lax.broadcasted_iota(jnp.int32, (REACH, XBW), 0).astype(jnp.float32)
    across = lax.broadcasted_iota(jnp.int32, (1, XBW), 1).astype(jnp.float32)
    for slot in range(slots):
        cosine, sine, first_tap = reach_of(angles[tilt ^ slot])
        tap = place + first_tap.astype(jnp.float32)

        def one_slice(c, carry):
            offset = (local_first + c).astype(jnp.float32) - 0.5 * (SLAB - 1)
            centre = 0.5 * XBW + across * cosine + offset * sine
            there = pl.ds(pl.multiple_of(c * XBW, XBW), XBW)
            weights = jnp.maximum(0.0, 1.0 - jnp.abs(tap - centre)).astype(jnp.bfloat16)
            weights_ref[slot, :REACH, there] = weights
            for block in range(1, XBLK):
                weights_ref[slot, MAIN + block * REST : MAIN + (block + 1) * REST, there] = weights[MAIN:]
            return carry

        lax.fori_loop(0, slices_owned, one_slice, 0, unroll=2)


def prepared(slots, slices_owned, rows, full_rows, angles, defocus):
    smem, vmem = pl.BlockSpec(memory_space=pltpu.SMEM), pl.BlockSpec(memory_space=pltpu.VMEM)
    return pl.pallas_call(
        functools.partial(prepare_kernel, slots, slices_owned),
        out_shape=[
            jax.ShapeDtypeStruct((slots * rows, full_rows), jnp.bfloat16),
            jax.ShapeDtypeStruct((slots, MAIN + XBLK * REST, slices_owned * XBW), jnp.bfloat16),
        ],
        in_specs=[smem] * 2 + [vmem],
        out_specs=[vmem] * 2,
        scratch_shapes=[
            pltpu.VMEM((2, slots * rows, full_rows), jnp.bfloat16),
            pltpu.VMEM((2, full_rows, full_rows), jnp.bfloat16),
        ],
        compiler_params=pltpu.CompilerParams(vmem_limit_bytes=32 * 2**20),
        cost_estimate=pl.CostEstimate(flops=2**31, bytes_accessed=6 * 2**20, transcendentals=0),
        name="prepare",
    )(angles, defocus, jnp.asarray(row_tables(full_rows)))


def unpacked(packed):
    rows = 4 * packed.shape[0] // 9
    rest = packed[2 * rows :].astype(jnp.float32)
    quarters = []
    for tile in range(2):
        both = rest[:, tile * MAIN : (tile + 1) * MAIN]
        quarters += [both, pltpu.roll(both, MAIN - XBLK * REST, 1)]
    rest = jnp.concatenate(quarters, 0).astype(jnp.bfloat16)
    return jnp.concatenate([packed[:rows], packed[rows : 2 * rows], rest], 1)


def corrected_patches(slots, row_devices, rows_ref, patch_refs):
    parts = []
    for group in slots:
        refs, patch_refs = patch_refs[:row_devices], patch_refs[row_devices:]
        height = refs[0].shape[0] // len(group)
        for i, slot in enumerate(group):
            patches = jnp.concatenate([unpacked(ref[i * height : (i + 1) * height]) for ref in refs], 0)
            rows = patches.shape[0] // row_devices
            image = jnp.dot(rows_ref[slot * rows : (slot + 1) * rows, :], patches, preferred_element_type=jnp.float32)
            lane = lax.broadcasted_iota(jnp.int32, (rows, MAIN), 1) // REST
            main = jnp.concatenate([image[:, block * MAIN : (block + 1) * MAIN] for block in range(XBLK)], 0)
            rest = [jnp.where(lane == block, image[:, XBLK * MAIN :], 0.0) for block in range(XBLK)]
            rest = jnp.concatenate(rest, 0)[:, : XBLK * REST]
            parts.append((slot, jnp.concatenate([main, rest], 1).astype(jnp.bfloat16)))
    return parts


def sum_kernel(slots, row_devices, rows_ref, weights_ref, *refs):
    total_ref = refs[-1]
    (slot, part), *others = corrected_patches(slots, row_devices, rows_ref, refs[:-1])
    step = 4 * XBW
    for first in range(0, total_ref.shape[1], step):
        here = slice(first, first + step)
        total = jnp.dot(part, weights_ref[slot, :, here], preferred_element_type=jnp.float32)
        for other, more in others:
            total += jnp.dot(more, weights_ref[other, :, here], preferred_element_type=jnp.float32)
        total_ref[:, here] = total


def finish_kernel(factor, slots, row_devices, rows_ref, weights_ref, total_ref, *refs):
    patch_refs = refs[: len(slots) * row_devices]
    out_ref, out, sems = refs[len(slots) * row_devices :]
    rows = total_ref.shape[0] // XBLK
    parts = corrected_patches(slots, row_devices, rows_ref, patch_refs)
    step = 4
    copies = []
    for group in range(out.shape[0] // step):
        here = slice(group * step * XBW, (group + 1) * step * XBW)
        total = total_ref[:, here]
        for slot, part in parts:
            total += jnp.dot(part, weights_ref[slot, :, here], preferred_element_type=jnp.float32)
        for c in range(step):
            for block in range(XBLK):
                out[group * step + c, :, block * XBW : (block + 1) * XBW] = (
                    factor * total[block * rows : (block + 1) * rows, c * XBW : (c + 1) * XBW]
                ).astype(jnp.bfloat16)
        part = pl.ds(group * step, step)
        copies.append(pltpu.make_async_copy(out.at[part], out_ref.at[part], sems.at[group]))
        copies[-1].start()
    for copy in copies:
        copy.wait()


def interpolation(kernel, slots, weights, row_filters, patches, totals, **call):
    vmem = pl.BlockSpec(memory_space=pltpu.VMEM)
    operands = [row_filters, weights, *totals, *(block for group in patches for block in group)]
    return pl.pallas_call(
        functools.partial(kernel, slots, len(patches[0])),
        in_specs=[vmem] * len(operands),
        compiler_params=pltpu.CompilerParams(vmem_limit_bytes=32 * 2**20),
        cost_estimate=pl.CostEstimate(flops=0, bytes_accessed=0, transcendentals=0),
        **call,
    )(*operands)


def summed(row_filters, weights, patches, slots):
    return interpolation(
        sum_kernel,
        slots,
        weights,
        row_filters,
        patches,
        [],
        out_shape=jax.ShapeDtypeStruct((XBLK * row_filters.shape[0] // weights.shape[0], weights.shape[2]), jnp.float32),
        out_specs=pl.BlockSpec(memory_space=pltpu.VMEM),
        name="sum_early_tilts",
    )


def finished(row_filters, weights, total, patches, slots, factor):
    shape = (weights.shape[2] // XBW, row_filters.shape[0] // weights.shape[0], XBLK * XBW)
    return interpolation(
        functools.partial(finish_kernel, factor),
        slots,
        weights,
        row_filters,
        patches,
        [total],
        out_shape=jax.ShapeDtypeStruct(shape, jnp.bfloat16),
        out_specs=pl.BlockSpec(memory_space=pl.ANY),
        scratch_shapes=[pltpu.VMEM(shape, jnp.bfloat16), pltpu.SemaphoreType.DMA((shape[0] // 4,))],
        name="finish_volume",
    )


def exchange(array, axis, distance):
    count = lax.axis_size(axis)
    return lax.ppermute(array, axis, [(i, i ^ distance) for i in range(count)])


def gather_rows(array, awaited=()):
    blocks = {0: array}
    bit = lax.axis_size("row") // 2
    while bit:
        if bit == 1 and awaited:
            blocks = {d: after(block, *awaited) if d else block for d, block in blocks.items()}
        blocks.update({d ^ bit: exchange(block, "row", bit) for d, block in blocks.items()})
        bit //= 2
    return [blocks[d] for d in sorted(blocks)]


def per_device(projections, tilt_angle, band_start, defocus):
    _, rows, _ = projections.shape
    row_devices, tilt_devices = lax.axis_size("row"), lax.axis_size("tilt")
    slices_owned = SLICES // tilt_devices
    far, near = list(range(tilt_devices - 1, 1, -1)), list(range(min(2, tilt_devices)))
    sent = column_filtered(far + near, slices_owned, projections[0], tilt_angle, defocus, band_start)
    arrived = {d: exchange(sent[d], "tilt", d) if d else sent[d] for d in far + near}
    row_filters, weights = prepared(tilt_devices, slices_owned, rows, rows * row_devices, tilt_angle, defocus)
    early = [gather_rows(jnp.concatenate([arrived[d] for d in near]))]
    total = summed(row_filters, weights, early, [near])
    late = [gather_rows(after(arrived[d], row_filters) if d == far[-1] else arrived[d]) for d in far]
    return finished(row_filters, weights, total, late, [[d] for d in far], 1.0 / math.sqrt(tilt_devices))


def solution(mesh):
    in_specs = (
        P(("group", "tilt"), "row", None),
        P("group"),
        P("group", None, None),
        P("group", None),
    )
    out_specs = P(("group", "tilt"), "row", None)
    return jax.shard_map(
        per_device, mesh=mesh, in_specs=in_specs, out_specs=out_specs, check_vma=False
    )
```

```python
import functools
import math

import jax
import jax.numpy as jnp
import numpy as np
from jax import lax
from jax.experimental import pallas as pl
from jax.experimental.pallas import tpu as pltpu
from jax.sharding import PartitionSpec as P

SLAB = 16
XBW = 128
BAND = 256
XBLK = 4
SLICES = 64
RADIX = 8
MAIN = 128
REST = 16
REACH = MAIN + REST
WINDOW = 384
ROOT = math.sqrt(0.5)


def split(table):
    high = table.astype(jnp.bfloat16)
    return high, (table - high.astype(np.float64)).astype(jnp.bfloat16)


def column_tables(columns):
    size = columns // RADIX
    half = size // 2
    u = np.arange(size)[:, None]

    def angles(freq):
        return 2.0 * np.pi * ((u * freq[None, :]) % columns) / columns

    k0, s0 = RADIX * np.arange(half + 1), RADIX * np.arange(1, half)
    k4 = RADIX * np.arange(half) + 4
    m0 = np.concatenate([np.cos(angles(k0)), -np.sin(angles(s0))], 1)
    m4 = np.concatenate([np.cos(angles(k4)), -np.sin(angles(k4))], 1)
    full = angles(RADIX * np.arange(size))
    waves = np.concatenate([np.cos(full), np.sin(full)], 1)
    ends = np.concatenate([m0, m4], 1)

    matrices = np.stack([*split(ends), *split(waves), np.concatenate([m0.T, m4.T], 1).astype(jnp.bfloat16)])
    return matrices


def column_lines(columns):
    size = columns // RADIX
    half = size // 2
    line = lax.broadcasted_iota(jnp.int32, (8, size), 0)
    u = lax.broadcasted_iota(jnp.int32, (8, size), 1)
    freq = jnp.where(line == 0, RADIX * jnp.where(u <= half, u, u - half), RADIX * (u & (half - 1)) + 4)
    freq = jnp.where(line < 2, freq, RADIX * u + line // 2)
    fold = jnp.minimum(freq, columns - freq)
    count = jnp.where((fold == 0) | (fold == columns // 2), 1.0, 2.0)
    gain = count * (fold.astype(jnp.float32) + 0.5) * (2.0 / (columns * columns))
    angle = (u * (line + 1)).astype(jnp.float32) * (2.0 * math.pi / columns)
    return fold * fold, gain, jnp.cos(angle), jnp.sin(angle)


def row_tables(full_rows):
    half = full_rows // 2
    column = np.arange(full_rows)
    freq = np.where(column <= half, column, column - half)
    angle = 2.0 * np.pi * (np.arange(full_rows)[:, None] * freq[None, :] % full_rows) / full_rows
    return np.stack(split(np.where(column[None, :] <= half, np.cos(angle), np.sin(angle))))


def packed_shape(rows):
    return (2 * rows + rows // 4, 2 * MAIN)


def flip_sign(squares, defocus, length):
    cycles = lax.div(squares * defocus, jnp.int32(length * length))
    return (1 - 2 * (cycles & 1)).astype(jnp.float32)


def fetched(sources, targets, sems):
    copies = [pltpu.make_async_copy(s, t, sems.at[i]) for i, (s, t) in enumerate(zip(sources, targets))]
    for copy in copies:
        copy.start()
    return copies


def reach_of(angle):
    line = jnp.full((8, XBW), angle, jnp.float32)
    cosine, sine = jnp.cos(line), jnp.sin(line)
    lowest = 0.5 * XBW + jnp.minimum((XBW - 1) * cosine, 0.0) - 0.5 * (SLAB - 1) * jnp.abs(sine)
    first = jnp.clip(jnp.floor(lowest) - 4.0, 0.0, float(BAND - REACH))
    return cosine[:1], sine[:1], jnp.max(first).astype(jnp.int32)


def butterflies(image, turns, zhi, zlo):
    rows, columns = image.shape
    size = columns // RADIX

    def step(i, carry):
        here = pl.ds(pl.multiple_of(i * 16, 16), 16)
        x = [image[here, m * size : (m + 1) * size].astype(jnp.float32) for m in range(8)]
        p0, p1, p2, p3 = (x[m] + x[m + 4] for m in range(4))
        q0, q1, q2, q3 = (x[m] - x[m + 4] for m in range(4))
        e, f = p0 + p2, p1 + p3
        g, h = ROOT * (q1 - q3), ROOT * (q1 + q3)
        z = [e + f, e - f]
        for j, (real, imag) in enumerate([(q0 + g, -q2 - h), (p0 - p2, p3 - p1), (q0 - g, q2 - h)]):
            c, s = turns[2 * j], turns[2 * j + 1]
            z += [real * c + imag * s, imag * c - real * s]
        for line in range(8):
            top = z[line].astype(jnp.bfloat16)
            zhi[line, here, :] = top
            zlo[line, here, :] = (z[line] - top.astype(jnp.float32)).astype(jnp.bfloat16)
        return carry

    lax.fori_loop(0, rows // 16, step, 0)


def inverse_butterflies(ends, waves, turns, turned):
    rows, columns = turned.shape
    size = columns // RADIX

    def step(i, carry):
        here = pl.ds(pl.multiple_of(i * 8, 8), 8)
        r, s = [], []
        for j in range(3):
            c, d = turns[2 * j], turns[2 * j + 1]
            real = waves[2 * j, here, :size] - waves[2 * j + 1, here, size:]
            imag = waves[2 * j, here, size:] + waves[2 * j + 1, here, :size]
            r.append(real * c - imag * d)
            s.append(real * d + imag * c)
        e, f = ends[0, here, :] + ends[1, here, :], ends[0, here, :] - ends[1, here, :]
        a, b, c, d = r[0] + r[2], r[0] - r[2], s[0] + s[2], s[0] - s[2]
        even0, even2, odd1, odd3 = e + r[1], e - r[1], f - s[1], f + s[1]
        g, h = ROOT * (b - c), ROOT * (b + c)
        out = [even0 + a, odd1 + g, even2 - d, odd3 - h, even0 - a, odd1 - g, even2 + d, odd3 + h]
        for m in range(8):
            turned[here, m * size : (m + 1) * size] = out[m]
        return carry

    lax.fori_loop(0, rows // 8, step, 0)


def send_patches(slots, slices_owned, spectrum, wave_table, end_table, columns, facts, scratch, out_refs):
    squares, ramp, turns, angles, defocus, starts = facts
    ends, waves, turned, out, out_sems = scratch
    rows, size = spectrum[0].shape
    tilt = lax.axis_index("tilt")
    slabs = [(tilt ^ slot) * slices_owned // SLAB for slot in slots]
    gains = [flip_sign(squares, defocus[tilt, slab], columns) * ramp for slab in slabs]
    filtered = [
        jnp.concatenate([(spectrum[i] * gain[i : i + 1, :]).astype(jnp.bfloat16) for gain in gains], 0) for i in range(8)
    ]
    for i in range(2):
        ends[i] = jnp.dot(filtered[i], end_table[:, i * size : (i + 1) * size], preferred_element_type=jnp.float32)
    for i in range(6):
        waves[i] = jnp.dot(filtered[2 + i], wave_table[...], preferred_element_type=jnp.float32)
    inverse_butterflies(ends, waves, turns, turned)
    lane = lax.broadcasted_iota(jnp.int32, (rows, MAIN), 1) // REST
    _, _, first_tap = reach_of(angles[tilt])
    sends = []
    for i, slab in enumerate(slabs):
        rest = jnp.zeros((rows, MAIN), jnp.float32)
        for block in range(XBLK):
            start = starts[tilt, slab, block] + first_tap
            base = pl.multiple_of(jnp.minimum((start // 128) * 128, columns - WINDOW), 128)
            window = turned[i * rows : (i + 1) * rows, pl.ds(base, WINDOW)]
            shift = base - start
            reach = pltpu.roll(window, jnp.where(shift < 0, shift + WINDOW, shift), 1)[:, : 2 * MAIN]
            there = slice(block // 2 * rows, (block // 2 + 1) * rows), slice(block % 2 * MAIN, (block % 2 + 1) * MAIN)
            out[i, *there] = reach[:, :MAIN].astype(jnp.bfloat16)
            last = reach[:, MAIN:]
            rest = jnp.where(lane == block, pltpu.roll(last, block * REST, 1) if block else last, rest)
        quarters = [rest[q * rows // 4 : (q + 1) * rows // 4] for q in range(4)]
        for tile in range(2):
            right = pltpu.roll(quarters[2 * tile + 1], XBLK * REST, 1)
            both = jnp.where(lane[: rows // 4] < XBLK, quarters[2 * tile], right)
            out[i, 2 * rows :, tile * MAIN : (tile + 1) * MAIN] = both.astype(jnp.bfloat16)
        sends.append(pltpu.make_async_copy(out.at[i], out_refs[i], out_sems.at[i]))
        sends[-1].start()
    return sends


def column_kernel(slots, slices_owned, image_ref, matrix_ref, angle_ref, defocus_ref, starts_ref, *refs):
    count = len(slots)
    out_refs = refs[:count]
    image, matrix, angles, defocus, starts, zhi, zlo, *scratch, sems = refs[count:]
    rows, columns = image.shape
    size = columns // RADIX
    copies = fetched(
        [image_ref, angle_ref, defocus_ref, starts_ref] + [matrix_ref.at[i] for i in range(5)],
        [image, angles, defocus, starts] + [matrix.at[i] for i in range(5)],
        sems,
    )
    squares, ramp, cosine_turns, sine_turns = column_lines(columns)
    turns = [t[j : j + 1, :] for j in range(3) for t in (cosine_turns, sine_turns)]
    copies[0].wait()
    butterflies(image, turns, zhi, zlo)
    for copy in copies[1:]:
        copy.wait()

    def product(first, lines, table, here):
        top = zhi[first : first + lines].reshape(lines * rows, size)
        rest = zlo[first : first + lines].reshape(lines * rows, size)
        total = jnp.dot(top, matrix[table, :, here], preferred_element_type=jnp.float32)
        total += jnp.dot(top, matrix[table + 1, :, here], preferred_element_type=jnp.float32)
        return total + jnp.dot(rest, matrix[table, :, here], preferred_element_type=jnp.float32)

    spectrum = [product(0, 1, 0, slice(0, size)), product(1, 1, 0, slice(size, 2 * size))]
    mixed = product(2, 6, 2, slice(None))
    for j in range(3):
        real, imag = mixed[2 * j * rows : (2 * j + 1) * rows], mixed[(2 * j + 1) * rows : (2 * j + 2) * rows]
        spectrum += [real[:, :size] + imag[:, size:], imag[:, :size] - real[:, size:]]
    facts = (squares, ramp, turns, angles, defocus, starts)
    sends = send_patches(
        slots, slices_owned, spectrum, matrix.at[2], matrix.at[4], columns, facts, scratch, out_refs
    )
    for copy in sends:
        copy.wait()


def column_filtered(slots, slices_owned, image, angles, defocus, starts):
    rows, columns = image.shape
    size = columns // RADIX
    count = len(slots)
    matrices = jnp.asarray(column_tables(columns))
    away = pl.BlockSpec(memory_space=pl.ANY)
    flops = 2 * rows * size * size * (42 + 14 * count)
    sent = pl.pallas_call(
        functools.partial(column_kernel, slots, slices_owned),
        out_shape=[jax.ShapeDtypeStruct(packed_shape(rows), jnp.bfloat16)] * count,
        in_specs=[away] * 5,
        out_specs=[away] * count,
        scratch_shapes=[
            pltpu.VMEM((rows, columns), jnp.bfloat16),
            pltpu.VMEM(matrices.shape, jnp.bfloat16),
            pltpu.SMEM(angles.shape, jnp.float32),
            pltpu.SMEM(defocus.shape, jnp.int32),
            pltpu.SMEM(starts.shape, jnp.int32),
            pltpu.VMEM((8, rows, size), jnp.bfloat16),
            pltpu.VMEM((8, rows, size), jnp.bfloat16),
            pltpu.VMEM((2, count * rows, size), jnp.float32),
            pltpu.VMEM((6, count * rows, 2 * size), jnp.float32),
            pltpu.VMEM((count * rows, columns), jnp.float32),
            pltpu.VMEM((count, *packed_shape(rows)), jnp.bfloat16),
            pltpu.SemaphoreType.DMA((count,)),
            pltpu.SemaphoreType.DMA((9,)),
        ],
        compiler_params=pltpu.CompilerParams(vmem_limit_bytes=60 * 2**20),
        cost_estimate=pl.CostEstimate(flops=flops, bytes_accessed=3 * 2**20, transcendentals=0),
        name="column_filter",
    )(image, matrices, angles, defocus, starts)
    return dict(zip(slots, sent))


def after(array, *others):
    away = pl.BlockSpec(memory_space=pl.ANY)
    return pl.pallas_call(
        lambda *refs: None,
        out_shape=jax.ShapeDtypeStruct(array.shape, array.dtype),
        in_specs=[away] * (1 + len(others)),
        out_specs=away,
        input_output_aliases={0: 0},
        compiler_params=pltpu.CompilerParams(vmem_limit_bytes=2**20),
        cost_estimate=pl.CostEstimate(flops=0, bytes_accessed=0, transcendentals=0),
        name="after",
    )(array, *others)


def prepare_kernel(slots, slices_owned, angles, defocus, waves, rows_ref, weights_ref, mine, order):
    tilt, row = lax.axis_index("tilt"), lax.axis_index("row")
    slab, local_first = tilt * slices_owned // SLAB, tilt * slices_owned % SLAB
    full_rows = waves.shape[1]
    rows = rows_ref.shape[0] // slots
    half = full_rows // 2
    column = lax.broadcasted_iota(jnp.int32, (8, full_rows), 1)
    freq = jnp.where(column <= half, column, column - half)
    count = jnp.where((freq == 0) | (freq == half), 1.0, 2.0) / full_rows
    scales = [(flip_sign(freq * freq, defocus[tilt ^ slot, slab], full_rows) * count)[:1] for slot in range(slots)]
    for part in range(2):
        for block in range(full_rows // rows):
            there = pl.ds(pl.multiple_of((row ^ block) * rows, rows), rows)
            order[part, block * rows : (block + 1) * rows, :] = waves[part, there, :]
        own = order[part, :rows, :].astype(jnp.float32)
        for slot in range(slots):
            mine[part, slot * rows : (slot + 1) * rows, :] = (own * scales[slot]).astype(jnp.bfloat16)

    def product(left, right):
        over = (((1,), (1,)), ((), ()))
        return lax.dot_general(mine[left], order[right], over, preferred_element_type=jnp.float32)

    rows_ref[...] = (product(0, 0) + product(0, 1) + product(1, 0)).astype(jnp.bfloat16)

    place = lax.broadcasted_iota(jnp.int32, (REACH, XBW), 0).astype(jnp.float32)
    across = lax.broadcasted_iota(jnp.int32, (1, XBW), 1).astype(jnp.float32)
    for slot in range(slots):
        cosine, sine, first_tap = reach_of(angles[tilt ^ slot])
        tap = place + first_tap.astype(jnp.float32)

        def one_slice(c, carry):
            offset = (local_first + c).astype(jnp.float32) - 0.5 * (SLAB - 1)
            centre = 0.5 * XBW + across * cosine + offset * sine
            there = pl.ds(pl.multiple_of(c * XBW, XBW), XBW)
            weights = jnp.maximum(0.0, 1.0 - jnp.abs(tap - centre)).astype(jnp.bfloat16)
            weights_ref[slot, :REACH, there] = weights
            for block in range(1, XBLK):
                weights_ref[slot, MAIN + block * REST : MAIN + (block + 1) * REST, there] = weights[MAIN:]
            return carry

        lax.fori_loop(0, slices_owned, one_slice, 0, unroll=2)


def prepared(slots, slices_owned, rows, full_rows, angles, defocus):
    smem, vmem = pl.BlockSpec(memory_space=pltpu.SMEM), pl.BlockSpec(memory_space=pltpu.VMEM)
    return pl.pallas_call(
        functools.partial(prepare_kernel, slots, slices_owned),
        out_shape=[
            jax.ShapeDtypeStruct((slots * rows, full_rows), jnp.bfloat16),
            jax.ShapeDtypeStruct((slots, MAIN + XBLK * REST, slices_owned * XBW), jnp.bfloat16),
        ],
        in_specs=[smem] * 2 + [vmem],
        out_specs=[vmem] * 2,
        scratch_shapes=[
            pltpu.VMEM((2, slots * rows, full_rows), jnp.bfloat16),
            pltpu.VMEM((2, full_rows, full_rows), jnp.bfloat16),
        ],
        compiler_params=pltpu.CompilerParams(vmem_limit_bytes=32 * 2**20),
        cost_estimate=pl.CostEstimate(flops=2**31, bytes_accessed=6 * 2**20, transcendentals=0),
        name="prepare",
    )(angles, defocus, jnp.asarray(row_tables(full_rows)))


def unpacked(packed):
    rows = 4 * packed.shape[0] // 9
    rest = packed[2 * rows :].astype(jnp.float32)
    quarters = []
    for tile in range(2):
        both = rest[:, tile * MAIN : (tile + 1) * MAIN]
        quarters += [both, pltpu.roll(both, MAIN - XBLK * REST, 1)]
    rest = jnp.concatenate(quarters, 0).astype(jnp.bfloat16)
    return jnp.concatenate([packed[:rows], packed[rows : 2 * rows], rest], 1)


def corrected_patches(slots, row_devices, rows_ref, patch_refs):
    parts = []
    for group in slots:
        refs, patch_refs = patch_refs[:row_devices], patch_refs[row_devices:]
        height = refs[0].shape[0] // len(group)
        for i, slot in enumerate(group):
            patches = jnp.concatenate([unpacked(ref[i * height : (i + 1) * height]) for ref in refs], 0)
            rows = patches.shape[0] // row_devices
            image = jnp.dot(rows_ref[slot * rows : (slot + 1) * rows, :], patches, preferred_element_type=jnp.float32)
            lane = lax.broadcasted_iota(jnp.int32, (rows, MAIN), 1) // REST
            main = jnp.concatenate([image[:, block * MAIN : (block + 1) * MAIN] for block in range(XBLK)], 0)
            rest = [jnp.where(lane == block, image[:, XBLK * MAIN :], 0.0) for block in range(XBLK)]
            rest = jnp.concatenate(rest, 0)[:, : XBLK * REST]
            parts.append((slot, jnp.concatenate([main, rest], 1).astype(jnp.bfloat16)))
    return parts


def sum_kernel(slots, row_devices, rows_ref, weights_ref, *refs):
    total_ref = refs[-1]
    (slot, part), *others = corrected_patches(slots, row_devices, rows_ref, refs[:-1])
    step = 4 * XBW
    for first in range(0, total_ref.shape[1], step):
        here = slice(first, first + step)
        total = jnp.dot(part, weights_ref[slot, :, here], preferred_element_type=jnp.float32)
        for other, more in others:
            total += jnp.dot(more, weights_ref[other, :, here], preferred_element_type=jnp.float32)
        total_ref[:, here] = total


def finish_kernel(factor, slots, row_devices, rows_ref, weights_ref, total_ref, *refs):
    patch_refs = refs[: len(slots) * row_devices]
    out_ref, out, sems = refs[len(slots) * row_devices :]
    rows = total_ref.shape[0] // XBLK
    parts = corrected_patches(slots, row_devices, rows_ref, patch_refs)
    step = 4
    copies = []
    for group in range(out.shape[0] // step):
        here = slice(group * step * XBW, (group + 1) * step * XBW)
        total = total_ref[:, here]
        for slot, part in parts:
            total += jnp.dot(part, weights_ref[slot, :, here], preferred_element_type=jnp.float32)
        for c in range(step):
            for block in range(XBLK):
                out[group * step + c, :, block * XBW : (block + 1) * XBW] = (
                    factor * total[block * rows : (block + 1) * rows, c * XBW : (c + 1) * XBW]
                ).astype(jnp.bfloat16)
        part = pl.ds(group * step, step)
        copies.append(pltpu.make_async_copy(out.at[part], out_ref.at[part], sems.at[group]))
        copies[-1].start()
    for copy in copies:
        copy.wait()


def interpolation(kernel, slots, weights, row_filters, patches, totals, **call):
    vmem = pl.BlockSpec(memory_space=pltpu.VMEM)
    operands = [row_filters, weights, *totals, *(block for group in patches for block in group)]
    return pl.pallas_call(
        functools.partial(kernel, slots, len(patches[0])),
        in_specs=[vmem] * len(operands),
        compiler_params=pltpu.CompilerParams(vmem_limit_bytes=32 * 2**20),
        cost_estimate=pl.CostEstimate(flops=0, bytes_accessed=0, transcendentals=0),
        **call,
    )(*operands)


def summed(row_filters, weights, patches, slots):
    return interpolation(
        sum_kernel,
        slots,
        weights,
        row_filters,
        patches,
        [],
        out_shape=jax.ShapeDtypeStruct((XBLK * row_filters.shape[0] // weights.shape[0], weights.shape[2]), jnp.float32),
        out_specs=pl.BlockSpec(memory_space=pltpu.VMEM),
        name="sum_early_tilts",
    )


def finished(row_filters, weights, total, patches, slots, factor):
    shape = (weights.shape[2] // XBW, row_filters.shape[0] // weights.shape[0], XBLK * XBW)
    return interpolation(
        functools.partial(finish_kernel, factor),
        slots,
        weights,
        row_filters,
        patches,
        [total],
        out_shape=jax.ShapeDtypeStruct(shape, jnp.bfloat16),
        out_specs=pl.BlockSpec(memory_space=pl.ANY),
        scratch_shapes=[pltpu.VMEM(shape, jnp.bfloat16), pltpu.SemaphoreType.DMA((shape[0] // 4,))],
        name="finish_volume",
    )


def exchange(array, axis, distance):
    count = lax.axis_size(axis)
    return lax.ppermute(array, axis, [(i, i ^ distance) for i in range(count)])


def gather_rows(array, awaited=()):
    blocks = {0: array}
    bit = lax.axis_size("row") // 2
    while bit:
        if bit == 1 and awaited:
            blocks = {d: after(block, *awaited) if d else block for d, block in blocks.items()}
        blocks.update({d ^ bit: exchange(block, "row", bit) for d, block in blocks.items()})
        bit //= 2
    return [blocks[d] for d in sorted(blocks)]


def per_device(projections, tilt_angle, band_start, defocus):
    _, rows, _ = projections.shape
    row_devices, tilt_devices = lax.axis_size("row"), lax.axis_size("tilt")
    slices_owned = SLICES // tilt_devices
    far, near = list(range(tilt_devices - 1, 1, -1)), list(range(min(2, tilt_devices)))
    sent = column_filtered(far + near, slices_owned, projections[0], tilt_angle, defocus, band_start)
    arrived = {d: exchange(sent[d], "tilt", d) if d else sent[d] for d in far + near}
    row_filters, weights = prepared(tilt_devices, slices_owned, rows, rows * row_devices, tilt_angle, defocus)
    early = [gather_rows(arrived[d], (row_filters,)) for d in near]
    total = summed(row_filters, weights, early, [[d] for d in near])
    late = [gather_rows(arrived[d], (row_filters,) if d == far[0] else ()) for d in far]
    return finished(row_filters, weights, total, late, [[d] for d in far], 1.0 / math.sqrt(tilt_devices))


def solution(mesh):
    in_specs = (
        P(("group", "tilt"), "row", None),
        P("group"),
        P("group", None, None),
        P("group", None),
    )
    out_specs = P(("group", "tilt"), "row", None)
    return jax.shard_map(
        per_device, mesh=mesh, in_specs=in_specs, out_specs=out_specs, check_vma=False
    )
```

```python
import functools
import math

import jax
import jax.numpy as jnp
import numpy as np
from jax import lax
from jax.experimental import pallas as pl
from jax.experimental.pallas import tpu as pltpu
from jax.sharding import PartitionSpec as P

SLAB = 16
XBW = 128
BAND = 256
XBLK = 4
SLICES = 64
RADIX = 8
MAIN = 128
REST = 16
REACH = MAIN + REST
WINDOW = 384
ROOT = math.sqrt(0.5)


def split(table):
    high = table.astype(jnp.bfloat16)
    return high, (table - high.astype(np.float64)).astype(jnp.bfloat16)


def column_tables(columns):
    size = columns // RADIX
    half = size // 2
    u = np.arange(size)[:, None]

    def angles(freq):
        return 2.0 * np.pi * ((u * freq[None, :]) % columns) / columns

    k0, s0 = RADIX * np.arange(half + 1), RADIX * np.arange(1, half)
    k4 = RADIX * np.arange(half) + 4
    m0 = np.concatenate([np.cos(angles(k0)), -np.sin(angles(s0))], 1)
    m4 = np.concatenate([np.cos(angles(k4)), -np.sin(angles(k4))], 1)
    full = angles(RADIX * np.arange(size))
    waves = np.concatenate([np.cos(full), np.sin(full)], 1)
    ends = np.concatenate([m0, m4], 1)

    matrices = np.stack([*split(ends), *split(waves), np.concatenate([m0.T, m4.T], 1).astype(jnp.bfloat16)])
    return matrices


def column_lines(columns):
    size = columns // RADIX
    half = size // 2
    line = lax.broadcasted_iota(jnp.int32, (8, size), 0)
    u = lax.broadcasted_iota(jnp.int32, (8, size), 1)
    freq = jnp.where(line == 0, RADIX * jnp.where(u <= half, u, u - half), RADIX * (u & (half - 1)) + 4)
    freq = jnp.where(line < 2, freq, RADIX * u + line // 2)
    fold = jnp.minimum(freq, columns - freq)
    count = jnp.where((fold == 0) | (fold == columns // 2), 1.0, 2.0)
    gain = count * (fold.astype(jnp.float32) + 0.5) * (2.0 / (columns * columns))
    angle = (u * (line + 1)).astype(jnp.float32) * (2.0 * math.pi / columns)
    return fold * fold, gain, jnp.cos(angle), jnp.sin(angle)


def row_tables(full_rows):
    half = full_rows // 2
    column = np.arange(full_rows)
    freq = np.where(column <= half, column, column - half)
    angle = 2.0 * np.pi * (np.arange(full_rows)[:, None] * freq[None, :] % full_rows) / full_rows
    return np.stack(split(np.where(column[None, :] <= half, np.cos(angle), np.sin(angle))))


def packed_shape(rows):
    return (2 * rows + rows // 4, 2 * MAIN)


def flip_sign(squares, defocus, length):
    cycles = lax.div(squares * defocus, jnp.int32(length * length))
    return (1 - 2 * (cycles & 1)).astype(jnp.float32)


def fetched(sources, targets, sems):
    copies = [pltpu.make_async_copy(s, t, sems.at[i]) for i, (s, t) in enumerate(zip(sources, targets))]
    for copy in copies:
        copy.start()
    return copies


def reach_of(angle):
    line = jnp.full((8, XBW), angle, jnp.float32)
    cosine, sine = jnp.cos(line), jnp.sin(line)
    lowest = 0.5 * XBW + jnp.minimum((XBW - 1) * cosine, 0.0) - 0.5 * (SLAB - 1) * jnp.abs(sine)
    first = jnp.clip(jnp.floor(lowest) - 4.0, 0.0, float(BAND - REACH))
    return cosine[:1], sine[:1], jnp.max(first).astype(jnp.int32)


def butterflies(image, turns, zhi, zlo):
    rows, columns = image.shape
    size = columns // RADIX

    def step(i, carry):
        here = pl.ds(pl.multiple_of(i * 16, 16), 16)
        x = [image[here, m * size : (m + 1) * size].astype(jnp.float32) for m in range(8)]
        p0, p1, p2, p3 = (x[m] + x[m + 4] for m in range(4))
        q0, q1, q2, q3 = (x[m] - x[m + 4] for m in range(4))
        e, f = p0 + p2, p1 + p3
        g, h = ROOT * (q1 - q3), ROOT * (q1 + q3)
        z = [e + f, e - f]
        for j, (real, imag) in enumerate([(q0 + g, -q2 - h), (p0 - p2, p3 - p1), (q0 - g, q2 - h)]):
            c, s = turns[2 * j], turns[2 * j + 1]
            z += [real * c + imag * s, imag * c - real * s]
        for line in range(8):
            top = z[line].astype(jnp.bfloat16)
            zhi[line, here, :] = top
            zlo[line, here, :] = (z[line] - top.astype(jnp.float32)).astype(jnp.bfloat16)
        return carry

    lax.fori_loop(0, rows // 16, step, 0)


def inverse_butterflies(ends, waves, turns, turned):
    rows, columns = turned.shape
    size = columns // RADIX

    def step(i, carry):
        here = pl.ds(pl.multiple_of(i * 8, 8), 8)
        r, s = [], []
        for j in range(3):
            c, d = turns[2 * j], turns[2 * j + 1]
            real = waves[2 * j, here, :size] - waves[2 * j + 1, here, size:]
            imag = waves[2 * j, here, size:] + waves[2 * j + 1, here, :size]
            r.append(real * c - imag * d)
            s.append(real * d + imag * c)
        e, f = ends[0, here, :] + ends[1, here, :], ends[0, here, :] - ends[1, here, :]
        a, b, c, d = r[0] + r[2], r[0] - r[2], s[0] + s[2], s[0] - s[2]
        even0, even2, odd1, odd3 = e + r[1], e - r[1], f - s[1], f + s[1]
        g, h = ROOT * (b - c), ROOT * (b + c)
        out = [even0 + a, odd1 + g, even2 - d, odd3 - h, even0 - a, odd1 - g, even2 + d, odd3 + h]
        for m in range(8):
            turned[here, m * size : (m + 1) * size] = out[m]
        return carry

    lax.fori_loop(0, rows // 8, step, 0)


def send_patches(slots, slices_owned, spectrum, wave_table, end_table, columns, facts, scratch, out_refs):
    squares, ramp, turns, angles, defocus, starts = facts
    ends, waves, turned, out, out_sems = scratch
    rows, size = spectrum[0].shape
    tilt = lax.axis_index("tilt")
    slabs = [(tilt ^ slot) * slices_owned // SLAB for slot in slots]
    gains = [flip_sign(squares, defocus[tilt, slab], columns) * ramp for slab in slabs]
    filtered = [
        jnp.concatenate([(spectrum[i] * gain[i : i + 1, :]).astype(jnp.bfloat16) for gain in gains], 0) for i in range(8)
    ]
    for i in range(2):
        ends[i] = jnp.dot(filtered[i], end_table[:, i * size : (i + 1) * size], preferred_element_type=jnp.float32)
    for i in range(6):
        waves[i] = jnp.dot(filtered[2 + i], wave_table[...], preferred_element_type=jnp.float32)
    inverse_butterflies(ends, waves, turns, turned)
    lane = lax.broadcasted_iota(jnp.int32, (rows, MAIN), 1) // REST
    _, _, first_tap = reach_of(angles[tilt])
    sends = []
    for i, slab in enumerate(slabs):
        rest = jnp.zeros((rows, MAIN), jnp.float32)
        for block in range(XBLK):
            start = starts[tilt, slab, block] + first_tap
            base = pl.multiple_of(jnp.minimum((start // 128) * 128, columns - WINDOW), 128)
            window = turned[i * rows : (i + 1) * rows, pl.ds(base, WINDOW)]
            shift = base - start
            reach = pltpu.roll(window, jnp.where(shift < 0, shift + WINDOW, shift), 1)[:, : 2 * MAIN]
            there = slice(block // 2 * rows, (block // 2 + 1) * rows), slice(block % 2 * MAIN, (block % 2 + 1) * MAIN)
            out[i, *there] = reach[:, :MAIN].astype(jnp.bfloat16)
            last = reach[:, MAIN:]
            rest = jnp.where(lane == block, pltpu.roll(last, block * REST, 1) if block else last, rest)
        quarters = [rest[q * rows // 4 : (q + 1) * rows // 4] for q in range(4)]
        for tile in range(2):
            right = pltpu.roll(quarters[2 * tile + 1], XBLK * REST, 1)
            both = jnp.where(lane[: rows // 4] < XBLK, quarters[2 * tile], right)
            out[i, 2 * rows :, tile * MAIN : (tile + 1) * MAIN] = both.astype(jnp.bfloat16)
        sends.append(pltpu.make_async_copy(out.at[i], out_refs[i], out_sems.at[i]))
        sends[-1].start()
    return sends


def column_kernel(slots, slices_owned, image_ref, matrix_ref, angle_ref, defocus_ref, starts_ref, *refs):
    count = len(slots)
    out_refs = refs[:count]
    image, matrix, angles, defocus, starts, zhi, zlo, *scratch, sems = refs[count:]
    rows, columns = image.shape
    size = columns // RADIX
    copies = fetched(
        [image_ref, angle_ref, defocus_ref, starts_ref] + [matrix_ref.at[i] for i in range(5)],
        [image, angles, defocus, starts] + [matrix.at[i] for i in range(5)],
        sems,
    )
    squares, ramp, cosine_turns, sine_turns = column_lines(columns)
    turns = [t[j : j + 1, :] for j in range(3) for t in (cosine_turns, sine_turns)]
    copies[0].wait()
    butterflies(image, turns, zhi, zlo)
    for copy in copies[1:]:
        copy.wait()

    def product(first, lines, table, here):
        top = zhi[first : first + lines].reshape(lines * rows, size)
        rest = zlo[first : first + lines].reshape(lines * rows, size)
        total = jnp.dot(top, matrix[table, :, here], preferred_element_type=jnp.float32)
        total += jnp.dot(top, matrix[table + 1, :, here], preferred_element_type=jnp.float32)
        return total + jnp.dot(rest, matrix[table, :, here], preferred_element_type=jnp.float32)

    spectrum = [product(0, 1, 0, slice(0, size)), product(1, 1, 0, slice(size, 2 * size))]
    mixed = product(2, 6, 2, slice(None))
    for j in range(3):
        real, imag = mixed[2 * j * rows : (2 * j + 1) * rows], mixed[(2 * j + 1) * rows : (2 * j + 2) * rows]
        spectrum += [real[:, :size] + imag[:, size:], imag[:, :size] - real[:, size:]]
    facts = (squares, ramp, turns, angles, defocus, starts)
    sends = send_patches(
        slots, slices_owned, spectrum, matrix.at[2], matrix.at[4], columns, facts, scratch, out_refs
    )
    for copy in sends:
        copy.wait()


def column_filtered(slots, slices_owned, image, angles, defocus, starts):
    rows, columns = image.shape
    size = columns // RADIX
    count = len(slots)
    matrices = jnp.asarray(column_tables(columns))
    away = pl.BlockSpec(memory_space=pl.ANY)
    flops = 2 * rows * size * size * (42 + 14 * count)
    sent = pl.pallas_call(
        functools.partial(column_kernel, slots, slices_owned),
        out_shape=[jax.ShapeDtypeStruct(packed_shape(rows), jnp.bfloat16)] * count,
        in_specs=[away] * 5,
        out_specs=[away] * count,
        scratch_shapes=[
            pltpu.VMEM((rows, columns), jnp.bfloat16),
            pltpu.VMEM(matrices.shape, jnp.bfloat16),
            pltpu.SMEM(angles.shape, jnp.float32),
            pltpu.SMEM(defocus.shape, jnp.int32),
            pltpu.SMEM(starts.shape, jnp.int32),
            pltpu.VMEM((8, rows, size), jnp.bfloat16),
            pltpu.VMEM((8, rows, size), jnp.bfloat16),
            pltpu.VMEM((2, count * rows, size), jnp.float32),
            pltpu.VMEM((6, count * rows, 2 * size), jnp.float32),
            pltpu.VMEM((count * rows, columns), jnp.float32),
            pltpu.VMEM((count, *packed_shape(rows)), jnp.bfloat16),
            pltpu.SemaphoreType.DMA((count,)),
            pltpu.SemaphoreType.DMA((9,)),
        ],
        compiler_params=pltpu.CompilerParams(vmem_limit_bytes=60 * 2**20),
        cost_estimate=pl.CostEstimate(flops=flops, bytes_accessed=3 * 2**20, transcendentals=0),
        name="column_filter",
    )(image, matrices, angles, defocus, starts)
    return dict(zip(slots, sent))


def after(array, *others):
    away = pl.BlockSpec(memory_space=pl.ANY)
    return pl.pallas_call(
        lambda *refs: None,
        out_shape=jax.ShapeDtypeStruct(array.shape, array.dtype),
        in_specs=[away] * (1 + len(others)),
        out_specs=away,
        input_output_aliases={0: 0},
        compiler_params=pltpu.CompilerParams(vmem_limit_bytes=2**20),
        cost_estimate=pl.CostEstimate(flops=0, bytes_accessed=0, transcendentals=0),
        name="after",
    )(array, *others)


def prepare_kernel(slots, slices_owned, angles, defocus, waves, rows_ref, weights_ref, mine, order):
    tilt, row = lax.axis_index("tilt"), lax.axis_index("row")
    slab, local_first = tilt * slices_owned // SLAB, tilt * slices_owned % SLAB
    full_rows = waves.shape[1]
    rows = rows_ref.shape[0] // slots
    half = full_rows // 2
    column = lax.broadcasted_iota(jnp.int32, (8, full_rows), 1)
    freq = jnp.where(column <= half, column, column - half)
    count = jnp.where((freq == 0) | (freq == half), 1.0, 2.0) / full_rows
    scales = [(flip_sign(freq * freq, defocus[tilt ^ slot, slab], full_rows) * count)[:1] for slot in range(slots)]
    for part in range(2):
        for block in range(full_rows // rows):
            there = pl.ds(pl.multiple_of((row ^ block) * rows, rows), rows)
            order[part, block * rows : (block + 1) * rows, :] = waves[part, there, :]
        own = order[part, :rows, :].astype(jnp.float32)
        for slot in range(slots):
            mine[part, slot * rows : (slot + 1) * rows, :] = (own * scales[slot]).astype(jnp.bfloat16)

    def product(left, right):
        over = (((1,), (1,)), ((), ()))
        return lax.dot_general(mine[left], order[right], over, preferred_element_type=jnp.float32)

    rows_ref[...] = (product(0, 0) + product(0, 1) + product(1, 0)).astype(jnp.bfloat16)

    place = lax.broadcasted_iota(jnp.int32, (REACH, XBW), 0).astype(jnp.float32)
    across = lax.broadcasted_iota(jnp.int32, (1, XBW), 1).astype(jnp.float32)
    for slot in range(slots):
        cosine, sine, first_tap = reach_of(angles[tilt ^ slot])
        tap = place + first_tap.astype(jnp.float32)

        def one_slice(c, carry):
            offset = (local_first + c).astype(jnp.float32) - 0.5 * (SLAB - 1)
            centre = 0.5 * XBW + across * cosine + offset * sine
            there = pl.ds(pl.multiple_of(c * XBW, XBW), XBW)
            weights = jnp.maximum(0.0, 1.0 - jnp.abs(tap - centre)).astype(jnp.bfloat16)
            weights_ref[slot, :REACH, there] = weights
            for block in range(1, XBLK):
                weights_ref[slot, MAIN + block * REST : MAIN + (block + 1) * REST, there] = weights[MAIN:]
            return carry

        lax.fori_loop(0, slices_owned, one_slice, 0, unroll=2)


def prepared(slots, slices_owned, rows, full_rows, angles, defocus):
    smem, vmem = pl.BlockSpec(memory_space=pltpu.SMEM), pl.BlockSpec(memory_space=pltpu.VMEM)
    return pl.pallas_call(
        functools.partial(prepare_kernel, slots, slices_owned),
        out_shape=[
            jax.ShapeDtypeStruct((slots * rows, full_rows), jnp.bfloat16),
            jax.ShapeDtypeStruct((slots, MAIN + XBLK * REST, slices_owned * XBW), jnp.bfloat16),
        ],
        in_specs=[smem] * 2 + [vmem],
        out_specs=[vmem] * 2,
        scratch_shapes=[
            pltpu.VMEM((2, slots * rows, full_rows), jnp.bfloat16),
            pltpu.VMEM((2, full_rows, full_rows), jnp.bfloat16),
        ],
        compiler_params=pltpu.CompilerParams(vmem_limit_bytes=32 * 2**20),
        cost_estimate=pl.CostEstimate(flops=2**31, bytes_accessed=6 * 2**20, transcendentals=0),
        name="prepare",
    )(angles, defocus, jnp.asarray(row_tables(full_rows)))


def unpacked(packed):
    rows = 4 * packed.shape[0] // 9
    rest = packed[2 * rows :].astype(jnp.float32)
    quarters = []
    for tile in range(2):
        both = rest[:, tile * MAIN : (tile + 1) * MAIN]
        quarters += [both, pltpu.roll(both, MAIN - XBLK * REST, 1)]
    rest = jnp.concatenate(quarters, 0).astype(jnp.bfloat16)
    return jnp.concatenate([packed[:rows], packed[rows : 2 * rows], rest], 1)


def corrected_patches(slots, row_devices, rows_ref, patch_refs):
    parts = []
    for group in slots:
        refs, patch_refs = patch_refs[:row_devices], patch_refs[row_devices:]
        height = refs[0].shape[0] // len(group)
        for i, slot in enumerate(group):
            patches = jnp.concatenate([unpacked(ref[i * height : (i + 1) * height]) for ref in refs], 0)
            rows = patches.shape[0] // row_devices
            image = jnp.dot(rows_ref[slot * rows : (slot + 1) * rows, :], patches, preferred_element_type=jnp.float32)
            lane = lax.broadcasted_iota(jnp.int32, (rows, MAIN), 1) // REST
            main = jnp.concatenate([image[:, block * MAIN : (block + 1) * MAIN] for block in range(XBLK)], 0)
            rest = [jnp.where(lane == block, image[:, XBLK * MAIN :], 0.0) for block in range(XBLK)]
            rest = jnp.concatenate(rest, 0)[:, : XBLK * REST]
            parts.append((slot, jnp.concatenate([main, rest], 1).astype(jnp.bfloat16)))
    return parts


def sum_kernel(slots, row_devices, rows_ref, weights_ref, *refs):
    total_ref = refs[-1]
    (slot, part), *others = corrected_patches(slots, row_devices, rows_ref, refs[:-1])
    step = 4 * XBW
    for first in range(0, total_ref.shape[1], step):
        here = slice(first, first + step)
        total = jnp.dot(part, weights_ref[slot, :, here], preferred_element_type=jnp.float32)
        for other, more in others:
            total += jnp.dot(more, weights_ref[other, :, here], preferred_element_type=jnp.float32)
        total_ref[:, here] = total


def finish_kernel(factor, slots, row_devices, rows_ref, weights_ref, total_ref, *refs):
    patch_refs = refs[: len(slots) * row_devices]
    out_ref, out, sems = refs[len(slots) * row_devices :]
    rows = total_ref.shape[0] // XBLK
    parts = corrected_patches(slots, row_devices, rows_ref, patch_refs)
    step = 4
    copies = []
    for group in range(out.shape[0] // step):
        here = slice(group * step * XBW, (group + 1) * step * XBW)
        total = total_ref[:, here]
        for slot, part in parts:
            total += jnp.dot(part, weights_ref[slot, :, here], preferred_element_type=jnp.float32)
        for c in range(step):
            for block in range(XBLK):
                out[group * step + c, :, block * XBW : (block + 1) * XBW] = (
                    factor * total[block * rows : (block + 1) * rows, c * XBW : (c + 1) * XBW]
                ).astype(jnp.bfloat16)
        part = pl.ds(group * step, step)
        copies.append(pltpu.make_async_copy(out.at[part], out_ref.at[part], sems.at[group]))
        copies[-1].start()
    for copy in copies:
        copy.wait()


def interpolation(kernel, slots, weights, row_filters, patches, totals, **call):
    vmem = pl.BlockSpec(memory_space=pltpu.VMEM)
    operands = [row_filters, weights, *totals, *(block for group in patches for block in group)]
    return pl.pallas_call(
        functools.partial(kernel, slots, len(patches[0])),
        in_specs=[vmem] * len(operands),
        compiler_params=pltpu.CompilerParams(vmem_limit_bytes=32 * 2**20),
        cost_estimate=pl.CostEstimate(flops=0, bytes_accessed=0, transcendentals=0),
        **call,
    )(*operands)


def summed(row_filters, weights, patches, slots):
    return interpolation(
        sum_kernel,
        slots,
        weights,
        row_filters,
        patches,
        [],
        out_shape=jax.ShapeDtypeStruct((XBLK * row_filters.shape[0] // weights.shape[0], weights.shape[2]), jnp.float32),
        out_specs=pl.BlockSpec(memory_space=pltpu.VMEM),
        name="sum_early_tilts",
    )


def finished(row_filters, weights, total, patches, slots, factor):
    shape = (weights.shape[2] // XBW, row_filters.shape[0] // weights.shape[0], XBLK * XBW)
    return interpolation(
        functools.partial(finish_kernel, factor),
        slots,
        weights,
        row_filters,
        patches,
        [total],
        out_shape=jax.ShapeDtypeStruct(shape, jnp.bfloat16),
        out_specs=pl.BlockSpec(memory_space=pl.ANY),
        scratch_shapes=[pltpu.VMEM(shape, jnp.bfloat16), pltpu.SemaphoreType.DMA((shape[0] // 4,))],
        name="finish_volume",
    )


def exchange(array, axis, distance):
    count = lax.axis_size(axis)
    return lax.ppermute(array, axis, [(i, i ^ distance) for i in range(count)])


def gather_rows(array, awaited=()):
    blocks = {0: array}
    bit = lax.axis_size("row") // 2
    while bit:
        if bit == 1 and awaited:
            blocks = {d: after(block, *awaited) if d else block for d, block in blocks.items()}
        blocks.update({d ^ bit: exchange(block, "row", bit) for d, block in blocks.items()})
        bit //= 2
    return [blocks[d] for d in sorted(blocks)]


def per_device(projections, tilt_angle, band_start, defocus):
    _, rows, _ = projections.shape
    row_devices, tilt_devices = lax.axis_size("row"), lax.axis_size("tilt")
    slices_owned = SLICES // tilt_devices
    first, later = [0, tilt_devices - 1], list(range(1, tilt_devices - 1))
    sent = column_filtered(first[::-1] + later, slices_owned, projections[0], tilt_angle, defocus, band_start)
    arrived = {d: exchange(sent[d], "tilt", d) if d else sent[d] for d in first[::-1] + later}
    row_filters, weights = prepared(tilt_devices, slices_owned, rows, rows * row_devices, tilt_angle, defocus)
    early = [gather_rows(jnp.concatenate([arrived[d] for d in first]))]
    total = summed(row_filters, weights, early, [first])
    late = [gather_rows(after(arrived[d], row_filters) if d == later[-1] else arrived[d]) for d in later]
    return finished(row_filters, weights, total, late, [[d] for d in later], 1.0 / math.sqrt(tilt_devices))


def solution(mesh):
    in_specs = (
        P(("group", "tilt"), "row", None),
        P("group"),
        P("group", None, None),
        P("group", None),
    )
    out_specs = P(("group", "tilt"), "row", None)
    return jax.shard_map(
        per_device, mesh=mesh, in_specs=in_specs, out_specs=out_specs, check_vma=False
    )
```

```python
import functools
import math

import jax
import jax.numpy as jnp
import numpy as np
from jax import lax
from jax.experimental import pallas as pl
from jax.experimental.pallas import tpu as pltpu
from jax.sharding import PartitionSpec as P

SLAB = 16
XBW = 128
BAND = 256
XBLK = 4
SLICES = 64
RADIX = 8
MAIN = 128
REST = 16
REACH = MAIN + REST
WINDOW = 384
ROOT = math.sqrt(0.5)


def split(table):
    high = table.astype(jnp.bfloat16)
    return high, (table - high.astype(np.float64)).astype(jnp.bfloat16)


def column_tables(columns):
    size = columns // RADIX
    half = size // 2
    u = np.arange(size)[:, None]

    def angles(freq):
        return 2.0 * np.pi * ((u * freq[None, :]) % columns) / columns

    k0, s0 = RADIX * np.arange(half + 1), RADIX * np.arange(1, half)
    k4 = RADIX * np.arange(half) + 4
    m0 = np.concatenate([np.cos(angles(k0)), -np.sin(angles(s0))], 1)
    m4 = np.concatenate([np.cos(angles(k4)), -np.sin(angles(k4))], 1)
    full = angles(RADIX * np.arange(size))
    waves = np.concatenate([np.cos(full), np.sin(full)], 1)
    ends = np.concatenate([m0, m4], 1)

    matrices = np.stack([*split(ends), *split(waves), np.concatenate([m0.T, m4.T], 1).astype(jnp.bfloat16)])
    return matrices


def column_lines(columns):
    size = columns // RADIX
    half = size // 2
    line = lax.broadcasted_iota(jnp.int32, (8, size), 0)
    u = lax.broadcasted_iota(jnp.int32, (8, size), 1)
    freq = jnp.where(line == 0, RADIX * jnp.where(u <= half, u, u - half), RADIX * (u & (half - 1)) + 4)
    freq = jnp.where(line < 2, freq, RADIX * u + line // 2)
    fold = jnp.minimum(freq, columns - freq)
    count = jnp.where((fold == 0) | (fold == columns // 2), 1.0, 2.0)
    gain = count * (fold.astype(jnp.float32) + 0.5) * (2.0 / (columns * columns))
    angle = (u * (line + 1)).astype(jnp.float32) * (2.0 * math.pi / columns)
    return fold * fold, gain, jnp.cos(angle), jnp.sin(angle)


def row_tables(full_rows):
    half = full_rows // 2
    column = np.arange(full_rows)
    freq = np.where(column <= half, column, column - half)
    angle = 2.0 * np.pi * (np.arange(full_rows)[:, None] * freq[None, :] % full_rows) / full_rows
    return np.stack(split(np.where(column[None, :] <= half, np.cos(angle), np.sin(angle))))


def packed_shape(rows):
    return (2 * rows + rows // 4, 2 * MAIN)


def flip_sign(squares, defocus, length):
    cycles = lax.div(squares * defocus, jnp.int32(length * length))
    return (1 - 2 * (cycles & 1)).astype(jnp.float32)


def fetched(sources, targets, sems):
    copies = [pltpu.make_async_copy(s, t, sems.at[i]) for i, (s, t) in enumerate(zip(sources, targets))]
    for copy in copies:
        copy.start()
    return copies


def reach_of(angle):
    line = jnp.full((8, XBW), angle, jnp.float32)
    cosine, sine = jnp.cos(line), jnp.sin(line)
    lowest = 0.5 * XBW + jnp.minimum((XBW - 1) * cosine, 0.0) - 0.5 * (SLAB - 1) * jnp.abs(sine)
    first = jnp.clip(jnp.floor(lowest) - 4.0, 0.0, float(BAND - REACH))
    return cosine[:1], sine[:1], jnp.max(first).astype(jnp.int32)


def butterflies(image, turns, zhi, zlo):
    rows, columns = image.shape
    size = columns // RADIX

    def step(i, carry):
        here = pl.ds(pl.multiple_of(i * 16, 16), 16)
        x = [image[here, m * size : (m + 1) * size].astype(jnp.float32) for m in range(8)]
        p0, p1, p2, p3 = (x[m] + x[m + 4] for m in range(4))
        q0, q1, q2, q3 = (x[m] - x[m + 4] for m in range(4))
        e, f = p0 + p2, p1 + p3
        g, h = ROOT * (q1 - q3), ROOT * (q1 + q3)
        z = [e + f, e - f]
        for j, (real, imag) in enumerate([(q0 + g, -q2 - h), (p0 - p2, p3 - p1), (q0 - g, q2 - h)]):
            c, s = turns[2 * j], turns[2 * j + 1]
            z += [real * c + imag * s, imag * c - real * s]
        for line in range(8):
            top = z[line].astype(jnp.bfloat16)
            zhi[line, here, :] = top
            zlo[line, here, :] = (z[line] - top.astype(jnp.float32)).astype(jnp.bfloat16)
        return carry

    lax.fori_loop(0, rows // 16, step, 0)


def inverse_butterflies(ends, waves, turns, turned):
    rows, columns = turned.shape
    size = columns // RADIX

    def step(i, carry):
        here = pl.ds(pl.multiple_of(i * 8, 8), 8)
        r, s = [], []
        for j in range(3):
            c, d = turns[2 * j], turns[2 * j + 1]
            real = waves[2 * j, here, :size] - waves[2 * j + 1, here, size:]
            imag = waves[2 * j, here, size:] + waves[2 * j + 1, here, :size]
            r.append(real * c - imag * d)
            s.append(real * d + imag * c)
        e, f = ends[0, here, :] + ends[1, here, :], ends[0, here, :] - ends[1, here, :]
        a, b, c, d = r[0] + r[2], r[0] - r[2], s[0] + s[2], s[0] - s[2]
        even0, even2, odd1, odd3 = e + r[1], e - r[1], f - s[1], f + s[1]
        g, h = ROOT * (b - c), ROOT * (b + c)
        out = [even0 + a, odd1 + g, even2 - d, odd3 - h, even0 - a, odd1 - g, even2 + d, odd3 + h]
        for m in range(8):
            turned[here, m * size : (m + 1) * size] = out[m]
        return carry

    lax.fori_loop(0, rows // 8, step, 0)


def send_patches(slots, slices_owned, spectrum, wave_table, end_table, columns, facts, scratch, out_refs):
    squares, ramp, turns, angles, defocus, starts = facts
    ends, waves, turned, out, out_sems = scratch
    rows, size = spectrum[0].shape
    tilt = lax.axis_index("tilt")
    slabs = [(tilt ^ slot) * slices_owned // SLAB for slot in slots]
    gains = [flip_sign(squares, defocus[tilt, slab], columns) * ramp for slab in slabs]
    filtered = [
        jnp.concatenate([(spectrum[i] * gain[i : i + 1, :]).astype(jnp.bfloat16) for gain in gains], 0) for i in range(8)
    ]
    for i in range(2):
        ends[i] = jnp.dot(filtered[i], end_table[:, i * size : (i + 1) * size], preferred_element_type=jnp.float32)
    for i in range(6):
        waves[i] = jnp.dot(filtered[2 + i], wave_table[...], preferred_element_type=jnp.float32)
    inverse_butterflies(ends, waves, turns, turned)
    lane = lax.broadcasted_iota(jnp.int32, (rows, MAIN), 1) // REST
    _, _, first_tap = reach_of(angles[tilt])
    sends = []
    for i, slab in enumerate(slabs):
        rest = jnp.zeros((rows, MAIN), jnp.float32)
        for block in range(XBLK):
            start = starts[tilt, slab, block] + first_tap
            base = pl.multiple_of(jnp.minimum((start // 128) * 128, columns - WINDOW), 128)
            window = turned[i * rows : (i + 1) * rows, pl.ds(base, WINDOW)]
            shift = base - start
            reach = pltpu.roll(window, jnp.where(shift < 0, shift + WINDOW, shift), 1)[:, : 2 * MAIN]
            there = slice(block // 2 * rows, (block // 2 + 1) * rows), slice(block % 2 * MAIN, (block % 2 + 1) * MAIN)
            out[i, *there] = reach[:, :MAIN].astype(jnp.bfloat16)
            last = reach[:, MAIN:]
            rest = jnp.where(lane == block, pltpu.roll(last, block * REST, 1) if block else last, rest)
        quarters = [rest[q * rows // 4 : (q + 1) * rows // 4] for q in range(4)]
        for tile in range(2):
            right = pltpu.roll(quarters[2 * tile + 1], XBLK * REST, 1)
            both = jnp.where(lane[: rows // 4] < XBLK, quarters[2 * tile], right)
            out[i, 2 * rows :, tile * MAIN : (tile + 1) * MAIN] = both.astype(jnp.bfloat16)
        sends.append(pltpu.make_async_copy(out.at[i], out_refs[i], out_sems.at[i]))
        sends[-1].start()
    return sends


def column_kernel(slots, slices_owned, image_ref, matrix_ref, angle_ref, defocus_ref, starts_ref, *refs):
    count = len(slots)
    out_refs = refs[:count]
    image, matrix, angles, defocus, starts, zhi, zlo, *scratch, sems = refs[count:]
    rows, columns = image.shape
    size = columns // RADIX
    copies = fetched(
        [image_ref, angle_ref, defocus_ref, starts_ref] + [matrix_ref.at[i] for i in range(5)],
        [image, angles, defocus, starts] + [matrix.at[i] for i in range(5)],
        sems,
    )
    squares, ramp, cosine_turns, sine_turns = column_lines(columns)
    turns = [t[j : j + 1, :] for j in range(3) for t in (cosine_turns, sine_turns)]
    copies[0].wait()
    butterflies(image, turns, zhi, zlo)
    for copy in copies[1:]:
        copy.wait()

    def product(first, lines, table, here):
        top = zhi[first : first + lines].reshape(lines * rows, size)
        rest = zlo[first : first + lines].reshape(lines * rows, size)
        total = jnp.dot(top, matrix[table, :, here], preferred_element_type=jnp.float32)
        total += jnp.dot(top, matrix[table + 1, :, here], preferred_element_type=jnp.float32)
        return total + jnp.dot(rest, matrix[table, :, here], preferred_element_type=jnp.float32)

    spectrum = [product(0, 1, 0, slice(0, size)), product(1, 1, 0, slice(size, 2 * size))]
    mixed = product(2, 6, 2, slice(None))
    for j in range(3):
        real, imag = mixed[2 * j * rows : (2 * j + 1) * rows], mixed[(2 * j + 1) * rows : (2 * j + 2) * rows]
        spectrum += [real[:, :size] + imag[:, size:], imag[:, :size] - real[:, size:]]
    facts = (squares, ramp, turns, angles, defocus, starts)
    sends = send_patches(
        slots, slices_owned, spectrum, matrix.at[2], matrix.at[4], columns, facts, scratch, out_refs
    )
    for copy in sends:
        copy.wait()


def column_filtered(slots, slices_owned, image, angles, defocus, starts):
    rows, columns = image.shape
    size = columns // RADIX
    count = len(slots)
    matrices = jnp.asarray(column_tables(columns))
    away = pl.BlockSpec(memory_space=pl.ANY)
    flops = 2 * rows * size * size * (42 + 14 * count)
    sent = pl.pallas_call(
        functools.partial(column_kernel, slots, slices_owned),
        out_shape=[jax.ShapeDtypeStruct(packed_shape(rows), jnp.bfloat16)] * count,
        in_specs=[away] * 5,
        out_specs=[away] * count,
        scratch_shapes=[
            pltpu.VMEM((rows, columns), jnp.bfloat16),
            pltpu.VMEM(matrices.shape, jnp.bfloat16),
            pltpu.SMEM(angles.shape, jnp.float32),
            pltpu.SMEM(defocus.shape, jnp.int32),
            pltpu.SMEM(starts.shape, jnp.int32),
            pltpu.VMEM((8, rows, size), jnp.bfloat16),
            pltpu.VMEM((8, rows, size), jnp.bfloat16),
            pltpu.VMEM((2, count * rows, size), jnp.float32),
            pltpu.VMEM((6, count * rows, 2 * size), jnp.float32),
            pltpu.VMEM((count * rows, columns), jnp.float32),
            pltpu.VMEM((count, *packed_shape(rows)), jnp.bfloat16),
            pltpu.SemaphoreType.DMA((count,)),
            pltpu.SemaphoreType.DMA((9,)),
        ],
        compiler_params=pltpu.CompilerParams(vmem_limit_bytes=60 * 2**20),
        cost_estimate=pl.CostEstimate(flops=flops, bytes_accessed=3 * 2**20, transcendentals=0),
        name="column_filter",
    )(image, matrices, angles, defocus, starts)
    return dict(zip(slots, sent))


def after(array, *others):
    away = pl.BlockSpec(memory_space=pl.ANY)
    return pl.pallas_call(
        lambda *refs: None,
        out_shape=jax.ShapeDtypeStruct(array.shape, array.dtype),
        in_specs=[away] * (1 + len(others)),
        out_specs=away,
        input_output_aliases={0: 0},
        compiler_params=pltpu.CompilerParams(vmem_limit_bytes=2**20),
        cost_estimate=pl.CostEstimate(flops=0, bytes_accessed=0, transcendentals=0),
        name="after",
    )(array, *others)


def prepare_kernel(slots, slices_owned, angles, defocus, waves, awaited, rows_ref, weights_ref, mine, order):
    tilt, row = lax.axis_index("tilt"), lax.axis_index("row")
    slab, local_first = tilt * slices_owned // SLAB, tilt * slices_owned % SLAB
    full_rows = waves.shape[1]
    rows = rows_ref.shape[0] // slots
    half = full_rows // 2
    column = lax.broadcasted_iota(jnp.int32, (8, full_rows), 1)
    freq = jnp.where(column <= half, column, column - half)
    count = jnp.where((freq == 0) | (freq == half), 1.0, 2.0) / full_rows
    scales = [(flip_sign(freq * freq, defocus[tilt ^ slot, slab], full_rows) * count)[:1] for slot in range(slots)]
    for part in range(2):
        for block in range(full_rows // rows):
            there = pl.ds(pl.multiple_of((row ^ block) * rows, rows), rows)
            order[part, block * rows : (block + 1) * rows, :] = waves[part, there, :]
        own = order[part, :rows, :].astype(jnp.float32)
        for slot in range(slots):
            mine[part, slot * rows : (slot + 1) * rows, :] = (own * scales[slot]).astype(jnp.bfloat16)

    def product(left, right):
        over = (((1,), (1,)), ((), ()))
        return lax.dot_general(mine[left], order[right], over, preferred_element_type=jnp.float32)

    rows_ref[...] = (product(0, 0) + product(0, 1) + product(1, 0)).astype(jnp.bfloat16)

    place = lax.broadcasted_iota(jnp.int32, (REACH, XBW), 0).astype(jnp.float32)
    across = lax.broadcasted_iota(jnp.int32, (1, XBW), 1).astype(jnp.float32)
    for slot in range(slots):
        cosine, sine, first_tap = reach_of(angles[tilt ^ slot])
        tap = place + first_tap.astype(jnp.float32)

        def one_slice(c, carry):
            offset = (local_first + c).astype(jnp.float32) - 0.5 * (SLAB - 1)
            centre = 0.5 * XBW + across * cosine + offset * sine
            there = pl.ds(pl.multiple_of(c * XBW, XBW), XBW)
            weights = jnp.maximum(0.0, 1.0 - jnp.abs(tap - centre)).astype(jnp.bfloat16)
            weights_ref[slot, :REACH, there] = weights
            for block in range(1, XBLK):
                weights_ref[slot, MAIN + block * REST : MAIN + (block + 1) * REST, there] = weights[MAIN:]
            return carry

        lax.fori_loop(0, slices_owned, one_slice, 0, unroll=2)


def prepared(slots, slices_owned, rows, full_rows, angles, defocus, awaited):
    smem, vmem = pl.BlockSpec(memory_space=pltpu.SMEM), pl.BlockSpec(memory_space=pltpu.VMEM)
    return pl.pallas_call(
        functools.partial(prepare_kernel, slots, slices_owned),
        out_shape=[
            jax.ShapeDtypeStruct((slots * rows, full_rows), jnp.bfloat16),
            jax.ShapeDtypeStruct((slots, MAIN + XBLK * REST, slices_owned * XBW), jnp.bfloat16),
        ],
        in_specs=[smem] * 2 + [vmem, pl.BlockSpec(memory_space=pl.ANY)],
        out_specs=[vmem] * 2,
        scratch_shapes=[
            pltpu.VMEM((2, slots * rows, full_rows), jnp.bfloat16),
            pltpu.VMEM((2, full_rows, full_rows), jnp.bfloat16),
        ],
        compiler_params=pltpu.CompilerParams(vmem_limit_bytes=32 * 2**20),
        cost_estimate=pl.CostEstimate(flops=2**31, bytes_accessed=6 * 2**20, transcendentals=0),
        name="prepare",
    )(angles, defocus, jnp.asarray(row_tables(full_rows)), awaited)


def unpacked(packed):
    rows = 4 * packed.shape[0] // 9
    rest = packed[2 * rows :].astype(jnp.float32)
    quarters = []
    for tile in range(2):
        both = rest[:, tile * MAIN : (tile + 1) * MAIN]
        quarters += [both, pltpu.roll(both, MAIN - XBLK * REST, 1)]
    rest = jnp.concatenate(quarters, 0).astype(jnp.bfloat16)
    return jnp.concatenate([packed[:rows], packed[rows : 2 * rows], rest], 1)


def corrected_patches(slots, row_devices, rows_ref, patch_refs):
    parts = []
    for group in slots:
        refs, patch_refs = patch_refs[:row_devices], patch_refs[row_devices:]
        height = refs[0].shape[0] // len(group)
        for i, slot in enumerate(group):
            patches = jnp.concatenate([unpacked(ref[i * height : (i + 1) * height]) for ref in refs], 0)
            rows = patches.shape[0] // row_devices
            image = jnp.dot(rows_ref[slot * rows : (slot + 1) * rows, :], patches, preferred_element_type=jnp.float32)
            lane = lax.broadcasted_iota(jnp.int32, (rows, MAIN), 1) // REST
            main = jnp.concatenate([image[:, block * MAIN : (block + 1) * MAIN] for block in range(XBLK)], 0)
            rest = [jnp.where(lane == block, image[:, XBLK * MAIN :], 0.0) for block in range(XBLK)]
            rest = jnp.concatenate(rest, 0)[:, : XBLK * REST]
            parts.append((slot, jnp.concatenate([main, rest], 1).astype(jnp.bfloat16)))
    return parts


def sum_kernel(slots, row_devices, *refs):
    *patch_refs, rows_ref, weights_ref, total_ref = refs
    (slot, part), *others = corrected_patches(slots, row_devices, rows_ref, patch_refs)
    step = 4 * XBW
    for first in range(0, total_ref.shape[1], step):
        here = slice(first, first + step)
        total = jnp.dot(part, weights_ref[slot, :, here], preferred_element_type=jnp.float32)
        for other, more in others:
            total += jnp.dot(more, weights_ref[other, :, here], preferred_element_type=jnp.float32)
        total_ref[:, here] = total


def finish_kernel(factor, slots, row_devices, total_ref, *refs):
    *patch_refs, rows_ref, weights_ref, out_ref, out, sems = refs
    rows = total_ref.shape[0] // XBLK
    parts = corrected_patches(slots, row_devices, rows_ref, patch_refs)
    step = 4
    copies = []
    for group in range(out.shape[0] // step):
        here = slice(group * step * XBW, (group + 1) * step * XBW)
        total = total_ref[:, here]
        for slot, part in parts:
            total += jnp.dot(part, weights_ref[slot, :, here], preferred_element_type=jnp.float32)
        for c in range(step):
            for block in range(XBLK):
                out[group * step + c, :, block * XBW : (block + 1) * XBW] = (
                    factor * total[block * rows : (block + 1) * rows, c * XBW : (c + 1) * XBW]
                ).astype(jnp.bfloat16)
        part = pl.ds(group * step, step)
        copies.append(pltpu.make_async_copy(out.at[part], out_ref.at[part], sems.at[group]))
        copies[-1].start()
    for copy in copies:
        copy.wait()


def interpolation(kernel, slots, weights, row_filters, patches, totals, **call):
    vmem = pl.BlockSpec(memory_space=pltpu.VMEM)
    operands = [*totals, *(block for group in patches for block in group), row_filters, weights]
    return pl.pallas_call(
        functools.partial(kernel, slots, len(patches[0])),
        in_specs=[vmem] * len(operands),
        compiler_params=pltpu.CompilerParams(vmem_limit_bytes=32 * 2**20),
        cost_estimate=pl.CostEstimate(flops=0, bytes_accessed=0, transcendentals=0),
        **call,
    )(*operands)


def summed(row_filters, weights, patches, slots):
    return interpolation(
        sum_kernel,
        slots,
        weights,
        row_filters,
        patches,
        [],
        out_shape=jax.ShapeDtypeStruct((XBLK * row_filters.shape[0] // weights.shape[0], weights.shape[2]), jnp.float32),
        out_specs=pl.BlockSpec(memory_space=pltpu.VMEM),
        name="sum_early_tilts",
    )


def finished(row_filters, weights, total, patches, slots, factor):
    shape = (weights.shape[2] // XBW, row_filters.shape[0] // weights.shape[0], XBLK * XBW)
    return interpolation(
        functools.partial(finish_kernel, factor),
        slots,
        weights,
        row_filters,
        patches,
        [total],
        out_shape=jax.ShapeDtypeStruct(shape, jnp.bfloat16),
        out_specs=pl.BlockSpec(memory_space=pl.ANY),
        scratch_shapes=[pltpu.VMEM(shape, jnp.bfloat16), pltpu.SemaphoreType.DMA((shape[0] // 4,))],
        name="finish_volume",
    )


def exchange(array, axis, distance):
    count = lax.axis_size(axis)
    return lax.ppermute(array, axis, [(i, i ^ distance) for i in range(count)])


def gather_rows(array, awaited=()):
    blocks = {0: array}
    bit = lax.axis_size("row") // 2
    while bit:
        if bit == 1 and awaited:
            blocks = {d: after(block, *awaited) if d else block for d, block in blocks.items()}
        blocks.update({d ^ bit: exchange(block, "row", bit) for d, block in blocks.items()})
        bit //= 2
    return [blocks[d] for d in sorted(blocks)]


def per_device(projections, tilt_angle, band_start, defocus):
    _, rows, _ = projections.shape
    row_devices, tilt_devices = lax.axis_size("row"), lax.axis_size("tilt")
    slices_owned = SLICES // tilt_devices
    far, near = list(range(tilt_devices - 1, 1, -1)), list(range(min(2, tilt_devices)))
    sent = column_filtered(far + near, slices_owned, projections[0], tilt_angle, defocus, band_start)
    arrived = {d: exchange(sent[d], "tilt", d) if d else sent[d] for d in far + near}
    row_filters, weights = prepared(tilt_devices, slices_owned, rows, rows * row_devices, tilt_angle, defocus, arrived[far[0]])
    early = [gather_rows(jnp.concatenate([arrived[d] for d in near]))]
    total = summed(row_filters, weights, early, [near])
    late = [gather_rows(after(arrived[d], row_filters) if d == far[-1] else arrived[d]) for d in far]
    return finished(row_filters, weights, total, late, [[d] for d in far], 1.0 / math.sqrt(tilt_devices))


def solution(mesh):
    in_specs = (
        P(("group", "tilt"), "row", None),
        P("group"),
        P("group", None, None),
        P("group", None),
    )
    out_specs = P(("group", "tilt"), "row", None)
    return jax.shard_map(
        per_device, mesh=mesh, in_specs=in_specs, out_specs=out_specs, check_vma=False
    )
```

```python
import functools
import math

import jax
import jax.numpy as jnp
import numpy as np
from jax import lax
from jax.experimental import pallas as pl
from jax.experimental.pallas import tpu as pltpu
from jax.sharding import PartitionSpec as P

SLAB = 16
XBW = 128
BAND = 256
XBLK = 4
SLICES = 64
RADIX = 8
MAIN = 128
REST = 16
REACH = MAIN + REST
WINDOW = 384
ROOT = math.sqrt(0.5)


def split(table):
    high = table.astype(jnp.bfloat16)
    return high, (table - high.astype(np.float64)).astype(jnp.bfloat16)


def column_tables(columns):
    size = columns // RADIX
    half = size // 2
    u = np.arange(size)[:, None]

    def angles(freq):
        return 2.0 * np.pi * ((u * freq[None, :]) % columns) / columns

    k0, s0 = RADIX * np.arange(half + 1), RADIX * np.arange(1, half)
    k4 = RADIX * np.arange(half) + 4
    m0 = np.concatenate([np.cos(angles(k0)), -np.sin(angles(s0))], 1)
    m4 = np.concatenate([np.cos(angles(k4)), -np.sin(angles(k4))], 1)
    full = angles(RADIX * np.arange(size))
    waves = np.concatenate([np.cos(full), np.sin(full)], 1)
    ends = np.concatenate([m0, m4], 1)

    matrices = np.stack([*split(ends), *split(waves), np.concatenate([m0.T, m4.T], 1).astype(jnp.bfloat16)])
    return matrices


def column_lines(columns):
    size = columns // RADIX
    half = size // 2
    line = lax.broadcasted_iota(jnp.int32, (8, size), 0)
    u = lax.broadcasted_iota(jnp.int32, (8, size), 1)
    freq = jnp.where(line == 0, RADIX * jnp.where(u <= half, u, u - half), RADIX * (u & (half - 1)) + 4)
    freq = jnp.where(line < 2, freq, RADIX * u + line // 2)
    fold = jnp.minimum(freq, columns - freq)
    count = jnp.where((fold == 0) | (fold == columns // 2), 1.0, 2.0)
    gain = count * (fold.astype(jnp.float32) + 0.5) * (2.0 / (columns * columns))
    angle = (u * (line + 1)).astype(jnp.float32) * (2.0 * math.pi / columns)
    return fold * fold, gain, jnp.cos(angle), jnp.sin(angle)


def row_tables(full_rows):
    half = full_rows // 2
    column = np.arange(full_rows)
    freq = np.where(column <= half, column, column - half)
    angle = 2.0 * np.pi * (np.arange(full_rows)[:, None] * freq[None, :] % full_rows) / full_rows
    return np.stack(split(np.where(column[None, :] <= half, np.cos(angle), np.sin(angle))))


def packed_shape(rows):
    return (2 * rows + rows // 4, 2 * MAIN)


def flip_sign(squares, defocus, length):
    cycles = lax.div(squares * defocus, jnp.int32(length * length))
    return (1 - 2 * (cycles & 1)).astype(jnp.float32)


def fetched(sources, targets, sems):
    copies = [pltpu.make_async_copy(s, t, sems.at[i]) for i, (s, t) in enumerate(zip(sources, targets))]
    for copy in copies:
        copy.start()
    return copies


def reach_of(angle):
    line = jnp.full((8, XBW), angle, jnp.float32)
    cosine, sine = jnp.cos(line), jnp.sin(line)
    lowest = 0.5 * XBW + jnp.minimum((XBW - 1) * cosine, 0.0) - 0.5 * (SLAB - 1) * jnp.abs(sine)
    first = jnp.clip(jnp.floor(lowest) - 4.0, 0.0, float(BAND - REACH))
    return cosine[:1], sine[:1], jnp.max(first).astype(jnp.int32)


def butterflies(image, turns, zhi, zlo):
    rows, columns = image.shape
    size = columns // RADIX

    def step(i, carry):
        here = pl.ds(pl.multiple_of(i * 16, 16), 16)
        x = [image[here, m * size : (m + 1) * size].astype(jnp.float32) for m in range(8)]
        p0, p1, p2, p3 = (x[m] + x[m + 4] for m in range(4))
        q0, q1, q2, q3 = (x[m] - x[m + 4] for m in range(4))
        e, f = p0 + p2, p1 + p3
        g, h = ROOT * (q1 - q3), ROOT * (q1 + q3)
        z = [e + f, e - f]
        for j, (real, imag) in enumerate([(q0 + g, -q2 - h), (p0 - p2, p3 - p1), (q0 - g, q2 - h)]):
            c, s = turns[2 * j], turns[2 * j + 1]
            z += [real * c + imag * s, imag * c - real * s]
        for line in range(8):
            top = z[line].astype(jnp.bfloat16)
            zhi[line, here, :] = top
            zlo[line, here, :] = (z[line] - top.astype(jnp.float32)).astype(jnp.bfloat16)
        return carry

    lax.fori_loop(0, rows // 16, step, 0)


def inverse_butterflies(ends, waves, turns, turned, first, rows):
    columns = turned.shape[1]
    size = columns // RADIX
    for top in range(first, first + rows, 8):
        here = slice(top, top + 8)
        r, s = [], []
        for j in range(3):
            c, d = turns[2 * j], turns[2 * j + 1]
            real = waves[2 * j, here, :size] - waves[2 * j + 1, here, size:]
            imag = waves[2 * j, here, size:] + waves[2 * j + 1, here, :size]
            r.append(real * c - imag * d)
            s.append(real * d + imag * c)
        e, f = ends[0, here, :] + ends[1, here, :], ends[0, here, :] - ends[1, here, :]
        a, b, c, d = r[0] + r[2], r[0] - r[2], s[0] + s[2], s[0] - s[2]
        even0, even2, odd1, odd3 = e + r[1], e - r[1], f - s[1], f + s[1]
        g, h = ROOT * (b - c), ROOT * (b + c)
        out = [even0 + a, odd1 + g, even2 - d, odd3 - h, even0 - a, odd1 - g, even2 + d, odd3 + h]
        for m in range(8):
            turned[here, m * size : (m + 1) * size] = out[m]


def send_patches(slots, slices_owned, spectrum, wave_table, end_table, columns, facts, scratch, out_refs):
    squares, ramp, turns, angles, defocus, starts = facts
    ends, waves, turned, out, out_sems = scratch
    rows, size = spectrum[0].shape
    tilt = lax.axis_index("tilt")
    lane = lax.broadcasted_iota(jnp.int32, (rows, MAIN), 1) // REST
    _, _, first_tap = reach_of(angles[tilt])
    slabs = [(tilt ^ slot) * slices_owned // SLAB for slot in slots]

    def transform(k):
        slab = slabs[k]
        mine = slice(k * rows, (k + 1) * rows)
        gain = flip_sign(squares, defocus[tilt, slab], columns) * ramp
        filtered = [(spectrum[i] * gain[i : i + 1, :]).astype(jnp.bfloat16) for i in range(8)]
        for i in range(2):
            table = end_table[:, i * size : (i + 1) * size]
            ends[i, mine, :] = jnp.dot(filtered[i], table, preferred_element_type=jnp.float32)
        both = jnp.dot(jnp.concatenate(filtered[2:], 0), wave_table[...], preferred_element_type=jnp.float32)
        for i in range(6):
            waves[i, mine, :] = both[i * rows : (i + 1) * rows]
    sends = []
    transform(0)
    for k, slab in enumerate(slabs):
        if k + 1 < len(slabs):
            transform(k + 1)
        inverse_butterflies(ends, waves, turns, turned, k * rows, rows)
        rest = jnp.zeros((rows, MAIN), jnp.float32)
        for block in range(XBLK):
            start = starts[tilt, slab, block] + first_tap
            base = pl.multiple_of(jnp.minimum((start // 128) * 128, columns - WINDOW), 128)
            window = turned[k * rows : (k + 1) * rows, pl.ds(base, WINDOW)]
            shift = base - start
            reach = pltpu.roll(window, jnp.where(shift < 0, shift + WINDOW, shift), 1)[:, : 2 * MAIN]
            there = slice(block // 2 * rows, (block // 2 + 1) * rows), slice(block % 2 * MAIN, (block % 2 + 1) * MAIN)
            out[k, *there] = reach[:, :MAIN].astype(jnp.bfloat16)
            last = reach[:, MAIN:]
            rest = jnp.where(lane == block, pltpu.roll(last, block * REST, 1) if block else last, rest)
        quarters = [rest[q * rows // 4 : (q + 1) * rows // 4] for q in range(4)]
        for tile in range(2):
            right = pltpu.roll(quarters[2 * tile + 1], XBLK * REST, 1)
            both = jnp.where(lane[: rows // 4] < XBLK, quarters[2 * tile], right)
            out[k, 2 * rows :, tile * MAIN : (tile + 1) * MAIN] = both.astype(jnp.bfloat16)
        sends.append(pltpu.make_async_copy(out.at[k], out_refs[k], out_sems.at[k]))
        sends[-1].start()
    return sends


def column_kernel(slots, slices_owned, image_ref, matrix_ref, angle_ref, defocus_ref, starts_ref, *refs):
    count = len(slots)
    out_refs = refs[:count]
    image, matrix, angles, defocus, starts, zhi, zlo, *scratch, sems = refs[count:]
    rows, columns = image.shape
    size = columns // RADIX
    copies = fetched(
        [image_ref, angle_ref, defocus_ref, starts_ref] + [matrix_ref.at[i] for i in range(5)],
        [image, angles, defocus, starts] + [matrix.at[i] for i in range(5)],
        sems,
    )
    squares, ramp, cosine_turns, sine_turns = column_lines(columns)
    turns = [t[j : j + 1, :] for j in range(3) for t in (cosine_turns, sine_turns)]
    copies[0].wait()
    butterflies(image, turns, zhi, zlo)
    for copy in copies[4:8]:
        copy.wait()

    def product(first, lines, table, here):
        top = zhi[first : first + lines].reshape(lines * rows, size)
        rest = zlo[first : first + lines].reshape(lines * rows, size)
        total = jnp.dot(top, matrix[table, :, here], preferred_element_type=jnp.float32)
        total += jnp.dot(top, matrix[table + 1, :, here], preferred_element_type=jnp.float32)
        return total + jnp.dot(rest, matrix[table, :, here], preferred_element_type=jnp.float32)

    spectrum = [product(0, 1, 0, slice(0, size)), product(1, 1, 0, slice(size, 2 * size))]
    mixed = product(2, 6, 2, slice(None))
    for j in range(3):
        real, imag = mixed[2 * j * rows : (2 * j + 1) * rows], mixed[(2 * j + 1) * rows : (2 * j + 2) * rows]
        spectrum += [real[:, :size] + imag[:, size:], imag[:, :size] - real[:, size:]]
    for copy in copies[1:4] + copies[8:]:
        copy.wait()
    facts = (squares, ramp, turns, angles, defocus, starts)
    sends = send_patches(
        slots, slices_owned, spectrum, matrix.at[2], matrix.at[4], columns, facts, scratch, out_refs
    )
    for copy in sends:
        copy.wait()


def column_filtered(slots, slices_owned, image, angles, defocus, starts):
    rows, columns = image.shape
    size = columns // RADIX
    count = len(slots)
    matrices = jnp.asarray(column_tables(columns))
    away = pl.BlockSpec(memory_space=pl.ANY)
    flops = 2 * rows * size * size * (42 + 14 * count)
    sent = pl.pallas_call(
        functools.partial(column_kernel, slots, slices_owned),
        out_shape=[jax.ShapeDtypeStruct(packed_shape(rows), jnp.bfloat16)] * count,
        in_specs=[away] * 5,
        out_specs=[away] * count,
        scratch_shapes=[
            pltpu.VMEM((rows, columns), jnp.bfloat16),
            pltpu.VMEM(matrices.shape, jnp.bfloat16),
            pltpu.SMEM(angles.shape, jnp.float32),
            pltpu.SMEM(defocus.shape, jnp.int32),
            pltpu.SMEM(starts.shape, jnp.int32),
            pltpu.VMEM((8, rows, size), jnp.bfloat16),
            pltpu.VMEM((8, rows, size), jnp.bfloat16),
            pltpu.VMEM((2, count * rows, size), jnp.float32),
            pltpu.VMEM((6, count * rows, 2 * size), jnp.float32),
            pltpu.VMEM((count * rows, columns), jnp.float32),
            pltpu.VMEM((count, *packed_shape(rows)), jnp.bfloat16),
            pltpu.SemaphoreType.DMA((count,)),
            pltpu.SemaphoreType.DMA((9,)),
        ],
        compiler_params=pltpu.CompilerParams(vmem_limit_bytes=60 * 2**20),
        cost_estimate=pl.CostEstimate(flops=flops, bytes_accessed=3 * 2**20, transcendentals=0),
        name="column_filter",
    )(image, matrices, angles, defocus, starts)
    return dict(zip(slots, sent))


def after(array, *others):
    away = pl.BlockSpec(memory_space=pl.ANY)
    return pl.pallas_call(
        lambda *refs: None,
        out_shape=jax.ShapeDtypeStruct(array.shape, array.dtype),
        in_specs=[away] * (1 + len(others)),
        out_specs=away,
        input_output_aliases={0: 0},
        compiler_params=pltpu.CompilerParams(vmem_limit_bytes=2**20),
        cost_estimate=pl.CostEstimate(flops=0, bytes_accessed=0, transcendentals=0),
        name="after",
    )(array, *others)


def prepare_kernel(slots, slices_owned, angles, defocus, waves, rows_ref, weights_ref, mine, order):
    tilt, row = lax.axis_index("tilt"), lax.axis_index("row")
    slab, local_first = tilt * slices_owned // SLAB, tilt * slices_owned % SLAB
    full_rows = waves.shape[1]
    rows = rows_ref.shape[0] // slots
    half = full_rows // 2
    column = lax.broadcasted_iota(jnp.int32, (8, full_rows), 1)
    freq = jnp.where(column <= half, column, column - half)
    count = jnp.where((freq == 0) | (freq == half), 1.0, 2.0) / full_rows
    scales = [(flip_sign(freq * freq, defocus[tilt ^ slot, slab], full_rows) * count)[:1] for slot in range(slots)]
    for part in range(2):
        for block in range(full_rows // rows):
            there = pl.ds(pl.multiple_of((row ^ block) * rows, rows), rows)
            order[part, block * rows : (block + 1) * rows, :] = waves[part, there, :]
        own = order[part, :rows, :].astype(jnp.float32)
        for slot in range(slots):
            mine[part, slot * rows : (slot + 1) * rows, :] = (own * scales[slot]).astype(jnp.bfloat16)

    def product(left, right):
        over = (((1,), (1,)), ((), ()))
        return lax.dot_general(mine[left], order[right], over, preferred_element_type=jnp.float32)

    rows_ref[...] = (product(0, 0) + product(0, 1) + product(1, 0)).astype(jnp.bfloat16)

    place = lax.broadcasted_iota(jnp.int32, (REACH, XBW), 0).astype(jnp.float32)
    across = lax.broadcasted_iota(jnp.int32, (1, XBW), 1).astype(jnp.float32)
    for slot in range(slots):
        cosine, sine, first_tap = reach_of(angles[tilt ^ slot])
        tap = place + first_tap.astype(jnp.float32)

        def one_slice(c, carry):
            offset = (local_first + c).astype(jnp.float32) - 0.5 * (SLAB - 1)
            centre = 0.5 * XBW + across * cosine + offset * sine
            there = pl.ds(pl.multiple_of(c * XBW, XBW), XBW)
            weights = jnp.maximum(0.0, 1.0 - jnp.abs(tap - centre)).astype(jnp.bfloat16)
            weights_ref[slot, :REACH, there] = weights
            for block in range(1, XBLK):
                weights_ref[slot, MAIN + block * REST : MAIN + (block + 1) * REST, there] = weights[MAIN:]
            return carry

        lax.fori_loop(0, slices_owned, one_slice, 0, unroll=2)


def prepared(slots, slices_owned, rows, full_rows, angles, defocus):
    smem, vmem = pl.BlockSpec(memory_space=pltpu.SMEM), pl.BlockSpec(memory_space=pltpu.VMEM)
    return pl.pallas_call(
        functools.partial(prepare_kernel, slots, slices_owned),
        out_shape=[
            jax.ShapeDtypeStruct((slots * rows, full_rows), jnp.bfloat16),
            jax.ShapeDtypeStruct((slots, MAIN + XBLK * REST, slices_owned * XBW), jnp.bfloat16),
        ],
        in_specs=[smem] * 2 + [vmem],
        out_specs=[vmem] * 2,
        scratch_shapes=[
            pltpu.VMEM((2, slots * rows, full_rows), jnp.bfloat16),
            pltpu.VMEM((2, full_rows, full_rows), jnp.bfloat16),
        ],
        compiler_params=pltpu.CompilerParams(vmem_limit_bytes=32 * 2**20),
        cost_estimate=pl.CostEstimate(flops=2**31, bytes_accessed=6 * 2**20, transcendentals=0),
        name="prepare",
    )(angles, defocus, jnp.asarray(row_tables(full_rows)))


def unpacked(packed):
    rows = 4 * packed.shape[0] // 9
    rest = packed[2 * rows :].astype(jnp.float32)
    quarters = []
    for tile in range(2):
        both = rest[:, tile * MAIN : (tile + 1) * MAIN]
        quarters += [both, pltpu.roll(both, MAIN - XBLK * REST, 1)]
    rest = jnp.concatenate(quarters, 0).astype(jnp.bfloat16)
    return jnp.concatenate([packed[:rows], packed[rows : 2 * rows], rest], 1)


def corrected_patches(slots, row_devices, rows_ref, patch_refs):
    parts = []
    for group in slots:
        refs, patch_refs = patch_refs[:row_devices], patch_refs[row_devices:]
        height = refs[0].shape[0] // len(group)
        for i, slot in enumerate(group):
            patches = jnp.concatenate([unpacked(ref[i * height : (i + 1) * height]) for ref in refs], 0)
            rows = patches.shape[0] // row_devices
            image = jnp.dot(rows_ref[slot * rows : (slot + 1) * rows, :], patches, preferred_element_type=jnp.float32)
            lane = lax.broadcasted_iota(jnp.int32, (rows, MAIN), 1) // REST
            main = jnp.concatenate([image[:, block * MAIN : (block + 1) * MAIN] for block in range(XBLK)], 0)
            rest = [jnp.where(lane == block, image[:, XBLK * MAIN :], 0.0) for block in range(XBLK)]
            rest = jnp.concatenate(rest, 0)[:, : XBLK * REST]
            parts.append((slot, jnp.concatenate([main, rest], 1).astype(jnp.bfloat16)))
    return parts


def sum_kernel(slots, row_devices, rows_ref, weights_ref, *refs):
    total_ref = refs[-1]
    (slot, part), *others = corrected_patches(slots, row_devices, rows_ref, refs[:-1])
    step = 4 * XBW
    for first in range(0, total_ref.shape[1], step):
        here = slice(first, first + step)
        total = jnp.dot(part, weights_ref[slot, :, here], preferred_element_type=jnp.float32)
        for other, more in others:
            total += jnp.dot(more, weights_ref[other, :, here], preferred_element_type=jnp.float32)
        total_ref[:, here] = total


def finish_kernel(factor, slots, row_devices, rows_ref, weights_ref, total_ref, *refs):
    patch_refs = refs[: len(slots) * row_devices]
    out_ref, out, sems = refs[len(slots) * row_devices :]
    rows = total_ref.shape[0] // XBLK
    parts = corrected_patches(slots, row_devices, rows_ref, patch_refs)
    step = 4
    copies = []
    for group in range(out.shape[0] // step):
        here = slice(group * step * XBW, (group + 1) * step * XBW)
        total = total_ref[:, here]
        for slot, part in parts:
            total += jnp.dot(part, weights_ref[slot, :, here], preferred_element_type=jnp.float32)
        for c in range(step):
            for block in range(XBLK):
                out[group * step + c, :, block * XBW : (block + 1) * XBW] = (
                    factor * total[block * rows : (block + 1) * rows, c * XBW : (c + 1) * XBW]
                ).astype(jnp.bfloat16)
        part = pl.ds(group * step, step)
        copies.append(pltpu.make_async_copy(out.at[part], out_ref.at[part], sems.at[group]))
        copies[-1].start()
    for copy in copies:
        copy.wait()


def interpolation(kernel, slots, weights, row_filters, patches, totals, **call):
    vmem = pl.BlockSpec(memory_space=pltpu.VMEM)
    operands = [row_filters, weights, *totals, *(block for group in patches for block in group)]
    return pl.pallas_call(
        functools.partial(kernel, slots, len(patches[0])),
        in_specs=[vmem] * len(operands),
        compiler_params=pltpu.CompilerParams(vmem_limit_bytes=32 * 2**20),
        cost_estimate=pl.CostEstimate(flops=0, bytes_accessed=0, transcendentals=0),
        **call,
    )(*operands)


def summed(row_filters, weights, patches, slots):
    return interpolation(
        sum_kernel,
        slots,
        weights,
        row_filters,
        patches,
        [],
        out_shape=jax.ShapeDtypeStruct((XBLK * row_filters.shape[0] // weights.shape[0], weights.shape[2]), jnp.float32),
        out_specs=pl.BlockSpec(memory_space=pltpu.VMEM),
        name="sum_early_tilts",
    )


def finished(row_filters, weights, total, patches, slots, factor):
    shape = (weights.shape[2] // XBW, row_filters.shape[0] // weights.shape[0], XBLK * XBW)
    return interpolation(
        functools.partial(finish_kernel, factor),
        slots,
        weights,
        row_filters,
        patches,
        [total],
        out_shape=jax.ShapeDtypeStruct(shape, jnp.bfloat16),
        out_specs=pl.BlockSpec(memory_space=pl.ANY),
        scratch_shapes=[pltpu.VMEM(shape, jnp.bfloat16), pltpu.SemaphoreType.DMA((shape[0] // 4,))],
        name="finish_volume",
    )


def exchange(array, axis, distance):
    count = lax.axis_size(axis)
    return lax.ppermute(array, axis, [(i, i ^ distance) for i in range(count)])


def gather_rows(array, awaited=()):
    blocks = {0: array}
    bit = lax.axis_size("row") // 2
    while bit:
        if bit == 1 and awaited:
            blocks = {d: after(block, *awaited) if d else block for d, block in blocks.items()}
        blocks.update({d ^ bit: exchange(block, "row", bit) for d, block in blocks.items()})
        bit //= 2
    return [blocks[d] for d in sorted(blocks)]


def per_device(projections, tilt_angle, band_start, defocus):
    _, rows, _ = projections.shape
    row_devices, tilt_devices = lax.axis_size("row"), lax.axis_size("tilt")
    slices_owned = SLICES // tilt_devices
    far, near = list(range(tilt_devices - 1, 1, -1)), list(range(min(2, tilt_devices)))
    sent = column_filtered(far + near, slices_owned, projections[0], tilt_angle, defocus, band_start)
    arrived = {d: exchange(sent[d], "tilt", d) if d else sent[d] for d in far + near}
    row_filters, weights = prepared(tilt_devices, slices_owned, rows, rows * row_devices, tilt_angle, defocus)
    early = [gather_rows(jnp.concatenate([arrived[d] for d in near]))]
    total = summed(row_filters, weights, early, [near])
    late = [gather_rows(after(arrived[d], row_filters) if d == far[-1] else arrived[d]) for d in far]
    return finished(row_filters, weights, total, late, [[d] for d in far], 1.0 / math.sqrt(tilt_devices))


def solution(mesh):
    in_specs = (
        P(("group", "tilt"), "row", None),
        P("group"),
        P("group", None, None),
        P("group", None),
    )
    out_specs = P(("group", "tilt"), "row", None)
    return jax.shard_map(
        per_device, mesh=mesh, in_specs=in_specs, out_specs=out_specs, check_vma=False
    )
```

```python
import functools
import math

import jax
import jax.numpy as jnp
import numpy as np
from jax import lax
from jax.experimental import pallas as pl
from jax.experimental.pallas import tpu as pltpu
from jax.sharding import PartitionSpec as P

SLAB = 16
XBW = 128
BAND = 256
XBLK = 4
SLICES = 64
RADIX = 8
MAIN = 128
REST = 8
REACH = MAIN + REST
WINDOW = 384
ROOT = math.sqrt(0.5)


def split(table):
    high = table.astype(jnp.bfloat16)
    return high, (table - high.astype(np.float64)).astype(jnp.bfloat16)


def column_tables(columns):
    size = columns // RADIX
    half = size // 2
    u = np.arange(size)[:, None]

    def angles(freq):
        return 2.0 * np.pi * ((u * freq[None, :]) % columns) / columns

    k0, s0 = RADIX * np.arange(half + 1), RADIX * np.arange(1, half)
    k4 = RADIX * np.arange(half) + 4
    m0 = np.concatenate([np.cos(angles(k0)), -np.sin(angles(s0))], 1)
    m4 = np.concatenate([np.cos(angles(k4)), -np.sin(angles(k4))], 1)
    full = angles(RADIX * np.arange(size))
    waves = np.concatenate([np.cos(full), np.sin(full)], 1)
    ends = np.concatenate([m0, m4], 1)

    matrices = np.stack([*split(ends), *split(waves), np.concatenate([m0.T, m4.T], 1).astype(jnp.bfloat16)])
    return matrices


def column_lines(columns):
    size = columns // RADIX
    half = size // 2
    line = lax.broadcasted_iota(jnp.int32, (8, size), 0)
    u = lax.broadcasted_iota(jnp.int32, (8, size), 1)
    freq = jnp.where(line == 0, RADIX * jnp.where(u <= half, u, u - half), RADIX * (u & (half - 1)) + 4)
    freq = jnp.where(line < 2, freq, RADIX * u + line // 2)
    fold = jnp.minimum(freq, columns - freq)
    count = jnp.where((fold == 0) | (fold == columns // 2), 1.0, 2.0)
    gain = count * (fold.astype(jnp.float32) + 0.5) * (2.0 / (columns * columns))
    angle = (u * (line + 1)).astype(jnp.float32) * (2.0 * math.pi / columns)
    return fold * fold, gain, jnp.cos(angle), jnp.sin(angle)


def row_tables(full_rows):
    half = full_rows // 2
    column = np.arange(full_rows)
    freq = np.where(column <= half, column, column - half)
    angle = 2.0 * np.pi * (np.arange(full_rows)[:, None] * freq[None, :] % full_rows) / full_rows
    return np.stack(split(np.where(column[None, :] <= half, np.cos(angle), np.sin(angle))))


def packed_shape(rows):
    return (XBLK * rows + rows // 4, MAIN)


def flip_sign(squares, defocus, length):
    cycles = lax.div(squares * defocus, jnp.int32(length * length))
    return (1 - 2 * (cycles & 1)).astype(jnp.float32)


def fetched(sources, targets, sems):
    copies = [pltpu.make_async_copy(s, t, sems.at[i]) for i, (s, t) in enumerate(zip(sources, targets))]
    for copy in copies:
        copy.start()
    return copies


def reach_of(angle):
    line = jnp.full((8, XBW), angle, jnp.float32)
    cosine, sine = jnp.cos(line), jnp.sin(line)
    lowest = 0.5 * XBW + jnp.minimum((XBW - 1) * cosine, 0.0) - 0.5 * (SLAB - 1) * jnp.abs(sine)
    first = jnp.clip(jnp.floor(lowest) - 2.0, 0.0, float(BAND - REACH))
    return cosine[:1], sine[:1], jnp.max(first).astype(jnp.int32)


def butterflies(image, turns, zhi, zlo):
    rows, columns = image.shape
    size = columns // RADIX

    def step(i, carry):
        here = pl.ds(pl.multiple_of(i * 16, 16), 16)
        x = [image[here, m * size : (m + 1) * size].astype(jnp.float32) for m in range(8)]
        p0, p1, p2, p3 = (x[m] + x[m + 4] for m in range(4))
        q0, q1, q2, q3 = (x[m] - x[m + 4] for m in range(4))
        e, f = p0 + p2, p1 + p3
        g, h = ROOT * (q1 - q3), ROOT * (q1 + q3)
        z = [e + f, e - f]
        for j, (real, imag) in enumerate([(q0 + g, -q2 - h), (p0 - p2, p3 - p1), (q0 - g, q2 - h)]):
            c, s = turns[2 * j], turns[2 * j + 1]
            z += [real * c + imag * s, imag * c - real * s]
        for line in range(8):
            top = z[line].astype(jnp.bfloat16)
            zhi[line, here, :] = top
            zlo[line, here, :] = (z[line] - top.astype(jnp.float32)).astype(jnp.bfloat16)
        return carry

    lax.fori_loop(0, rows // 16, step, 0)


def inverse_butterflies(ends, waves, turns, turned, first, rows):
    columns = turned.shape[1]
    size = columns // RADIX
    for top in range(first, first + rows, 8):
        here = slice(top, top + 8)
        r, s = [], []
        for j in range(3):
            c, d = turns[2 * j], turns[2 * j + 1]
            real = waves[2 * j, here, :size] - waves[2 * j + 1, here, size:]
            imag = waves[2 * j, here, size:] + waves[2 * j + 1, here, :size]
            r.append(real * c - imag * d)
            s.append(real * d + imag * c)
        e, f = ends[0, here, :] + ends[1, here, :], ends[0, here, :] - ends[1, here, :]
        a, b, c, d = r[0] + r[2], r[0] - r[2], s[0] + s[2], s[0] - s[2]
        even0, even2, odd1, odd3 = e + r[1], e - r[1], f - s[1], f + s[1]
        g, h = ROOT * (b - c), ROOT * (b + c)
        out = [even0 + a, odd1 + g, even2 - d, odd3 - h, even0 - a, odd1 - g, even2 + d, odd3 + h]
        for m in range(8):
            turned[here, m * size : (m + 1) * size] = out[m]


def send_patches(slots, slices_owned, spectrum, wave_table, end_table, columns, facts, scratch, out_refs):
    squares, ramp, turns, angles, defocus, starts = facts
    ends, waves, turned, out, out_sems = scratch
    rows, size = spectrum[0].shape
    tilt = lax.axis_index("tilt")
    lane = lax.broadcasted_iota(jnp.int32, (rows, MAIN), 1) // REST
    _, _, first_tap = reach_of(angles[tilt])
    slabs = [(tilt ^ slot) * slices_owned // SLAB for slot in slots]

    def transform(k):
        slab = slabs[k]
        mine = slice(k * rows, (k + 1) * rows)
        gain = flip_sign(squares, defocus[tilt, slab], columns) * ramp
        filtered = [(spectrum[i] * gain[i : i + 1, :]).astype(jnp.bfloat16) for i in range(8)]
        for i in range(2):
            table = end_table[:, i * size : (i + 1) * size]
            ends[i, mine, :] = jnp.dot(filtered[i], table, preferred_element_type=jnp.float32)
        both = jnp.dot(jnp.concatenate(filtered[2:], 0), wave_table[...], preferred_element_type=jnp.float32)
        for i in range(6):
            waves[i, mine, :] = both[i * rows : (i + 1) * rows]
    sends = []
    transform(0)
    for k, slab in enumerate(slabs):
        if k + 1 < len(slabs):
            transform(k + 1)
        inverse_butterflies(ends, waves, turns, turned, k * rows, rows)
        rest = jnp.zeros((rows, MAIN), jnp.float32)
        for block in range(XBLK):
            start = starts[tilt, slab, block] + first_tap
            base = pl.multiple_of(jnp.minimum((start // 128) * 128, columns - WINDOW), 128)
            window = turned[k * rows : (k + 1) * rows, pl.ds(base, WINDOW)]
            shift = base - start
            reach = pltpu.roll(window, jnp.where(shift < 0, shift + WINDOW, shift), 1)[:, : 2 * MAIN]
            out[k, block * rows : (block + 1) * rows, :] = reach[:, :MAIN].astype(jnp.bfloat16)
            last = reach[:, MAIN:]
            rest = jnp.where(lane == block, pltpu.roll(last, block * REST, 1) if block else last, rest)
        quarter = rows // 4
        beside = rest[:quarter]
        for q in range(1, 4):
            moved = pltpu.roll(rest[q * quarter : (q + 1) * quarter], q * XBLK * REST, 1)
            beside = jnp.where(lane[:quarter] // XBLK == q, moved, beside)
        out[k, XBLK * rows :, :] = beside.astype(jnp.bfloat16)
        sends.append(pltpu.make_async_copy(out.at[k], out_refs[k], out_sems.at[k]))
        sends[-1].start()
    return sends


def column_kernel(slots, slices_owned, image_ref, matrix_ref, angle_ref, defocus_ref, starts_ref, *refs):
    count = len(slots)
    out_refs = refs[:count]
    image, matrix, angles, defocus, starts, zhi, zlo, *scratch, sems = refs[count:]
    rows, columns = image.shape
    size = columns // RADIX
    copies = fetched(
        [image_ref, angle_ref, defocus_ref, starts_ref] + [matrix_ref.at[i] for i in range(5)],
        [image, angles, defocus, starts] + [matrix.at[i] for i in range(5)],
        sems,
    )
    squares, ramp, cosine_turns, sine_turns = column_lines(columns)
    turns = [t[j : j + 1, :] for j in range(3) for t in (cosine_turns, sine_turns)]
    copies[0].wait()
    butterflies(image, turns, zhi, zlo)
    for copy in copies[4:8]:
        copy.wait()

    def product(first, lines, table, here):
        top = zhi[first : first + lines].reshape(lines * rows, size)
        rest = zlo[first : first + lines].reshape(lines * rows, size)
        total = jnp.dot(top, matrix[table, :, here], preferred_element_type=jnp.float32)
        total += jnp.dot(top, matrix[table + 1, :, here], preferred_element_type=jnp.float32)
        return total + jnp.dot(rest, matrix[table, :, here], preferred_element_type=jnp.float32)

    spectrum = [product(0, 1, 0, slice(0, size)), product(1, 1, 0, slice(size, 2 * size))]
    mixed = product(2, 6, 2, slice(None))
    for j in range(3):
        real, imag = mixed[2 * j * rows : (2 * j + 1) * rows], mixed[(2 * j + 1) * rows : (2 * j + 2) * rows]
        spectrum += [real[:, :size] + imag[:, size:], imag[:, :size] - real[:, size:]]
    for copy in copies[1:4] + copies[8:]:
        copy.wait()
    facts = (squares, ramp, turns, angles, defocus, starts)
    sends = send_patches(
        slots, slices_owned, spectrum, matrix.at[2], matrix.at[4], columns, facts, scratch, out_refs
    )
    for copy in sends:
        copy.wait()


def column_filtered(slots, slices_owned, image, angles, defocus, starts):
    rows, columns = image.shape
    size = columns // RADIX
    count = len(slots)
    matrices = jnp.asarray(column_tables(columns))
    away = pl.BlockSpec(memory_space=pl.ANY)
    flops = 2 * rows * size * size * (42 + 14 * count)
    sent = pl.pallas_call(
        functools.partial(column_kernel, slots, slices_owned),
        out_shape=[jax.ShapeDtypeStruct(packed_shape(rows), jnp.bfloat16)] * count,
        in_specs=[away] * 5,
        out_specs=[away] * count,
        scratch_shapes=[
            pltpu.VMEM((rows, columns), jnp.bfloat16),
            pltpu.VMEM(matrices.shape, jnp.bfloat16),
            pltpu.SMEM(angles.shape, jnp.float32),
            pltpu.SMEM(defocus.shape, jnp.int32),
            pltpu.SMEM(starts.shape, jnp.int32),
            pltpu.VMEM((8, rows, size), jnp.bfloat16),
            pltpu.VMEM((8, rows, size), jnp.bfloat16),
            pltpu.VMEM((2, count * rows, size), jnp.float32),
            pltpu.VMEM((6, count * rows, 2 * size), jnp.float32),
            pltpu.VMEM((count * rows, columns), jnp.float32),
            pltpu.VMEM((count, *packed_shape(rows)), jnp.bfloat16),
            pltpu.SemaphoreType.DMA((count,)),
            pltpu.SemaphoreType.DMA((9,)),
        ],
        compiler_params=pltpu.CompilerParams(vmem_limit_bytes=60 * 2**20),
        cost_estimate=pl.CostEstimate(flops=flops, bytes_accessed=3 * 2**20, transcendentals=0),
        name="column_filter",
    )(image, matrices, angles, defocus, starts)
    return dict(zip(slots, sent))


def after(array, *others):
    away = pl.BlockSpec(memory_space=pl.ANY)
    return pl.pallas_call(
        lambda *refs: None,
        out_shape=jax.ShapeDtypeStruct(array.shape, array.dtype),
        in_specs=[away] * (1 + len(others)),
        out_specs=away,
        input_output_aliases={0: 0},
        compiler_params=pltpu.CompilerParams(vmem_limit_bytes=2**20),
        cost_estimate=pl.CostEstimate(flops=0, bytes_accessed=0, transcendentals=0),
        name="after",
    )(array, *others)


def prepare_kernel(slots, slices_owned, angles, defocus, waves, rows_ref, weights_ref, mine, order):
    tilt, row = lax.axis_index("tilt"), lax.axis_index("row")
    slab, local_first = tilt * slices_owned // SLAB, tilt * slices_owned % SLAB
    full_rows = waves.shape[1]
    rows = rows_ref.shape[0] // slots
    half = full_rows // 2
    column = lax.broadcasted_iota(jnp.int32, (8, full_rows), 1)
    freq = jnp.where(column <= half, column, column - half)
    count = jnp.where((freq == 0) | (freq == half), 1.0, 2.0) / full_rows
    scales = [(flip_sign(freq * freq, defocus[tilt ^ slot, slab], full_rows) * count)[:1] for slot in range(slots)]
    for part in range(2):
        for block in range(full_rows // rows):
            there = pl.ds(pl.multiple_of((row ^ block) * rows, rows), rows)
            order[part, block * rows : (block + 1) * rows, :] = waves[part, there, :]
        own = order[part, :rows, :].astype(jnp.float32)
        for slot in range(slots):
            mine[part, slot * rows : (slot + 1) * rows, :] = (own * scales[slot]).astype(jnp.bfloat16)

    def product(left, right):
        over = (((1,), (1,)), ((), ()))
        return lax.dot_general(mine[left], order[right], over, preferred_element_type=jnp.float32)

    rows_ref[...] = (product(0, 0) + product(0, 1) + product(1, 0)).astype(jnp.bfloat16)

    place = lax.broadcasted_iota(jnp.int32, (REACH, XBW), 0).astype(jnp.float32)
    across = lax.broadcasted_iota(jnp.int32, (1, XBW), 1).astype(jnp.float32)
    for slot in range(slots):
        cosine, sine, first_tap = reach_of(angles[tilt ^ slot])
        tap = place + first_tap.astype(jnp.float32)

        def one_slice(c, carry):
            offset = (local_first + c).astype(jnp.float32) - 0.5 * (SLAB - 1)
            centre = 0.5 * XBW + across * cosine + offset * sine
            there = pl.ds(pl.multiple_of(c * XBW, XBW), XBW)
            weights = jnp.maximum(0.0, 1.0 - jnp.abs(tap - centre))
            weights_ref[slot, :MAIN, there] = weights[:MAIN].astype(jnp.bfloat16)
            rest = jnp.concatenate([weights[MAIN:]] * XBLK, 0)
            weights_ref[slot, MAIN:, there] = rest.astype(jnp.bfloat16)
            return carry

        lax.fori_loop(0, slices_owned, one_slice, 0, unroll=2)


def prepared(slots, slices_owned, rows, full_rows, angles, defocus):
    smem, vmem = pl.BlockSpec(memory_space=pltpu.SMEM), pl.BlockSpec(memory_space=pltpu.VMEM)
    return pl.pallas_call(
        functools.partial(prepare_kernel, slots, slices_owned),
        out_shape=[
            jax.ShapeDtypeStruct((slots * rows, full_rows), jnp.bfloat16),
            jax.ShapeDtypeStruct((slots, MAIN + XBLK * REST, slices_owned * XBW), jnp.bfloat16),
        ],
        in_specs=[smem] * 2 + [vmem],
        out_specs=[vmem] * 2,
        scratch_shapes=[
            pltpu.VMEM((2, slots * rows, full_rows), jnp.bfloat16),
            pltpu.VMEM((2, full_rows, full_rows), jnp.bfloat16),
        ],
        compiler_params=pltpu.CompilerParams(vmem_limit_bytes=32 * 2**20),
        cost_estimate=pl.CostEstimate(flops=2**31, bytes_accessed=6 * 2**20, transcendentals=0),
        name="prepare",
    )(angles, defocus, jnp.asarray(row_tables(full_rows)))


def unpacked(packed):
    rows = 4 * packed.shape[0] // (4 * XBLK + 1)
    beside = packed[XBLK * rows :].astype(jnp.float32)
    quarters = [pltpu.roll(beside, MAIN - q * XBLK * REST, 1) if q else beside for q in range(4)]
    rest = jnp.concatenate(quarters, 0).astype(jnp.bfloat16)
    return jnp.concatenate([packed[block * rows : (block + 1) * rows] for block in range(XBLK)] + [rest], 1)


def corrected_patches(slots, row_devices, rows_ref, patch_refs):
    parts = []
    for group in slots:
        refs, patch_refs = patch_refs[:row_devices], patch_refs[row_devices:]
        height = refs[0].shape[0] // len(group)
        for i, slot in enumerate(group):
            patches = jnp.concatenate([unpacked(ref[i * height : (i + 1) * height]) for ref in refs], 0)
            rows = patches.shape[0] // row_devices
            image = jnp.dot(rows_ref[slot * rows : (slot + 1) * rows, :], patches, preferred_element_type=jnp.float32)
            lane = lax.broadcasted_iota(jnp.int32, (rows, MAIN), 1) // REST
            main = jnp.concatenate([image[:, block * MAIN : (block + 1) * MAIN] for block in range(XBLK)], 0)
            rest = [jnp.where(lane == block, image[:, XBLK * MAIN :], 0.0) for block in range(XBLK)]
            rest = jnp.concatenate(rest, 0)[:, : XBLK * REST]
            parts.append((slot, jnp.concatenate([main, rest], 1).astype(jnp.bfloat16)))
    return parts


def sum_kernel(slots, row_devices, rows_ref, weights_ref, *refs):
    total_ref = refs[-1]
    (slot, part), *others = corrected_patches(slots, row_devices, rows_ref, refs[:-1])
    step = 4 * XBW
    for first in range(0, total_ref.shape[1], step):
        here = slice(first, first + step)
        total = jnp.dot(part, weights_ref[slot, :, here], preferred_element_type=jnp.float32)
        for other, more in others:
            total += jnp.dot(more, weights_ref[other, :, here], preferred_element_type=jnp.float32)
        total_ref[:, here] = total


def finish_kernel(factor, slots, row_devices, rows_ref, weights_ref, total_ref, *refs):
    patch_refs = refs[: len(slots) * row_devices]
    out_ref, out, sems = refs[len(slots) * row_devices :]
    rows = total_ref.shape[0] // XBLK
    parts = corrected_patches(slots, row_devices, rows_ref, patch_refs)
    step = 4
    copies = []
    for group in range(out.shape[0] // step):
        here = slice(group * step * XBW, (group + 1) * step * XBW)
        total = total_ref[:, here]
        for slot, part in parts:
            total += jnp.dot(part, weights_ref[slot, :, here], preferred_element_type=jnp.float32)
        for c in range(step):
            for block in range(XBLK):
                out[group * step + c, :, block * XBW : (block + 1) * XBW] = (
                    factor * total[block * rows : (block + 1) * rows, c * XBW : (c + 1) * XBW]
                ).astype(jnp.bfloat16)
        part = pl.ds(group * step, step)
        copies.append(pltpu.make_async_copy(out.at[part], out_ref.at[part], sems.at[group]))
        copies[-1].start()
    for copy in copies:
        copy.wait()


def interpolation(kernel, slots, weights, row_filters, patches, totals, **call):
    vmem = pl.BlockSpec(memory_space=pltpu.VMEM)
    operands = [row_filters, weights, *totals, *(block for group in patches for block in group)]
    return pl.pallas_call(
        functools.partial(kernel, slots, len(patches[0])),
        in_specs=[vmem] * len(operands),
        compiler_params=pltpu.CompilerParams(vmem_limit_bytes=32 * 2**20),
        cost_estimate=pl.CostEstimate(flops=0, bytes_accessed=0, transcendentals=0),
        **call,
    )(*operands)


def summed(row_filters, weights, patches, slots):
    return interpolation(
        sum_kernel,
        slots,
        weights,
        row_filters,
        patches,
        [],
        out_shape=jax.ShapeDtypeStruct((XBLK * row_filters.shape[0] // weights.shape[0], weights.shape[2]), jnp.float32),
        out_specs=pl.BlockSpec(memory_space=pltpu.VMEM),
        name="sum_early_tilts",
    )


def finished(row_filters, weights, total, patches, slots, factor):
    shape = (weights.shape[2] // XBW, row_filters.shape[0] // weights.shape[0], XBLK * XBW)
    return interpolation(
        functools.partial(finish_kernel, factor),
        slots,
        weights,
        row_filters,
        patches,
        [total],
        out_shape=jax.ShapeDtypeStruct(shape, jnp.bfloat16),
        out_specs=pl.BlockSpec(memory_space=pl.ANY),
        scratch_shapes=[pltpu.VMEM(shape, jnp.bfloat16), pltpu.SemaphoreType.DMA((shape[0] // 4,))],
        name="finish_volume",
    )


def exchange(array, axis, distance):
    count = lax.axis_size(axis)
    return lax.ppermute(array, axis, [(i, i ^ distance) for i in range(count)])


def gather_rows(array, awaited=()):
    blocks = {0: array}
    bit = lax.axis_size("row") // 2
    while bit:
        if bit == 1 and awaited:
            blocks = {d: after(block, *awaited) if d else block for d, block in blocks.items()}
        blocks.update({d ^ bit: exchange(block, "row", bit) for d, block in blocks.items()})
        bit //= 2
    return [blocks[d] for d in sorted(blocks)]


def per_device(projections, tilt_angle, band_start, defocus):
    _, rows, _ = projections.shape
    row_devices, tilt_devices = lax.axis_size("row"), lax.axis_size("tilt")
    slices_owned = SLICES // tilt_devices
    far, near = list(range(tilt_devices - 1, 1, -1)), list(range(min(2, tilt_devices)))
    sent = column_filtered(far + near, slices_owned, projections[0], tilt_angle, defocus, band_start)
    arrived = {d: exchange(sent[d], "tilt", d) if d else sent[d] for d in far + near}
    row_filters, weights = prepared(tilt_devices, slices_owned, rows, rows * row_devices, tilt_angle, defocus)
    early = [gather_rows(jnp.concatenate([arrived[d] for d in near]))]
    total = summed(row_filters, weights, early, [near])
    late = [gather_rows(after(arrived[d], row_filters) if d == far[-1] else arrived[d]) for d in far]
    return finished(row_filters, weights, total, late, [[d] for d in far], 1.0 / math.sqrt(tilt_devices))


def solution(mesh):
    in_specs = (
        P(("group", "tilt"), "row", None),
        P("group"),
        P("group", None, None),
        P("group", None),
    )
    out_specs = P(("group", "tilt"), "row", None)
    return jax.shard_map(
        per_device, mesh=mesh, in_specs=in_specs, out_specs=out_specs, check_vma=False
    )
```

```python
import functools
import math

import jax
import jax.numpy as jnp
import numpy as np
from jax import lax
from jax.experimental import pallas as pl
from jax.experimental.pallas import tpu as pltpu
from jax.sharding import PartitionSpec as P

SLAB = 16
XBW = 128
BAND = 256
XBLK = 4
SLICES = 64
RADIX = 8
MAIN = 128
REST = 8
REACH = MAIN + REST
WINDOW = 384
ROOT = math.sqrt(0.5)


def split(table):
    high = table.astype(jnp.bfloat16)
    return high, (table - high.astype(np.float64)).astype(jnp.bfloat16)


def column_tables(columns):
    size = columns // RADIX
    half = size // 2
    u = np.arange(size)[:, None]

    def angles(freq):
        return 2.0 * np.pi * ((u * freq[None, :]) % columns) / columns

    k0, s0 = RADIX * np.arange(half + 1), RADIX * np.arange(1, half)
    k4 = RADIX * np.arange(half) + 4
    m0 = np.concatenate([np.cos(angles(k0)), -np.sin(angles(s0))], 1)
    m4 = np.concatenate([np.cos(angles(k4)), -np.sin(angles(k4))], 1)
    full = angles(RADIX * np.arange(size))
    waves = np.concatenate([np.cos(full), np.sin(full)], 1)
    ends = np.concatenate([m0, m4], 1)

    matrices = np.stack([*split(ends), *split(waves), np.concatenate([m0.T, m4.T], 1).astype(jnp.bfloat16)])
    return matrices


def column_lines(columns):
    size = columns // RADIX
    half = size // 2
    line = lax.broadcasted_iota(jnp.int32, (8, size), 0)
    u = lax.broadcasted_iota(jnp.int32, (8, size), 1)
    freq = jnp.where(line == 0, RADIX * jnp.where(u <= half, u, u - half), RADIX * (u & (half - 1)) + 4)
    freq = jnp.where(line < 2, freq, RADIX * u + line // 2)
    fold = jnp.minimum(freq, columns - freq)
    count = jnp.where((fold == 0) | (fold == columns // 2), 1.0, 2.0)
    gain = count * (fold.astype(jnp.float32) + 0.5) * (2.0 / (columns * columns))
    angle = (u * (line + 1)).astype(jnp.float32) * (2.0 * math.pi / columns)
    return fold * fold, gain, jnp.cos(angle), jnp.sin(angle)


def row_tables(full_rows):
    half = full_rows // 2
    column = np.arange(full_rows)
    freq = np.where(column <= half, column, column - half)
    angle = 2.0 * np.pi * (np.arange(full_rows)[:, None] * freq[None, :] % full_rows) / full_rows
    return np.stack(split(np.where(column[None, :] <= half, np.cos(angle), np.sin(angle))))


def packed_shape(rows):
    return (XBLK * rows + rows // 4, MAIN)


def flip_sign(squares, defocus, length):
    cycles = lax.div(squares * defocus, jnp.int32(length * length))
    return (1 - 2 * (cycles & 1)).astype(jnp.float32)


def fetched(sources, targets, sems):
    copies = [pltpu.make_async_copy(s, t, sems.at[i]) for i, (s, t) in enumerate(zip(sources, targets))]
    for copy in copies:
        copy.start()
    return copies


def reach_of(angle):
    line = jnp.full((8, XBW), angle, jnp.float32)
    cosine, sine = jnp.cos(line), jnp.sin(line)
    lowest = 0.5 * XBW + jnp.minimum((XBW - 1) * cosine, 0.0) - 0.5 * (SLAB - 1) * jnp.abs(sine)
    first = jnp.clip(jnp.floor(lowest) - 2.0, 0.0, float(BAND - REACH))
    return cosine[:1], sine[:1], jnp.max(first).astype(jnp.int32)


def butterflies(image, turns, zhi, zlo, first, count):
    size = image.shape[1] // RADIX
    for top_row in range(first, first + count, 16):
        here = slice(top_row, top_row + 16)
        x = [image[here, m * size : (m + 1) * size].astype(jnp.float32) for m in range(8)]
        p0, p1, p2, p3 = (x[m] + x[m + 4] for m in range(4))
        q0, q1, q2, q3 = (x[m] - x[m + 4] for m in range(4))
        e, f = p0 + p2, p1 + p3
        g, h = ROOT * (q1 - q3), ROOT * (q1 + q3)
        z = [e + f, e - f]
        for j, (real, imag) in enumerate([(q0 + g, -q2 - h), (p0 - p2, p3 - p1), (q0 - g, q2 - h)]):
            c, s = turns[2 * j], turns[2 * j + 1]
            z += [real * c + imag * s, imag * c - real * s]
        for line in range(8):
            top = z[line].astype(jnp.bfloat16)
            zhi[line, here, :] = top
            zlo[line, here, :] = (z[line] - top.astype(jnp.float32)).astype(jnp.bfloat16)


def inverse_butterflies(ends, waves, turns, turned, first, rows):
    columns = turned.shape[1]
    size = columns // RADIX
    for top in range(first, first + rows, 8):
        here = slice(top, top + 8)
        r, s = [], []
        for j in range(3):
            c, d = turns[2 * j], turns[2 * j + 1]
            real = waves[2 * j, here, :size] - waves[2 * j + 1, here, size:]
            imag = waves[2 * j, here, size:] + waves[2 * j + 1, here, :size]
            r.append(real * c - imag * d)
            s.append(real * d + imag * c)
        e, f = ends[0, here, :] + ends[1, here, :], ends[0, here, :] - ends[1, here, :]
        a, b, c, d = r[0] + r[2], r[0] - r[2], s[0] + s[2], s[0] - s[2]
        even0, even2, odd1, odd3 = e + r[1], e - r[1], f - s[1], f + s[1]
        g, h = ROOT * (b - c), ROOT * (b + c)
        out = [even0 + a, odd1 + g, even2 - d, odd3 - h, even0 - a, odd1 - g, even2 + d, odd3 + h]
        for m in range(8):
            turned[here, m * size : (m + 1) * size] = out[m]


def send_patches(slots, slices_owned, spectrum, wave_table, end_table, columns, facts, scratch, out_refs):
    squares, ramp, turns, angles, defocus, starts = facts
    ends, waves, turned, out, out_sems = scratch
    rows, size = spectrum[0].shape
    tilt = lax.axis_index("tilt")
    lane = lax.broadcasted_iota(jnp.int32, (rows, MAIN), 1) // REST
    _, _, first_tap = reach_of(angles[tilt])
    slabs = [(tilt ^ slot) * slices_owned // SLAB for slot in slots]

    def transform(k):
        slab = slabs[k]
        mine = slice(k * rows, (k + 1) * rows)
        gain = flip_sign(squares, defocus[tilt, slab], columns) * ramp
        filtered = [(spectrum[i] * gain[i : i + 1, :]).astype(jnp.bfloat16) for i in range(8)]
        for i in range(2):
            table = end_table[:, i * size : (i + 1) * size]
            ends[i, mine, :] = jnp.dot(filtered[i], table, preferred_element_type=jnp.float32)
        both = jnp.dot(jnp.concatenate(filtered[2:], 0), wave_table[...], preferred_element_type=jnp.float32)
        for i in range(6):
            waves[i, mine, :] = both[i * rows : (i + 1) * rows]
    sends = []
    transform(0)
    for k, slab in enumerate(slabs):
        if k + 1 < len(slabs):
            transform(k + 1)
        inverse_butterflies(ends, waves, turns, turned, k * rows, rows)
        rest = jnp.zeros((rows, MAIN), jnp.float32)
        for block in range(XBLK):
            start = starts[tilt, slab, block] + first_tap
            base = pl.multiple_of(jnp.minimum((start // 128) * 128, columns - WINDOW), 128)
            window = turned[k * rows : (k + 1) * rows, pl.ds(base, WINDOW)]
            shift = base - start
            reach = pltpu.roll(window, jnp.where(shift < 0, shift + WINDOW, shift), 1)[:, : 2 * MAIN]
            out[k, block * rows : (block + 1) * rows, :] = reach[:, :MAIN].astype(jnp.bfloat16)
            last = reach[:, MAIN:]
            rest = jnp.where(lane == block, pltpu.roll(last, block * REST, 1) if block else last, rest)
        quarter = rows // 4
        beside = rest[:quarter]
        for q in range(1, 4):
            moved = pltpu.roll(rest[q * quarter : (q + 1) * quarter], q * XBLK * REST, 1)
            beside = jnp.where(lane[:quarter] // XBLK == q, moved, beside)
        out[k, XBLK * rows :, :] = beside.astype(jnp.bfloat16)
        sends.append(pltpu.make_async_copy(out.at[k], out_refs[k], out_sems.at[k]))
        sends[-1].start()
    return sends


def column_kernel(slots, slices_owned, image_ref, matrix_ref, angle_ref, defocus_ref, starts_ref, *refs):
    count = len(slots)
    out_refs = refs[:count]
    image, matrix, angles, defocus, starts, zhi, zlo, *scratch, sems = refs[count:]
    rows, columns = image.shape
    size = columns // RADIX
    halves = [pl.ds(0, rows // 2), pl.ds(rows // 2, rows // 2)]
    order = [2, 3, 0, 1, 4]
    copies = fetched(
        [image_ref.at[h] for h in halves] + [matrix_ref.at[i] for i in order] + [angle_ref, defocus_ref, starts_ref],
        [image.at[h] for h in halves] + [matrix.at[i] for i in order] + [angles, defocus, starts],
        sems,
    )
    squares, ramp, cosine_turns, sine_turns = column_lines(columns)
    turns = [t[j : j + 1, :] for j in range(3) for t in (cosine_turns, sine_turns)]
    for i in range(2):
        copies[i].wait()
        butterflies(image, turns, zhi, zlo, i * rows // 2, rows // 2)
    for copy in copies[2:4]:
        copy.wait()

    def product(first, lines, table, here):
        top = zhi[first : first + lines].reshape(lines * rows, size)
        rest = zlo[first : first + lines].reshape(lines * rows, size)
        total = jnp.dot(top, matrix[table, :, here], preferred_element_type=jnp.float32)
        total += jnp.dot(top, matrix[table + 1, :, here], preferred_element_type=jnp.float32)
        return total + jnp.dot(rest, matrix[table, :, here], preferred_element_type=jnp.float32)

    mixed = product(2, 6, 2, slice(None))
    for copy in copies[4:]:
        copy.wait()
    spectrum = [product(0, 1, 0, slice(0, size)), product(1, 1, 0, slice(size, 2 * size))]
    for j in range(3):
        real, imag = mixed[2 * j * rows : (2 * j + 1) * rows], mixed[(2 * j + 1) * rows : (2 * j + 2) * rows]
        spectrum += [real[:, :size] + imag[:, size:], imag[:, :size] - real[:, size:]]
    facts = (squares, ramp, turns, angles, defocus, starts)
    sends = send_patches(
        slots, slices_owned, spectrum, matrix.at[2], matrix.at[4], columns, facts, scratch, out_refs
    )
    for copy in sends:
        copy.wait()


def column_filtered(slots, slices_owned, image, angles, defocus, starts):
    rows, columns = image.shape
    size = columns // RADIX
    count = len(slots)
    matrices = jnp.asarray(column_tables(columns))
    away = pl.BlockSpec(memory_space=pl.ANY)
    flops = 2 * rows * size * size * (42 + 14 * count)
    sent = pl.pallas_call(
        functools.partial(column_kernel, slots, slices_owned),
        out_shape=[jax.ShapeDtypeStruct(packed_shape(rows), jnp.bfloat16)] * count,
        in_specs=[away] * 5,
        out_specs=[away] * count,
        scratch_shapes=[
            pltpu.VMEM((rows, columns), jnp.bfloat16),
            pltpu.VMEM(matrices.shape, jnp.bfloat16),
            pltpu.SMEM(angles.shape, jnp.float32),
            pltpu.SMEM(defocus.shape, jnp.int32),
            pltpu.SMEM(starts.shape, jnp.int32),
            pltpu.VMEM((8, rows, size), jnp.bfloat16),
            pltpu.VMEM((8, rows, size), jnp.bfloat16),
            pltpu.VMEM((2, count * rows, size), jnp.float32),
            pltpu.VMEM((6, count * rows, 2 * size), jnp.float32),
            pltpu.VMEM((count * rows, columns), jnp.float32),
            pltpu.VMEM((count, *packed_shape(rows)), jnp.bfloat16),
            pltpu.SemaphoreType.DMA((count,)),
            pltpu.SemaphoreType.DMA((10,)),
        ],
        compiler_params=pltpu.CompilerParams(vmem_limit_bytes=60 * 2**20),
        cost_estimate=pl.CostEstimate(flops=flops, bytes_accessed=3 * 2**20, transcendentals=0),
        name="column_filter",
    )(image, matrices, angles, defocus, starts)
    return dict(zip(slots, sent))


def after(array, *others):
    away = pl.BlockSpec(memory_space=pl.ANY)
    return pl.pallas_call(
        lambda *refs: None,
        out_shape=jax.ShapeDtypeStruct(array.shape, array.dtype),
        in_specs=[away] * (1 + len(others)),
        out_specs=away,
        input_output_aliases={0: 0},
        compiler_params=pltpu.CompilerParams(vmem_limit_bytes=2**20),
        cost_estimate=pl.CostEstimate(flops=0, bytes_accessed=0, transcendentals=0),
        name="after",
    )(array, *others)


def prepare_kernel(slots, slices_owned, angles, defocus, waves, rows_ref, weights_ref, mine, order):
    tilt, row = lax.axis_index("tilt"), lax.axis_index("row")
    slab, local_first = tilt * slices_owned // SLAB, tilt * slices_owned % SLAB
    full_rows = waves.shape[1]
    rows = rows_ref.shape[0] // slots
    half = full_rows // 2
    column = lax.broadcasted_iota(jnp.int32, (8, full_rows), 1)
    freq = jnp.where(column <= half, column, column - half)
    count = jnp.where((freq == 0) | (freq == half), 1.0, 2.0) / full_rows
    scales = [(flip_sign(freq * freq, defocus[tilt ^ slot, slab], full_rows) * count)[:1] for slot in range(slots)]
    for part in range(2):
        for block in range(full_rows // rows):
            there = pl.ds(pl.multiple_of((row ^ block) * rows, rows), rows)
            order[part, block * rows : (block + 1) * rows, :] = waves[part, there, :]
        own = order[part, :rows, :].astype(jnp.float32)
        for slot in range(slots):
            mine[part, slot * rows : (slot + 1) * rows, :] = (own * scales[slot]).astype(jnp.bfloat16)

    def product(left, right):
        over = (((1,), (1,)), ((), ()))
        return lax.dot_general(mine[left], order[right], over, preferred_element_type=jnp.float32)

    rows_ref[...] = (product(0, 0) + product(0, 1) + product(1, 0)).astype(jnp.bfloat16)

    place = lax.broadcasted_iota(jnp.int32, (REACH, XBW), 0).astype(jnp.float32)
    across = lax.broadcasted_iota(jnp.int32, (1, XBW), 1).astype(jnp.float32)
    for slot in range(slots):
        cosine, sine, first_tap = reach_of(angles[tilt ^ slot])
        tap = place + first_tap.astype(jnp.float32)

        def one_slice(c, carry):
            offset = (local_first + c).astype(jnp.float32) - 0.5 * (SLAB - 1)
            centre = 0.5 * XBW + across * cosine + offset * sine
            there = pl.ds(pl.multiple_of(c * XBW, XBW), XBW)
            weights = jnp.maximum(0.0, 1.0 - jnp.abs(tap - centre))
            weights_ref[slot, :MAIN, there] = weights[:MAIN].astype(jnp.bfloat16)
            rest = jnp.concatenate([weights[MAIN:]] * XBLK, 0)
            weights_ref[slot, MAIN:, there] = rest.astype(jnp.bfloat16)
            return carry

        lax.fori_loop(0, slices_owned, one_slice, 0, unroll=2)


def prepared(slots, slices_owned, rows, full_rows, angles, defocus):
    smem, vmem = pl.BlockSpec(memory_space=pltpu.SMEM), pl.BlockSpec(memory_space=pltpu.VMEM)
    return pl.pallas_call(
        functools.partial(prepare_kernel, slots, slices_owned),
        out_shape=[
            jax.ShapeDtypeStruct((slots * rows, full_rows), jnp.bfloat16),
            jax.ShapeDtypeStruct((slots, MAIN + XBLK * REST, slices_owned * XBW), jnp.bfloat16),
        ],
        in_specs=[smem] * 2 + [vmem],
        out_specs=[vmem] * 2,
        scratch_shapes=[
            pltpu.VMEM((2, slots * rows, full_rows), jnp.bfloat16),
            pltpu.VMEM((2, full_rows, full_rows), jnp.bfloat16),
        ],
        compiler_params=pltpu.CompilerParams(vmem_limit_bytes=32 * 2**20),
        cost_estimate=pl.CostEstimate(flops=2**31, bytes_accessed=6 * 2**20, transcendentals=0),
        name="prepare",
    )(angles, defocus, jnp.asarray(row_tables(full_rows)))


def unpacked(packed):
    rows = 4 * packed.shape[0] // (4 * XBLK + 1)
    beside = packed[XBLK * rows :].astype(jnp.float32)
    quarters = [pltpu.roll(beside, MAIN - q * XBLK * REST, 1) if q else beside for q in range(4)]
    rest = jnp.concatenate(quarters, 0).astype(jnp.bfloat16)
    return jnp.concatenate([packed[block * rows : (block + 1) * rows] for block in range(XBLK)] + [rest], 1)


def corrected_patches(slots, row_devices, rows_ref, patch_refs):
    parts = []
    for group in slots:
        refs, patch_refs = patch_refs[:row_devices], patch_refs[row_devices:]
        height = refs[0].shape[0] // len(group)
        for i, slot in enumerate(group):
            patches = jnp.concatenate([unpacked(ref[i * height : (i + 1) * height]) for ref in refs], 0)
            rows = patches.shape[0] // row_devices
            image = jnp.dot(rows_ref[slot * rows : (slot + 1) * rows, :], patches, preferred_element_type=jnp.float32)
            lane = lax.broadcasted_iota(jnp.int32, (rows, MAIN), 1) // REST
            main = jnp.concatenate([image[:, block * MAIN : (block + 1) * MAIN] for block in range(XBLK)], 0)
            rest = [jnp.where(lane == block, image[:, XBLK * MAIN :], 0.0) for block in range(XBLK)]
            rest = jnp.concatenate(rest, 0)[:, : XBLK * REST]
            parts.append((slot, jnp.concatenate([main, rest], 1).astype(jnp.bfloat16)))
    return parts


def sum_kernel(slots, row_devices, rows_ref, weights_ref, *refs):
    total_ref = refs[-1]
    (slot, part), *others = corrected_patches(slots, row_devices, rows_ref, refs[:-1])
    step = 4 * XBW
    for first in range(0, total_ref.shape[1], step):
        here = slice(first, first + step)
        total = jnp.dot(part, weights_ref[slot, :, here], preferred_element_type=jnp.float32)
        for other, more in others:
            total += jnp.dot(more, weights_ref[other, :, here], preferred_element_type=jnp.float32)
        total_ref[:, here] = total


def finish_kernel(factor, slots, row_devices, rows_ref, weights_ref, total_ref, *refs):
    patch_refs = refs[: len(slots) * row_devices]
    out_ref, out, sems = refs[len(slots) * row_devices :]
    rows = total_ref.shape[0] // XBLK
    parts = corrected_patches(slots, row_devices, rows_ref, patch_refs)
    step = 2
    copies = []
    for group in range(out.shape[0] // step):
        here = slice(group * step * XBW, (group + 1) * step * XBW)
        total = total_ref[:, here]
        for slot, part in parts:
            total += jnp.dot(part, weights_ref[slot, :, here], preferred_element_type=jnp.float32)
        for c in range(step):
            for block in range(XBLK):
                out[group * step + c, :, block * XBW : (block + 1) * XBW] = (
                    factor * total[block * rows : (block + 1) * rows, c * XBW : (c + 1) * XBW]
                ).astype(jnp.bfloat16)
        part = pl.ds(group * step, step)
        copies.append(pltpu.make_async_copy(out.at[part], out_ref.at[part], sems.at[group]))
        copies[-1].start()
    for copy in copies:
        copy.wait()


def interpolation(kernel, slots, weights, row_filters, patches, totals, **call):
    vmem = pl.BlockSpec(memory_space=pltpu.VMEM)
    operands = [row_filters, weights, *totals, *(block for group in patches for block in group)]
    return pl.pallas_call(
        functools.partial(kernel, slots, len(patches[0])),
        in_specs=[vmem] * len(operands),
        compiler_params=pltpu.CompilerParams(vmem_limit_bytes=32 * 2**20),
        cost_estimate=pl.CostEstimate(flops=0, bytes_accessed=0, transcendentals=0),
        **call,
    )(*operands)


def summed(row_filters, weights, patches, slots):
    return interpolation(
        sum_kernel,
        slots,
        weights,
        row_filters,
        patches,
        [],
        out_shape=jax.ShapeDtypeStruct((XBLK * row_filters.shape[0] // weights.shape[0], weights.shape[2]), jnp.float32),
        out_specs=pl.BlockSpec(memory_space=pltpu.VMEM),
        name="sum_early_tilts",
    )


def finished(row_filters, weights, total, patches, slots, factor):
    shape = (weights.shape[2] // XBW, row_filters.shape[0] // weights.shape[0], XBLK * XBW)
    return interpolation(
        functools.partial(finish_kernel, factor),
        slots,
        weights,
        row_filters,
        patches,
        [total],
        out_shape=jax.ShapeDtypeStruct(shape, jnp.bfloat16),
        out_specs=pl.BlockSpec(memory_space=pl.ANY),
        scratch_shapes=[pltpu.VMEM(shape, jnp.bfloat16), pltpu.SemaphoreType.DMA((shape[0] // 2,))],
        name="finish_volume",
    )


def exchange(array, axis, distance):
    count = lax.axis_size(axis)
    return lax.ppermute(array, axis, [(i, i ^ distance) for i in range(count)])


def gather_rows(array, awaited=()):
    blocks = {0: array}
    bit = lax.axis_size("row") // 2
    while bit:
        if bit == 1 and awaited:
            blocks = {d: after(block, *awaited) if d else block for d, block in blocks.items()}
        blocks.update({d ^ bit: exchange(block, "row", bit) for d, block in blocks.items()})
        bit //= 2
    return [blocks[d] for d in sorted(blocks)]


def per_device(projections, tilt_angle, band_start, defocus):
    _, rows, _ = projections.shape
    row_devices, tilt_devices = lax.axis_size("row"), lax.axis_size("tilt")
    slices_owned = SLICES // tilt_devices
    far, near = list(range(tilt_devices - 1, 1, -1)), list(range(min(2, tilt_devices)))
    sent = column_filtered(far + near, slices_owned, projections[0], tilt_angle, defocus, band_start)
    arrived = {d: exchange(sent[d], "tilt", d) if d else sent[d] for d in far + near}
    row_filters, weights = prepared(tilt_devices, slices_owned, rows, rows * row_devices, tilt_angle, defocus)
    early = [gather_rows(jnp.concatenate([arrived[d] for d in near]))]
    total = summed(row_filters, weights, early, [near])
    late = [gather_rows(after(arrived[d], row_filters) if d == far[-1] else arrived[d]) for d in far]
    return finished(row_filters, weights, total, late, [[d] for d in far], 1.0 / math.sqrt(tilt_devices))


def solution(mesh):
    in_specs = (
        P(("group", "tilt"), "row", None),
        P("group"),
        P("group", None, None),
        P("group", None),
    )
    out_specs = P(("group", "tilt"), "row", None)
    return jax.shard_map(
        per_device, mesh=mesh, in_specs=in_specs, out_specs=out_specs, check_vma=False
    )
```

```python
import functools
import math

import jax
import jax.numpy as jnp
import numpy as np
from jax import lax
from jax.experimental import pallas as pl
from jax.experimental.pallas import tpu as pltpu
from jax.sharding import PartitionSpec as P

SLAB = 16
XBW = 128
BAND = 256
XBLK = 4
SLICES = 64
RADIX = 8
MAIN = 128
REST = 8
REACH = MAIN + REST
WINDOW = 384
ROOT = math.sqrt(0.5)


def split(table):
    high = table.astype(jnp.bfloat16)
    return high, (table - high.astype(np.float64)).astype(jnp.bfloat16)


def column_tables(columns):
    size = columns // RADIX
    half = size // 2
    u = np.arange(size)[:, None]

    def angles(freq):
        return 2.0 * np.pi * ((u * freq[None, :]) % columns) / columns

    k0, s0 = RADIX * np.arange(half + 1), RADIX * np.arange(1, half)
    k4 = RADIX * np.arange(half) + 4
    m0 = np.concatenate([np.cos(angles(k0)), -np.sin(angles(s0))], 1)
    m4 = np.concatenate([np.cos(angles(k4)), -np.sin(angles(k4))], 1)
    full = angles(RADIX * np.arange(size))
    waves = np.concatenate([np.cos(full), np.sin(full)], 1)
    ends = np.concatenate([m0, m4], 1)

    matrices = np.stack([*split(ends), *split(waves), np.concatenate([m0.T, m4.T], 1).astype(jnp.bfloat16)])
    return matrices


def column_lines(columns):
    size = columns // RADIX
    half = size // 2
    line = lax.broadcasted_iota(jnp.int32, (8, size), 0)
    u = lax.broadcasted_iota(jnp.int32, (8, size), 1)
    freq = jnp.where(line == 0, RADIX * jnp.where(u <= half, u, u - half), RADIX * (u & (half - 1)) + 4)
    freq = jnp.where(line < 2, freq, RADIX * u + line // 2)
    fold = jnp.minimum(freq, columns - freq)
    count = jnp.where((fold == 0) | (fold == columns // 2), 1.0, 2.0)
    gain = count * (fold.astype(jnp.float32) + 0.5) * (2.0 / (columns * columns))
    angle = (u * (line + 1)).astype(jnp.float32) * (2.0 * math.pi / columns)
    return fold * fold, gain, jnp.cos(angle), jnp.sin(angle)


def row_tables(full_rows):
    half = full_rows // 2
    column = np.arange(full_rows)
    freq = np.where(column <= half, column, column - half)
    angle = 2.0 * np.pi * (np.arange(full_rows)[:, None] * freq[None, :] % full_rows) / full_rows
    return np.stack(split(np.where(column[None, :] <= half, np.cos(angle), np.sin(angle))))


def packed_shape(rows):
    return (XBLK * rows + rows // 4, MAIN)


def flip_sign(squares, defocus, length):
    cycles = lax.div(squares * defocus, jnp.int32(length * length))
    return (1 - 2 * (cycles & 1)).astype(jnp.float32)


def fetched(sources, targets, sems):
    copies = [pltpu.make_async_copy(s, t, sems.at[i]) for i, (s, t) in enumerate(zip(sources, targets))]
    for copy in copies:
        copy.start()
    return copies


def reach_of(angle):
    line = jnp.full((8, XBW), angle, jnp.float32)
    cosine, sine = jnp.cos(line), jnp.sin(line)
    lowest = 0.5 * XBW + jnp.minimum((XBW - 1) * cosine, 0.0) - 0.5 * (SLAB - 1) * jnp.abs(sine)
    first = jnp.clip(jnp.floor(lowest) - 2.0, 0.0, float(BAND - REACH))
    return cosine[:1], sine[:1], jnp.max(first).astype(jnp.int32)


def butterflies(image, turns, zhi, zlo):
    rows, columns = image.shape
    size = columns // RADIX

    def step(i, carry):
        here = pl.ds(pl.multiple_of(i * 16, 16), 16)
        x = [image[here, m * size : (m + 1) * size].astype(jnp.float32) for m in range(8)]
        p0, p1, p2, p3 = (x[m] + x[m + 4] for m in range(4))
        q0, q1, q2, q3 = (x[m] - x[m + 4] for m in range(4))
        e, f = p0 + p2, p1 + p3
        g, h = ROOT * (q1 - q3), ROOT * (q1 + q3)
        z = [e + f, e - f]
        for j, (real, imag) in enumerate([(q0 + g, -q2 - h), (p0 - p2, p3 - p1), (q0 - g, q2 - h)]):
            c, s = turns[2 * j], turns[2 * j + 1]
            z += [real * c + imag * s, imag * c - real * s]
        for line in range(8):
            top = z[line].astype(jnp.bfloat16)
            zhi[line, here, :] = top
            zlo[line, here, :] = (z[line] - top.astype(jnp.float32)).astype(jnp.bfloat16)
        return carry

    lax.fori_loop(0, rows // 16, step, 0)


def inverse_butterflies(ends, waves, turns, turned, first, rows):
    columns = turned.shape[1]
    size = columns // RADIX
    for top in range(first, first + rows, 8):
        here = slice(top, top + 8)
        r, s = [], []
        for j in range(3):
            c, d = turns[2 * j], turns[2 * j + 1]
            real = waves[2 * j, here, :size] - waves[2 * j + 1, here, size:]
            imag = waves[2 * j, here, size:] + waves[2 * j + 1, here, :size]
            r.append(real * c - imag * d)
            s.append(real * d + imag * c)
        e, f = ends[0, here, :] + ends[1, here, :], ends[0, here, :] - ends[1, here, :]
        a, b, c, d = r[0] + r[2], r[0] - r[2], s[0] + s[2], s[0] - s[2]
        even0, even2, odd1, odd3 = e + r[1], e - r[1], f - s[1], f + s[1]
        g, h = ROOT * (b - c), ROOT * (b + c)
        out = [even0 + a, odd1 + g, even2 - d, odd3 - h, even0 - a, odd1 - g, even2 + d, odd3 + h]
        for m in range(8):
            turned[here, m * size : (m + 1) * size] = out[m]


def send_patches(slots, slices_owned, spectrum, wave_table, end_table, columns, facts, scratch, out_refs):
    squares, ramp, turns, angles, defocus, starts = facts
    ends, waves, turned, out, out_sems = scratch
    rows, size = spectrum[0].shape
    tilt = lax.axis_index("tilt")
    lane = lax.broadcasted_iota(jnp.int32, (rows, MAIN), 1) // REST
    _, _, first_tap = reach_of(angles[tilt])
    slabs = [(tilt ^ slot) * slices_owned // SLAB for slot in slots]

    def transform(k):
        slab = slabs[k]
        mine = slice(k * rows, (k + 1) * rows)
        gain = flip_sign(squares, defocus[tilt, slab], columns) * ramp
        filtered = [(spectrum[i] * gain[i : i + 1, :]).astype(jnp.bfloat16) for i in range(8)]
        for i in range(2):
            table = end_table[:, i * size : (i + 1) * size]
            ends[i, mine, :] = jnp.dot(filtered[i], table, preferred_element_type=jnp.float32)
        both = jnp.dot(jnp.concatenate(filtered[2:], 0), wave_table[...], preferred_element_type=jnp.float32)
        for i in range(6):
            waves[i, mine, :] = both[i * rows : (i + 1) * rows]
    sends = []
    transform(0)
    for k, slab in enumerate(slabs):
        if k + 1 < len(slabs):
            transform(k + 1)
        inverse_butterflies(ends, waves, turns, turned, k * rows, rows)
        rest = jnp.zeros((rows, MAIN), jnp.float32)
        for block in range(XBLK):
            start = starts[tilt, slab, block] + first_tap
            base = pl.multiple_of(jnp.minimum((start // 128) * 128, columns - WINDOW), 128)
            window = turned[k * rows : (k + 1) * rows, pl.ds(base, WINDOW)]
            shift = base - start
            reach = pltpu.roll(window, jnp.where(shift < 0, shift + WINDOW, shift), 1)[:, : 2 * MAIN]
            out[k, block * rows : (block + 1) * rows, :] = reach[:, :MAIN].astype(jnp.bfloat16)
            last = reach[:, MAIN:]
            rest = jnp.where(lane == block, pltpu.roll(last, block * REST, 1) if block else last, rest)
        quarter = rows // 4
        beside = rest[:quarter]
        for q in range(1, 4):
            moved = pltpu.roll(rest[q * quarter : (q + 1) * quarter], q * XBLK * REST, 1)
            beside = jnp.where(lane[:quarter] // XBLK == q, moved, beside)
        out[k, XBLK * rows :, :] = beside.astype(jnp.bfloat16)
        sends.append(pltpu.make_async_copy(out.at[k], out_refs[k], out_sems.at[k]))
        sends[-1].start()
    return sends


def column_kernel(slots, slices_owned, image_ref, matrix_ref, angle_ref, defocus_ref, starts_ref, *refs):
    count = len(slots)
    out_refs = refs[:count]
    image, matrix, angles, defocus, starts, zhi, zlo, *scratch, sems = refs[count:]
    rows, columns = image.shape
    size = columns // RADIX
    copies = fetched(
        [image_ref, angle_ref, defocus_ref, starts_ref] + [matrix_ref.at[i] for i in range(5)],
        [image, angles, defocus, starts] + [matrix.at[i] for i in range(5)],
        sems,
    )
    squares, ramp, cosine_turns, sine_turns = column_lines(columns)
    turns = [t[j : j + 1, :] for j in range(3) for t in (cosine_turns, sine_turns)]
    copies[0].wait()
    butterflies(image, turns, zhi, zlo)
    for copy in copies[4:8]:
        copy.wait()

    def product(first, lines, table, here):
        top = zhi[first : first + lines].reshape(lines * rows, size)
        rest = zlo[first : first + lines].reshape(lines * rows, size)
        total = jnp.dot(top, matrix[table, :, here], preferred_element_type=jnp.float32)
        total += jnp.dot(top, matrix[table + 1, :, here], preferred_element_type=jnp.float32)
        return total + jnp.dot(rest, matrix[table, :, here], preferred_element_type=jnp.float32)

    spectrum = [product(0, 1, 0, slice(0, size)), product(1, 1, 0, slice(size, 2 * size))]
    mixed = product(2, 6, 2, slice(None))
    for j in range(3):
        real, imag = mixed[2 * j * rows : (2 * j + 1) * rows], mixed[(2 * j + 1) * rows : (2 * j + 2) * rows]
        spectrum += [real[:, :size] + imag[:, size:], imag[:, :size] - real[:, size:]]
    for copy in copies[1:4] + copies[8:]:
        copy.wait()
    facts = (squares, ramp, turns, angles, defocus, starts)
    sends = send_patches(
        slots, slices_owned, spectrum, matrix.at[2], matrix.at[4], columns, facts, scratch, out_refs
    )
    for copy in sends:
        copy.wait()


def column_filtered(slots, slices_owned, image, angles, defocus, starts):
    rows, columns = image.shape
    size = columns // RADIX
    count = len(slots)
    matrices = jnp.asarray(column_tables(columns))
    away = pl.BlockSpec(memory_space=pl.ANY)
    flops = 2 * rows * size * size * (42 + 14 * count)
    sent = pl.pallas_call(
        functools.partial(column_kernel, slots, slices_owned),
        out_shape=[jax.ShapeDtypeStruct(packed_shape(rows), jnp.bfloat16)] * count,
        in_specs=[away] * 5,
        out_specs=[away] * count,
        scratch_shapes=[
            pltpu.VMEM((rows, columns), jnp.bfloat16),
            pltpu.VMEM(matrices.shape, jnp.bfloat16),
            pltpu.SMEM(angles.shape, jnp.float32),
            pltpu.SMEM(defocus.shape, jnp.int32),
            pltpu.SMEM(starts.shape, jnp.int32),
            pltpu.VMEM((8, rows, size), jnp.bfloat16),
            pltpu.VMEM((8, rows, size), jnp.bfloat16),
            pltpu.VMEM((2, count * rows, size), jnp.float32),
            pltpu.VMEM((6, count * rows, 2 * size), jnp.float32),
            pltpu.VMEM((count * rows, columns), jnp.float32),
            pltpu.VMEM((count, *packed_shape(rows)), jnp.bfloat16),
            pltpu.SemaphoreType.DMA((count,)),
            pltpu.SemaphoreType.DMA((9,)),
        ],
        compiler_params=pltpu.CompilerParams(vmem_limit_bytes=60 * 2**20),
        cost_estimate=pl.CostEstimate(flops=flops, bytes_accessed=3 * 2**20, transcendentals=0),
        name="column_filter",
    )(image, matrices, angles, defocus, starts)
    return dict(zip(slots, sent))


def after(array, *others):
    away = pl.BlockSpec(memory_space=pl.ANY)
    return pl.pallas_call(
        lambda *refs: None,
        out_shape=jax.ShapeDtypeStruct(array.shape, array.dtype),
        in_specs=[away] * (1 + len(others)),
        out_specs=away,
        input_output_aliases={0: 0},
        compiler_params=pltpu.CompilerParams(vmem_limit_bytes=2**20),
        cost_estimate=pl.CostEstimate(flops=0, bytes_accessed=0, transcendentals=0),
        name="after",
    )(array, *others)


def prepare_kernel(slots, slices_owned, angles, defocus, waves, rows_ref, weights_ref, mine, order):
    tilt, row = lax.axis_index("tilt"), lax.axis_index("row")
    slab, local_first = tilt * slices_owned // SLAB, tilt * slices_owned % SLAB
    full_rows = waves.shape[1]
    rows = rows_ref.shape[0] // slots
    half = full_rows // 2
    column = lax.broadcasted_iota(jnp.int32, (8, full_rows), 1)
    freq = jnp.where(column <= half, column, column - half)
    count = jnp.where((freq == 0) | (freq == half), 1.0, 2.0) / full_rows
    scales = [(flip_sign(freq * freq, defocus[tilt ^ slot, slab], full_rows) * count)[:1] for slot in range(slots)]
    for part in range(2):
        for block in range(full_rows // rows):
            there = pl.ds(pl.multiple_of((row ^ block) * rows, rows), rows)
            order[part, block * rows : (block + 1) * rows, :] = waves[part, there, :]
        own = order[part, :rows, :].astype(jnp.float32)
        for slot in range(slots):
            mine[part, slot * rows : (slot + 1) * rows, :] = (own * scales[slot]).astype(jnp.bfloat16)

    def product(left, right):
        over = (((1,), (1,)), ((), ()))
        return lax.dot_general(mine[left], order[right], over, preferred_element_type=jnp.float32)

    rows_ref[...] = (product(0, 0) + product(0, 1) + product(1, 0)).astype(jnp.bfloat16)

    place = lax.broadcasted_iota(jnp.int32, (REACH, XBW), 0).astype(jnp.float32)
    across = lax.broadcasted_iota(jnp.int32, (1, XBW), 1).astype(jnp.float32)
    for slot in range(slots):
        cosine, sine, first_tap = reach_of(angles[tilt ^ slot])
        tap = place + first_tap.astype(jnp.float32)

        def one_slice(c, carry):
            offset = (local_first + c).astype(jnp.float32) - 0.5 * (SLAB - 1)
            centre = 0.5 * XBW + across * cosine + offset * sine
            there = pl.ds(pl.multiple_of(c * XBW, XBW), XBW)
            weights = jnp.maximum(0.0, 1.0 - jnp.abs(tap - centre))
            weights_ref[slot, :MAIN, there] = weights[:MAIN].astype(jnp.bfloat16)
            rest = jnp.concatenate([weights[MAIN:]] * XBLK, 0)
            weights_ref[slot, MAIN:, there] = rest.astype(jnp.bfloat16)
            return carry

        lax.fori_loop(0, slices_owned, one_slice, 0, unroll=2)


def prepared(slots, slices_owned, rows, full_rows, angles, defocus):
    smem, vmem = pl.BlockSpec(memory_space=pltpu.SMEM), pl.BlockSpec(memory_space=pltpu.VMEM)
    return pl.pallas_call(
        functools.partial(prepare_kernel, slots, slices_owned),
        out_shape=[
            jax.ShapeDtypeStruct((slots * rows, full_rows), jnp.bfloat16),
            jax.ShapeDtypeStruct((slots, MAIN + XBLK * REST, slices_owned * XBW), jnp.bfloat16),
        ],
        in_specs=[smem] * 2 + [vmem],
        out_specs=[vmem] * 2,
        scratch_shapes=[
            pltpu.VMEM((2, slots * rows, full_rows), jnp.bfloat16),
            pltpu.VMEM((2, full_rows, full_rows), jnp.bfloat16),
        ],
        compiler_params=pltpu.CompilerParams(vmem_limit_bytes=32 * 2**20),
        cost_estimate=pl.CostEstimate(flops=2**31, bytes_accessed=6 * 2**20, transcendentals=0),
        name="prepare",
    )(angles, defocus, jnp.asarray(row_tables(full_rows)))


def unpacked(packed):
    rows = 4 * packed.shape[0] // (4 * XBLK + 1)
    beside = packed[XBLK * rows :].astype(jnp.float32)
    quarters = [pltpu.roll(beside, MAIN - q * XBLK * REST, 1) if q else beside for q in range(4)]
    rest = jnp.concatenate(quarters, 0).astype(jnp.bfloat16)
    return jnp.concatenate([packed[block * rows : (block + 1) * rows] for block in range(XBLK)] + [rest], 1)


def corrected_patches(slots, row_devices, rows_ref, patch_refs):
    parts = []
    for group in slots:
        refs, patch_refs = patch_refs[:row_devices], patch_refs[row_devices:]
        height = refs[0].shape[0] // len(group)
        for i, slot in enumerate(group):
            patches = jnp.concatenate([unpacked(ref[i * height : (i + 1) * height]) for ref in refs], 0)
            rows = patches.shape[0] // row_devices
            image = jnp.dot(rows_ref[slot * rows : (slot + 1) * rows, :], patches, preferred_element_type=jnp.float32)
            lane = lax.broadcasted_iota(jnp.int32, (rows, MAIN), 1) // REST
            main = jnp.concatenate([image[:, block * MAIN : (block + 1) * MAIN] for block in range(XBLK)], 0)
            rest = [jnp.where(lane == block, image[:, XBLK * MAIN :], 0.0) for block in range(XBLK)]
            rest = jnp.concatenate(rest, 0)[:, : XBLK * REST]
            parts.append((slot, jnp.concatenate([main, rest], 1).astype(jnp.bfloat16)))
    return parts


def sum_kernel(slots, row_devices, rows_ref, weights_ref, *refs):
    total_ref = refs[-1]
    (slot, part), *others = corrected_patches(slots, row_devices, rows_ref, refs[:-1])
    step = 4 * XBW
    for first in range(0, total_ref.shape[1], step):
        here = slice(first, first + step)
        total = jnp.dot(part, weights_ref[slot, :, here], preferred_element_type=jnp.float32)
        for other, more in others:
            total += jnp.dot(more, weights_ref[other, :, here], preferred_element_type=jnp.float32)
        total_ref[:, here] = total


def finish_kernel(factor, slots, row_devices, rows_ref, weights_ref, total_ref, *refs):
    patch_refs = refs[: len(slots) * row_devices]
    out_ref, out, sems = refs[len(slots) * row_devices :]
    rows = total_ref.shape[0] // XBLK
    parts = corrected_patches(slots, row_devices, rows_ref, patch_refs)
    step = 4
    copies = []
    for group in range(out.shape[0] // step):
        here = slice(group * step * XBW, (group + 1) * step * XBW)
        total = total_ref[:, here]
        for slot, part in parts:
            total += jnp.dot(part, weights_ref[slot, :, here], preferred_element_type=jnp.float32)
        for c in range(step):
            for block in range(XBLK):
                out[group * step + c, :, block * XBW : (block + 1) * XBW] = (
                    factor * total[block * rows : (block + 1) * rows, c * XBW : (c + 1) * XBW]
                ).astype(jnp.bfloat16)
        part = pl.ds(group * step, step)
        copies.append(pltpu.make_async_copy(out.at[part], out_ref.at[part], sems.at[group]))
        copies[-1].start()
    for copy in copies:
        copy.wait()


def interpolation(kernel, slots, weights, row_filters, patches, totals, **call):
    vmem = pl.BlockSpec(memory_space=pltpu.VMEM)
    operands = [row_filters, weights, *totals, *(block for group in patches for block in group)]
    return pl.pallas_call(
        functools.partial(kernel, slots, len(patches[0])),
        in_specs=[vmem] * len(operands),
        compiler_params=pltpu.CompilerParams(vmem_limit_bytes=32 * 2**20),
        cost_estimate=pl.CostEstimate(flops=0, bytes_accessed=0, transcendentals=0),
        **call,
    )(*operands)


def summed(row_filters, weights, patches, slots):
    return interpolation(
        sum_kernel,
        slots,
        weights,
        row_filters,
        patches,
        [],
        out_shape=jax.ShapeDtypeStruct((XBLK * row_filters.shape[0] // weights.shape[0], weights.shape[2]), jnp.float32),
        out_specs=pl.BlockSpec(memory_space=pltpu.VMEM),
        name="sum_early_tilts",
    )


def finished(row_filters, weights, total, patches, slots, factor):
    shape = (weights.shape[2] // XBW, row_filters.shape[0] // weights.shape[0], XBLK * XBW)
    return interpolation(
        functools.partial(finish_kernel, factor),
        slots,
        weights,
        row_filters,
        patches,
        [total],
        out_shape=jax.ShapeDtypeStruct(shape, jnp.bfloat16),
        out_specs=pl.BlockSpec(memory_space=pl.ANY),
        scratch_shapes=[pltpu.VMEM(shape, jnp.bfloat16), pltpu.SemaphoreType.DMA((shape[0] // 4,))],
        name="finish_volume",
    )


def exchange(array, axis, distance):
    count = lax.axis_size(axis)
    return lax.ppermute(array, axis, [(i, i ^ distance) for i in range(count)])


def gather_rows(array, awaited=()):
    blocks = {0: array}
    bit = lax.axis_size("row") // 2
    while bit:
        if bit == 1 and awaited:
            blocks = {d: after(block, *awaited) if d else block for d, block in blocks.items()}
        blocks.update({d ^ bit: exchange(block, "row", bit) for d, block in blocks.items()})
        bit //= 2
    return [blocks[d] for d in sorted(blocks)]


def per_device(projections, tilt_angle, band_start, defocus):
    _, rows, _ = projections.shape
    row_devices, tilt_devices = lax.axis_size("row"), lax.axis_size("tilt")
    slices_owned = SLICES // tilt_devices
    far, near = list(range(tilt_devices - 1, 1, -1)), list(range(min(2, tilt_devices)))
    sent = column_filtered(far + near, slices_owned, projections[0], tilt_angle, defocus, band_start)
    arrived = {d: exchange(sent[d], "tilt", d) if d else sent[d] for d in far[:-1] + near}
    arrived[far[-1]] = exchange(after(sent[far[-1]], arrived[1]), "tilt", far[-1])
    row_filters, weights = prepared(tilt_devices, slices_owned, rows, rows * row_devices, tilt_angle, defocus)
    early = [gather_rows(jnp.concatenate([arrived[d] for d in near]))]
    total = summed(row_filters, weights, early, [near])
    late = [gather_rows(after(arrived[d], row_filters) if d == far[-1] else arrived[d]) for d in far]
    return finished(row_filters, weights, total, late, [[d] for d in far], 1.0 / math.sqrt(tilt_devices))


def solution(mesh):
    in_specs = (
        P(("group", "tilt"), "row", None),
        P("group"),
        P("group", None, None),
        P("group", None),
    )
    out_specs = P(("group", "tilt"), "row", None)
    return jax.shard_map(
        per_device, mesh=mesh, in_specs=in_specs, out_specs=out_specs, check_vma=False
    )
```

```python
import functools
import math

import jax
import jax.numpy as jnp
import numpy as np
from jax import lax
from jax.experimental import pallas as pl
from jax.experimental.pallas import tpu as pltpu
from jax.sharding import PartitionSpec as P

SLAB = 16
XBW = 128
BAND = 256
XBLK = 4
SLICES = 64
RADIX = 8
MAIN = 128
REST = 8
REACH = MAIN + REST
WINDOW = 384
ROOT = math.sqrt(0.5)


def split(table):
    high = table.astype(jnp.bfloat16)
    return high, (table - high.astype(np.float64)).astype(jnp.bfloat16)


def column_tables(columns):
    size = columns // RADIX
    half = size // 2
    u = np.arange(size)[:, None]

    def angles(freq):
        return 2.0 * np.pi * ((u * freq[None, :]) % columns) / columns

    k0, s0 = RADIX * np.arange(half + 1), RADIX * np.arange(1, half)
    k4 = RADIX * np.arange(half) + 4
    m0 = np.concatenate([np.cos(angles(k0)), -np.sin(angles(s0))], 1)
    m4 = np.concatenate([np.cos(angles(k4)), -np.sin(angles(k4))], 1)
    full = angles(RADIX * np.arange(size))
    waves = np.concatenate([np.cos(full), np.sin(full)], 1)
    ends = np.concatenate([m0, m4], 1)

    matrices = np.stack([*split(ends), *split(waves), np.concatenate([m0.T, m4.T], 1).astype(jnp.bfloat16)])
    return matrices


def column_lines(columns):
    size = columns // RADIX
    half = size // 2
    line = lax.broadcasted_iota(jnp.int32, (8, size), 0)
    u = lax.broadcasted_iota(jnp.int32, (8, size), 1)
    freq = jnp.where(line == 0, RADIX * jnp.where(u <= half, u, u - half), RADIX * (u & (half - 1)) + 4)
    freq = jnp.where(line < 2, freq, RADIX * u + line // 2)
    fold = jnp.minimum(freq, columns - freq)
    count = jnp.where((fold == 0) | (fold == columns // 2), 1.0, 2.0)
    gain = count * (fold.astype(jnp.float32) + 0.5) * (2.0 / (columns * columns))
    angle = (u * (line + 1)).astype(jnp.float32) * (2.0 * math.pi / columns)
    return fold * fold, gain, jnp.cos(angle), jnp.sin(angle)


def row_tables(full_rows):
    half = full_rows // 2
    column = np.arange(full_rows)
    freq = np.where(column <= half, column, column - half)
    angle = 2.0 * np.pi * (np.arange(full_rows)[:, None] * freq[None, :] % full_rows) / full_rows
    return np.stack(split(np.where(column[None, :] <= half, np.cos(angle), np.sin(angle))))


def packed_shape(rows):
    return (XBLK * rows + rows // 4, MAIN)


def flip_sign(squares, defocus, length):
    cycles = lax.div(squares * defocus, jnp.int32(length * length))
    return (1 - 2 * (cycles & 1)).astype(jnp.float32)


def fetched(sources, targets, sems):
    copies = [pltpu.make_async_copy(s, t, sems.at[i]) for i, (s, t) in enumerate(zip(sources, targets))]
    for copy in copies:
        copy.start()
    return copies


def reach_of(angle):
    line = jnp.full((8, XBW), angle, jnp.float32)
    cosine, sine = jnp.cos(line), jnp.sin(line)
    lowest = 0.5 * XBW + jnp.minimum((XBW - 1) * cosine, 0.0) - 0.5 * (SLAB - 1) * jnp.abs(sine)
    first = jnp.clip(jnp.floor(lowest) - 2.0, 0.0, float(BAND - REACH))
    return cosine[:1], sine[:1], jnp.max(first).astype(jnp.int32)


def butterflies(image, turns, zhi, zlo):
    rows, columns = image.shape
    size = columns // RADIX

    def step(i, carry):
        here = pl.ds(pl.multiple_of(i * 16, 16), 16)
        x = [image[here, m * size : (m + 1) * size].astype(jnp.float32) for m in range(8)]
        p0, p1, p2, p3 = (x[m] + x[m + 4] for m in range(4))
        q0, q1, q2, q3 = (x[m] - x[m + 4] for m in range(4))
        e, f = p0 + p2, p1 + p3
        g, h = ROOT * (q1 - q3), ROOT * (q1 + q3)
        z = [e + f, e - f]
        for j, (real, imag) in enumerate([(q0 + g, -q2 - h), (p0 - p2, p3 - p1), (q0 - g, q2 - h)]):
            c, s = turns[2 * j], turns[2 * j + 1]
            z += [real * c + imag * s, imag * c - real * s]
        for line in range(8):
            top = z[line].astype(jnp.bfloat16)
            zhi[line, here, :] = top
            zlo[line, here, :] = (z[line] - top.astype(jnp.float32)).astype(jnp.bfloat16)
        return carry

    lax.fori_loop(0, rows // 16, step, 0)


def inverse_butterflies(ends, waves, turns, turned, first, rows):
    columns = turned.shape[1]
    size = columns // RADIX
    for top in range(first, first + rows, 8):
        here = slice(top, top + 8)
        r, s = [], []
        for j in range(3):
            c, d = turns[2 * j], turns[2 * j + 1]
            real = waves[2 * j, here, :size] - waves[2 * j + 1, here, size:]
            imag = waves[2 * j, here, size:] + waves[2 * j + 1, here, :size]
            r.append(real * c - imag * d)
            s.append(real * d + imag * c)
        e, f = ends[0, here, :] + ends[1, here, :], ends[0, here, :] - ends[1, here, :]
        a, b, c, d = r[0] + r[2], r[0] - r[2], s[0] + s[2], s[0] - s[2]
        even0, even2, odd1, odd3 = e + r[1], e - r[1], f - s[1], f + s[1]
        g, h = ROOT * (b - c), ROOT * (b + c)
        out = [even0 + a, odd1 + g, even2 - d, odd3 - h, even0 - a, odd1 - g, even2 + d, odd3 + h]
        for m in range(8):
            turned[here, m * size : (m + 1) * size] = out[m]


def send_patches(slots, slices_owned, spectrum, wave_table, end_table, columns, facts, scratch, out_refs):
    squares, ramp, turns, angles, defocus, starts = facts
    ends, waves, turned, out, out_sems = scratch
    rows, size = spectrum[0].shape
    tilt = lax.axis_index("tilt")
    lane = lax.broadcasted_iota(jnp.int32, (rows, MAIN), 1) // REST
    _, _, first_tap = reach_of(angles[tilt])
    slabs = [(tilt ^ slot) * slices_owned // SLAB for slot in slots]

    def transform(k):
        slab = slabs[k]
        mine = slice(k * rows, (k + 1) * rows)
        gain = flip_sign(squares, defocus[tilt, slab], columns) * ramp
        filtered = [(spectrum[i] * gain[i : i + 1, :]).astype(jnp.bfloat16) for i in range(8)]
        for i in range(2):
            table = end_table[:, i * size : (i + 1) * size]
            ends[i, mine, :] = jnp.dot(filtered[i], table, preferred_element_type=jnp.float32)
        both = jnp.dot(jnp.concatenate(filtered[2:], 0), wave_table[...], preferred_element_type=jnp.float32)
        for i in range(6):
            waves[i, mine, :] = both[i * rows : (i + 1) * rows]
    sends = []
    transform(0)
    for k, slab in enumerate(slabs):
        if k + 1 < len(slabs):
            transform(k + 1)
        inverse_butterflies(ends, waves, turns, turned, k * rows, rows)
        rest = jnp.zeros((rows, MAIN), jnp.float32)
        for block in range(XBLK):
            start = starts[tilt, slab, block] + first_tap
            base = pl.multiple_of(jnp.minimum((start // 128) * 128, columns - WINDOW), 128)
            window = turned[k * rows : (k + 1) * rows, pl.ds(base, WINDOW)]
            shift = base - start
            reach = pltpu.roll(window, jnp.where(shift < 0, shift + WINDOW, shift), 1)[:, : 2 * MAIN]
            out[k, block * rows : (block + 1) * rows, :] = reach[:, :MAIN].astype(jnp.bfloat16)
            last = reach[:, MAIN:]
            rest = jnp.where(lane == block, pltpu.roll(last, block * REST, 1) if block else last, rest)
        quarter = rows // 4
        beside = rest[:quarter]
        for q in range(1, 4):
            moved = pltpu.roll(rest[q * quarter : (q + 1) * quarter], q * XBLK * REST, 1)
            beside = jnp.where(lane[:quarter] // XBLK == q, moved, beside)
        out[k, XBLK * rows :, :] = beside.astype(jnp.bfloat16)
        sends.append(pltpu.make_async_copy(out.at[k], out_refs[k], out_sems.at[k]))
        sends[-1].start()
    return sends


def column_kernel(slots, slices_owned, image_ref, matrix_ref, angle_ref, defocus_ref, starts_ref, *refs):
    count = len(slots)
    out_refs = refs[:count]
    image, matrix, angles, defocus, starts, zhi, zlo, *scratch, sems = refs[count:]
    rows, columns = image.shape
    size = columns // RADIX
    copies = fetched(
        [image_ref, angle_ref, defocus_ref, starts_ref] + [matrix_ref.at[i] for i in range(5)],
        [image, angles, defocus, starts] + [matrix.at[i] for i in range(5)],
        sems,
    )
    squares, ramp, cosine_turns, sine_turns = column_lines(columns)
    turns = [t[j : j + 1, :] for j in range(3) for t in (cosine_turns, sine_turns)]
    copies[0].wait()
    butterflies(image, turns, zhi, zlo)
    for copy in copies[4:8]:
        copy.wait()

    def product(first, lines, table, here):
        top = zhi[first : first + lines].reshape(lines * rows, size)
        rest = zlo[first : first + lines].reshape(lines * rows, size)
        total = jnp.dot(top, matrix[table, :, here], preferred_element_type=jnp.float32)
        total += jnp.dot(top, matrix[table + 1, :, here], preferred_element_type=jnp.float32)
        return total + jnp.dot(rest, matrix[table, :, here], preferred_element_type=jnp.float32)

    spectrum = [product(0, 1, 0, slice(0, size)), product(1, 1, 0, slice(size, 2 * size))]
    mixed = product(2, 6, 2, slice(None))
    for j in range(3):
        real, imag = mixed[2 * j * rows : (2 * j + 1) * rows], mixed[(2 * j + 1) * rows : (2 * j + 2) * rows]
        spectrum += [real[:, :size] + imag[:, size:], imag[:, :size] - real[:, size:]]
    for copy in copies[1:4] + copies[8:]:
        copy.wait()
    facts = (squares, ramp, turns, angles, defocus, starts)
    sends = send_patches(
        slots, slices_owned, spectrum, matrix.at[2], matrix.at[4], columns, facts, scratch, out_refs
    )
    for copy in sends:
        copy.wait()


def column_filtered(slots, slices_owned, image, angles, defocus, starts):
    rows, columns = image.shape
    size = columns // RADIX
    count = len(slots)
    matrices = jnp.asarray(column_tables(columns))
    away = pl.BlockSpec(memory_space=pl.ANY)
    flops = 2 * rows * size * size * (42 + 14 * count)
    sent = pl.pallas_call(
        functools.partial(column_kernel, slots, slices_owned),
        out_shape=[jax.ShapeDtypeStruct(packed_shape(rows), jnp.bfloat16)] * count,
        in_specs=[away] * 5,
        out_specs=[away] * count,
        scratch_shapes=[
            pltpu.VMEM((rows, columns), jnp.bfloat16),
            pltpu.VMEM(matrices.shape, jnp.bfloat16),
            pltpu.SMEM(angles.shape, jnp.float32),
            pltpu.SMEM(defocus.shape, jnp.int32),
            pltpu.SMEM(starts.shape, jnp.int32),
            pltpu.VMEM((8, rows, size), jnp.bfloat16),
            pltpu.VMEM((8, rows, size), jnp.bfloat16),
            pltpu.VMEM((2, count * rows, size), jnp.float32),
            pltpu.VMEM((6, count * rows, 2 * size), jnp.float32),
            pltpu.VMEM((count * rows, columns), jnp.float32),
            pltpu.VMEM((count, *packed_shape(rows)), jnp.bfloat16),
            pltpu.SemaphoreType.DMA((count,)),
            pltpu.SemaphoreType.DMA((9,)),
        ],
        compiler_params=pltpu.CompilerParams(vmem_limit_bytes=215 * 2**18),
        cost_estimate=pl.CostEstimate(flops=flops, bytes_accessed=3 * 2**20, transcendentals=0),
        name="column_filter",
    )(image, matrices, angles, defocus, starts)
    return dict(zip(slots, sent))


def after(array, *others):
    away = pl.BlockSpec(memory_space=pl.ANY)
    return pl.pallas_call(
        lambda *refs: None,
        out_shape=jax.ShapeDtypeStruct(array.shape, array.dtype),
        in_specs=[away] * (1 + len(others)),
        out_specs=away,
        input_output_aliases={0: 0},
        compiler_params=pltpu.CompilerParams(vmem_limit_bytes=2**20),
        cost_estimate=pl.CostEstimate(flops=0, bytes_accessed=0, transcendentals=0),
        name="after",
    )(array, *others)


def prepare_kernel(slots, slices_owned, angles, defocus, waves, rows_ref, weights_ref, mine, order):
    tilt, row = lax.axis_index("tilt"), lax.axis_index("row")
    slab, local_first = tilt * slices_owned // SLAB, tilt * slices_owned % SLAB
    full_rows = waves.shape[1]
    rows = rows_ref.shape[0] // slots
    half = full_rows // 2
    column = lax.broadcasted_iota(jnp.int32, (8, full_rows), 1)
    freq = jnp.where(column <= half, column, column - half)
    count = jnp.where((freq == 0) | (freq == half), 1.0, 2.0) / full_rows
    scales = [(flip_sign(freq * freq, defocus[tilt ^ slot, slab], full_rows) * count)[:1] for slot in range(slots)]
    for part in range(2):
        for block in range(full_rows // rows):
            there = pl.ds(pl.multiple_of((row ^ block) * rows, rows), rows)
            order[part, block * rows : (block + 1) * rows, :] = waves[part, there, :]
        own = order[part, :rows, :].astype(jnp.float32)
        for slot in range(slots):
            mine[part, slot * rows : (slot + 1) * rows, :] = (own * scales[slot]).astype(jnp.bfloat16)

    def product(left, right):
        over = (((1,), (1,)), ((), ()))
        return lax.dot_general(mine[left], order[right], over, preferred_element_type=jnp.float32)

    rows_ref[...] = (product(0, 0) + product(0, 1) + product(1, 0)).astype(jnp.bfloat16)

    place = lax.broadcasted_iota(jnp.int32, (REACH, XBW), 0).astype(jnp.float32)
    across = lax.broadcasted_iota(jnp.int32, (1, XBW), 1).astype(jnp.float32)
    for slot in range(slots):
        cosine, sine, first_tap = reach_of(angles[tilt ^ slot])
        tap = place + first_tap.astype(jnp.float32)

        def one_slice(c, carry):
            offset = (local_first + c).astype(jnp.float32) - 0.5 * (SLAB - 1)
            centre = 0.5 * XBW + across * cosine + offset * sine
            there = pl.ds(pl.multiple_of(c * XBW, XBW), XBW)
            weights = jnp.maximum(0.0, 1.0 - jnp.abs(tap - centre))
            weights_ref[slot, :MAIN, there] = weights[:MAIN].astype(jnp.bfloat16)
            rest = jnp.concatenate([weights[MAIN:]] * XBLK, 0)
            weights_ref[slot, MAIN:, there] = rest.astype(jnp.bfloat16)
            return carry

        lax.fori_loop(0, slices_owned, one_slice, 0, unroll=2)


def prepared(slots, slices_owned, rows, full_rows, angles, defocus):
    smem, vmem = pl.BlockSpec(memory_space=pltpu.SMEM), pl.BlockSpec(memory_space=pltpu.VMEM)
    return pl.pallas_call(
        functools.partial(prepare_kernel, slots, slices_owned),
        out_shape=[
            jax.ShapeDtypeStruct((slots * rows, full_rows), jnp.bfloat16),
            jax.ShapeDtypeStruct((slots, MAIN + XBLK * REST, slices_owned * XBW), jnp.bfloat16),
        ],
        in_specs=[smem] * 2 + [vmem],
        out_specs=[vmem] * 2,
        scratch_shapes=[
            pltpu.VMEM((2, slots * rows, full_rows), jnp.bfloat16),
            pltpu.VMEM((2, full_rows, full_rows), jnp.bfloat16),
        ],
        compiler_params=pltpu.CompilerParams(vmem_limit_bytes=32 * 2**20),
        cost_estimate=pl.CostEstimate(flops=2**31, bytes_accessed=6 * 2**20, transcendentals=0),
        name="prepare",
    )(angles, defocus, jnp.asarray(row_tables(full_rows)))


def unpacked(packed):
    rows = 4 * packed.shape[0] // (4 * XBLK + 1)
    beside = packed[XBLK * rows :].astype(jnp.float32)
    quarters = [pltpu.roll(beside, MAIN - q * XBLK * REST, 1) if q else beside for q in range(4)]
    rest = jnp.concatenate(quarters, 0).astype(jnp.bfloat16)
    return jnp.concatenate([packed[block * rows : (block + 1) * rows] for block in range(XBLK)] + [rest], 1)


def corrected_patches(slots, row_devices, rows_ref, patch_refs):
    parts = []
    for group in slots:
        refs, patch_refs = patch_refs[:row_devices], patch_refs[row_devices:]
        height = refs[0].shape[0] // len(group)
        for i, slot in enumerate(group):
            patches = jnp.concatenate([unpacked(ref[i * height : (i + 1) * height]) for ref in refs], 0)
            rows = patches.shape[0] // row_devices
            image = jnp.dot(rows_ref[slot * rows : (slot + 1) * rows, :], patches, preferred_element_type=jnp.float32)
            lane = lax.broadcasted_iota(jnp.int32, (rows, MAIN), 1) // REST
            main = jnp.concatenate([image[:, block * MAIN : (block + 1) * MAIN] for block in range(XBLK)], 0)
            rest = [jnp.where(lane == block, image[:, XBLK * MAIN :], 0.0) for block in range(XBLK)]
            rest = jnp.concatenate(rest, 0)[:, : XBLK * REST]
            parts.append((slot, jnp.concatenate([main, rest], 1).astype(jnp.bfloat16)))
    return parts


def sum_kernel(slots, row_devices, rows_ref, weights_ref, *refs):
    total_ref = refs[-1]
    (slot, part), *others = corrected_patches(slots, row_devices, rows_ref, refs[:-1])
    step = 4 * XBW
    for first in range(0, total_ref.shape[1], step):
        here = slice(first, first + step)
        total = jnp.dot(part, weights_ref[slot, :, here], preferred_element_type=jnp.float32)
        for other, more in others:
            total += jnp.dot(more, weights_ref[other, :, here], preferred_element_type=jnp.float32)
        total_ref[:, here] = total


def finish_kernel(factor, slots, row_devices, rows_ref, weights_ref, total_ref, *refs):
    patch_refs = refs[: len(slots) * row_devices]
    out_ref, out, sems = refs[len(slots) * row_devices :]
    rows = total_ref.shape[0] // XBLK
    parts = corrected_patches(slots, row_devices, rows_ref, patch_refs)
    step = 4
    copies = []
    for group in range(out.shape[0] // step):
        here = slice(group * step * XBW, (group + 1) * step * XBW)
        total = total_ref[:, here]
        for slot, part in parts:
            total += jnp.dot(part, weights_ref[slot, :, here], preferred_element_type=jnp.float32)
        for c in range(step):
            for block in range(XBLK):
                out[group * step + c, :, block * XBW : (block + 1) * XBW] = (
                    factor * total[block * rows : (block + 1) * rows, c * XBW : (c + 1) * XBW]
                ).astype(jnp.bfloat16)
        part = pl.ds(group * step, step)
        copies.append(pltpu.make_async_copy(out.at[part], out_ref.at[part], sems.at[group]))
        copies[-1].start()
    for copy in copies:
        copy.wait()


def interpolation(kernel, slots, weights, row_filters, patches, totals, **call):
    vmem = pl.BlockSpec(memory_space=pltpu.VMEM)
    operands = [row_filters, weights, *totals, *(block for group in patches for block in group)]
    return pl.pallas_call(
        functools.partial(kernel, slots, len(patches[0])),
        in_specs=[vmem] * len(operands),
        compiler_params=pltpu.CompilerParams(vmem_limit_bytes=32 * 2**20),
        cost_estimate=pl.CostEstimate(flops=0, bytes_accessed=0, transcendentals=0),
        **call,
    )(*operands)


def summed(row_filters, weights, patches, slots):
    return interpolation(
        sum_kernel,
        slots,
        weights,
        row_filters,
        patches,
        [],
        out_shape=jax.ShapeDtypeStruct((XBLK * row_filters.shape[0] // weights.shape[0], weights.shape[2]), jnp.float32),
        out_specs=pl.BlockSpec(memory_space=pltpu.VMEM),
        name="sum_early_tilts",
    )


def finished(row_filters, weights, total, patches, slots, factor):
    shape = (weights.shape[2] // XBW, row_filters.shape[0] // weights.shape[0], XBLK * XBW)
    return interpolation(
        functools.partial(finish_kernel, factor),
        slots,
        weights,
        row_filters,
        patches,
        [total],
        out_shape=jax.ShapeDtypeStruct(shape, jnp.bfloat16),
        out_specs=pl.BlockSpec(memory_space=pl.ANY),
        scratch_shapes=[pltpu.VMEM(shape, jnp.bfloat16), pltpu.SemaphoreType.DMA((shape[0] // 4,))],
        name="finish_volume",
    )


def exchange(array, axis, distance):
    count = lax.axis_size(axis)
    return lax.ppermute(array, axis, [(i, i ^ distance) for i in range(count)])


def gather_rows(array, awaited=()):
    blocks = {0: array}
    bit = lax.axis_size("row") // 2
    while bit:
        if bit == 1 and awaited:
            blocks = {d: after(block, *awaited) if d else block for d, block in blocks.items()}
        blocks.update({d ^ bit: exchange(block, "row", bit) for d, block in blocks.items()})
        bit //= 2
    return [blocks[d] for d in sorted(blocks)]


def per_device(projections, tilt_angle, band_start, defocus):
    _, rows, _ = projections.shape
    row_devices, tilt_devices = lax.axis_size("row"), lax.axis_size("tilt")
    slices_owned = SLICES // tilt_devices
    far, near = list(range(tilt_devices - 1, 1, -1)), list(range(min(2, tilt_devices)))
    sent = column_filtered(far + near, slices_owned, projections[0], tilt_angle, defocus, band_start)
    arrived = {d: exchange(sent[d], "tilt", d) if d else sent[d] for d in far + near}
    row_filters, weights = prepared(tilt_devices, slices_owned, rows, rows * row_devices, tilt_angle, defocus)
    early = [gather_rows(jnp.concatenate([arrived[d] for d in near]))]
    total = summed(row_filters, weights, early, [near])
    late = [gather_rows(after(arrived[d], row_filters) if d == far[-1] else arrived[d]) for d in far]
    return finished(row_filters, weights, total, late, [[d] for d in far], 1.0 / math.sqrt(tilt_devices))


def solution(mesh):
    in_specs = (
        P(("group", "tilt"), "row", None),
        P("group"),
        P("group", None, None),
        P("group", None),
    )
    out_specs = P(("group", "tilt"), "row", None)
    return jax.shard_map(
        per_device, mesh=mesh, in_specs=in_specs, out_specs=out_specs, check_vma=False
    )
```

```python
import functools
import math

import jax
import jax.numpy as jnp
import numpy as np
from jax import lax
from jax.experimental import pallas as pl
from jax.experimental.pallas import tpu as pltpu
from jax.sharding import PartitionSpec as P

SLAB = 16
XBW = 128
BAND = 256
XBLK = 4
SLICES = 64
RADIX = 8
MAIN = 128
REST = 8
REACH = MAIN + REST
WINDOW = 384
ROOT = math.sqrt(0.5)


def split(table):
    high = table.astype(jnp.bfloat16)
    return high, (table - high.astype(np.float64)).astype(jnp.bfloat16)


def column_tables(columns):
    size = columns // RADIX
    half = size // 2
    u = np.arange(size)[:, None]

    def angles(freq):
        return 2.0 * np.pi * ((u * freq[None, :]) % columns) / columns

    k0, s0 = RADIX * np.arange(half + 1), RADIX * np.arange(1, half)
    k4 = RADIX * np.arange(half) + 4
    m0 = np.concatenate([np.cos(angles(k0)), -np.sin(angles(s0))], 1)
    m4 = np.concatenate([np.cos(angles(k4)), -np.sin(angles(k4))], 1)
    full = angles(RADIX * np.arange(size))
    waves = np.concatenate([np.cos(full), np.sin(full)], 1)
    ends = np.concatenate([m0, m4], 1)

    matrices = np.stack([*split(ends), *split(waves), np.concatenate([m0.T, m4.T], 1).astype(jnp.bfloat16)])
    return matrices


def column_lines(columns):
    size = columns // RADIX
    half = size // 2
    line = lax.broadcasted_iota(jnp.int32, (8, size), 0)
    u = lax.broadcasted_iota(jnp.int32, (8, size), 1)
    freq = jnp.where(line == 0, RADIX * jnp.where(u <= half, u, u - half), RADIX * (u & (half - 1)) + 4)
    freq = jnp.where(line < 2, freq, RADIX * u + line // 2)
    fold = jnp.minimum(freq, columns - freq)
    count = jnp.where((fold == 0) | (fold == columns // 2), 1.0, 2.0)
    gain = count * (fold.astype(jnp.float32) + 0.5) * (2.0 / (columns * columns))
    angle = (u * (line + 1)).astype(jnp.float32) * (2.0 * math.pi / columns)
    return fold * fold, gain, jnp.cos(angle), jnp.sin(angle)


def row_tables(full_rows):
    half = full_rows // 2
    column = np.arange(full_rows)
    freq = np.where(column <= half, column, column - half)
    angle = 2.0 * np.pi * (np.arange(full_rows)[:, None] * freq[None, :] % full_rows) / full_rows
    return np.stack(split(np.where(column[None, :] <= half, np.cos(angle), np.sin(angle))))


def packed_shape(rows):
    return (XBLK * rows + rows // 4, MAIN)


def flip_sign(squares, defocus, length):
    cycles = lax.div(squares * defocus, jnp.int32(length * length))
    return (1 - 2 * (cycles & 1)).astype(jnp.float32)


def fetched(sources, targets, sems):
    copies = [pltpu.make_async_copy(s, t, sems.at[i]) for i, (s, t) in enumerate(zip(sources, targets))]
    for copy in copies:
        copy.start()
    return copies


def reach_of(angle):
    line = jnp.full((8, XBW), angle, jnp.float32)
    cosine, sine = jnp.cos(line), jnp.sin(line)
    lowest = 0.5 * XBW + jnp.minimum((XBW - 1) * cosine, 0.0) - 0.5 * (SLAB - 1) * jnp.abs(sine)
    first = jnp.clip(jnp.floor(lowest) - 2.0, 0.0, float(BAND - REACH))
    return cosine[:1], sine[:1], jnp.max(first).astype(jnp.int32)


def butterflies(image, turns, zhi, zlo, first, count):
    size = image.shape[1] // RADIX
    for top_row in range(first, first + count, 16):
        here = slice(top_row, top_row + 16)
        x = [image[here, m * size : (m + 1) * size].astype(jnp.float32) for m in range(8)]
        p0, p1, p2, p3 = (x[m] + x[m + 4] for m in range(4))
        q0, q1, q2, q3 = (x[m] - x[m + 4] for m in range(4))
        e, f = p0 + p2, p1 + p3
        g, h = ROOT * (q1 - q3), ROOT * (q1 + q3)
        z = [e + f, e - f]
        for j, (real, imag) in enumerate([(q0 + g, -q2 - h), (p0 - p2, p3 - p1), (q0 - g, q2 - h)]):
            c, s = turns[2 * j], turns[2 * j + 1]
            z += [real * c + imag * s, imag * c - real * s]
        for line in range(8):
            top = z[line].astype(jnp.bfloat16)
            zhi[line, here, :] = top
            zlo[line, here, :] = (z[line] - top.astype(jnp.float32)).astype(jnp.bfloat16)


def inverse_butterflies(ends, waves, turns, turned, first, rows):
    columns = turned.shape[1]
    size = columns // RADIX
    for top in range(first, first + rows, 8):
        here = slice(top, top + 8)
        r, s = [], []
        for j in range(3):
            c, d = turns[2 * j], turns[2 * j + 1]
            real = waves[2 * j, here, :size] - waves[2 * j + 1, here, size:]
            imag = waves[2 * j, here, size:] + waves[2 * j + 1, here, :size]
            r.append(real * c - imag * d)
            s.append(real * d + imag * c)
        e, f = ends[0, here, :] + ends[1, here, :], ends[0, here, :] - ends[1, here, :]
        a, b, c, d = r[0] + r[2], r[0] - r[2], s[0] + s[2], s[0] - s[2]
        even0, even2, odd1, odd3 = e + r[1], e - r[1], f - s[1], f + s[1]
        g, h = ROOT * (b - c), ROOT * (b + c)
        out = [even0 + a, odd1 + g, even2 - d, odd3 - h, even0 - a, odd1 - g, even2 + d, odd3 + h]
        for m in range(8):
            turned[here, m * size : (m + 1) * size] = out[m]


def send_patches(slots, slices_owned, spectrum, wave_table, end_table, columns, facts, scratch, out_refs):
    squares, ramp, turns, angles, defocus, starts = facts
    ends, waves, turned, out, out_sems = scratch
    rows, size = spectrum[0].shape
    tilt = lax.axis_index("tilt")
    lane = lax.broadcasted_iota(jnp.int32, (rows, MAIN), 1) // REST
    _, _, first_tap = reach_of(angles[tilt])
    slabs = [(tilt ^ slot) * slices_owned // SLAB for slot in slots]

    def transform(k):
        slab = slabs[k]
        mine = slice(k * rows, (k + 1) * rows)
        gain = flip_sign(squares, defocus[tilt, slab], columns) * ramp
        filtered = [(spectrum[i] * gain[i : i + 1, :]).astype(jnp.bfloat16) for i in range(8)]
        for i in range(2):
            table = end_table[:, i * size : (i + 1) * size]
            ends[i, mine, :] = jnp.dot(filtered[i], table, preferred_element_type=jnp.float32)
        both = jnp.dot(jnp.concatenate(filtered[2:], 0), wave_table[...], preferred_element_type=jnp.float32)
        for i in range(6):
            waves[i, mine, :] = both[i * rows : (i + 1) * rows]
    sends = []
    transform(0)
    for k, slab in enumerate(slabs):
        if k + 1 < len(slabs):
            transform(k + 1)
        inverse_butterflies(ends, waves, turns, turned, k * rows, rows)
        rest = jnp.zeros((rows, MAIN), jnp.float32)
        for block in range(XBLK):
            start = starts[tilt, slab, block] + first_tap
            base = pl.multiple_of(jnp.minimum((start // 128) * 128, columns - WINDOW), 128)
            window = turned[k * rows : (k + 1) * rows, pl.ds(base, WINDOW)]
            shift = base - start
            reach = pltpu.roll(window, jnp.where(shift < 0, shift + WINDOW, shift), 1)[:, : 2 * MAIN]
            out[k, block * rows : (block + 1) * rows, :] = reach[:, :MAIN].astype(jnp.bfloat16)
            last = reach[:, MAIN:]
            rest = jnp.where(lane == block, pltpu.roll(last, block * REST, 1) if block else last, rest)
        quarter = rows // 4
        beside = rest[:quarter]
        for q in range(1, 4):
            moved = pltpu.roll(rest[q * quarter : (q + 1) * quarter], q * XBLK * REST, 1)
            beside = jnp.where(lane[:quarter] // XBLK == q, moved, beside)
        out[k, XBLK * rows :, :] = beside.astype(jnp.bfloat16)
        sends.append(pltpu.make_async_copy(out.at[k], out_refs[k], out_sems.at[k]))
        sends[-1].start()
    return sends


def column_kernel(slots, slices_owned, image_ref, matrix_ref, angle_ref, defocus_ref, starts_ref, *refs):
    count = len(slots)
    out_refs = refs[:count]
    image, matrix, angles, defocus, starts, zhi, zlo, *scratch, sems = refs[count:]
    rows, columns = image.shape
    size = columns // RADIX
    halves = [pl.ds(0, rows // 2), pl.ds(rows // 2, rows // 2)]
    order = [2, 3, 0, 1, 4]
    copies = fetched(
        [image_ref.at[h] for h in halves] + [matrix_ref.at[i] for i in order] + [angle_ref, defocus_ref, starts_ref],
        [image.at[h] for h in halves] + [matrix.at[i] for i in order] + [angles, defocus, starts],
        sems,
    )
    squares, ramp, cosine_turns, sine_turns = column_lines(columns)
    turns = [t[j : j + 1, :] for j in range(3) for t in (cosine_turns, sine_turns)]
    for i in range(2):
        copies[i].wait()
        butterflies(image, turns, zhi, zlo, i * rows // 2, rows // 2)
    for copy in copies[2:4]:
        copy.wait()

    def product(first, lines, table, here):
        top = zhi[first : first + lines].reshape(lines * rows, size)
        rest = zlo[first : first + lines].reshape(lines * rows, size)
        total = jnp.dot(top, matrix[table, :, here], preferred_element_type=jnp.float32)
        total += jnp.dot(top, matrix[table + 1, :, here], preferred_element_type=jnp.float32)
        return total + jnp.dot(rest, matrix[table, :, here], preferred_element_type=jnp.float32)

    mixed = product(2, 6, 2, slice(None))
    for copy in copies[4:]:
        copy.wait()
    spectrum = [product(0, 1, 0, slice(0, size)), product(1, 1, 0, slice(size, 2 * size))]
    for j in range(3):
        real, imag = mixed[2 * j * rows : (2 * j + 1) * rows], mixed[(2 * j + 1) * rows : (2 * j + 2) * rows]
        spectrum += [real[:, :size] + imag[:, size:], imag[:, :size] - real[:, size:]]
    facts = (squares, ramp, turns, angles, defocus, starts)
    sends = send_patches(
        slots, slices_owned, spectrum, matrix.at[2], matrix.at[4], columns, facts, scratch, out_refs
    )
    for copy in sends:
        copy.wait()


def column_filtered(slots, slices_owned, image, angles, defocus, starts):
    rows, columns = image.shape
    size = columns // RADIX
    count = len(slots)
    matrices = jnp.asarray(column_tables(columns))
    away = pl.BlockSpec(memory_space=pl.ANY)
    flops = 2 * rows * size * size * (42 + 14 * count)
    sent = pl.pallas_call(
        functools.partial(column_kernel, slots, slices_owned),
        out_shape=[jax.ShapeDtypeStruct(packed_shape(rows), jnp.bfloat16)] * count,
        in_specs=[away] * 5,
        out_specs=[away] * count,
        scratch_shapes=[
            pltpu.VMEM((rows, columns), jnp.bfloat16),
            pltpu.VMEM(matrices.shape, jnp.bfloat16),
            pltpu.SMEM(angles.shape, jnp.float32),
            pltpu.SMEM(defocus.shape, jnp.int32),
            pltpu.SMEM(starts.shape, jnp.int32),
            pltpu.VMEM((8, rows, size), jnp.bfloat16),
            pltpu.VMEM((8, rows, size), jnp.bfloat16),
            pltpu.VMEM((2, count * rows, size), jnp.float32),
            pltpu.VMEM((6, count * rows, 2 * size), jnp.float32),
            pltpu.VMEM((count * rows, columns), jnp.float32),
            pltpu.VMEM((count, *packed_shape(rows)), jnp.bfloat16),
            pltpu.SemaphoreType.DMA((count,)),
            pltpu.SemaphoreType.DMA((10,)),
        ],
        compiler_params=pltpu.CompilerParams(vmem_limit_bytes=60 * 2**20),
        cost_estimate=pl.CostEstimate(flops=flops, bytes_accessed=3 * 2**20, transcendentals=0),
        name="column_filter",
    )(image, matrices, angles, defocus, starts)
    return dict(zip(slots, sent))


def after(array, *others):
    away = pl.BlockSpec(memory_space=pl.ANY)
    return pl.pallas_call(
        lambda *refs: None,
        out_shape=jax.ShapeDtypeStruct(array.shape, array.dtype),
        in_specs=[away] * (1 + len(others)),
        out_specs=away,
        input_output_aliases={0: 0},
        compiler_params=pltpu.CompilerParams(vmem_limit_bytes=2**20),
        cost_estimate=pl.CostEstimate(flops=0, bytes_accessed=0, transcendentals=0),
        name="after",
    )(array, *others)


def prepare_kernel(slots, slices_owned, angles, defocus, waves, rows_ref, weights_ref, mine, order):
    tilt, row = lax.axis_index("tilt"), lax.axis_index("row")
    slab, local_first = tilt * slices_owned // SLAB, tilt * slices_owned % SLAB
    full_rows = waves.shape[1]
    rows = rows_ref.shape[0] // slots
    half = full_rows // 2
    column = lax.broadcasted_iota(jnp.int32, (8, full_rows), 1)
    freq = jnp.where(column <= half, column, column - half)
    count = jnp.where((freq == 0) | (freq == half), 1.0, 2.0) / full_rows
    scales = [(flip_sign(freq * freq, defocus[tilt ^ slot, slab], full_rows) * count)[:1] for slot in range(slots)]
    for part in range(2):
        for block in range(full_rows // rows):
            there = pl.ds(pl.multiple_of((row ^ block) * rows, rows), rows)
            order[part, block * rows : (block + 1) * rows, :] = waves[part, there, :]
        own = order[part, :rows, :].astype(jnp.float32)
        for slot in range(slots):
            mine[part, slot * rows : (slot + 1) * rows, :] = (own * scales[slot]).astype(jnp.bfloat16)

    def product(left, right):
        over = (((1,), (1,)), ((), ()))
        return lax.dot_general(mine[left], order[right], over, preferred_element_type=jnp.float32)

    rows_ref[...] = (product(0, 0) + product(0, 1) + product(1, 0)).astype(jnp.bfloat16)

    place = lax.broadcasted_iota(jnp.int32, (REACH, XBW), 0).astype(jnp.float32)
    across = lax.broadcasted_iota(jnp.int32, (1, XBW), 1).astype(jnp.float32)
    for slot in range(slots):
        cosine, sine, first_tap = reach_of(angles[tilt ^ slot])
        tap = place + first_tap.astype(jnp.float32)

        def one_slice(c, carry):
            offset = (local_first + c).astype(jnp.float32) - 0.5 * (SLAB - 1)
            centre = 0.5 * XBW + across * cosine + offset * sine
            there = pl.ds(pl.multiple_of(c * XBW, XBW), XBW)
            weights = jnp.maximum(0.0, 1.0 - jnp.abs(tap - centre))
            weights_ref[slot, :MAIN, there] = weights[:MAIN].astype(jnp.bfloat16)
            rest = jnp.concatenate([weights[MAIN:]] * XBLK, 0)
            weights_ref[slot, MAIN:, there] = rest.astype(jnp.bfloat16)
            return carry

        lax.fori_loop(0, slices_owned, one_slice, 0, unroll=4)


def prepared(slots, slices_owned, rows, full_rows, angles, defocus):
    smem, vmem = pl.BlockSpec(memory_space=pltpu.SMEM), pl.BlockSpec(memory_space=pltpu.VMEM)
    return pl.pallas_call(
        functools.partial(prepare_kernel, slots, slices_owned),
        out_shape=[
            jax.ShapeDtypeStruct((slots * rows, full_rows), jnp.bfloat16),
            jax.ShapeDtypeStruct((slots, MAIN + XBLK * REST, slices_owned * XBW), jnp.bfloat16),
        ],
        in_specs=[smem] * 2 + [vmem],
        out_specs=[vmem] * 2,
        scratch_shapes=[
            pltpu.VMEM((2, slots * rows, full_rows), jnp.bfloat16),
            pltpu.VMEM((2, full_rows, full_rows), jnp.bfloat16),
        ],
        compiler_params=pltpu.CompilerParams(vmem_limit_bytes=32 * 2**20),
        cost_estimate=pl.CostEstimate(flops=2**31, bytes_accessed=6 * 2**20, transcendentals=0),
        name="prepare",
    )(angles, defocus, jnp.asarray(row_tables(full_rows)))


def unpacked(packed):
    rows = 4 * packed.shape[0] // (4 * XBLK + 1)
    beside = packed[XBLK * rows :].astype(jnp.float32)
    quarters = [pltpu.roll(beside, MAIN - q * XBLK * REST, 1) if q else beside for q in range(4)]
    rest = jnp.concatenate(quarters, 0).astype(jnp.bfloat16)
    return jnp.concatenate([packed[block * rows : (block + 1) * rows] for block in range(XBLK)] + [rest], 1)


def corrected_patches(slots, row_devices, rows_ref, patch_refs):
    parts = []
    for group in slots:
        refs, patch_refs = patch_refs[:row_devices], patch_refs[row_devices:]
        height = refs[0].shape[0] // len(group)
        for i, slot in enumerate(group):
            patches = jnp.concatenate([unpacked(ref[i * height : (i + 1) * height]) for ref in refs], 0)
            rows = patches.shape[0] // row_devices
            image = jnp.dot(rows_ref[slot * rows : (slot + 1) * rows, :], patches, preferred_element_type=jnp.float32)
            lane = lax.broadcasted_iota(jnp.int32, (rows, MAIN), 1) // REST
            main = jnp.concatenate([image[:, block * MAIN : (block + 1) * MAIN] for block in range(XBLK)], 0)
            rest = [jnp.where(lane == block, image[:, XBLK * MAIN :], 0.0) for block in range(XBLK)]
            rest = jnp.concatenate(rest, 0)[:, : XBLK * REST]
            parts.append((slot, jnp.concatenate([main, rest], 1).astype(jnp.bfloat16)))
    return parts


def sum_kernel(slots, row_devices, rows_ref, weights_ref, *refs):
    total_ref = refs[-1]
    (slot, part), *others = corrected_patches(slots, row_devices, rows_ref, refs[:-1])
    step = 4 * XBW
    for first in range(0, total_ref.shape[1], step):
        here = slice(first, first + step)
        total = jnp.dot(part, weights_ref[slot, :, here], preferred_element_type=jnp.float32)
        for other, more in others:
            total += jnp.dot(more, weights_ref[other, :, here], preferred_element_type=jnp.float32)
        total_ref[:, here] = total


def finish_kernel(factor, slots, row_devices, rows_ref, weights_ref, total_ref, *refs):
    patch_refs = refs[: len(slots) * row_devices]
    out_ref, out, sems = refs[len(slots) * row_devices :]
    rows = total_ref.shape[0] // XBLK
    parts = corrected_patches(slots, row_devices, rows_ref, patch_refs)
    step = 4
    copies = []
    for group in range(out.shape[0] // step):
        here = slice(group * step * XBW, (group + 1) * step * XBW)
        total = total_ref[:, here]
        for slot, part in parts:
            total += jnp.dot(part, weights_ref[slot, :, here], preferred_element_type=jnp.float32)
        for c in range(step):
            for block in range(XBLK):
                out[group * step + c, :, block * XBW : (block + 1) * XBW] = (
                    factor * total[block * rows : (block + 1) * rows, c * XBW : (c + 1) * XBW]
                ).astype(jnp.bfloat16)
        part = pl.ds(group * step, step)
        copies.append(pltpu.make_async_copy(out.at[part], out_ref.at[part], sems.at[group]))
        copies[-1].start()
    for copy in copies:
        copy.wait()


def interpolation(kernel, slots, weights, row_filters, patches, totals, **call):
    vmem = pl.BlockSpec(memory_space=pltpu.VMEM)
    operands = [row_filters, weights, *totals, *(block for group in patches for block in group)]
    return pl.pallas_call(
        functools.partial(kernel, slots, len(patches[0])),
        in_specs=[vmem] * len(operands),
        compiler_params=pltpu.CompilerParams(vmem_limit_bytes=32 * 2**20),
        cost_estimate=pl.CostEstimate(flops=0, bytes_accessed=0, transcendentals=0),
        **call,
    )(*operands)


def summed(row_filters, weights, patches, slots):
    return interpolation(
        sum_kernel,
        slots,
        weights,
        row_filters,
        patches,
        [],
        out_shape=jax.ShapeDtypeStruct((XBLK * row_filters.shape[0] // weights.shape[0], weights.shape[2]), jnp.float32),
        out_specs=pl.BlockSpec(memory_space=pltpu.VMEM),
        name="sum_early_tilts",
    )


def finished(row_filters, weights, total, patches, slots, factor):
    shape = (weights.shape[2] // XBW, row_filters.shape[0] // weights.shape[0], XBLK * XBW)
    return interpolation(
        functools.partial(finish_kernel, factor),
        slots,
        weights,
        row_filters,
        patches,
        [total],
        out_shape=jax.ShapeDtypeStruct(shape, jnp.bfloat16),
        out_specs=pl.BlockSpec(memory_space=pl.ANY),
        scratch_shapes=[pltpu.VMEM(shape, jnp.bfloat16), pltpu.SemaphoreType.DMA((shape[0] // 4,))],
        name="finish_volume",
    )


def exchange(array, axis, distance):
    count = lax.axis_size(axis)
    return lax.ppermute(array, axis, [(i, i ^ distance) for i in range(count)])


def gather_rows(array, awaited=()):
    blocks = {0: array}
    bit = lax.axis_size("row") // 2
    while bit:
        if bit == 1 and awaited:
            blocks = {d: after(block, *awaited) if d else block for d, block in blocks.items()}
        blocks.update({d ^ bit: exchange(block, "row", bit) for d, block in blocks.items()})
        bit //= 2
    return [blocks[d] for d in sorted(blocks)]


def per_device(projections, tilt_angle, band_start, defocus):
    _, rows, _ = projections.shape
    row_devices, tilt_devices = lax.axis_size("row"), lax.axis_size("tilt")
    slices_owned = SLICES // tilt_devices
    far, near = list(range(tilt_devices - 1, 1, -1)), list(range(min(2, tilt_devices)))
    sent = column_filtered(far + near, slices_owned, projections[0], tilt_angle, defocus, band_start)
    arrived = {d: exchange(sent[d], "tilt", d) if d else sent[d] for d in far + near}
    row_filters, weights = prepared(tilt_devices, slices_owned, rows, rows * row_devices, tilt_angle, defocus)
    early = [gather_rows(jnp.concatenate([arrived[d] for d in near]))]
    total = summed(row_filters, weights, early, [near])
    late = [gather_rows(after(arrived[d], row_filters) if d == far[-1] else arrived[d]) for d in far]
    return finished(row_filters, weights, total, late, [[d] for d in far], 1.0 / math.sqrt(tilt_devices))


def solution(mesh):
    in_specs = (
        P(("group", "tilt"), "row", None),
        P("group"),
        P("group", None, None),
        P("group", None),
    )
    out_specs = P(("group", "tilt"), "row", None)
    return jax.shard_map(
        per_device, mesh=mesh, in_specs=in_specs, out_specs=out_specs, check_vma=False
    )
```

```python
import functools
import math

import jax
import jax.numpy as jnp
import numpy as np
from jax import lax
from jax.experimental import pallas as pl
from jax.experimental.pallas import tpu as pltpu
from jax.sharding import PartitionSpec as P

SLAB = 16
XBW = 128
BAND = 256
XBLK = 4
SLICES = 64
RADIX = 8
MAIN = 128
REST = 8
REACH = MAIN + REST
WINDOW = 384
ROOT = math.sqrt(0.5)


def split(table):
    high = table.astype(jnp.bfloat16)
    return high, (table - high.astype(np.float64)).astype(jnp.bfloat16)


def column_tables(columns):
    size = columns // RADIX
    half = size // 2
    u = np.arange(size)[:, None]

    def angles(freq):
        return 2.0 * np.pi * ((u * freq[None, :]) % columns) / columns

    k0, s0 = RADIX * np.arange(half + 1), RADIX * np.arange(1, half)
    k4 = RADIX * np.arange(half) + 4
    m0 = np.concatenate([np.cos(angles(k0)), -np.sin(angles(s0))], 1)
    m4 = np.concatenate([np.cos(angles(k4)), -np.sin(angles(k4))], 1)
    full = angles(RADIX * np.arange(size))
    waves = np.concatenate([np.cos(full), np.sin(full)], 1)
    ends = np.concatenate([m0, m4], 1)

    matrices = np.stack([*split(ends), *split(waves), np.concatenate([m0.T, m4.T], 1).astype(jnp.bfloat16)])
    return matrices


def column_lines(columns):
    size = columns // RADIX
    half = size // 2
    line = lax.broadcasted_iota(jnp.int32, (8, size), 0)
    u = lax.broadcasted_iota(jnp.int32, (8, size), 1)
    freq = jnp.where(line == 0, RADIX * jnp.where(u <= half, u, u - half), RADIX * (u & (half - 1)) + 4)
    freq = jnp.where(line < 2, freq, RADIX * u + line // 2)
    fold = jnp.minimum(freq, columns - freq)
    count = jnp.where((fold == 0) | (fold == columns // 2), 1.0, 2.0)
    gain = count * (fold.astype(jnp.float32) + 0.5) * (2.0 / (columns * columns))
    angle = (u * (line + 1)).astype(jnp.float32) * (2.0 * math.pi / columns)
    return fold * fold, gain, jnp.cos(angle), jnp.sin(angle)


def row_tables(full_rows):
    half = full_rows // 2
    column = np.arange(full_rows)
    freq = np.where(column <= half, column, column - half)
    angle = 2.0 * np.pi * (np.arange(full_rows)[:, None] * freq[None, :] % full_rows) / full_rows
    return np.stack(split(np.where(column[None, :] <= half, np.cos(angle), np.sin(angle))))


def packed_shape(rows):
    return (XBLK * rows + rows // 4, MAIN)


def flip_sign(squares, defocus, length):
    cycles = lax.div(squares * defocus, jnp.int32(length * length))
    return (1 - 2 * (cycles & 1)).astype(jnp.float32)


def fetched(sources, targets, sems):
    copies = [pltpu.make_async_copy(s, t, sems.at[i]) for i, (s, t) in enumerate(zip(sources, targets))]
    for copy in copies:
        copy.start()
    return copies


def reach_of(angle):
    line = jnp.full((8, XBW), angle, jnp.float32)
    cosine, sine = jnp.cos(line), jnp.sin(line)
    lowest = 0.5 * XBW + jnp.minimum((XBW - 1) * cosine, 0.0) - 0.5 * (SLAB - 1) * jnp.abs(sine)
    first = jnp.clip(jnp.floor(lowest) - 2.0, 0.0, float(BAND - REACH))
    return cosine[:1], sine[:1], jnp.max(first).astype(jnp.int32)


def butterflies(image, turns, zhi, zlo):
    rows, columns = image.shape
    size = columns // RADIX

    def step(i, carry):
        here = pl.ds(pl.multiple_of(i * 16, 16), 16)
        x = [image[here, m * size : (m + 1) * size].astype(jnp.float32) for m in range(8)]
        p0, p1, p2, p3 = (x[m] + x[m + 4] for m in range(4))
        q0, q1, q2, q3 = (x[m] - x[m + 4] for m in range(4))
        e, f = p0 + p2, p1 + p3
        g, h = ROOT * (q1 - q3), ROOT * (q1 + q3)
        z = [e + f, e - f]
        for j, (real, imag) in enumerate([(q0 + g, -q2 - h), (p0 - p2, p3 - p1), (q0 - g, q2 - h)]):
            c, s = turns[2 * j], turns[2 * j + 1]
            z += [real * c + imag * s, imag * c - real * s]
        for line in range(8):
            top = z[line].astype(jnp.bfloat16)
            zhi[line, here, :] = top
            zlo[line, here, :] = (z[line] - top.astype(jnp.float32)).astype(jnp.bfloat16)
        return carry

    lax.fori_loop(0, rows // 16, step, 0)


def inverse_butterflies(ends, waves, turns, turned, first, rows):
    columns = turned.shape[1]
    size = columns // RADIX
    for top in range(first, first + rows, 8):
        here = slice(top, top + 8)
        r, s = [], []
        for j in range(3):
            c, d = turns[2 * j], turns[2 * j + 1]
            real = waves[2 * j, here, :size] - waves[2 * j + 1, here, size:]
            imag = waves[2 * j, here, size:] + waves[2 * j + 1, here, :size]
            r.append(real * c - imag * d)
            s.append(real * d + imag * c)
        e, f = ends[0, here, :] + ends[1, here, :], ends[0, here, :] - ends[1, here, :]
        a, b, c, d = r[0] + r[2], r[0] - r[2], s[0] + s[2], s[0] - s[2]
        even0, even2, odd1, odd3 = e + r[1], e - r[1], f - s[1], f + s[1]
        g, h = ROOT * (b - c), ROOT * (b + c)
        out = [even0 + a, odd1 + g, even2 - d, odd3 - h, even0 - a, odd1 - g, even2 + d, odd3 + h]
        for m in range(8):
            turned[here, m * size : (m + 1) * size] = out[m]


def send_patches(slots, slices_owned, spectrum, wave_table, end_table, columns, facts, scratch, out_refs):
    squares, ramp, turns, angles, defocus, starts = facts
    ends, waves, turned, out, out_sems = scratch
    rows, size = spectrum[0].shape
    tilt = lax.axis_index("tilt")
    lane = lax.broadcasted_iota(jnp.int32, (rows, MAIN), 1) // REST
    _, _, first_tap = reach_of(angles[tilt])
    slabs = [(tilt ^ slot) * slices_owned // SLAB for slot in slots]

    def transform(k):
        slab = slabs[k]
        mine = slice(k * rows, (k + 1) * rows)
        gain = flip_sign(squares, defocus[tilt, slab], columns) * ramp
        filtered = [(spectrum[i] * gain[i : i + 1, :]).astype(jnp.bfloat16) for i in range(8)]
        for i in range(2):
            table = end_table[:, i * size : (i + 1) * size]
            ends[i, mine, :] = jnp.dot(filtered[i], table, preferred_element_type=jnp.float32)
        both = jnp.dot(jnp.concatenate(filtered[2:], 0), wave_table[...], preferred_element_type=jnp.float32)
        for i in range(6):
            waves[i, mine, :] = both[i * rows : (i + 1) * rows]
    sends = []
    for k in range(len(slabs)):
        transform(k)
    for k, slab in enumerate(slabs):
        inverse_butterflies(ends, waves, turns, turned, k * rows, rows)
        rest = jnp.zeros((rows, MAIN), jnp.float32)
        for block in range(XBLK):
            start = starts[tilt, slab, block] + first_tap
            base = pl.multiple_of(jnp.minimum((start // 128) * 128, columns - WINDOW), 128)
            window = turned[k * rows : (k + 1) * rows, pl.ds(base, WINDOW)]
            shift = base - start
            reach = pltpu.roll(window, jnp.where(shift < 0, shift + WINDOW, shift), 1)[:, : 2 * MAIN]
            out[k, block * rows : (block + 1) * rows, :] = reach[:, :MAIN].astype(jnp.bfloat16)
            last = reach[:, MAIN:]
            rest = jnp.where(lane == block, pltpu.roll(last, block * REST, 1) if block else last, rest)
        quarter = rows // 4
        beside = rest[:quarter]
        for q in range(1, 4):
            moved = pltpu.roll(rest[q * quarter : (q + 1) * quarter], q * XBLK * REST, 1)
            beside = jnp.where(lane[:quarter] // XBLK == q, moved, beside)
        out[k, XBLK * rows :, :] = beside.astype(jnp.bfloat16)
        sends.append(pltpu.make_async_copy(out.at[k], out_refs[k], out_sems.at[k]))
        sends[-1].start()
    return sends


def column_kernel(slots, slices_owned, image_ref, matrix_ref, angle_ref, defocus_ref, starts_ref, *refs):
    count = len(slots)
    out_refs = refs[:count]
    image, matrix, angles, defocus, starts, zhi, zlo, *scratch, sems = refs[count:]
    rows, columns = image.shape
    size = columns // RADIX
    copies = fetched(
        [image_ref, angle_ref, defocus_ref, starts_ref] + [matrix_ref.at[i] for i in range(5)],
        [image, angles, defocus, starts] + [matrix.at[i] for i in range(5)],
        sems,
    )
    squares, ramp, cosine_turns, sine_turns = column_lines(columns)
    turns = [t[j : j + 1, :] for j in range(3) for t in (cosine_turns, sine_turns)]
    copies[0].wait()
    butterflies(image, turns, zhi, zlo)
    for copy in copies[4:8]:
        copy.wait()

    def product(first, lines, table, here):
        top = zhi[first : first + lines].reshape(lines * rows, size)
        rest = zlo[first : first + lines].reshape(lines * rows, size)
        total = jnp.dot(top, matrix[table, :, here], preferred_element_type=jnp.float32)
        total += jnp.dot(top, matrix[table + 1, :, here], preferred_element_type=jnp.float32)
        return total + jnp.dot(rest, matrix[table, :, here], preferred_element_type=jnp.float32)

    spectrum = [product(0, 1, 0, slice(0, size)), product(1, 1, 0, slice(size, 2 * size))]
    mixed = product(2, 6, 2, slice(None))
    for j in range(3):
        real, imag = mixed[2 * j * rows : (2 * j + 1) * rows], mixed[(2 * j + 1) * rows : (2 * j + 2) * rows]
        spectrum += [real[:, :size] + imag[:, size:], imag[:, :size] - real[:, size:]]
    for copy in copies[1:4] + copies[8:]:
        copy.wait()
    facts = (squares, ramp, turns, angles, defocus, starts)
    sends = send_patches(
        slots, slices_owned, spectrum, matrix.at[2], matrix.at[4], columns, facts, scratch, out_refs
    )
    for copy in sends:
        copy.wait()


def column_filtered(slots, slices_owned, image, angles, defocus, starts):
    rows, columns = image.shape
    size = columns // RADIX
    count = len(slots)
    matrices = jnp.asarray(column_tables(columns))
    away = pl.BlockSpec(memory_space=pl.ANY)
    flops = 2 * rows * size * size * (42 + 14 * count)
    sent = pl.pallas_call(
        functools.partial(column_kernel, slots, slices_owned),
        out_shape=[jax.ShapeDtypeStruct(packed_shape(rows), jnp.bfloat16)] * count,
        in_specs=[away] * 5,
        out_specs=[away] * count,
        scratch_shapes=[
            pltpu.VMEM((rows, columns), jnp.bfloat16),
            pltpu.VMEM(matrices.shape, jnp.bfloat16),
            pltpu.SMEM(angles.shape, jnp.float32),
            pltpu.SMEM(defocus.shape, jnp.int32),
            pltpu.SMEM(starts.shape, jnp.int32),
            pltpu.VMEM((8, rows, size), jnp.bfloat16),
            pltpu.VMEM((8, rows, size), jnp.bfloat16),
            pltpu.VMEM((2, count * rows, size), jnp.float32),
            pltpu.VMEM((6, count * rows, 2 * size), jnp.float32),
            pltpu.VMEM((count * rows, columns), jnp.float32),
            pltpu.VMEM((count, *packed_shape(rows)), jnp.bfloat16),
            pltpu.SemaphoreType.DMA((count,)),
            pltpu.SemaphoreType.DMA((9,)),
        ],
        compiler_params=pltpu.CompilerParams(vmem_limit_bytes=60 * 2**20),
        cost_estimate=pl.CostEstimate(flops=flops, bytes_accessed=3 * 2**20, transcendentals=0),
        name="column_filter",
    )(image, matrices, angles, defocus, starts)
    return dict(zip(slots, sent))


def after(array, *others):
    away = pl.BlockSpec(memory_space=pl.ANY)
    return pl.pallas_call(
        lambda *refs: None,
        out_shape=jax.ShapeDtypeStruct(array.shape, array.dtype),
        in_specs=[away] * (1 + len(others)),
        out_specs=away,
        input_output_aliases={0: 0},
        compiler_params=pltpu.CompilerParams(vmem_limit_bytes=2**20),
        cost_estimate=pl.CostEstimate(flops=0, bytes_accessed=0, transcendentals=0),
        name="after",
    )(array, *others)


def prepare_kernel(slots, slices_owned, angles, defocus, waves, rows_ref, weights_ref, mine, order):
    tilt, row = lax.axis_index("tilt"), lax.axis_index("row")
    slab, local_first = tilt * slices_owned // SLAB, tilt * slices_owned % SLAB
    full_rows = waves.shape[1]
    rows = rows_ref.shape[0] // slots
    half = full_rows // 2
    column = lax.broadcasted_iota(jnp.int32, (8, full_rows), 1)
    freq = jnp.where(column <= half, column, column - half)
    count = jnp.where((freq == 0) | (freq == half), 1.0, 2.0) / full_rows
    scales = [(flip_sign(freq * freq, defocus[tilt ^ slot, slab], full_rows) * count)[:1] for slot in range(slots)]
    for part in range(2):
        for block in range(full_rows // rows):
            there = pl.ds(pl.multiple_of((row ^ block) * rows, rows), rows)
            order[part, block * rows : (block + 1) * rows, :] = waves[part, there, :]
        own = order[part, :rows, :].astype(jnp.float32)
        for slot in range(slots):
            mine[part, slot * rows : (slot + 1) * rows, :] = (own * scales[slot]).astype(jnp.bfloat16)

    def product(left, right):
        over = (((1,), (1,)), ((), ()))
        return lax.dot_general(mine[left], order[right], over, preferred_element_type=jnp.float32)

    rows_ref[...] = (product(0, 0) + product(0, 1) + product(1, 0)).astype(jnp.bfloat16)

    place = lax.broadcasted_iota(jnp.int32, (REACH, XBW), 0).astype(jnp.float32)
    across = lax.broadcasted_iota(jnp.int32, (1, XBW), 1).astype(jnp.float32)
    for slot in range(slots):
        cosine, sine, first_tap = reach_of(angles[tilt ^ slot])
        tap = place + first_tap.astype(jnp.float32)

        def one_slice(c, carry):
            offset = (local_first + c).astype(jnp.float32) - 0.5 * (SLAB - 1)
            centre = 0.5 * XBW + across * cosine + offset * sine
            there = pl.ds(pl.multiple_of(c * XBW, XBW), XBW)
            weights = jnp.maximum(0.0, 1.0 - jnp.abs(tap - centre))
            weights_ref[slot, :MAIN, there] = weights[:MAIN].astype(jnp.bfloat16)
            rest = jnp.concatenate([weights[MAIN:]] * XBLK, 0)
            weights_ref[slot, MAIN:, there] = rest.astype(jnp.bfloat16)
            return carry

        lax.fori_loop(0, slices_owned, one_slice, 0, unroll=2)


def prepared(slots, slices_owned, rows, full_rows, angles, defocus):
    smem, vmem = pl.BlockSpec(memory_space=pltpu.SMEM), pl.BlockSpec(memory_space=pltpu.VMEM)
    return pl.pallas_call(
        functools.partial(prepare_kernel, slots, slices_owned),
        out_shape=[
            jax.ShapeDtypeStruct((slots * rows, full_rows), jnp.bfloat16),
            jax.ShapeDtypeStruct((slots, MAIN + XBLK * REST, slices_owned * XBW), jnp.bfloat16),
        ],
        in_specs=[smem] * 2 + [vmem],
        out_specs=[vmem] * 2,
        scratch_shapes=[
            pltpu.VMEM((2, slots * rows, full_rows), jnp.bfloat16),
            pltpu.VMEM((2, full_rows, full_rows), jnp.bfloat16),
        ],
        compiler_params=pltpu.CompilerParams(vmem_limit_bytes=32 * 2**20),
        cost_estimate=pl.CostEstimate(flops=2**31, bytes_accessed=6 * 2**20, transcendentals=0),
        name="prepare",
    )(angles, defocus, jnp.asarray(row_tables(full_rows)))


def unpacked(packed):
    rows = 4 * packed.shape[0] // (4 * XBLK + 1)
    beside = packed[XBLK * rows :].astype(jnp.float32)
    quarters = [pltpu.roll(beside, MAIN - q * XBLK * REST, 1) if q else beside for q in range(4)]
    rest = jnp.concatenate(quarters, 0).astype(jnp.bfloat16)
    return jnp.concatenate([packed[block * rows : (block + 1) * rows] for block in range(XBLK)] + [rest], 1)


def corrected_patches(slots, row_devices, rows_ref, patch_refs):
    parts = []
    for group in slots:
        refs, patch_refs = patch_refs[:row_devices], patch_refs[row_devices:]
        height = refs[0].shape[0] // len(group)
        for i, slot in enumerate(group):
            patches = jnp.concatenate([unpacked(ref[i * height : (i + 1) * height]) for ref in refs], 0)
            rows = patches.shape[0] // row_devices
            image = jnp.dot(rows_ref[slot * rows : (slot + 1) * rows, :], patches, preferred_element_type=jnp.float32)
            lane = lax.broadcasted_iota(jnp.int32, (rows, MAIN), 1) // REST
            main = jnp.concatenate([image[:, block * MAIN : (block + 1) * MAIN] for block in range(XBLK)], 0)
            rest = [jnp.where(lane == block, image[:, XBLK * MAIN :], 0.0) for block in range(XBLK)]
            rest = jnp.concatenate(rest, 0)[:, : XBLK * REST]
            parts.append((slot, jnp.concatenate([main, rest], 1).astype(jnp.bfloat16)))
    return parts


def sum_kernel(slots, row_devices, rows_ref, weights_ref, *refs):
    total_ref = refs[-1]
    (slot, part), *others = corrected_patches(slots, row_devices, rows_ref, refs[:-1])
    step = 4 * XBW
    for first in range(0, total_ref.shape[1], step):
        here = slice(first, first + step)
        total = jnp.dot(part, weights_ref[slot, :, here], preferred_element_type=jnp.float32)
        for other, more in others:
            total += jnp.dot(more, weights_ref[other, :, here], preferred_element_type=jnp.float32)
        total_ref[:, here] = total


def finish_kernel(factor, slots, row_devices, rows_ref, weights_ref, total_ref, *refs):
    patch_refs = refs[: len(slots) * row_devices]
    out_ref, out, sems = refs[len(slots) * row_devices :]
    rows = total_ref.shape[0] // XBLK
    parts = corrected_patches(slots, row_devices, rows_ref, patch_refs)
    step = 4
    copies = []
    for group in range(out.shape[0] // step):
        here = slice(group * step * XBW, (group + 1) * step * XBW)
        total = total_ref[:, here]
        for slot, part in parts:
            total += jnp.dot(part, weights_ref[slot, :, here], preferred_element_type=jnp.float32)
        for c in range(step):
            for block in range(XBLK):
                out[group * step + c, :, block * XBW : (block + 1) * XBW] = (
                    factor * total[block * rows : (block + 1) * rows, c * XBW : (c + 1) * XBW]
                ).astype(jnp.bfloat16)
        part = pl.ds(group * step, step)
        copies.append(pltpu.make_async_copy(out.at[part], out_ref.at[part], sems.at[group]))
        copies[-1].start()
    for copy in copies:
        copy.wait()


def interpolation(kernel, slots, weights, row_filters, patches, totals, **call):
    vmem = pl.BlockSpec(memory_space=pltpu.VMEM)
    operands = [row_filters, weights, *totals, *(block for group in patches for block in group)]
    return pl.pallas_call(
        functools.partial(kernel, slots, len(patches[0])),
        in_specs=[vmem] * len(operands),
        compiler_params=pltpu.CompilerParams(vmem_limit_bytes=32 * 2**20),
        cost_estimate=pl.CostEstimate(flops=0, bytes_accessed=0, transcendentals=0),
        **call,
    )(*operands)


def summed(row_filters, weights, patches, slots):
    return interpolation(
        sum_kernel,
        slots,
        weights,
        row_filters,
        patches,
        [],
        out_shape=jax.ShapeDtypeStruct((XBLK * row_filters.shape[0] // weights.shape[0], weights.shape[2]), jnp.float32),
        out_specs=pl.BlockSpec(memory_space=pltpu.VMEM),
        name="sum_early_tilts",
    )


def finished(row_filters, weights, total, patches, slots, factor):
    shape = (weights.shape[2] // XBW, row_filters.shape[0] // weights.shape[0], XBLK * XBW)
    return interpolation(
        functools.partial(finish_kernel, factor),
        slots,
        weights,
        row_filters,
        patches,
        [total],
        out_shape=jax.ShapeDtypeStruct(shape, jnp.bfloat16),
        out_specs=pl.BlockSpec(memory_space=pl.ANY),
        scratch_shapes=[pltpu.VMEM(shape, jnp.bfloat16), pltpu.SemaphoreType.DMA((shape[0] // 4,))],
        name="finish_volume",
    )


def exchange(array, axis, distance):
    count = lax.axis_size(axis)
    return lax.ppermute(array, axis, [(i, i ^ distance) for i in range(count)])


def gather_rows(array, awaited=()):
    blocks = {0: array}
    bit = lax.axis_size("row") // 2
    while bit:
        if bit == 1 and awaited:
            blocks = {d: after(block, *awaited) if d else block for d, block in blocks.items()}
        blocks.update({d ^ bit: exchange(block, "row", bit) for d, block in blocks.items()})
        bit //= 2
    return [blocks[d] for d in sorted(blocks)]


def per_device(projections, tilt_angle, band_start, defocus):
    _, rows, _ = projections.shape
    row_devices, tilt_devices = lax.axis_size("row"), lax.axis_size("tilt")
    slices_owned = SLICES // tilt_devices
    far, near = list(range(tilt_devices - 1, 1, -1)), list(range(min(2, tilt_devices)))
    sent = column_filtered(far + near, slices_owned, projections[0], tilt_angle, defocus, band_start)
    arrived = {d: exchange(sent[d], "tilt", d) if d else sent[d] for d in far + near}
    row_filters, weights = prepared(tilt_devices, slices_owned, rows, rows * row_devices, tilt_angle, defocus)
    early = [gather_rows(jnp.concatenate([arrived[d] for d in near]))]
    total = summed(row_filters, weights, early, [near])
    late = [gather_rows(after(arrived[d], row_filters) if d == far[-1] else arrived[d]) for d in far]
    return finished(row_filters, weights, total, late, [[d] for d in far], 1.0 / math.sqrt(tilt_devices))


def solution(mesh):
    in_specs = (
        P(("group", "tilt"), "row", None),
        P("group"),
        P("group", None, None),
        P("group", None),
    )
    out_specs = P(("group", "tilt"), "row", None)
    return jax.shard_map(
        per_device, mesh=mesh, in_specs=in_specs, out_specs=out_specs, check_vma=False
    )
```

```python
import functools
import math

import jax
import jax.numpy as jnp
import numpy as np
from jax import lax
from jax.experimental import pallas as pl
from jax.experimental.pallas import tpu as pltpu
from jax.sharding import PartitionSpec as P

SLAB = 16
XBW = 128
BAND = 256
XBLK = 4
SLICES = 64
RADIX = 8
MAIN = 128
REST = 8
REACH = MAIN + REST
WINDOW = 384
ROOT = math.sqrt(0.5)


def split(table):
    high = table.astype(jnp.bfloat16)
    return high, (table - high.astype(np.float64)).astype(jnp.bfloat16)


def column_tables(columns):
    size = columns // RADIX
    half = size // 2
    u = np.arange(size)[:, None]

    def angles(freq):
        return 2.0 * np.pi * ((u * freq[None, :]) % columns) / columns

    k0, s0 = RADIX * np.arange(half + 1), RADIX * np.arange(1, half)
    k4 = RADIX * np.arange(half) + 4
    m0 = np.concatenate([np.cos(angles(k0)), -np.sin(angles(s0))], 1)
    m4 = np.concatenate([np.cos(angles(k4)), -np.sin(angles(k4))], 1)
    full = angles(RADIX * np.arange(size))
    waves = np.concatenate([np.cos(full), np.sin(full)], 1)
    ends = np.concatenate([m0, m4], 1)

    matrices = np.stack([*split(ends), *split(waves), np.concatenate([m0.T, m4.T], 1).astype(jnp.bfloat16)])
    return matrices


def column_lines(columns):
    size = columns // RADIX
    half = size // 2
    line = lax.broadcasted_iota(jnp.int32, (8, size), 0)
    u = lax.broadcasted_iota(jnp.int32, (8, size), 1)
    freq = jnp.where(line == 0, RADIX * jnp.where(u <= half, u, u - half), RADIX * (u & (half - 1)) + 4)
    freq = jnp.where(line < 2, freq, RADIX * u + line // 2)
    fold = jnp.minimum(freq, columns - freq)
    count = jnp.where((fold == 0) | (fold == columns // 2), 1.0, 2.0)
    gain = count * (fold.astype(jnp.float32) + 0.5) * (2.0 / (columns * columns))
    angle = (u * (line + 1)).astype(jnp.float32) * (2.0 * math.pi / columns)
    return fold * fold, gain, jnp.cos(angle), jnp.sin(angle)


def row_tables(full_rows):
    half = full_rows // 2
    column = np.arange(full_rows)
    freq = np.where(column <= half, column, column - half)
    angle = 2.0 * np.pi * (np.arange(full_rows)[:, None] * freq[None, :] % full_rows) / full_rows
    return np.stack(split(np.where(column[None, :] <= half, np.cos(angle), np.sin(angle))))


def packed_shape(rows):
    return (XBLK * rows + rows // 4, MAIN)


def flip_sign(squares, defocus, length):
    cycles = lax.div(squares * defocus, jnp.int32(length * length))
    return (1 - 2 * (cycles & 1)).astype(jnp.float32)


def fetched(sources, targets, sems):
    copies = [pltpu.make_async_copy(s, t, sems.at[i]) for i, (s, t) in enumerate(zip(sources, targets))]
    for copy in copies:
        copy.start()
    return copies


def reach_of(angle):
    line = jnp.full((8, XBW), angle, jnp.float32)
    cosine, sine = jnp.cos(line), jnp.sin(line)
    lowest = 0.5 * XBW + jnp.minimum((XBW - 1) * cosine, 0.0) - 0.5 * (SLAB - 1) * jnp.abs(sine)
    first = jnp.clip(jnp.floor(lowest) - 2.0, 0.0, float(BAND - REACH))
    return cosine[:1], sine[:1], jnp.max(first).astype(jnp.int32)


def butterflies(image, turns, zhi, zlo):
    rows, columns = image.shape
    size = columns // RADIX

    def step(i, carry):
        here = pl.ds(pl.multiple_of(i * 16, 16), 16)
        x = [image[here, m * size : (m + 1) * size].astype(jnp.float32) for m in range(8)]
        p0, p1, p2, p3 = (x[m] + x[m + 4] for m in range(4))
        q0, q1, q2, q3 = (x[m] - x[m + 4] for m in range(4))
        e, f = p0 + p2, p1 + p3
        g, h = ROOT * (q1 - q3), ROOT * (q1 + q3)
        z = [e + f, e - f]
        for j, (real, imag) in enumerate([(q0 + g, -q2 - h), (p0 - p2, p3 - p1), (q0 - g, q2 - h)]):
            c, s = turns[2 * j], turns[2 * j + 1]
            z += [real * c + imag * s, imag * c - real * s]
        for line in range(8):
            top = z[line].astype(jnp.bfloat16)
            zhi[line, here, :] = top
            zlo[line, here, :] = (z[line] - top.astype(jnp.float32)).astype(jnp.bfloat16)
        return carry

    lax.fori_loop(0, rows // 16, step, 0)


def inverse_butterflies(ends, waves, turns, turned, first, rows):
    columns = turned.shape[1]
    size = columns // RADIX
    for top in range(first, first + rows, 8):
        here = slice(top, top + 8)
        r, s = [], []
        for j in range(3):
            c, d = turns[2 * j], turns[2 * j + 1]
            real = waves[2 * j, here, :size] - waves[2 * j + 1, here, size:]
            imag = waves[2 * j, here, size:] + waves[2 * j + 1, here, :size]
            r.append(real * c - imag * d)
            s.append(real * d + imag * c)
        e, f = ends[0, here, :] + ends[1, here, :], ends[0, here, :] - ends[1, here, :]
        a, b, c, d = r[0] + r[2], r[0] - r[2], s[0] + s[2], s[0] - s[2]
        even0, even2, odd1, odd3 = e + r[1], e - r[1], f - s[1], f + s[1]
        g, h = ROOT * (b - c), ROOT * (b + c)
        out = [even0 + a, odd1 + g, even2 - d, odd3 - h, even0 - a, odd1 - g, even2 + d, odd3 + h]
        for m in range(8):
            turned[here, m * size : (m + 1) * size] = out[m]


def send_patches(slots, slices_owned, spectrum, wave_table, end_table, columns, facts, scratch, out_refs):
    squares, ramp, turns, angles, defocus, starts = facts
    ends, waves, turned, out, out_sems = scratch
    rows, size = spectrum[0].shape
    tilt = lax.axis_index("tilt")
    lane = lax.broadcasted_iota(jnp.int32, (rows, MAIN), 1) // REST
    _, _, first_tap = reach_of(angles[tilt])
    slabs = [(tilt ^ slot) * slices_owned // SLAB for slot in slots]

    def transform(k):
        slab = slabs[k]
        mine = slice(k * rows, (k + 1) * rows)
        gain = flip_sign(squares, defocus[tilt, slab], columns) * ramp
        filtered = [(spectrum[i] * gain[i : i + 1, :]).astype(jnp.bfloat16) for i in range(8)]
        for i in range(2):
            table = end_table[:, i * size : (i + 1) * size]
            ends[i, mine, :] = jnp.dot(filtered[i], table, preferred_element_type=jnp.float32)
        both = jnp.dot(jnp.concatenate(filtered[2:], 0), wave_table[...], preferred_element_type=jnp.float32)
        for i in range(6):
            waves[i, mine, :] = both[i * rows : (i + 1) * rows]
    sends = []
    transform(0)
    for k, slab in enumerate(slabs):
        if k + 1 < len(slabs):
            transform(k + 1)
        inverse_butterflies(ends, waves, turns, turned, k * rows, rows)
        rest = jnp.zeros((rows, MAIN), jnp.float32)
        for block in range(XBLK):
            start = starts[tilt, slab, block] + first_tap
            base = pl.multiple_of(jnp.minimum((start // 128) * 128, columns - WINDOW), 128)
            window = turned[k * rows : (k + 1) * rows, pl.ds(base, WINDOW)]
            shift = base - start
            reach = pltpu.roll(window, jnp.where(shift < 0, shift + WINDOW, shift), 1)[:, : 2 * MAIN]
            out[k, block * rows : (block + 1) * rows, :] = reach[:, :MAIN].astype(jnp.bfloat16)
            last = reach[:, MAIN:]
            rest = jnp.where(lane == block, pltpu.roll(last, block * REST, 1) if block else last, rest)
        quarter = rows // 4
        beside = rest[:quarter]
        for q in range(1, 4):
            moved = pltpu.roll(rest[q * quarter : (q + 1) * quarter], q * XBLK * REST, 1)
            beside = jnp.where(lane[:quarter] // XBLK == q, moved, beside)
        out[k, XBLK * rows :, :] = beside.astype(jnp.bfloat16)
        sends.append(pltpu.make_async_copy(out.at[k], out_refs[k], out_sems.at[k]))
        sends[-1].start()
    return sends


def column_kernel(slots, slices_owned, image_ref, matrix_ref, angle_ref, defocus_ref, starts_ref, *refs):
    count = len(slots)
    out_refs = refs[:count]
    image, matrix, angles, defocus, starts, zhi, zlo, *scratch, sems = refs[count:]
    rows, columns = image.shape
    size = columns // RADIX
    copies = fetched(
        [image_ref, angle_ref, defocus_ref, starts_ref] + [matrix_ref.at[i] for i in range(5)],
        [image, angles, defocus, starts] + [matrix.at[i] for i in range(5)],
        sems,
    )
    squares, ramp, cosine_turns, sine_turns = column_lines(columns)
    turns = [t[j : j + 1, :] for j in range(3) for t in (cosine_turns, sine_turns)]
    copies[0].wait()
    butterflies(image, turns, zhi, zlo)
    for copy in copies[4:8]:
        copy.wait()

    def product(first, lines, table, here):
        top = zhi[first : first + lines].reshape(lines * rows, size)
        rest = zlo[first : first + lines].reshape(lines * rows, size)
        total = jnp.dot(top, matrix[table, :, here], preferred_element_type=jnp.float32)
        total += jnp.dot(top, matrix[table + 1, :, here], preferred_element_type=jnp.float32)
        return total + jnp.dot(rest, matrix[table, :, here], preferred_element_type=jnp.float32)

    spectrum = [product(0, 1, 0, slice(0, size)), product(1, 1, 0, slice(size, 2 * size))]
    mixed = product(2, 6, 2, slice(None))
    for j in range(3):
        real, imag = mixed[2 * j * rows : (2 * j + 1) * rows], mixed[(2 * j + 1) * rows : (2 * j + 2) * rows]
        spectrum += [real[:, :size] + imag[:, size:], imag[:, :size] - real[:, size:]]
    for copy in copies[1:4] + copies[8:]:
        copy.wait()
    facts = (squares, ramp, turns, angles, defocus, starts)
    sends = send_patches(
        slots, slices_owned, spectrum, matrix.at[2], matrix.at[4], columns, facts, scratch, out_refs
    )
    for copy in sends:
        copy.wait()


def column_filtered(slots, slices_owned, image, angles, defocus, starts):
    rows, columns = image.shape
    size = columns // RADIX
    count = len(slots)
    matrices = jnp.asarray(column_tables(columns))
    away = pl.BlockSpec(memory_space=pl.ANY)
    flops = 2 * rows * size * size * (42 + 14 * count)
    sent = pl.pallas_call(
        functools.partial(column_kernel, slots, slices_owned),
        out_shape=[jax.ShapeDtypeStruct(packed_shape(rows), jnp.bfloat16)] * count,
        in_specs=[away] * 5,
        out_specs=[away] * count,
        scratch_shapes=[
            pltpu.VMEM((rows, columns), jnp.bfloat16),
            pltpu.VMEM(matrices.shape, jnp.bfloat16),
            pltpu.SMEM(angles.shape, jnp.float32),
            pltpu.SMEM(defocus.shape, jnp.int32),
            pltpu.SMEM(starts.shape, jnp.int32),
            pltpu.VMEM((8, rows, size), jnp.bfloat16),
            pltpu.VMEM((8, rows, size), jnp.bfloat16),
            pltpu.VMEM((2, count * rows, size), jnp.float32),
            pltpu.VMEM((6, count * rows, 2 * size), jnp.float32),
            pltpu.VMEM((count * rows, columns), jnp.float32),
            pltpu.VMEM((count, *packed_shape(rows)), jnp.bfloat16),
            pltpu.SemaphoreType.DMA((count,)),
            pltpu.SemaphoreType.DMA((9,)),
        ],
        compiler_params=pltpu.CompilerParams(vmem_limit_bytes=60 * 2**20),
        cost_estimate=pl.CostEstimate(flops=flops, bytes_accessed=3 * 2**20, transcendentals=0),
        name="column_filter",
    )(image, matrices, angles, defocus, starts)
    return dict(zip(slots, sent))


def after(array, *others):
    away = pl.BlockSpec(memory_space=pl.ANY)
    return pl.pallas_call(
        lambda *refs: None,
        out_shape=jax.ShapeDtypeStruct(array.shape, array.dtype),
        in_specs=[away] * (1 + len(others)),
        out_specs=away,
        input_output_aliases={0: 0},
        compiler_params=pltpu.CompilerParams(vmem_limit_bytes=2**20),
        cost_estimate=pl.CostEstimate(flops=0, bytes_accessed=0, transcendentals=0),
        name="after",
    )(array, *others)


def prepare_kernel(slots, slices_owned, angles, defocus, waves, rows_ref, weights_ref, mine, order):
    tilt, row = lax.axis_index("tilt"), lax.axis_index("row")
    slab, local_first = tilt * slices_owned // SLAB, tilt * slices_owned % SLAB
    full_rows = waves.shape[1]
    rows = rows_ref.shape[0] // slots
    half = full_rows // 2
    column = lax.broadcasted_iota(jnp.int32, (8, full_rows), 1)
    freq = jnp.where(column <= half, column, column - half)
    count = jnp.where((freq == 0) | (freq == half), 1.0, 2.0) / full_rows
    scales = [(flip_sign(freq * freq, defocus[tilt ^ slot, slab], full_rows) * count)[:1] for slot in range(slots)]
    for part in range(2):
        for block in range(full_rows // rows):
            there = pl.ds(pl.multiple_of((row ^ block) * rows, rows), rows)
            order[part, block * rows : (block + 1) * rows, :] = waves[part, there, :]
        own = order[part, :rows, :].astype(jnp.float32)
        for slot in range(slots):
            mine[part, slot * rows : (slot + 1) * rows, :] = (own * scales[slot]).astype(jnp.bfloat16)

    def product(left, right):
        over = (((1,), (1,)), ((), ()))
        return lax.dot_general(mine[left], order[right], over, preferred_element_type=jnp.float32)

    rows_ref[...] = (product(0, 0) + product(0, 1) + product(1, 0)).astype(jnp.bfloat16)

    place = lax.broadcasted_iota(jnp.int32, (REACH, XBW), 0).astype(jnp.float32)
    across = lax.broadcasted_iota(jnp.int32, (1, XBW), 1).astype(jnp.float32)
    for slot in range(slots):
        cosine, sine, first_tap = reach_of(angles[tilt ^ slot])
        tap = place + first_tap.astype(jnp.float32)

        def one_slice(c, carry):
            offset = (local_first + c).astype(jnp.float32) - 0.5 * (SLAB - 1)
            centre = 0.5 * XBW + across * cosine + offset * sine
            there = pl.ds(pl.multiple_of(c * XBW, XBW), XBW)
            weights = jnp.maximum(0.0, 1.0 - jnp.abs(tap - centre))
            weights_ref[slot, :MAIN, there] = weights[:MAIN].astype(jnp.bfloat16)
            rest = jnp.concatenate([weights[MAIN:]] * XBLK, 0)
            weights_ref[slot, MAIN:, there] = rest.astype(jnp.bfloat16)
            return carry

        lax.fori_loop(0, slices_owned, one_slice, 0, unroll=2)


def prepared(slots, slices_owned, rows, full_rows, angles, defocus):
    smem, vmem = pl.BlockSpec(memory_space=pltpu.SMEM), pl.BlockSpec(memory_space=pltpu.VMEM)
    return pl.pallas_call(
        functools.partial(prepare_kernel, slots, slices_owned),
        out_shape=[
            jax.ShapeDtypeStruct((slots * rows, full_rows), jnp.bfloat16),
            jax.ShapeDtypeStruct((slots, MAIN + XBLK * REST, slices_owned * XBW), jnp.bfloat16),
        ],
        in_specs=[smem] * 2 + [vmem],
        out_specs=[vmem] * 2,
        scratch_shapes=[
            pltpu.VMEM((2, slots * rows, full_rows), jnp.bfloat16),
            pltpu.VMEM((2, full_rows, full_rows), jnp.bfloat16),
        ],
        compiler_params=pltpu.CompilerParams(vmem_limit_bytes=32 * 2**20),
        cost_estimate=pl.CostEstimate(flops=2**31, bytes_accessed=6 * 2**20, transcendentals=0),
        name="prepare",
    )(angles, defocus, jnp.asarray(row_tables(full_rows)))


def unpacked(packed):
    rows = 4 * packed.shape[0] // (4 * XBLK + 1)
    beside = packed[XBLK * rows :].astype(jnp.float32)
    quarters = [pltpu.roll(beside, MAIN - q * XBLK * REST, 1) if q else beside for q in range(4)]
    rest = jnp.concatenate(quarters, 0).astype(jnp.bfloat16)
    return jnp.concatenate([packed[block * rows : (block + 1) * rows] for block in range(XBLK)] + [rest], 1)


def corrected_patches(slots, row_devices, rows_ref, patch_refs):
    parts = []
    for group in slots:
        refs, patch_refs = patch_refs[:row_devices], patch_refs[row_devices:]
        height = refs[0].shape[0] // len(group)
        for i, slot in enumerate(group):
            patches = jnp.concatenate([unpacked(ref[i * height : (i + 1) * height]) for ref in refs], 0)
            rows = patches.shape[0] // row_devices
            image = jnp.dot(rows_ref[slot * rows : (slot + 1) * rows, :], patches, preferred_element_type=jnp.float32)
            lane = lax.broadcasted_iota(jnp.int32, (rows, MAIN), 1) // REST
            main = jnp.concatenate([image[:, block * MAIN : (block + 1) * MAIN] for block in range(XBLK)], 0)
            rest = [jnp.where(lane == block, image[:, XBLK * MAIN :], 0.0) for block in range(XBLK)]
            rest = jnp.concatenate(rest, 0)[:, : XBLK * REST]
            parts.append((slot, jnp.concatenate([main, rest], 1).astype(jnp.bfloat16)))
    return parts


def sum_kernel(slots, row_devices, rows_ref, weights_ref, *refs):
    total_ref = refs[-1]
    (slot, part), *others = corrected_patches(slots, row_devices, rows_ref, refs[:-1])
    step = 4 * XBW
    for first in range(0, total_ref.shape[1], step):
        here = slice(first, first + step)
        total = jnp.dot(part, weights_ref[slot, :, here], preferred_element_type=jnp.float32)
        for other, more in others:
            total += jnp.dot(more, weights_ref[other, :, here], preferred_element_type=jnp.float32)
        total_ref[:, here] = total


def finish_kernel(factor, slots, row_devices, rows_ref, weights_ref, total_ref, *refs):
    patch_refs = refs[: len(slots) * row_devices]
    out_ref, out, sems = refs[len(slots) * row_devices :]
    rows = total_ref.shape[0] // XBLK
    parts = corrected_patches(slots, row_devices, rows_ref, patch_refs)
    step = 8
    copies = []
    for group in range(out.shape[0] // step):
        here = slice(group * step * XBW, (group + 1) * step * XBW)
        total = total_ref[:, here]
        for slot, part in parts:
            total += jnp.dot(part, weights_ref[slot, :, here], preferred_element_type=jnp.float32)
        for c in range(step):
            for block in range(XBLK):
                out[group * step + c, :, block * XBW : (block + 1) * XBW] = (
                    factor * total[block * rows : (block + 1) * rows, c * XBW : (c + 1) * XBW]
                ).astype(jnp.bfloat16)
        part = pl.ds(group * step, step)
        copies.append(pltpu.make_async_copy(out.at[part], out_ref.at[part], sems.at[group]))
        copies[-1].start()
    for copy in copies:
        copy.wait()


def interpolation(kernel, slots, weights, row_filters, patches, totals, **call):
    vmem = pl.BlockSpec(memory_space=pltpu.VMEM)
    operands = [row_filters, weights, *totals, *(block for group in patches for block in group)]
    return pl.pallas_call(
        functools.partial(kernel, slots, len(patches[0])),
        in_specs=[vmem] * len(operands),
        compiler_params=pltpu.CompilerParams(vmem_limit_bytes=32 * 2**20),
        cost_estimate=pl.CostEstimate(flops=0, bytes_accessed=0, transcendentals=0),
        **call,
    )(*operands)


def summed(row_filters, weights, patches, slots):
    return interpolation(
        sum_kernel,
        slots,
        weights,
        row_filters,
        patches,
        [],
        out_shape=jax.ShapeDtypeStruct((XBLK * row_filters.shape[0] // weights.shape[0], weights.shape[2]), jnp.float32),
        out_specs=pl.BlockSpec(memory_space=pltpu.VMEM),
        name="sum_early_tilts",
    )


def finished(row_filters, weights, total, patches, slots, factor):
    shape = (weights.shape[2] // XBW, row_filters.shape[0] // weights.shape[0], XBLK * XBW)
    return interpolation(
        functools.partial(finish_kernel, factor),
        slots,
        weights,
        row_filters,
        patches,
        [total],
        out_shape=jax.ShapeDtypeStruct(shape, jnp.bfloat16),
        out_specs=pl.BlockSpec(memory_space=pl.ANY),
        scratch_shapes=[pltpu.VMEM(shape, jnp.bfloat16), pltpu.SemaphoreType.DMA((shape[0] // 4,))],
        name="finish_volume",
    )


def exchange(array, axis, distance):
    count = lax.axis_size(axis)
    return lax.ppermute(array, axis, [(i, i ^ distance) for i in range(count)])


def gather_rows(array, awaited=()):
    blocks = {0: array}
    bit = lax.axis_size("row") // 2
    while bit:
        if bit == 1 and awaited:
            blocks = {d: after(block, *awaited) if d else block for d, block in blocks.items()}
        blocks.update({d ^ bit: exchange(block, "row", bit) for d, block in blocks.items()})
        bit //= 2
    return [blocks[d] for d in sorted(blocks)]


def per_device(projections, tilt_angle, band_start, defocus):
    _, rows, _ = projections.shape
    row_devices, tilt_devices = lax.axis_size("row"), lax.axis_size("tilt")
    slices_owned = SLICES // tilt_devices
    far, near = list(range(tilt_devices - 1, 1, -1)), list(range(min(2, tilt_devices)))
    sent = column_filtered(far + near, slices_owned, projections[0], tilt_angle, defocus, band_start)
    arrived = {d: exchange(sent[d], "tilt", d) if d else sent[d] for d in far + near}
    row_filters, weights = prepared(tilt_devices, slices_owned, rows, rows * row_devices, tilt_angle, defocus)
    early = [gather_rows(jnp.concatenate([arrived[d] for d in near]))]
    total = summed(row_filters, weights, early, [near])
    late = [gather_rows(after(arrived[d], row_filters) if d == far[-1] else arrived[d]) for d in far]
    return finished(row_filters, weights, total, late, [[d] for d in far], 1.0 / math.sqrt(tilt_devices))


def solution(mesh):
    in_specs = (
        P(("group", "tilt"), "row", None),
        P("group"),
        P("group", None, None),
        P("group", None),
    )
    out_specs = P(("group", "tilt"), "row", None)
    return jax.shard_map(
        per_device, mesh=mesh, in_specs=in_specs, out_specs=out_specs, check_vma=False
    )
```
